32 devices in a mesh: dp: 8 (over z, x), fsdp: 4 (over y, core).
Axes of the slice: x: 2, y: 2, z: 4, core: 2. Of those that a mesh axis runs over, the one named last changes fastest.
Arguments:
- tokens: bfloat16 [25600, 768], P(('dp', 'fsdp')), may hold values from -6 to 6
- prev_kv: bfloat16 [2, 25600, 768], P(None, ('dp', 'fsdp')), may hold values from -6 to 6
- memory: bfloat16 [2, 6400, 768], P(None, ('dp', 'fsdp')), may hold values from -6 to 6
- valid_frames: int32 [32], P(('dp', 'fsdp')), may hold values from 4 to 8, as said below
- mem_len: int32 [32], P(('dp', 'fsdp')), may hold values from 50 to 200, as said below
- ln1_gain: float32 [768], replicated, may hold values from 0.1 to 1.9
- ln1_bias: float32 [768], replicated, may hold values from -1.75 to 1.75
- w_qkv: bfloat16 [768, 2304], P('dp', 'fsdp'), may hold values from -0.21875 to 0.21875
- qkv_bias: float32 [2304], replicated, may hold values from -1.75 to 1.75
- pool_conv: float32 [3, 27, 96], replicated, may hold values from -1.25 to 1.25
- pool_gain: float32 [3, 96], replicated, may hold values from 0.1 to 1.9
- pool_bias: float32 [3, 96], replicated, may hold values from -1.75 to 1.75
- rel_time: float32 [15, 96], replicated, may hold values from -0.625 to 0.625
- rel_space: float32 [2, 19, 96], replicated, may hold values from -0.625 to 0.625
- compress: float32 [2, 4, 96], replicated, may hold values from -3 to 3
- w_proj: bfloat16 [768, 768], P('dp', 'fsdp'), may hold values from -0.21875 to 0.21875
- proj_bias: float32 [768], replicated, may hold values from -1.75 to 1.75
- ln2_gain: float32 [768], replicated, may hold values from 0.1 to 1.9
- ln2_bias: float32 [768], replicated, may hold values from -1.75 to 1.75
- w_fc1: bfloat16 [768, 3072], P('dp', 'fsdp'), may hold values from -0.21875 to 0.21875
- fc1_bias: float32 [3072], replicated, may hold values from -1.75 to 1.75
- w_fc2: bfloat16 [3072, 768], P('dp', 'fsdp'), may hold values from -0.109375 to 0.109375
- fc2_bias: float32 [768], replicated, may hold values from -1.75 to 1.75
- cotangent: bfloat16 [25600, 768], P(('dp', 'fsdp')), may hold values from -6 to 6
Outputs:
- out: bfloat16 [25600, 768], P(('dp', 'fsdp'))
- grad_tokens: float32 [25600, 768], P(('dp', 'fsdp'))
- grad_ln1_gain: float32 [768], replicated
- grad_ln1_bias: float32 [768], replicated
- grad_w_qkv: float32 [768, 2304], P('dp', 'fsdp')
- grad_qkv_bias: float32 [2304], replicated
- grad_pool_conv: float32 [3, 27, 96], replicated
- grad_pool_gain: float32 [3, 96], replicated
- grad_pool_bias: float32 [3, 96], replicated
- grad_rel_time: float32 [15, 96], replicated
- grad_rel_space: float32 [2, 19, 96], replicated
- grad_compress: float32 [2, 4, 96], replicated
- grad_w_proj: float32 [768, 768], P('dp', 'fsdp')
- grad_proj_bias: float32 [768], replicated
- grad_ln2_gain: float32 [768], replicated
- grad_ln2_bias: float32 [768], replicated
- grad_w_fc1: float32 [768, 3072], P('dp', 'fsdp')
- grad_fc1_bias: float32 [3072], replicated
- grad_w_fc2: float32 [3072, 768], P('dp', 'fsdp')
- grad_fc2_bias: float32 [768], replicated
The draws below stay inside these ranges and needn't reach their ends.
Inputs may be any that keep to these rules, and one draw needn't show every extreme that they name: `valid_frames`: some clip has all 8 frames. `mem_len`: some clip has all 200 memory rows.
All inputs are finite; a program needn't handle non-finite values.
Results may differ from the reference program's by a relative error of at most 0.017.
Values may be sent and summed in bfloat16 or wider, within the bound.
A program may use at most 576 MiB of HBM per device.

```python
from functools import partial
import jax
import jax.numpy as jnp
from jax import lax

D = 768
FF = 3072
HEADS = 8
HEAD_DIM = 96
FRAMES = 8
HEIGHT = 10
WIDTH = 10
ROWS = 800
MEM = 200
CLIPS = 32
TOKENS = 25600


def draw_valid_frames(key, part):
    key = jax.random.fold_in(key, 5)
    count_key, full_key = jax.random.split(key)
    counts = jax.random.randint(count_key, (CLIPS,), FRAMES // 2, FRAMES + 1)
    chosen = jax.random.randint(full_key, (), 0, CLIPS)
    return jnp.where(jnp.arange(CLIPS) == chosen, FRAMES, counts).astype(jnp.int32)


def draw_mem_len(key, part):
    key = jax.random.fold_in(key, 9)
    count_key, full_key = jax.random.split(key)
    counts = jax.random.randint(count_key, (CLIPS,), MEM // 4, MEM + 1)
    chosen = jax.random.randint(full_key, (), 0, CLIPS)
    return jnp.where(jnp.arange(CLIPS) == chosen, MEM, counts).astype(jnp.int32)


def steps_of(own_key, shape, cuts, least, top_value):
    level, own = 1.0, jax.random.fold_in(own_key, 6)
    for dim, shards_of in cuts:
        heights = jnp.exp(jax.random.uniform(jax.random.fold_in(own, dim), (shards_of,), jnp.float32, least / len(cuts), top_value / len(cuts)))
        level = level * jnp.repeat(heights, shape[dim] // shards_of).reshape([-1 if axis == dim else 1 for axis in range(len(shape))])
    return level


def gaussian(own_key, dims, width, reach, cuts=(), kind=jnp.bfloat16):
    entries = jax.random.normal(own_key, dims, jnp.float32) * width
    if len(cuts) > 0:
        entries = steps_of(own_key, dims, cuts, -0.22, 0.18) * entries
    return jnp.clip(entries, min=-reach, max=reach).astype(kind)


def setup_inputs(seed: int = 0) -> dict:
    key_of = jax.random.split(jax.random.key(seed), 25)
    return {
        "tokens": gaussian(key_of[0], (TOKENS, D), 1.0, 6.0, ((0, 32),)),
        "prev_kv": gaussian(key_of[1], (2, TOKENS, D), 1.0, 6.0, ((1, 32),)),
        "memory": gaussian(key_of[2], (2, CLIPS * MEM, D), 1.0, 6.0, ((1, 32),)),
        "valid_frames": draw_valid_frames(jax.random.fold_in(key_of[24], 71), 0),
        "mem_len": draw_mem_len(jax.random.fold_in(key_of[24], 71), 0),
        "ln1_gain": jnp.clip(1.0 + 0.18 * jax.random.normal(key_of[5], (D,), jnp.float32), 0.1, 1.9),
        "ln1_bias": gaussian(key_of[6], (D,), 0.3, 1.75, (), jnp.float32),
        "w_qkv": gaussian(key_of[7], (D, 3 * D), D ** -0.5, 0.21875, ((0, 8), (1, 4))),
        "qkv_bias": gaussian(key_of[8], (3 * D,), 0.3, 1.75, (), jnp.float32),
        "pool_conv": gaussian(key_of[9], (3, 27, HEAD_DIM), 27 ** -0.5, 1.25, (), jnp.float32),
        "pool_gain": jnp.clip(1.0 + 0.18 * jax.random.normal(key_of[10], (3, HEAD_DIM), jnp.float32), 0.1, 1.9),
        "pool_bias": gaussian(key_of[11], (3, HEAD_DIM), 0.3, 1.75, (), jnp.float32),
        "rel_time": gaussian(key_of[12], (2 * FRAMES - 1, HEAD_DIM), 0.1, 0.625, (), jnp.float32),
        "rel_space": gaussian(key_of[13], (2, 2 * HEIGHT - 1, HEAD_DIM), 0.1, 0.625, (), jnp.float32),
        "compress": gaussian(key_of[14], (2, 4, HEAD_DIM), 0.5, 3.0, (), jnp.float32),
        "w_proj": gaussian(key_of[15], (D, D), D ** -0.5, 0.21875, ((0, 8), (1, 4))),
        "proj_bias": gaussian(key_of[16], (D,), 0.3, 1.75, (), jnp.float32),
        "ln2_gain": jnp.clip(1.0 + 0.18 * jax.random.normal(key_of[17], (D,), jnp.float32), 0.1, 1.9),
        "ln2_bias": gaussian(key_of[18], (D,), 0.3, 1.75, (), jnp.float32),
        "w_fc1": gaussian(key_of[19], (D, FF), D ** -0.5, 0.21875, ((0, 8), (1, 4))),
        "fc1_bias": gaussian(key_of[20], (FF,), 0.3, 1.75, (), jnp.float32),
        "w_fc2": gaussian(key_of[21], (FF, D), FF ** -0.5, 0.109375, ((0, 8), (1, 4))),
        "fc2_bias": gaussian(key_of[22], (D,), 0.3, 1.75, (), jnp.float32),
        "cotangent": gaussian(key_of[23], (TOKENS, D), 1.0, 6.0, ((0, 32),)),
    }


@jax.custom_vjp
def low(v):
    return lax.optimization_barrier(v.astype(jnp.bfloat16)).astype(jnp.float32)

@jax.custom_vjp
def low_back(v):
    return v

def low_keep(v):
    return (low(v), None)

def low_pass(kept, grad):
    return (grad,)

def back_keep(v):
    return (v, None)

def back_low(kept, grad):
    return (low(grad),)
low.defvjp(low_keep, low_pass)
low_back.defvjp(back_keep, back_low)
EPSILON = 1e-06
MATMUL_MODE = lax.Precision.HIGHEST

def normalize(values, scale_gain, shift_bias):
    average = lax.optimization_barrier(jnp.mean(values, axis=-1, keepdims=True))
    centred = values - average
    variance = lax.optimization_barrier(jnp.mean(centred * centred, axis=-1, keepdims=True))
    return centred * lax.rsqrt(variance + EPSILON) * scale_gain + shift_bias

def relative_index(length):
    counter = jnp.arange(length, dtype=jnp.int32)
    return counter[:, None] - counter[None, :] + (length - 1)

def attend_head(inputs, key_ok, tables, precision):
    query, keys, values = inputs
    time_table, height_table, width_table = tables
    grid = query.reshape(FRAMES, HEIGHT, WIDTH, HEAD_DIM)
    along_time = low_back(jnp.einsum('thwc,tkc->thwk', grid, time_table, precision=precision))
    along_height = low_back(jnp.einsum('thwc,hkc->thwk', grid, height_table, precision=precision))
    along_width = low_back(jnp.einsum('thwc,wkc->thwk', grid, width_table, precision=precision))
    relative = (along_time[:, :, :, :, None, None] + along_height[:, :, :, None, :, None] + along_width[:, :, :, None, None, :]).reshape(ROWS, ROWS)
    scores = jnp.dot(query, keys.T, precision=precision) * HEAD_DIM ** (-0.5)
    scores = jnp.concatenate([scores[:, :2 * MEM], scores[:, 2 * MEM:] + relative], axis=1)
    scores = low_back(scores)
    scores = jnp.where(key_ok[None, :] > 0, scores, -1000000000.0)
    largest = lax.optimization_barrier(jnp.max(scores, axis=1, keepdims=True))
    weights = jnp.exp(scores - largest)
    probs = low(weights / lax.optimization_barrier(jnp.sum(weights, axis=1, keepdims=True)))
    return jnp.dot(probs, values, precision=precision) + query

def clip_forward(big, small, tokens, previous, older_memory, frames, length, precision):
    w_qkv, w_proj, w_fc1, w_fc2 = big
    ln1_gain, ln1_bias, qkv_bias, pool_conv, pool_gain, pool_bias, rel_time, rel_space, compress, proj_bias, ln2_gain, ln2_bias, fc1_bias, fc2_bias = small
    row_frame = jnp.arange(ROWS, dtype=jnp.int32) // (HEIGHT * WIDTH)
    valid = (row_frame < frames).astype(jnp.float32)
    normed = low(normalize(tokens, ln1_gain, ln1_bias))
    mixed = low_back(jnp.dot(normed, low(w_qkv), precision=precision) + qkv_bias) * valid[:, None]
    grid = mixed.reshape(FRAMES, HEIGHT, WIDTH, 3, HEADS, HEAD_DIM)
    padded = jnp.pad(grid, ((1, 1), (1, 1), (1, 1), (0, 0), (0, 0), (0, 0)))
    pooled = jnp.zeros_like(grid)
    for offset in range(27):
        step_time, step_height, step_width = (offset // 9, offset // 3 % 3, offset % 3)
        window = padded[step_time:step_time + FRAMES, step_height:step_height + HEIGHT, step_width:step_width + WIDTH]
        pooled = pooled + window * pool_conv[:, offset, :][:, None, :]
    pooled = low(low_back(normalize(pooled, pool_gain[:, None, :], pool_bias[:, None, :])))
    heads_first = pooled.reshape(ROWS, 3, HEADS, HEAD_DIM).transpose(1, 2, 0, 3)
    earlier = previous.reshape(2, FRAMES, HEIGHT // 2, 2, WIDTH // 2, 2, HEADS, HEAD_DIM)
    squeezed = jnp.zeros((2, FRAMES, HEIGHT // 2, WIDTH // 2, HEADS, HEAD_DIM), jnp.float32)
    for offset in range(4):
        squeezed = squeezed + earlier[:, :, :, offset // 2, :, offset % 2] * compress[:, offset, :][:, None, None, None, None, :]
    squeezed = low(squeezed).reshape(2, MEM, HEADS, HEAD_DIM).transpose(0, 2, 1, 3)
    older = older_memory.reshape(2, MEM, HEADS, HEAD_DIM).transpose(0, 2, 1, 3)
    keys = jnp.concatenate([older[0], squeezed[0], heads_first[1]], axis=1)
    values = jnp.concatenate([older[1], squeezed[1], heads_first[2]], axis=1)
    key_ok = jnp.concatenate([(jnp.arange(MEM, dtype=jnp.int32) < length).astype(jnp.float32), jnp.ones((MEM,), jnp.float32), valid])
    tables = (low(rel_time[relative_index(FRAMES)]), low(rel_space[0][relative_index(HEIGHT)]), low(rel_space[1][relative_index(WIDTH)]))
    head_fn = jax.checkpoint(partial(attend_head, key_ok=key_ok, tables=tables, precision=precision))
    attended = lax.map(head_fn, (heads_first[0], keys, values))
    attended = low(low_back(attended.transpose(1, 0, 2).reshape(ROWS, D)))
    middle = tokens + low_back(jnp.dot(attended, low(w_proj), precision=precision) + proj_bias)
    hidden = low(normalize(middle, ln2_gain, ln2_bias))
    before = low_back(jnp.dot(hidden, low(w_fc1), precision=precision) + fc1_bias)
    activated = low(jax.nn.gelu(before, approximate=False))
    return middle + jnp.dot(activated, low(w_fc2), precision=precision) + fc2_bias

def reference(tokens, prev_kv, memory, valid_frames, mem_len, ln1_gain, ln1_bias, w_qkv, qkv_bias, pool_conv, pool_gain, pool_bias, rel_time, rel_space, compress, w_proj, proj_bias, ln2_gain, ln2_bias, w_fc1, fc1_bias, w_fc2, fc2_bias, cotangent):
    big = (w_qkv.astype(jnp.float32), w_proj.astype(jnp.float32), w_fc1.astype(jnp.float32), w_fc2.astype(jnp.float32))
    small = (ln1_gain, ln1_bias, qkv_bias, pool_conv, pool_gain, pool_bias, rel_time, rel_space, compress, proj_bias, ln2_gain, ln2_bias, fc1_bias, fc2_bias)
    inputs = tokens.astype(jnp.float32).reshape(CLIPS, ROWS, D)
    earlier = prev_kv.astype(jnp.float32).reshape(2, CLIPS, ROWS, D).transpose(1, 0, 2, 3)
    older = memory.astype(jnp.float32).reshape(2, CLIPS, MEM, D).transpose(1, 0, 2, 3)
    incoming = cotangent.astype(jnp.float32).reshape(CLIPS, ROWS, D)

    def one_clip(totals, item):
        clip_tokens, clip_prev, clip_memory, frames, length, clip_grad = item

        def local(big_terms, small_terms, block_tokens):
            return clip_forward(big_terms, small_terms, block_tokens, clip_prev, clip_memory, frames, length, MATMUL_MODE)
        result, pullback = jax.vjp(local, big, small, clip_tokens)
        big_grads, small_grads, token_grads = pullback(clip_grad)
        totals = jax.tree.map(jnp.add, totals, (big_grads, small_grads))
        return (totals, (result.astype(jnp.bfloat16), token_grads))
    start = jax.tree.map(jnp.zeros_like, (big, small))
    (big_sum, small_sum), (results, token_grads) = lax.scan(one_clip, start, (inputs, earlier, older, valid_frames, mem_len, incoming))
    return (results.reshape(TOKENS, D), token_grads.reshape(TOKENS, D), small_sum[0], small_sum[1], big_sum[0], small_sum[2], small_sum[3], small_sum[4], small_sum[5], small_sum[6], small_sum[7], small_sum[8], big_sum[1], small_sum[9], small_sum[10], small_sum[11], big_sum[2], small_sum[12], big_sum[3], small_sum[13])
```

```python
import functools

import jax
import jax.numpy as jnp
import numpy as np
from jax import lax
from jax.experimental import pallas as pl
from jax.experimental.pallas import tpu as pltpu
from jax.sharding import PartitionSpec as P

D = 768
FF = 3072
HEADS = 8
HEAD_DIM = 96
LANES = 128
FRAMES = 8
HEIGHT = 10
WIDTH = 10
PLACES = HEIGHT * WIDTH
ROWS = 800
MEM = 200
GROUP = 384
GROUP_HEADS = 4
QKV = 3 * D
KEY_ROWS = 1280
MEM_AT = 800
SQUEEZE_AT = 1024
REST = KEY_ROWS - ROWS
TABLE = 384
EPSILON = 1e-06
SCALE = HEAD_DIM**-0.5
ROOT = HEAD_DIM**0.5
LOG2E = 1.4426950408889634
MASKED = -1e9
MASK_LANE = 124
ROW_BLOCK = 160
BF16 = jnp.bfloat16
F32 = jnp.float32
VMEM_LIMIT = 60 * 1024 * 1024


def constants():
    place = np.arange(PLACES).repeat(FRAMES)
    row_t = np.tile(np.arange(FRAMES), PLACES)
    row_i, row_j = place // WIDTH, place % WIDTH
    one_hot = np.zeros((KEY_ROWS, LANES), np.float32)
    rows = np.arange(ROWS)
    one_hot[rows, 96 + row_t] = 1
    one_hot[rows, 104 + row_i] = 1
    one_hot[rows, 114 + row_j] = 1
    own = np.zeros((ROWS, TABLE), np.float32)
    fold = np.zeros((TABLE, LANES), np.float32)
    pick = np.zeros((TABLE, LANES), np.float32)
    for base, length, row_at, lane, offset in (
        (0, FRAMES, row_t, 96, 0),
        (64, HEIGHT, row_i, 104, 15),
        (164, WIDTH, row_j, 114, 34),
    ):
        for a in range(length):
            for b in range(length):
                column = base + a * length + b
                own[:, column] = row_at == a
                fold[column, lane + b] = 1
                pick[column, offset + a - b + length - 1] = 1
    return one_hot, own, fold, pick


def lane_index(shape):
    return lax.broadcasted_iota(jnp.int32, shape, len(shape) - 1)


def dot(a, b, contract=((1,), (0,)), precision=None):
    return lax.dot_general(a, b, (contract, ((), ())), preferred_element_type=F32, precision=precision)


def layer_stats(values, width):
    average = jnp.sum(values, axis=-1, keepdims=True) * (1.0 / width)
    centred = values - average
    variance = jnp.sum(centred * centred, axis=-1, keepdims=True) * (1.0 / width)
    return centred, lax.rsqrt(variance + EPSILON)


def params(**more):
    return pltpu.CompilerParams(vmem_limit_bytes=VMEM_LIMIT, **more)


def whole(shape):
    return pl.BlockSpec(shape, lambda *_: (0,) * len(shape))


def tiles_of(values):
    return [values[:, at : at + LANES] for at in range(0, values.shape[1], LANES)]


def read_place(wide_ref, place):
    parts = [wide_ref[tile, pl.ds(place, FRAMES, stride=PLACES), :] for tile in range(wide_ref.shape[0])]
    return jnp.concatenate(parts, axis=1)


def write_place(wide_ref, place, values):
    for tile, part in enumerate(tiles_of(values)):
        wide_ref[tile, pl.ds(place, FRAMES, stride=PLACES), :] = part


def wide_scratch(columns):
    return pltpu.VMEM((columns // LANES, ROWS, LANES), F32)


def prepare_kernel(
    frames_ref, length_ref, tokens_ref, cot_ref, gain_ref, bias_ref, one_hot_ref, tables_ref, pick_ref,
    x_ref, normed_ref, upstream_ref, aug_ref, table_ref, wide_ref,
):
    def permute(source_ref, target_ref):
        for tile, part in enumerate(tiles_of(source_ref[...])):
            wide_ref[tile] = part.astype(F32)

        @pl.loop(0, PLACES // 2)
        def _(pair):
            first = read_place(wide_ref, 2 * pair)
            second = read_place(wide_ref, 2 * pair + 1)
            at = pl.multiple_of(pair * 16, 16)
            target_ref[pl.ds(at, 16), :] = jnp.concatenate([first, second], axis=0).astype(BF16)

    permute(cot_ref, upstream_ref)
    permute(tokens_ref, x_ref)
    centred, rs = layer_stats(x_ref[...].astype(F32), D)
    normed_ref[...] = (centred * rs * gain_ref[...] + bias_ref[...]).astype(BF16)
    row = lax.broadcasted_iota(jnp.int32, (KEY_ROWS, LANES), 0)
    frames, length = frames_ref[0], length_ref[0]
    place = jnp.where(row < MEM_AT, row & 7, jnp.where(row < SQUEEZE_AT, row - MEM_AT, row - SQUEEZE_AT))
    limit = jnp.where(row < MEM_AT, frames, jnp.where(row < SQUEEZE_AT, length, MEM))
    off = jnp.where(place >= limit, jnp.where(lane_index((KEY_ROWS, LANES)) == MASK_LANE, MASKED, 0.0), 0.0)
    aug_ref[...] = (one_hot_ref[...].astype(F32) + off).astype(BF16)
    table_ref[...] = dot(pick_ref[...], tables_ref[...].astype(BF16)).astype(BF16)


def prepare(frames, length, tokens, cot, gain, bias, one_hot, tables, pick):
    smem = pl.BlockSpec(memory_space=pltpu.SMEM)
    vmem = pl.BlockSpec(memory_space=pltpu.VMEM)
    return pl.pallas_call(
        prepare_kernel,
        out_shape=(
            jax.ShapeDtypeStruct((ROWS, D), BF16),
            jax.ShapeDtypeStruct((ROWS, D), BF16),
            jax.ShapeDtypeStruct((ROWS, D), BF16),
            jax.ShapeDtypeStruct((KEY_ROWS, LANES), BF16),
            jax.ShapeDtypeStruct((TABLE, LANES), BF16),
        ),
        in_specs=[smem, smem] + [vmem] * 7,
        out_specs=(vmem,) * 5,
        scratch_shapes=[wide_scratch(D)],
        compiler_params=params(),
        name="prepare",
    )(frames, length, tokens, cot, gain, bias, one_hot, tables, pick)


def squeeze_kernel(prev_ref, mem_ref, taps_ref, rest_ref, tap_ref, wide_ref, sums_ref, parts_ref):
    for tile, part in enumerate(tiles_of(prev_ref[0])):
        wide_ref[tile] = part.astype(F32)

    @pl.loop(0, HEIGHT // 2)
    def _(i):
        for j in range(WIDTH // 2):
            total = None
            at = pl.multiple_of((i * (WIDTH // 2) + j) * FRAMES, FRAMES)
            for tap in range(4):
                place = (2 * i + tap // 2) * WIDTH + 2 * j + tap % 2
                part = read_place(wide_ref, place)
                parts_ref[tap, pl.ds(at, FRAMES), :] = part
                term = part * taps_ref[0, tap : tap + 1, :]
                total = term if total is None else total + term
            sums_ref[pl.ds(at, FRAMES), :] = total

    def head_of(values, head):
        return values[:, HEAD_DIM * head : HEAD_DIM * head + HEAD_DIM]

    old = mem_ref[0].astype(F32)
    for head in range(GROUP_HEADS):
        rest = jnp.concatenate(
            [
                head_of(old, head),
                jnp.zeros((SQUEEZE_AT - MEM_AT - MEM, HEAD_DIM), F32),
                head_of(sums_ref[...], head),
                jnp.zeros((KEY_ROWS - SQUEEZE_AT - MEM, HEAD_DIM), F32),
            ],
            axis=0,
        )
        rest = jnp.concatenate([rest, jnp.zeros((REST, LANES - HEAD_DIM), F32)], axis=1)
        rest_ref[0, head] = rest.astype(BF16)
        for tap in range(4):
            part = jnp.concatenate([head_of(parts_ref[tap], head), jnp.zeros((8, HEAD_DIM), F32)], axis=0)
            part = jnp.concatenate([part, jnp.zeros((208, LANES - HEAD_DIM), F32)], axis=1)
            tap_ref[0, head, tap] = part.astype(BF16)


def squeeze(prev, memory, taps):
    return pl.pallas_call(
        squeeze_kernel,
        grid=(2, 2),
        out_shape=(
            jax.ShapeDtypeStruct((2, HEADS, REST, LANES), BF16),
            jax.ShapeDtypeStruct((2, HEADS, 4, 208, LANES), BF16),
        ),
        in_specs=[
            pl.BlockSpec((1, ROWS, GROUP), lambda s, g: (s, 0, g)),
            pl.BlockSpec((1, MEM, GROUP), lambda s, g: (s, 0, g)),
            pl.BlockSpec((1, 4, GROUP), lambda s, g: (s, 0, 0)),
        ],
        out_specs=(
            pl.BlockSpec((1, GROUP_HEADS, REST, LANES), lambda s, g: (s, g, 0, 0)),
            pl.BlockSpec((1, GROUP_HEADS, 4, 208, LANES), lambda s, g: (s, g, 0, 0, 0)),
        ),
        scratch_shapes=[
            wide_scratch(GROUP),
            pltpu.VMEM((MEM, GROUP), F32),
            pltpu.VMEM((4, MEM, GROUP), F32),
        ],
        compiler_params=params(),
        name="squeeze",
    )(prev, memory, taps)


def shift_frames(values, step):
    frame = lax.broadcasted_iota(jnp.int32, values.shape, values.ndim - 2)
    moved = pltpu.roll(values, step % FRAMES, values.ndim - 2)
    edge = 0 if step == 1 else FRAMES - 1
    return jnp.where(frame == edge, 0.0, moved)


def convolve(grid_ref, taps_ref, flip, i, lanes):
    sums = [None, None, None]
    for b in range(3):
        for e in range(3):
            window = grid_ref[i + b, e : e + WIDTH, :, lanes]
            for a in range(3):
                tap = 9 * a + 3 * b + e
                term = window * taps_ref[0, 26 - tap if flip else tap, :, lanes][None]
                sums[a] = term if sums[a] is None else sums[a] + term
    return sums[1] + shift_frames(sums[0], 1) + shift_frames(sums[2], -1)


def clear_border(grid_ref):
    grid_ref[...] = jnp.zeros(grid_ref.shape, grid_ref.dtype)


def qkv_kernel(
    frames_ref, normed_ref, shards_ref, qkv_bias_ref, taps_ref, gain_ref, bias_ref,
    heads_ref, vhat_ref, mixed_ref, weight_ref, grid_ref, pooled_ref,
):
    step = pl.program_id(0)

    @pl.when(step == 0)
    def _():
        clear_border(grid_ref)
        columns = shards_ref.shape[3]
        for f in range(shards_ref.shape[1]):
            weight_ref[:, f * columns : (f + 1) * columns] = shards_ref[:, f].reshape(D, columns)

    at = pl.multiple_of(step * GROUP, LANES)
    mixed = dot(normed_ref[...], weight_ref[:, pl.ds(at, GROUP)]) + qkv_bias_ref[...]
    row = lax.broadcasted_iota(jnp.int32, (ROWS, GROUP), 0)
    mixed = jnp.where((row & 7) < frames_ref[0], mixed, 0.0)
    mixed_ref[...] = mixed.astype(BF16)
    grid_ref[1 : HEIGHT + 1, 1 : WIDTH + 1] = mixed.reshape(HEIGHT, WIDTH, FRAMES, GROUP)

    @pl.loop(0, HEIGHT)
    def _(i):
        for tile in range(GROUP // LANES):
            lanes = slice(tile * LANES, tile * LANES + LANES)
            line = convolve(grid_ref, taps_ref, False, i, lanes)
            at = pl.multiple_of(i * WIDTH * FRAMES, WIDTH * FRAMES)
            pooled_ref[pl.ds(at, WIDTH * FRAMES), lanes] = line.reshape(WIDTH * FRAMES, LANES)

    lane = lane_index((ROWS, LANES))
    for head in range(GROUP_HEADS):
        values = pooled_ref[:, HEAD_DIM * head : HEAD_DIM * head + LANES]
        values = jnp.where(lane < HEAD_DIM, values, 0.0)
        average = jnp.sum(values, axis=-1, keepdims=True) * (1.0 / HEAD_DIM)
        centred = jnp.where(lane < HEAD_DIM, values - average, 0.0)
        variance = jnp.sum(centred * centred, axis=-1, keepdims=True) * (1.0 / HEAD_DIM)
        rs = lax.rsqrt(variance + EPSILON)
        vhat = centred * rs
        heads_ref[head] = (vhat * gain_ref[0] + bias_ref[0]).astype(BF16)
        high = rs.astype(BF16).astype(F32)
        extra = jnp.where(lane == HEAD_DIM, high, jnp.where(lane == HEAD_DIM + 1, rs - high, 0.0))
        vhat_ref[head] = (vhat + extra).astype(BF16)


def query_key_value(frames, normed, shards, qkv_bias, taps, gain, bias):
    smem = pl.BlockSpec(memory_space=pltpu.SMEM)
    return pl.pallas_call(
        qkv_kernel,
        grid=(6,),
        out_shape=(
            jax.ShapeDtypeStruct((3 * HEADS, ROWS, LANES), BF16),
            jax.ShapeDtypeStruct((3 * HEADS, ROWS, LANES), BF16),
            jax.ShapeDtypeStruct((ROWS, QKV), BF16),
            jax.ShapeDtypeStruct((D, QKV), BF16),
        ),
        in_specs=[
            smem,
            whole((ROWS, D)),
            whole(shards.shape),
            pl.BlockSpec((1, GROUP), lambda g: (0, g)),
            pl.BlockSpec((1, 27, 8, GROUP), lambda g: (g // 2, 0, 0, 0)),
            pl.BlockSpec((1, 1, LANES), lambda g: (g // 2, 0, 0)),
            pl.BlockSpec((1, 1, LANES), lambda g: (g // 2, 0, 0)),
        ],
        out_specs=(
            pl.BlockSpec((GROUP_HEADS, ROWS, LANES), lambda g: (g, 0, 0)),
            pl.BlockSpec((GROUP_HEADS, ROWS, LANES), lambda g: (g, 0, 0)),
            pl.BlockSpec((ROWS, GROUP), lambda g: (0, g)),
            whole((D, QKV)),
        ),
        scratch_shapes=[
            pltpu.VMEM((HEIGHT + 2, WIDTH + 2, FRAMES, GROUP), F32),
            pltpu.VMEM((ROWS, GROUP + LANES), F32),
        ],
        compiler_params=params(),
        name="query_key_value",
    )(frames, normed, shards, qkv_bias, taps, gain, bias)


def attend_kernel(
    q_ref, k_ref, v_ref, krest_ref, vrest_ref, aug_ref, table_ref, own_ref, fold_ref,
    weights_ref, pv_ref, out_ref, keys_ref, vals_ref, query_ref,
):
    lane = lane_index((KEY_ROWS, LANES))
    keys_ref[:ROWS] = k_ref[0] + aug_ref[:ROWS]
    keys_ref[ROWS:] = krest_ref[0, 0] + aug_ref[ROWS:]
    one = jnp.where(lane == HEAD_DIM, 1.0, 0.0).astype(BF16)
    vals_ref[:ROWS] = v_ref[0] + one[:ROWS]
    vals_ref[ROWS:] = vrest_ref[0, 0] + one[ROWS:]
    query = q_ref[0]
    every = (dot(query, table_ref[...], ((1,), (1,))) * ROOT).astype(BF16) * own_ref[...]
    relative = dot(every, fold_ref[...])
    marked = jnp.where(lane[:ROWS] == MASK_LANE, 1.0, relative)
    query_ref[...] = (query.astype(F32) + marked).astype(BF16)

    @pl.loop(0, ROWS // ROW_BLOCK)
    def _(block):
        rows = pl.ds(pl.multiple_of(block * ROW_BLOCK, ROW_BLOCK), ROW_BLOCK)
        scores = dot(query_ref[rows, :], keys_ref[...], ((1,), (1,)))
        largest = jnp.max(scores, axis=1, keepdims=True)
        weights = jnp.exp2((scores - largest) * (SCALE * LOG2E)).astype(BF16)
        weights_ref[0, rows, :] = weights
        total = dot(weights, vals_ref[...])
        inverse = 1.0 / total[:, HEAD_DIM : HEAD_DIM + 1]
        lane = lane_index((ROW_BLOCK, LANES))
        pv = jnp.where(lane < HEAD_DIM, total * inverse, 0.0)
        out_ref[0, rows, :] = (pv + q_ref[0, rows, :].astype(F32)).astype(BF16)
        high = inverse.astype(BF16).astype(F32)
        extra = jnp.where(lane == HEAD_DIM, high, jnp.where(lane == HEAD_DIM + 1, inverse - high, 0.0))
        pv_ref[0, rows, :] = (pv + extra).astype(BF16)


def attend(heads, rest, aug, table, own, fold):
    head = (1, ROWS, LANES)
    tail = (1, 1, REST, LANES)
    return pl.pallas_call(
        attend_kernel,
        grid=(HEADS,),
        out_shape=(
            jax.ShapeDtypeStruct((HEADS, ROWS, KEY_ROWS), BF16),
            jax.ShapeDtypeStruct((HEADS, ROWS, LANES), BF16),
            jax.ShapeDtypeStruct((HEADS, ROWS, LANES), BF16),
        ),
        in_specs=[
            pl.BlockSpec(head, lambda h: (h, 0, 0)),
            pl.BlockSpec(head, lambda h: (HEADS + h, 0, 0)),
            pl.BlockSpec(head, lambda h: (2 * HEADS + h, 0, 0)),
            pl.BlockSpec(tail, lambda h: (0, h, 0, 0)),
            pl.BlockSpec(tail, lambda h: (1, h, 0, 0)),
            whole((KEY_ROWS, LANES)),
            whole((TABLE, LANES)),
            whole((ROWS, TABLE)),
            whole((TABLE, LANES)),
        ],
        out_specs=(
            pl.BlockSpec((1, ROWS, KEY_ROWS), lambda h: (h, 0, 0)),
            pl.BlockSpec(head, lambda h: (h, 0, 0)),
            pl.BlockSpec(head, lambda h: (h, 0, 0)),
        ),
        scratch_shapes=[
            pltpu.VMEM((KEY_ROWS, LANES), BF16),
            pltpu.VMEM((KEY_ROWS, LANES), BF16),
            pltpu.VMEM((ROWS, LANES), BF16),
        ],
        compiler_params=params(),
        name="attend",
    )(heads, heads, heads, rest, rest, aug, table, own, fold)


CHUNK = 384
CHUNKS = FF // CHUNK


def middle_kernel(
    att_ref, x_ref, up_ref, wp_ref, w1_ref, w2_ref, pb_ref, g2_ref, b2_ref, fb1_ref, fb2_ref,
    out_ref, dmid_ref, datt_ref, gp_ref, gw1_ref, gw2_ref, small_ref, gb1_ref,
    packed_ref, proj_ref, mid_ref, hidden_ref, total_ref, dhid_ref, wide_ref,
):
    step = pl.program_id(0)
    sides = wp_ref.shape[1]
    part = D // sides

    @pl.when(step == 0)
    def _():
        for head in range(HEADS):
            packed_ref[:, HEAD_DIM * head : HEAD_DIM * (head + 1)] = att_ref[head][:, :HEAD_DIM]
        for f in range(sides):
            proj_ref[:, f * part : (f + 1) * part] = wp_ref[:, f].reshape(D, part)
        middle = x_ref[...].astype(F32) + dot(packed_ref[...], proj_ref[...]) + pb_ref[...]
        mid_ref[...] = middle
        centred, rs = layer_stats(middle, D)
        hidden_ref[...] = (centred * rs * g2_ref[...] + b2_ref[...]).astype(BF16)
        total_ref[...] = middle + fb2_ref[...]
        dhid_ref[...] = jnp.zeros((ROWS, D), F32)

    w1 = w1_ref[:, 0].reshape(D, CHUNK)
    w2 = jnp.concatenate([w2_ref[0, f] for f in range(sides)], axis=1)
    before = dot(hidden_ref[...], w1) + fb1_ref[...]
    erf = lax.erf(before * (2.0**-0.5))
    cdf = 0.5 * (1.0 + erf)
    activated = (before * cdf).astype(BF16)
    slope = cdf + before * (jnp.exp(before * before * -0.5) * 0.3989422804014327)
    dbefore = dot(up_ref[...], w2, ((1,), (1,))) * slope
    dbefore_low = dbefore.astype(BF16)
    gb1_ref[...] = jnp.sum(dbefore_low.astype(F32), axis=0, keepdims=True)
    total_ref[...] += dot(activated, w2)
    grad_two = dot(activated, up_ref[...], ((0,), (0,))).astype(BF16)
    for f in range(sides):
        gw2_ref[0, f] = grad_two[:, f * part : (f + 1) * part]
    dhid_ref[...] += dot(dbefore_low, w1, ((1,), (1,)))
    gw1_ref[:, 0] = dot(hidden_ref[...], dbefore_low, ((0,), (0,))).astype(BF16).reshape(gw1_ref.shape[0], -1, CHUNK)

    @pl.when(step == CHUNKS - 1)
    def _():
        @pl.loop(0, PLACES)
        def _(place):
            at = pl.multiple_of(place * FRAMES, FRAMES)
            write_place(wide_ref, place, total_ref[pl.ds(at, FRAMES), :])

        for tile in range(D // LANES):
            out_ref[:, tile * LANES : (tile + 1) * LANES] = wide_ref[tile].astype(BF16)
        upstream = up_ref[...].astype(F32)
        dhidden = dhid_ref[...]
        centred, rs = layer_stats(mid_ref[...], D)
        vhat = centred * rs
        dgain = jnp.sum(dhidden * vhat, axis=0, keepdims=True)
        dbias = jnp.sum(dhidden, axis=0, keepdims=True)
        scaled = dhidden * g2_ref[...]
        first = jnp.sum(scaled, axis=1, keepdims=True) * (1.0 / D)
        second = jnp.sum(scaled * vhat, axis=1, keepdims=True) * (1.0 / D)
        dmiddle = upstream + rs * (scaled - first - vhat * second)
        dmid_ref[...] = dmiddle
        dproj = dmiddle.astype(BF16)
        small_ref[0:1, :] = jnp.sum(dproj.astype(F32), axis=0, keepdims=True)
        small_ref[1:2, :] = dgain
        small_ref[2:3, :] = dbias
        small_ref[3:4, :] = jnp.sum(upstream, axis=0, keepdims=True)
        small_ref[4:8, :] = jnp.zeros((4, D), F32)
        grad_proj = dot(packed_ref[...], dproj, ((0,), (0,))).astype(BF16)
        for f in range(sides):
            gp_ref[:, f] = grad_proj[:, f * part : (f + 1) * part].reshape(gp_ref.shape[0], -1, part)
        datt = dot(dproj, proj_ref[...], ((1,), (1,))).astype(BF16)
        for head in range(HEADS):
            datt_ref[head] = jnp.concatenate(
                [datt[:, HEAD_DIM * head : HEAD_DIM * (head + 1)], jnp.zeros((ROWS, LANES - HEAD_DIM), BF16)],
                axis=1,
            )


def feed_forward(att, x, up, wp, w1, w2, pb, g2, b2, fb1, fb2):
    once = pl.Buffered(1)

    def kept(shape):
        return pl.BlockSpec(shape, lambda *_: (0,) * len(shape), pipeline_mode=once)

    w1_block = (w1.shape[0], 1, w1.shape[2], CHUNK)
    w2_block = (1,) + w2.shape[1:]
    w1_spec = pl.BlockSpec(w1_block, lambda c: (0, c // 2, 0, c % 2))
    w2_spec = pl.BlockSpec(w2_block, lambda c: (c, 0, 0, 0))
    return pl.pallas_call(
        middle_kernel,
        grid=(CHUNKS,),
        out_shape=(
            jax.ShapeDtypeStruct((ROWS, D), BF16),
            jax.ShapeDtypeStruct((ROWS, D), F32),
            jax.ShapeDtypeStruct((HEADS, ROWS, LANES), BF16),
            jax.ShapeDtypeStruct(wp.shape, BF16),
            jax.ShapeDtypeStruct(w1.shape, BF16),
            jax.ShapeDtypeStruct(w2.shape, BF16),
            jax.ShapeDtypeStruct((8, D), F32),
            jax.ShapeDtypeStruct((1, FF), F32),
        ),
        in_specs=[
            kept((HEADS, ROWS, LANES)),
            kept((ROWS, D)),
            kept((ROWS, D)),
            kept(wp.shape),
            w1_spec,
            w2_spec,
            kept((1, D)),
            kept((1, D)),
            kept((1, D)),
            pl.BlockSpec((1, CHUNK), lambda c: (0, c)),
            kept((1, D)),
        ],
        out_specs=(
            kept((ROWS, D)),
            kept((ROWS, D)),
            kept((HEADS, ROWS, LANES)),
            kept(wp.shape),
            w1_spec,
            w2_spec,
            kept((8, D)),
            pl.BlockSpec((1, CHUNK), lambda c: (0, c)),
        ),
        scratch_shapes=[
            pltpu.VMEM((ROWS, D), BF16),
            pltpu.VMEM((D, D), BF16),
            pltpu.VMEM((ROWS, D), F32),
            pltpu.VMEM((ROWS, D), BF16),
            pltpu.VMEM((ROWS, D), F32),
            pltpu.VMEM((ROWS, D), F32),
            wide_scratch(D),
        ],
        compiler_params=params(),
        name="feed_forward",
    )(att, x, up, wp, w1, w2, pb, g2, b2, fb1, fb2)


def attend_back_kernel(
    q_ref, k_ref, v_ref, krest_ref, vrest_ref, aug_ref, table_ref, own_ref, fold_ref, pick_ref,
    weights_ref, pv_ref, datt_ref, parts_ref,
    grads_ref, gtable_ref, gtaps_ref,
    keys_ref, vals_ref, up_ref, slopes_ref, gsum_ref,
):
    step = pl.program_id(0)
    lane = lane_index((KEY_ROWS, LANES))
    row_lane = lane[:ROWS]

    @pl.when(step == 0)
    def _():
        gsum_ref[...] = jnp.zeros((TABLE, LANES), F32)
        gtaps_ref[...] = jnp.zeros((2, 4, LANES), F32)

    keys_ref[:ROWS] = k_ref[0] + aug_ref[:ROWS]
    keys_ref[ROWS:] = krest_ref[0, 0] + aug_ref[ROWS:]
    one = jnp.where((lane >= HEAD_DIM) & (lane < HEAD_DIM + 3), 1.0, 0.0).astype(BF16)
    vals_ref[:ROWS] = v_ref[0] + one[:ROWS]
    vals_ref[ROWS:] = vrest_ref[0, 0] + one[ROWS:]
    pv = pv_ref[0].astype(F32)
    inverse = pv[:, HEAD_DIM : HEAD_DIM + 1] + pv[:, HEAD_DIM + 1 : HEAD_DIM + 2]
    datt = datt_ref[0].astype(F32)
    upstream = (datt * inverse).astype(BF16).astype(F32)
    mean = jnp.sum(upstream * pv, axis=1, keepdims=True)
    high = mean.astype(BF16).astype(F32)
    low = (mean - high).astype(BF16).astype(F32)
    least = mean - high - low
    extra = jnp.where(
        row_lane == HEAD_DIM,
        -high,
        jnp.where(row_lane == HEAD_DIM + 1, -low, jnp.where(row_lane == HEAD_DIM + 2, -least, 0.0)),
    )
    up_ref[...] = (upstream + extra).astype(BF16)

    @pl.loop(0, ROWS // ROW_BLOCK)
    def _(block):
        rows = pl.ds(pl.multiple_of(block * ROW_BLOCK, ROW_BLOCK), ROW_BLOCK)
        dprobs = dot(up_ref[rows, :], vals_ref[...], ((1,), (1,)))
        slopes_ref[rows, :] = (weights_ref[0, rows, :].astype(F32) * dprobs).astype(BF16)

    dvals = dot(weights_ref[0], up_ref[...], ((0,), (0,)))
    dkeys = dot(slopes_ref[...], q_ref[0], ((0,), (0,))) * SCALE
    dquery = dot(slopes_ref[...], keys_ref[...])
    spread = dot(dquery.astype(BF16), fold_ref[...], ((1,), (1,))).astype(BF16) * own_ref[...]
    gsum_ref[...] += dot(spread, q_ref[0], ((0,), (0,)))
    dquery = dquery * SCALE + datt + dot(spread, table_ref[...])
    grads_ref[0, 0] = dquery.astype(BF16)
    grads_ref[1, 0] = dkeys[:ROWS].astype(BF16)
    grads_ref[2, 0] = dvals[:ROWS].astype(BF16)
    for s, whole_grad in ((0, dkeys), (1, dvals)):
        piece = whole_grad[SQUEEZE_AT : SQUEEZE_AT + MEM]
        for tap in range(4):
            product = piece * parts_ref[s, 0, tap].astype(F32)[:MEM]
            gtaps_ref[s, tap : tap + 1, :] += jnp.sum(product, axis=0, keepdims=True)

    @pl.when(step == HEADS - 1)
    def _():
        gtable_ref[...] = dot(pick_ref[...], gsum_ref[...], ((0,), (0,)), lax.Precision.HIGHEST)


def attend_back(heads, rest, aug, table, own, fold, pick, weights, pv, datt, parts):
    head = (1, ROWS, LANES)
    tail = (1, 1, REST, LANES)
    own_head = pl.BlockSpec(head, lambda h: (h, 0, 0))
    return pl.pallas_call(
        attend_back_kernel,
        grid=(HEADS,),
        out_shape=(
            jax.ShapeDtypeStruct((3, HEADS, ROWS, LANES), BF16),
            jax.ShapeDtypeStruct((LANES, LANES), F32),
            jax.ShapeDtypeStruct((2, 4, LANES), F32),
        ),
        in_specs=[
            own_head,
            pl.BlockSpec(head, lambda h: (HEADS + h, 0, 0)),
            pl.BlockSpec(head, lambda h: (2 * HEADS + h, 0, 0)),
            pl.BlockSpec(tail, lambda h: (0, h, 0, 0)),
            pl.BlockSpec(tail, lambda h: (1, h, 0, 0)),
            whole((KEY_ROWS, LANES)),
            whole((TABLE, LANES)),
            whole((ROWS, TABLE)),
            whole((TABLE, LANES)),
            whole((TABLE, LANES)),
            pl.BlockSpec((1, ROWS, KEY_ROWS), lambda h: (h, 0, 0)),
            own_head,
            own_head,
            pl.BlockSpec((2, 1, 4, 208, LANES), lambda h: (0, h, 0, 0, 0)),
        ],
        out_specs=(
            pl.BlockSpec((3, 1, ROWS, LANES), lambda h: (0, h, 0, 0)),
            whole((LANES, LANES)),
            whole((2, 4, LANES)),
        ),
        scratch_shapes=[
            pltpu.VMEM((KEY_ROWS, LANES), BF16),
            pltpu.VMEM((KEY_ROWS, LANES), BF16),
            pltpu.VMEM((ROWS, LANES), BF16),
            pltpu.VMEM((ROWS, KEY_ROWS), BF16),
            pltpu.VMEM((TABLE, LANES), F32),
        ],
        compiler_params=params(),
        name="attend_back",
    )(heads, heads, heads, rest, rest, aug, table, own, fold, pick.astype(F32), weights, pv, datt, parts)


def qkv_back_kernel(
    frames_ref, grads_ref, vhat_ref, mixed_ref, weight_ref, normed_ref, x_ref, dmid_ref, taps_ref, gain_ref, g1_ref,
    gtok_ref, gqkv_ref, gbias_ref, gtaps_ref, gpool_ref, small_ref,
    grid_ref, dgrid_ref, dpool_ref, dmix_ref, dnorm_ref, sums_ref, wide_ref,
):
    step = pl.program_id(0)

    @pl.when(step == 0)
    def _():
        clear_border(grid_ref)
        clear_border(dgrid_ref)
        dnorm_ref[...] = jnp.zeros((ROWS, D), F32)

    lane = lane_index((ROWS, LANES))
    for head in range(GROUP_HEADS):
        dy = grads_ref[0, head].astype(F32)
        dy = jnp.where(lane < HEAD_DIM, dy, 0.0)
        vhat = vhat_ref[head].astype(F32)
        rs = vhat[:, HEAD_DIM : HEAD_DIM + 1] + vhat[:, HEAD_DIM + 1 : HEAD_DIM + 2]
        product = dy * vhat
        gpool_ref[head, 0:1, :] = jnp.sum(product, axis=0, keepdims=True)
        gpool_ref[head, 1:2, :] = jnp.sum(dy, axis=0, keepdims=True)
        scaled = dy * gain_ref[0]
        first = jnp.sum(scaled, axis=1, keepdims=True) * (1.0 / HEAD_DIM)
        second = jnp.sum(product * gain_ref[0], axis=1, keepdims=True) * (1.0 / HEAD_DIM)
        dpool = rs * (scaled - first - vhat * second)
        dpool_ref[:, HEAD_DIM * head : HEAD_DIM * (head + 1)] = dpool[:, :HEAD_DIM]
    dgrid_ref[1 : HEIGHT + 1, 1 : WIDTH + 1] = dpool_ref[...].reshape(HEIGHT, WIDTH, FRAMES, GROUP)
    grid_ref[1 : HEIGHT + 1, 1 : WIDTH + 1] = mixed_ref[...].astype(F32).reshape(HEIGHT, WIDTH, FRAMES, GROUP)
    sums_ref[...] = jnp.zeros(sums_ref.shape, F32)

    @pl.loop(0, HEIGHT)
    def _(i):
        for tile in range(GROUP // LANES):
            lanes = slice(tile * LANES, tile * LANES + LANES)
            line = convolve(dgrid_ref, taps_ref, True, i, lanes)
            frame = lax.broadcasted_iota(jnp.int32, line.shape, 1)
            line = jnp.where(frame < frames_ref[0], line, 0.0)
            at = pl.multiple_of(i * WIDTH * FRAMES, WIDTH * FRAMES)
            dmix_ref[pl.ds(at, WIDTH * FRAMES), lanes] = line.reshape(WIDTH * FRAMES, LANES).astype(BF16)
            own = dgrid_ref[i + 1, 1 : WIDTH + 1, :, lanes]
            moved = (shift_frames(own, -1), own, shift_frames(own, 1))
            for b in range(3):
                for e in range(3):
                    window = grid_ref[i + b, e : e + WIDTH, :, lanes]
                    for a in range(3):
                        tap = 9 * a + 3 * b + e
                        sums_ref[tap, :, lanes] += jnp.sum(window * moved[a], axis=0)

    for tap in range(27):
        gtaps_ref[0, tap : tap + 1, :] = jnp.sum(sums_ref[tap], axis=0, keepdims=True)
    dmixed = dmix_ref[...]
    gbias_ref[...] = jnp.sum(dmixed.astype(F32), axis=0, keepdims=True)
    gqkv_ref[...] = dot(normed_ref[...], dmixed, ((0,), (0,))).astype(BF16)
    dnorm_ref[...] += dot(dmixed, weight_ref[...], ((1,), (1,)))

    @pl.when(step == 5)
    def _():
        dy = dnorm_ref[...]
        centred, rs = layer_stats(x_ref[...].astype(F32), D)
        vhat = centred * rs
        small_ref[0:1, :] = jnp.sum(dy * vhat, axis=0, keepdims=True)
        small_ref[1:2, :] = jnp.sum(dy, axis=0, keepdims=True)
        small_ref[2:8, :] = jnp.zeros((6, D), F32)
        scaled = dy * g1_ref[...]
        first = jnp.sum(scaled, axis=1, keepdims=True) * (1.0 / D)
        second = jnp.sum(scaled * vhat, axis=1, keepdims=True) * (1.0 / D)
        dnorm_ref[...] = dmid_ref[...] + rs * (scaled - first - vhat * second)

        @pl.loop(0, PLACES)
        def _(place):
            at = pl.multiple_of(place * FRAMES, FRAMES)
            write_place(wide_ref, place, dnorm_ref[pl.ds(at, FRAMES), :])

        for tile in range(D // LANES):
            gtok_ref[:, tile * LANES : (tile + 1) * LANES] = wide_ref[tile]


def qkv_back(frames, grads, vhat, mixed, weight, normed, x, dmid, taps, gain, g1):
    smem = pl.BlockSpec(memory_space=pltpu.SMEM)
    once = pl.Buffered(1)

    def kept(shape):
        return pl.BlockSpec(shape, lambda *_: (0,) * len(shape), pipeline_mode=once)

    return pl.pallas_call(
        qkv_back_kernel,
        grid=(6,),
        out_shape=(
            jax.ShapeDtypeStruct((ROWS, D), F32),
            jax.ShapeDtypeStruct((D, QKV), BF16),
            jax.ShapeDtypeStruct((1, QKV), F32),
            jax.ShapeDtypeStruct((6, 27, GROUP), F32),
            jax.ShapeDtypeStruct((3 * HEADS, 2, LANES), F32),
            jax.ShapeDtypeStruct((8, D), F32),
        ),
        in_specs=[
            smem,
            pl.BlockSpec((1, GROUP_HEADS, ROWS, LANES), lambda g: (g // 2, g % 2, 0, 0)),
            pl.BlockSpec((GROUP_HEADS, ROWS, LANES), lambda g: (g, 0, 0)),
            pl.BlockSpec((ROWS, GROUP), lambda g: (0, g)),
            pl.BlockSpec((D, GROUP), lambda g: (0, g)),
            kept((ROWS, D)),
            kept((ROWS, D)),
            kept((ROWS, D)),
            pl.BlockSpec((1, 27, 8, GROUP), lambda g: (g // 2, 0, 0, 0)),
            pl.BlockSpec((1, 1, LANES), lambda g: (g // 2, 0, 0)),
            kept((1, D)),
        ],
        out_specs=(
            kept((ROWS, D)),
            pl.BlockSpec((D, GROUP), lambda g: (0, g)),
            pl.BlockSpec((1, GROUP), lambda g: (0, g)),
            pl.BlockSpec((1, 27, GROUP), lambda g: (g, 0, 0)),
            pl.BlockSpec((GROUP_HEADS, 2, LANES), lambda g: (g, 0, 0)),
            kept((8, D)),
        ),
        scratch_shapes=[
            pltpu.VMEM((HEIGHT + 2, WIDTH + 2, FRAMES, GROUP), F32),
            pltpu.VMEM((HEIGHT + 2, WIDTH + 2, FRAMES, GROUP), F32),
            pltpu.VMEM((ROWS, GROUP), F32),
            pltpu.VMEM((ROWS, GROUP), BF16),
            pltpu.VMEM((ROWS, D), F32),
            pltpu.VMEM((27, FRAMES, GROUP), F32),
            wide_scratch(D),
        ],
        compiler_params=params(),
        name="qkv_back",
    )(frames, grads, vhat, mixed, weight, normed, x, dmid, taps, gain, g1)


def row(vector):
    return vector.reshape(1, -1)


def tiled_lanes(array):
    return jnp.concatenate([array] * GROUP_HEADS, axis=-1)


def head_lanes(array):
    return jnp.pad(array, [(0, 0)] * (array.ndim - 1) + [(0, LANES - HEAD_DIM)])


def clip_work(
    tokens, prev_kv, memory, valid_frames, mem_len, ln1_gain, ln1_bias, qkv_bias, pool_conv, pool_gain, pool_bias,
    rel_time, rel_space, compress, proj_bias, ln2_gain, ln2_bias, fc1_bias, fc2_bias, cotangent, gathered,
):
    one_hot, own, fold, pick = (jnp.asarray(c, BF16) for c in constants())
    tables = jnp.concatenate([rel_time, rel_space[0], rel_space[1]], axis=0)
    tables = jnp.pad(tables, ((0, LANES - tables.shape[0]), (0, LANES - HEAD_DIM)))
    taps = jnp.broadcast_to(tiled_lanes(pool_conv)[:, :, None, :], (3, 27, 8, GROUP))
    gains, biases = head_lanes(pool_gain)[:, None], head_lanes(pool_bias)[:, None]
    x, normed, upstream, aug, table = prepare(
        valid_frames, mem_len, tokens, cotangent, row(ln1_gain), row(ln1_bias), one_hot, tables, pick
    )
    rest, parts = squeeze(prev_kv, memory, tiled_lanes(compress))
    w_qkv, w_proj, w_fc1, w_fc2 = gathered
    heads, vhat, mixed, weight = query_key_value(valid_frames, normed, w_qkv, row(qkv_bias), taps, gains, biases)
    weights, pv, attended = attend(heads, rest, aug, table, own, fold)
    out, dmid, datt, gp, gw1, gw2, small_two, gb1 = feed_forward(
        attended, x, upstream, w_proj, w_fc1, w_fc2, row(proj_bias), row(ln2_gain), row(ln2_bias),
        row(fc1_bias), row(fc2_bias),
    )
    grads, gtable, gcompress = attend_back(heads, rest, aug, table, own, fold, pick, weights, pv, datt, parts)
    gtok, gqkv, gqkv_bias, gtaps, gpool, small_one = qkv_back(
        valid_frames, grads, vhat, mixed, weight, normed, x, dmid, taps, gains, row(ln1_gain)
    )
    gconv = jnp.sum(gtaps.reshape(3, 2, 27, GROUP_HEADS, HEAD_DIM), axis=(1, 3))
    gpool = jnp.sum(gpool.reshape(3, HEADS, 2, LANES), axis=1)[:, :, :HEAD_DIM]
    smalls = (
        small_one[0], small_one[1], gqkv_bias[0], gconv, gpool[:, 0], gpool[:, 1],
        gtable[:15, :HEAD_DIM], gtable[15:53, :HEAD_DIM].reshape(2, 19, HEAD_DIM), gcompress[:, :, :HEAD_DIM],
        small_two[0], small_two[1], small_two[2], gb1[0], small_two[3],
    )
    return out, gtok, (gqkv, gp, gw1, gw2), smalls


DP_BLOCKS = 8


def canonical(gathered, dp, fsdp):
    rows, columns = gathered.shape[2:]
    if dp == DP_BLOCKS:
        return gathered
    joined = gathered.reshape(DP_BLOCKS, dp // DP_BLOCKS, fsdp, rows, columns).transpose(0, 2, 1, 3, 4)
    return joined.reshape(DP_BLOCKS, fsdp, dp // DP_BLOCKS * rows, columns)


def device_blocks(blocks, dp, fsdp):
    rows, columns = blocks.shape[2:]
    if dp == DP_BLOCKS:
        return blocks
    split = blocks.reshape(DP_BLOCKS, fsdp, dp // DP_BLOCKS, rows * DP_BLOCKS // dp, columns).transpose(0, 2, 1, 3, 4)
    return split.reshape(dp, fsdp, rows * DP_BLOCKS // dp, columns)


def on_device(dp, fsdp):
    axes = ("dp", "fsdp")

    def gather(shard):
        flat = lax.all_gather(shard, axes, axis=0, tiled=False)
        return canonical(flat.reshape((dp, fsdp) + shard.shape), dp, fsdp)

    def scatter(blocks):
        split = device_blocks(blocks, dp, fsdp)
        split = split.reshape((dp * fsdp,) + split.shape[2:])
        return lax.psum_scatter(split, axes, scatter_dimension=0, tiled=False).astype(F32)

    def run(
        tokens, prev_kv, memory, valid_frames, mem_len, ln1_gain, ln1_bias, w_qkv, qkv_bias, pool_conv, pool_gain,
        pool_bias, rel_time, rel_space, compress, w_proj, proj_bias, ln2_gain, ln2_bias, w_fc1, fc1_bias, w_fc2,
        fc2_bias, cotangent,
    ):
        gathered = tuple(gather(shard) for shard in (w_qkv, w_proj, w_fc1, w_fc2))
        out, gtok, big, smalls = clip_work(
            tokens, prev_kv, memory, valid_frames, mem_len, ln1_gain, ln1_bias, qkv_bias, pool_conv, pool_gain,
            pool_bias, rel_time, rel_space, compress, proj_bias, ln2_gain, ln2_bias, fc1_bias, fc2_bias, cotangent,
            gathered,
        )
        gqkv, gp, gw1, gw2 = big
        gqkv = gqkv.reshape(DP_BLOCKS, D // DP_BLOCKS, fsdp, QKV // fsdp).transpose(0, 2, 1, 3)
        sums = [scatter(g) for g in (gqkv, gp, gw1, gw2)]
        flat = jnp.concatenate([s.reshape(-1) for s in smalls])
        flat = lax.psum(flat, axes)
        totals, at = [], 0
        for s in smalls:
            totals.append(flat[at : at + s.size].reshape(s.shape))
            at += s.size
        return (
            out, gtok, totals[0], totals[1], sums[0], totals[2], totals[3], totals[4], totals[5], totals[6],
            totals[7], totals[8], sums[1], totals[9], totals[10], totals[11], sums[2], totals[12], sums[3], totals[13],
        )

    return run


def solution(mesh):
    both = P(("dp", "fsdp"))
    rows = P(("dp", "fsdp"), None)
    second = P(None, ("dp", "fsdp"), None)
    blocks = P("dp", "fsdp")
    none = P()
    return jax.shard_map(
        on_device(mesh.shape["dp"], mesh.shape["fsdp"]),
        mesh=mesh,
        in_specs=(
            rows, second, second, both, both, none, none, blocks, none, none, none, none, none, none, none, blocks,
            none, none, none, blocks, none, blocks, none, rows,
        ),
        out_specs=(
            rows, rows, none, none, blocks, none, none, none, none, none, none, none, blocks, none, none, none,
            blocks, none, blocks, none,
        ),
        check_vma=False,
    )
```

```python
import functools

import jax
import jax.numpy as jnp
import numpy as np
from jax import lax
from jax.experimental import pallas as pl
from jax.experimental.pallas import tpu as pltpu
from jax.sharding import PartitionSpec as P

D = 768
FF = 3072
HEADS = 8
HEAD_DIM = 96
LANES = 128
FRAMES = 8
HEIGHT = 10
WIDTH = 10
PLACES = HEIGHT * WIDTH
ROWS = 800
MEM = 200
GROUP = 384
GROUP_HEADS = 4
QKV = 3 * D
KEY_ROWS = 1280
MEM_AT = 800
SQUEEZE_AT = 1024
REST = KEY_ROWS - ROWS
TABLE = 384
EPSILON = 1e-06
SCALE = HEAD_DIM**-0.5
ROOT = HEAD_DIM**0.5
LOG2E = 1.4426950408889634
MASKED = -1e9
MASK_LANE = 124
ROW_BLOCK = 160
BF16 = jnp.bfloat16
F32 = jnp.float32
VMEM_LIMIT = 60 * 1024 * 1024


def constants():
    place = np.arange(PLACES).repeat(FRAMES)
    row_t = np.tile(np.arange(FRAMES), PLACES)
    row_i, row_j = place // WIDTH, place % WIDTH
    one_hot = np.zeros((KEY_ROWS, LANES), np.float32)
    rows = np.arange(ROWS)
    one_hot[rows, 96 + row_t] = 1
    one_hot[rows, 104 + row_i] = 1
    one_hot[rows, 114 + row_j] = 1
    own = np.zeros((ROWS, TABLE), np.float32)
    fold = np.zeros((TABLE, LANES), np.float32)
    pick = np.zeros((TABLE, LANES), np.float32)
    for base, length, row_at, lane, offset in (
        (0, FRAMES, row_t, 96, 0),
        (64, HEIGHT, row_i, 104, 15),
        (164, WIDTH, row_j, 114, 34),
    ):
        for a in range(length):
            for b in range(length):
                column = base + a * length + b
                own[:, column] = row_at == a
                fold[column, lane + b] = 1
                pick[column, offset + a - b + length - 1] = 1
    return one_hot, own, fold, pick


def lane_index(shape):
    return lax.broadcasted_iota(jnp.int32, shape, len(shape) - 1)


def dot(a, b, contract=((1,), (0,)), precision=None):
    return lax.dot_general(a, b, (contract, ((), ())), preferred_element_type=F32, precision=precision)


def layer_stats(values, width):
    average = jnp.sum(values, axis=-1, keepdims=True) * (1.0 / width)
    centred = values - average
    variance = jnp.sum(centred * centred, axis=-1, keepdims=True) * (1.0 / width)
    return centred, lax.rsqrt(variance + EPSILON)


def params(**more):
    return pltpu.CompilerParams(vmem_limit_bytes=VMEM_LIMIT, **more)


def whole(shape):
    return pl.BlockSpec(shape, lambda *_: (0,) * len(shape))


def tiles_of(values):
    return [values[:, at : at + LANES] for at in range(0, values.shape[1], LANES)]


def read_place(wide_ref, place):
    parts = [wide_ref[tile, pl.ds(place, FRAMES, stride=PLACES), :] for tile in range(wide_ref.shape[0])]
    return jnp.concatenate(parts, axis=1)


def write_place(wide_ref, place, values):
    for tile, part in enumerate(tiles_of(values)):
        wide_ref[tile, pl.ds(place, FRAMES, stride=PLACES), :] = part


def wide_scratch(columns):
    return pltpu.VMEM((columns // LANES, ROWS, LANES), F32)


def prepare_kernel(
    frames_ref, length_ref, tokens_ref, cot_ref, gain_ref, bias_ref, one_hot_ref, tables_ref, pick_ref,
    x_ref, normed_ref, upstream_ref, aug_ref, table_ref, wide_ref,
):
    def permute(source_ref, target_ref):
        for tile, part in enumerate(tiles_of(source_ref[...])):
            wide_ref[tile] = part.astype(F32)

        @pl.loop(0, PLACES // 2)
        def _(pair):
            first = read_place(wide_ref, 2 * pair)
            second = read_place(wide_ref, 2 * pair + 1)
            at = pl.multiple_of(pair * 16, 16)
            target_ref[pl.ds(at, 16), :] = jnp.concatenate([first, second], axis=0).astype(BF16)

    permute(cot_ref, upstream_ref)
    permute(tokens_ref, x_ref)
    centred, rs = layer_stats(x_ref[...].astype(F32), D)
    normed_ref[...] = (centred * rs * gain_ref[...] + bias_ref[...]).astype(BF16)
    row = lax.broadcasted_iota(jnp.int32, (KEY_ROWS, LANES), 0)
    frames, length = frames_ref[0], length_ref[0]
    place = jnp.where(row < MEM_AT, row & 7, jnp.where(row < SQUEEZE_AT, row - MEM_AT, row - SQUEEZE_AT))
    limit = jnp.where(row < MEM_AT, frames, jnp.where(row < SQUEEZE_AT, length, MEM))
    off = jnp.where(place >= limit, jnp.where(lane_index((KEY_ROWS, LANES)) == MASK_LANE, MASKED, 0.0), 0.0)
    aug_ref[...] = (one_hot_ref[...].astype(F32) + off).astype(BF16)
    table_ref[...] = dot(pick_ref[...], tables_ref[...].astype(BF16)).astype(BF16)


def prepare(frames, length, tokens, cot, gain, bias, one_hot, tables, pick):
    smem = pl.BlockSpec(memory_space=pltpu.SMEM)
    vmem = pl.BlockSpec(memory_space=pltpu.VMEM)
    return pl.pallas_call(
        prepare_kernel,
        out_shape=(
            jax.ShapeDtypeStruct((ROWS, D), BF16),
            jax.ShapeDtypeStruct((ROWS, D), BF16),
            jax.ShapeDtypeStruct((ROWS, D), BF16),
            jax.ShapeDtypeStruct((KEY_ROWS, LANES), BF16),
            jax.ShapeDtypeStruct((TABLE, LANES), BF16),
        ),
        in_specs=[smem, smem] + [vmem] * 7,
        out_specs=(vmem,) * 5,
        scratch_shapes=[wide_scratch(D)],
        compiler_params=params(),
        name="prepare",
    )(frames, length, tokens, cot, gain, bias, one_hot, tables, pick)


def squeeze_kernel(prev_ref, mem_ref, taps_ref, rest_ref, tap_ref, wide_ref, sums_ref, parts_ref):
    for tile, part in enumerate(tiles_of(prev_ref[0])):
        wide_ref[tile] = part.astype(F32)

    @pl.loop(0, HEIGHT // 2)
    def _(i):
        for j in range(WIDTH // 2):
            total = None
            at = pl.multiple_of((i * (WIDTH // 2) + j) * FRAMES, FRAMES)
            for tap in range(4):
                place = (2 * i + tap // 2) * WIDTH + 2 * j + tap % 2
                part = read_place(wide_ref, place)
                parts_ref[tap, pl.ds(at, FRAMES), :] = part
                term = part * taps_ref[0, tap : tap + 1, :]
                total = term if total is None else total + term
            sums_ref[pl.ds(at, FRAMES), :] = total

    def head_of(values, head):
        return values[:, HEAD_DIM * head : HEAD_DIM * head + HEAD_DIM]

    old = mem_ref[0].astype(F32)
    for head in range(GROUP_HEADS):
        rest = jnp.concatenate(
            [
                head_of(old, head),
                jnp.zeros((SQUEEZE_AT - MEM_AT - MEM, HEAD_DIM), F32),
                head_of(sums_ref[...], head),
                jnp.zeros((KEY_ROWS - SQUEEZE_AT - MEM, HEAD_DIM), F32),
            ],
            axis=0,
        )
        rest = jnp.concatenate([rest, jnp.zeros((REST, LANES - HEAD_DIM), F32)], axis=1)
        rest_ref[0, head] = rest.astype(BF16)
        for tap in range(4):
            part = jnp.concatenate([head_of(parts_ref[tap], head), jnp.zeros((8, HEAD_DIM), F32)], axis=0)
            part = jnp.concatenate([part, jnp.zeros((208, LANES - HEAD_DIM), F32)], axis=1)
            tap_ref[0, head, tap] = part.astype(BF16)


def squeeze(prev, memory, taps):
    return pl.pallas_call(
        squeeze_kernel,
        grid=(2, 2),
        out_shape=(
            jax.ShapeDtypeStruct((2, HEADS, REST, LANES), BF16),
            jax.ShapeDtypeStruct((2, HEADS, 4, 208, LANES), BF16),
        ),
        in_specs=[
            pl.BlockSpec((1, ROWS, GROUP), lambda s, g: (s, 0, g)),
            pl.BlockSpec((1, MEM, GROUP), lambda s, g: (s, 0, g)),
            pl.BlockSpec((1, 4, GROUP), lambda s, g: (s, 0, 0)),
        ],
        out_specs=(
            pl.BlockSpec((1, GROUP_HEADS, REST, LANES), lambda s, g: (s, g, 0, 0)),
            pl.BlockSpec((1, GROUP_HEADS, 4, 208, LANES), lambda s, g: (s, g, 0, 0, 0)),
        ),
        scratch_shapes=[
            wide_scratch(GROUP),
            pltpu.VMEM((MEM, GROUP), F32),
            pltpu.VMEM((4, MEM, GROUP), F32),
        ],
        compiler_params=params(),
        name="squeeze",
    )(prev, memory, taps)


def shift_frames(values, step):
    frame = lax.broadcasted_iota(jnp.int32, values.shape, values.ndim - 2)
    moved = pltpu.roll(values, step % FRAMES, values.ndim - 2)
    edge = 0 if step == 1 else FRAMES - 1
    return jnp.where(frame == edge, 0.0, moved)


def convolve(grid_ref, taps_ref, flip, i, lanes):
    sums = [None, None, None]
    for b in range(3):
        for e in range(3):
            window = grid_ref[i + b, e : e + WIDTH, :, lanes]
            for a in range(3):
                tap = 9 * a + 3 * b + e
                term = window * taps_ref[0, 26 - tap if flip else tap, :, lanes][None]
                sums[a] = term if sums[a] is None else sums[a] + term
    return sums[1] + shift_frames(sums[0], 1) + shift_frames(sums[2], -1)


def clear_border(grid_ref):
    grid_ref[...] = jnp.zeros(grid_ref.shape, grid_ref.dtype)


def relative_bits(place_ref, d, f):
    return {
        "x": (d & 1) ^ place_ref[0],
        "z1": ((d >> 1) & 1) ^ place_ref[1],
        "z2": ((d >> 2) & 1) ^ place_ref[2],
        "y": ((f >> 1) & 1) ^ place_ref[3],
        "c": (f & 1) ^ place_ref[4],
    }


def slot(bits, order):
    return sum(bits[name] << at for at, name in enumerate(order))


def qkv_kernel(
    frames_ref, place_ref, normed_ref, first_ref, second_ref, qkv_bias_ref, taps_ref, gain_ref, bias_ref,
    heads_ref, vhat_ref, mixed_ref, weight_ref, grid_ref, pooled_ref,
):
    step = pl.program_id(0)

    @pl.when(step == 0)
    def _():
        clear_border(grid_ref)
        half, columns = first_ref.shape[1:]
        for f in range(QKV // columns):

            @pl.loop(0, DP_BLOCKS)
            def _(d):
                bits = relative_bits(place_ref, d, f)
                for part, (source_ref, order) in enumerate(((first_ref, ROUTE_ONE), (second_ref, ROUTE_TWO))):
                    at = pl.multiple_of((2 * d + part) * half, half)
                    weight_ref[pl.ds(at, half), f * columns : (f + 1) * columns] = source_ref[slot(bits, order)]

    at = pl.multiple_of(step * GROUP, LANES)
    mixed = dot(normed_ref[...], weight_ref[:, pl.ds(at, GROUP)]) + qkv_bias_ref[...]
    row = lax.broadcasted_iota(jnp.int32, (ROWS, GROUP), 0)
    mixed = jnp.where((row & 7) < frames_ref[0], mixed, 0.0)
    mixed_ref[...] = mixed.astype(BF16)
    grid_ref[1 : HEIGHT + 1, 1 : WIDTH + 1] = mixed.reshape(HEIGHT, WIDTH, FRAMES, GROUP)

    @pl.loop(0, HEIGHT)
    def _(i):
        for tile in range(GROUP // LANES):
            lanes = slice(tile * LANES, tile * LANES + LANES)
            line = convolve(grid_ref, taps_ref, False, i, lanes)
            at = pl.multiple_of(i * WIDTH * FRAMES, WIDTH * FRAMES)
            pooled_ref[pl.ds(at, WIDTH * FRAMES), lanes] = line.reshape(WIDTH * FRAMES, LANES)

    lane = lane_index((ROWS, LANES))
    for head in range(GROUP_HEADS):
        values = pooled_ref[:, HEAD_DIM * head : HEAD_DIM * head + LANES]
        values = jnp.where(lane < HEAD_DIM, values, 0.0)
        average = jnp.sum(values, axis=-1, keepdims=True) * (1.0 / HEAD_DIM)
        centred = jnp.where(lane < HEAD_DIM, values - average, 0.0)
        variance = jnp.sum(centred * centred, axis=-1, keepdims=True) * (1.0 / HEAD_DIM)
        rs = lax.rsqrt(variance + EPSILON)
        vhat = centred * rs
        heads_ref[head] = (vhat * gain_ref[0] + bias_ref[0]).astype(BF16)
        high = rs.astype(BF16).astype(F32)
        extra = jnp.where(lane == HEAD_DIM, high, jnp.where(lane == HEAD_DIM + 1, rs - high, 0.0))
        vhat_ref[head] = (vhat + extra).astype(BF16)


def query_key_value(frames, place, normed, first, second, qkv_bias, taps, gain, bias):
    smem = pl.BlockSpec(memory_space=pltpu.SMEM)
    return pl.pallas_call(
        qkv_kernel,
        grid=(6,),
        out_shape=(
            jax.ShapeDtypeStruct((3 * HEADS, ROWS, LANES), BF16),
            jax.ShapeDtypeStruct((3 * HEADS, ROWS, LANES), BF16),
            jax.ShapeDtypeStruct((ROWS, QKV), BF16),
            jax.ShapeDtypeStruct((D, QKV), BF16),
        ),
        in_specs=[
            smem,
            smem,
            whole((ROWS, D)),
            whole(first.shape),
            whole(second.shape),
            pl.BlockSpec((1, GROUP), lambda g: (0, g)),
            pl.BlockSpec((1, 27, 8, GROUP), lambda g: (g // 2, 0, 0, 0)),
            pl.BlockSpec((1, 1, LANES), lambda g: (g // 2, 0, 0)),
            pl.BlockSpec((1, 1, LANES), lambda g: (g // 2, 0, 0)),
        ],
        out_specs=(
            pl.BlockSpec((GROUP_HEADS, ROWS, LANES), lambda g: (g, 0, 0)),
            pl.BlockSpec((GROUP_HEADS, ROWS, LANES), lambda g: (g, 0, 0)),
            pl.BlockSpec((ROWS, GROUP), lambda g: (0, g)),
            whole((D, QKV)),
        ),
        scratch_shapes=[
            pltpu.VMEM((HEIGHT + 2, WIDTH + 2, FRAMES, GROUP), F32),
            pltpu.VMEM((ROWS, GROUP + LANES), F32),
        ],
        compiler_params=params(),
        name="query_key_value",
    )(frames, place, normed, first, second, qkv_bias, taps, gain, bias)


def attend_kernel(
    q_ref, k_ref, v_ref, krest_ref, vrest_ref, aug_ref, table_ref, own_ref, fold_ref,
    weights_ref, pv_ref, out_ref, keys_ref, vals_ref, query_ref,
):
    lane = lane_index((KEY_ROWS, LANES))
    keys_ref[:ROWS] = k_ref[0] + aug_ref[:ROWS]
    keys_ref[ROWS:] = krest_ref[0, 0] + aug_ref[ROWS:]
    one = jnp.where(lane == HEAD_DIM, 1.0, 0.0).astype(BF16)
    vals_ref[:ROWS] = v_ref[0] + one[:ROWS]
    vals_ref[ROWS:] = vrest_ref[0, 0] + one[ROWS:]
    query = q_ref[0]
    every = (dot(query, table_ref[...], ((1,), (1,))) * ROOT).astype(BF16) * own_ref[...]
    relative = dot(every, fold_ref[...])
    marked = jnp.where(lane[:ROWS] == MASK_LANE, 1.0, relative)
    query_ref[...] = (query.astype(F32) + marked).astype(BF16)

    @pl.loop(0, ROWS // ROW_BLOCK)
    def _(block):
        rows = pl.ds(pl.multiple_of(block * ROW_BLOCK, ROW_BLOCK), ROW_BLOCK)
        scores = dot(query_ref[rows, :], keys_ref[...], ((1,), (1,)))
        largest = jnp.max(scores, axis=1, keepdims=True)
        weights = jnp.exp2((scores - largest) * (SCALE * LOG2E)).astype(BF16)
        weights_ref[0, rows, :] = weights
        total = dot(weights, vals_ref[...])
        inverse = 1.0 / total[:, HEAD_DIM : HEAD_DIM + 1]
        lane = lane_index((ROW_BLOCK, LANES))
        pv = jnp.where(lane < HEAD_DIM, total * inverse, 0.0)
        out_ref[0, rows, :] = (pv + q_ref[0, rows, :].astype(F32)).astype(BF16)
        high = inverse.astype(BF16).astype(F32)
        extra = jnp.where(lane == HEAD_DIM, high, jnp.where(lane == HEAD_DIM + 1, inverse - high, 0.0))
        pv_ref[0, rows, :] = (pv + extra).astype(BF16)


def attend(heads, rest, aug, table, own, fold):
    head = (1, ROWS, LANES)
    tail = (1, 1, REST, LANES)
    return pl.pallas_call(
        attend_kernel,
        grid=(HEADS,),
        out_shape=(
            jax.ShapeDtypeStruct((HEADS, ROWS, KEY_ROWS), BF16),
            jax.ShapeDtypeStruct((HEADS, ROWS, LANES), BF16),
            jax.ShapeDtypeStruct((HEADS, ROWS, LANES), BF16),
        ),
        in_specs=[
            pl.BlockSpec(head, lambda h: (h, 0, 0)),
            pl.BlockSpec(head, lambda h: (HEADS + h, 0, 0)),
            pl.BlockSpec(head, lambda h: (2 * HEADS + h, 0, 0)),
            pl.BlockSpec(tail, lambda h: (0, h, 0, 0)),
            pl.BlockSpec(tail, lambda h: (1, h, 0, 0)),
            whole((KEY_ROWS, LANES)),
            whole((TABLE, LANES)),
            whole((ROWS, TABLE)),
            whole((TABLE, LANES)),
        ],
        out_specs=(
            pl.BlockSpec((1, ROWS, KEY_ROWS), lambda h: (h, 0, 0)),
            pl.BlockSpec(head, lambda h: (h, 0, 0)),
            pl.BlockSpec(head, lambda h: (h, 0, 0)),
        ),
        scratch_shapes=[
            pltpu.VMEM((KEY_ROWS, LANES), BF16),
            pltpu.VMEM((KEY_ROWS, LANES), BF16),
            pltpu.VMEM((ROWS, LANES), BF16),
        ],
        compiler_params=params(),
        name="attend",
    )(heads, heads, heads, rest, rest, aug, table, own, fold)


CHUNK = 384
CHUNKS = FF // CHUNK


def middle_kernel(
    place_ref, att_ref, x_ref, up_ref, wp_ref, w1_ref, w2_ref, pb_ref, g2_ref, b2_ref, fb1_ref, fb2_ref,
    out_ref, dmid_ref, datt_ref, gp_ref, gw1_ref, gw2_ref, small_ref, gb1_ref,
    packed_ref, proj_ref, mid_ref, hidden_ref, total_ref, dhid_ref, wide_ref, w1_scr, w2_scr,
):
    step = pl.program_id(0)
    sides = wp_ref.shape[1]
    part = D // sides
    depth = D // DP_BLOCKS

    @pl.when(step == 0)
    def _():
        for head in range(HEADS):
            packed_ref[:, HEAD_DIM * head : HEAD_DIM * (head + 1)] = att_ref[head][:, :HEAD_DIM]
        for f in range(sides):
            for d in range(DP_BLOCKS):
                rows = slice(d * depth, (d + 1) * depth)
                proj_ref[rows, f * part : f * part + LANES] = wp_ref[d, f, :depth]
                proj_ref[rows, f * part + LANES : (f + 1) * part] = wp_ref[d, f, depth:, : part - LANES]
        middle = x_ref[...].astype(F32) + dot(packed_ref[...], proj_ref[...]) + pb_ref[...]
        mid_ref[...] = middle
        centred, rs = layer_stats(middle, D)
        hidden_ref[...] = (centred * rs * g2_ref[...] + b2_ref[...]).astype(BF16)
        total_ref[...] = middle + fb2_ref[...]
        dhid_ref[...] = jnp.zeros((ROWS, D), F32)

    for tile in range(CHUNK // LANES):
        lanes = slice(tile * LANES, (tile + 1) * LANES)
        for d in range(DP_BLOCKS):
            w1_scr[d * depth : (d + 1) * depth, lanes] = w1_ref[d, 0, tile * depth : (tile + 1) * depth]
        for f in range(sides):
            w2_scr[f * part : (f + 1) * part, lanes] = w2_ref[0, f, tile * part : (tile + 1) * part]
    w1, w2 = w1_scr[...], w2_scr[...]
    before = dot(hidden_ref[...], w1) + fb1_ref[...]
    erf = lax.erf(before * (2.0**-0.5))
    cdf = 0.5 * (1.0 + erf)
    activated = (before * cdf).astype(BF16)
    slope = cdf + before * (jnp.exp(before * before * -0.5) * 0.3989422804014327)
    dbefore = dot(up_ref[...], w2) * slope
    dbefore_low = dbefore.astype(BF16)
    gb1_ref[...] = jnp.sum(dbefore_low.astype(F32), axis=0, keepdims=True)
    total_ref[...] += dot(activated, w2, ((1,), (1,)))
    grad_two = dot(activated, up_ref[...], ((0,), (0,))).astype(BF16)
    for f in range(sides):
        bits = relative_bits(place_ref, 0, f)
        gw2_ref[bits["c"], bits["y"], 0, 0, 0] = grad_two[:, f * part : (f + 1) * part]
    dhid_ref[...] += dot(dbefore_low, w1, ((1,), (1,)))
    grad_one = dot(hidden_ref[...], dbefore_low, ((0,), (0,))).astype(BF16)
    for d in range(DP_BLOCKS):
        bits = relative_bits(place_ref, d, 0)
        gw1_ref[0, bits["x"], 0, bits["z1"], bits["z2"]] = grad_one[d * depth : (d + 1) * depth]

    @pl.when(step == CHUNKS - 1)
    def _():
        @pl.loop(0, PLACES)
        def _(place):
            at = pl.multiple_of(place * FRAMES, FRAMES)
            write_place(wide_ref, place, total_ref[pl.ds(at, FRAMES), :])

        for tile in range(D // LANES):
            out_ref[:, tile * LANES : (tile + 1) * LANES] = wide_ref[tile].astype(BF16)
        upstream = up_ref[...].astype(F32)
        dhidden = dhid_ref[...]
        centred, rs = layer_stats(mid_ref[...], D)
        vhat = centred * rs
        dgain = jnp.sum(dhidden * vhat, axis=0, keepdims=True)
        dbias = jnp.sum(dhidden, axis=0, keepdims=True)
        scaled = dhidden * g2_ref[...]
        first = jnp.sum(scaled, axis=1, keepdims=True) * (1.0 / D)
        second = jnp.sum(scaled * vhat, axis=1, keepdims=True) * (1.0 / D)
        dmiddle = upstream + rs * (scaled - first - vhat * second)
        dmid_ref[...] = dmiddle
        dproj = dmiddle.astype(BF16)
        small_ref[0:1, :] = jnp.sum(dproj.astype(F32), axis=0, keepdims=True)
        small_ref[1:2, :] = dgain
        small_ref[2:3, :] = dbias
        small_ref[3:4, :] = jnp.sum(upstream, axis=0, keepdims=True)
        small_ref[4:8, :] = jnp.zeros((4, D), F32)
        grad_proj = dot(packed_ref[...], dproj, ((0,), (0,))).astype(BF16)
        for d in range(DP_BLOCKS):
            for f in range(sides):
                bits = relative_bits(place_ref, d, f)
                block = grad_proj[d * depth : (d + 1) * depth, f * part : (f + 1) * part]
                gp_ref[bits["c"], bits["y"], bits["x"], bits["z1"], bits["z2"]] = block
        datt = dot(dproj, proj_ref[...], ((1,), (1,))).astype(BF16)
        for head in range(HEADS):
            datt_ref[head] = jnp.concatenate(
                [datt[:, HEAD_DIM * head : HEAD_DIM * (head + 1)], jnp.zeros((ROWS, LANES - HEAD_DIM), BF16)],
                axis=1,
            )


def feed_forward(place, att, x, up, flat, pb, g2, b2, fb1, fb2):
    once = pl.Buffered(1)
    sides = flat.shape[1]
    part, depth = D // sides, D // DP_BLOCKS

    def kept(shape):
        return pl.BlockSpec(shape, lambda *_: (0,) * len(shape), pipeline_mode=once)

    def one_place(c, place):
        return (place[4] ^ ((c // 2) & 1), 0, place[3] ^ (c // 4), 0, 0, 0, c % 2)

    def two_place(c, place):
        return (0, 0, place[0] ^ (c & 1), place[1] ^ ((c >> 1) & 1), place[2] ^ (c >> 2), 0, 0)

    def clear(c, place):
        return (0, c)

    return pl.pallas_call(
        middle_kernel,
        out_shape=(
            jax.ShapeDtypeStruct((ROWS, D), BF16),
            jax.ShapeDtypeStruct((ROWS, D), F32),
            jax.ShapeDtypeStruct((HEADS, ROWS, LANES), BF16),
            jax.ShapeDtypeStruct((2, 2, 2, 2, 2, depth, part), BF16),
            jax.ShapeDtypeStruct((2, 2, 2, 2, 2, depth, FF // sides), BF16),
            jax.ShapeDtypeStruct((2, 2, 2, 2, 2, FF // DP_BLOCKS, part), BF16),
            jax.ShapeDtypeStruct((8, D), F32),
            jax.ShapeDtypeStruct((1, FF), F32),
        ),
        grid_spec=pltpu.PrefetchScalarGridSpec(
            num_scalar_prefetch=1,
            grid=(CHUNKS,),
            in_specs=[
                kept((HEADS, ROWS, LANES)),
                kept((ROWS, D)),
                kept((ROWS, D)),
                pl.BlockSpec((DP_BLOCKS, sides, 2 * depth, LANES), lambda c, place: (0, 0, 6, 0), pipeline_mode=once),
                pl.BlockSpec((DP_BLOCKS, 1, 3 * depth, LANES), lambda c, place: (0, c // 2, c % 2, 0)),
                pl.BlockSpec((1, sides, 3 * part, LANES), lambda c, place: (c, 0, 1, 0)),
                kept((1, D)),
                kept((1, D)),
                kept((1, D)),
                pl.BlockSpec((1, CHUNK), clear),
                kept((1, D)),
            ],
            out_specs=(
                kept((ROWS, D)),
                kept((ROWS, D)),
                kept((HEADS, ROWS, LANES)),
                kept((2, 2, 2, 2, 2, depth, part)),
                pl.BlockSpec((1, 2, 1, 2, 2, depth, CHUNK), one_place),
                pl.BlockSpec((2, 2, 1, 1, 1, FF // DP_BLOCKS, part), two_place),
                kept((8, D)),
                pl.BlockSpec((1, CHUNK), clear),
            ),
            scratch_shapes=[
                pltpu.VMEM((ROWS, D), BF16),
                pltpu.VMEM((D, D), BF16),
                pltpu.VMEM((ROWS, D), F32),
                pltpu.VMEM((ROWS, D), BF16),
                pltpu.VMEM((ROWS, D), F32),
                pltpu.VMEM((ROWS, D), F32),
                wide_scratch(D),
                pltpu.VMEM((D, CHUNK), BF16),
                pltpu.VMEM((D, CHUNK), BF16),
            ],
        ),
        compiler_params=params(),
        name="feed_forward",
    )(place, att, x, up, flat, flat, flat, pb, g2, b2, fb1, fb2)


def attend_back_kernel(
    q_ref, k_ref, v_ref, krest_ref, vrest_ref, aug_ref, table_ref, own_ref, fold_ref, pick_ref,
    weights_ref, pv_ref, datt_ref, parts_ref,
    grads_ref, gtable_ref, gtaps_ref,
    keys_ref, vals_ref, up_ref, slopes_ref, gsum_ref,
):
    step = pl.program_id(0)
    lane = lane_index((KEY_ROWS, LANES))
    row_lane = lane[:ROWS]

    @pl.when(step == 0)
    def _():
        gsum_ref[...] = jnp.zeros((TABLE, LANES), F32)
        gtaps_ref[...] = jnp.zeros((2, 4, LANES), F32)

    keys_ref[:ROWS] = k_ref[0] + aug_ref[:ROWS]
    keys_ref[ROWS:] = krest_ref[0, 0] + aug_ref[ROWS:]
    one = jnp.where((lane >= HEAD_DIM) & (lane < HEAD_DIM + 3), 1.0, 0.0).astype(BF16)
    vals_ref[:ROWS] = v_ref[0] + one[:ROWS]
    vals_ref[ROWS:] = vrest_ref[0, 0] + one[ROWS:]
    pv = pv_ref[0].astype(F32)
    inverse = pv[:, HEAD_DIM : HEAD_DIM + 1] + pv[:, HEAD_DIM + 1 : HEAD_DIM + 2]
    datt = datt_ref[0].astype(F32)
    upstream = (datt * inverse).astype(BF16).astype(F32)
    mean = jnp.sum(upstream * pv, axis=1, keepdims=True)
    high = mean.astype(BF16).astype(F32)
    low = (mean - high).astype(BF16).astype(F32)
    least = mean - high - low
    extra = jnp.where(
        row_lane == HEAD_DIM,
        -high,
        jnp.where(row_lane == HEAD_DIM + 1, -low, jnp.where(row_lane == HEAD_DIM + 2, -least, 0.0)),
    )
    up_ref[...] = (upstream + extra).astype(BF16)

    @pl.loop(0, ROWS // ROW_BLOCK)
    def _(block):
        rows = pl.ds(pl.multiple_of(block * ROW_BLOCK, ROW_BLOCK), ROW_BLOCK)
        dprobs = dot(up_ref[rows, :], vals_ref[...], ((1,), (1,)))
        slopes_ref[rows, :] = (weights_ref[0, rows, :].astype(F32) * dprobs).astype(BF16)

    dvals = dot(weights_ref[0], up_ref[...], ((0,), (0,)))
    dkeys = dot(slopes_ref[...], q_ref[0], ((0,), (0,))) * SCALE
    dquery = dot(slopes_ref[...], keys_ref[...])
    spread = dot(dquery.astype(BF16), fold_ref[...], ((1,), (1,))).astype(BF16) * own_ref[...]
    gsum_ref[...] += dot(spread, q_ref[0], ((0,), (0,)))
    dquery = dquery * SCALE + datt + dot(spread, table_ref[...])
    grads_ref[0, 0] = dquery.astype(BF16)
    grads_ref[1, 0] = dkeys[:ROWS].astype(BF16)
    grads_ref[2, 0] = dvals[:ROWS].astype(BF16)
    for s, whole_grad in ((0, dkeys), (1, dvals)):
        piece = whole_grad[SQUEEZE_AT : SQUEEZE_AT + MEM]
        for tap in range(4):
            product = piece * parts_ref[s, 0, tap].astype(F32)[:MEM]
            gtaps_ref[s, tap : tap + 1, :] += jnp.sum(product, axis=0, keepdims=True)

    @pl.when(step == pl.num_programs(0) - 1)
    def _():
        gtable_ref[...] = dot(pick_ref[...], gsum_ref[...], ((0,), (0,)), lax.Precision.HIGHEST)


def attend_back(start, count, heads, rest, aug, table, own, fold, pick, weights, pv, datt, parts):
    head = (1, ROWS, LANES)
    tail = (1, 1, REST, LANES)
    own_head = pl.BlockSpec(head, lambda h: (start + h, 0, 0))
    return pl.pallas_call(
        attend_back_kernel,
        grid=(count,),
        out_shape=(
            jax.ShapeDtypeStruct((3, count, ROWS, LANES), BF16),
            jax.ShapeDtypeStruct((LANES, LANES), F32),
            jax.ShapeDtypeStruct((2, 4, LANES), F32),
        ),
        in_specs=[
            own_head,
            pl.BlockSpec(head, lambda h: (HEADS + start + h, 0, 0)),
            pl.BlockSpec(head, lambda h: (2 * HEADS + start + h, 0, 0)),
            pl.BlockSpec(tail, lambda h: (0, start + h, 0, 0)),
            pl.BlockSpec(tail, lambda h: (1, start + h, 0, 0)),
            whole((KEY_ROWS, LANES)),
            whole((TABLE, LANES)),
            whole((ROWS, TABLE)),
            whole((TABLE, LANES)),
            whole((TABLE, LANES)),
            pl.BlockSpec((1, ROWS, KEY_ROWS), lambda h: (start + h, 0, 0)),
            own_head,
            own_head,
            pl.BlockSpec((2, 1, 4, 208, LANES), lambda h: (0, start + h, 0, 0, 0)),
        ],
        out_specs=(
            pl.BlockSpec((3, 1, ROWS, LANES), lambda h: (0, h, 0, 0)),
            whole((LANES, LANES)),
            whole((2, 4, LANES)),
        ),
        scratch_shapes=[
            pltpu.VMEM((KEY_ROWS, LANES), BF16),
            pltpu.VMEM((KEY_ROWS, LANES), BF16),
            pltpu.VMEM((ROWS, LANES), BF16),
            pltpu.VMEM((ROWS, KEY_ROWS), BF16),
            pltpu.VMEM((TABLE, LANES), F32),
        ],
        compiler_params=params(),
        name="attend_back",
    )(heads, heads, heads, rest, rest, aug, table, own, fold, pick.astype(F32), weights, pv, datt, parts)


def pool_back_kernel(
    frames_ref, first_ref, second_ref, vhat_ref, mixed_ref, taps_ref, gain_ref,
    dmix_ref, gbias_ref, gtaps_ref, gpool_ref,
    grid_ref, dgrid_ref, dpool_ref, sums_ref,
):
    step = pl.program_id(0)

    @pl.when(step == 0)
    def _():
        clear_border(grid_ref)
        clear_border(dgrid_ref)

    lane = lane_index((ROWS, LANES))
    for head in range(GROUP_HEADS):
        dy = jnp.where(step == 0, first_ref[0, head].astype(F32), second_ref[0, head].astype(F32))
        dy = jnp.where(lane < HEAD_DIM, dy, 0.0)
        vhat = vhat_ref[head].astype(F32)
        rs = vhat[:, HEAD_DIM : HEAD_DIM + 1] + vhat[:, HEAD_DIM + 1 : HEAD_DIM + 2]
        product = dy * vhat
        gpool_ref[head, 0:1, :] = jnp.sum(product, axis=0, keepdims=True)
        gpool_ref[head, 1:2, :] = jnp.sum(dy, axis=0, keepdims=True)
        scaled = dy * gain_ref[0]
        first = jnp.sum(scaled, axis=1, keepdims=True) * (1.0 / HEAD_DIM)
        second = jnp.sum(product * gain_ref[0], axis=1, keepdims=True) * (1.0 / HEAD_DIM)
        dpool = rs * (scaled - first - vhat * second)
        dpool_ref[:, HEAD_DIM * head : HEAD_DIM * (head + 1)] = dpool[:, :HEAD_DIM]
    dgrid_ref[1 : HEIGHT + 1, 1 : WIDTH + 1] = dpool_ref[...].reshape(HEIGHT, WIDTH, FRAMES, GROUP)
    grid_ref[1 : HEIGHT + 1, 1 : WIDTH + 1] = mixed_ref[...].astype(F32).reshape(HEIGHT, WIDTH, FRAMES, GROUP)
    sums_ref[...] = jnp.zeros(sums_ref.shape, F32)

    @pl.loop(0, HEIGHT)
    def _(i):
        for tile in range(GROUP // LANES):
            lanes = slice(tile * LANES, tile * LANES + LANES)
            line = convolve(dgrid_ref, taps_ref, True, i, lanes)
            frame = lax.broadcasted_iota(jnp.int32, line.shape, 1)
            line = jnp.where(frame < frames_ref[0], line, 0.0)
            at = pl.multiple_of(i * WIDTH * FRAMES, WIDTH * FRAMES)
            dmix_ref[pl.ds(at, WIDTH * FRAMES), lanes] = line.reshape(WIDTH * FRAMES, LANES).astype(BF16)
            own = dgrid_ref[i + 1, 1 : WIDTH + 1, :, lanes]
            moved = (shift_frames(own, -1), own, shift_frames(own, 1))
            for b in range(3):
                for e in range(3):
                    window = grid_ref[i + b, e : e + WIDTH, :, lanes]
                    for a in range(3):
                        tap = 9 * a + 3 * b + e
                        sums_ref[tap, :, lanes] += jnp.sum(window * moved[a], axis=0)

    for tap in range(27):
        gtaps_ref[0, tap : tap + 1, :] = jnp.sum(sums_ref[tap], axis=0, keepdims=True)
    gbias_ref[...] = jnp.sum(dmix_ref[...].astype(F32), axis=0, keepdims=True)


def pool_back(kind, frames, grads_a, grads_b, vhat, mixed, taps, gain):
    smem = pl.BlockSpec(memory_space=pltpu.SMEM)
    return pl.pallas_call(
        pool_back_kernel,
        grid=(2,),
        out_shape=(
            jax.ShapeDtypeStruct((ROWS, D), BF16),
            jax.ShapeDtypeStruct((1, D), F32),
            jax.ShapeDtypeStruct((2, 27, GROUP), F32),
            jax.ShapeDtypeStruct((HEADS, 2, LANES), F32),
        ),
        in_specs=[
            smem,
            pl.BlockSpec((1, GROUP_HEADS, ROWS, LANES), lambda g: (kind, 0, 0, 0)),
            pl.BlockSpec((1, GROUP_HEADS, ROWS, LANES), lambda g: (kind, 0, 0, 0)),
            pl.BlockSpec((GROUP_HEADS, ROWS, LANES), lambda g: (2 * kind + g, 0, 0)),
            pl.BlockSpec((ROWS, GROUP), lambda g: (0, 2 * kind + g)),
            pl.BlockSpec((1, 27, 8, GROUP), lambda g: (kind, 0, 0, 0)),
            pl.BlockSpec((1, 1, LANES), lambda g: (kind, 0, 0)),
        ],
        out_specs=(
            pl.BlockSpec((ROWS, GROUP), lambda g: (0, g)),
            pl.BlockSpec((1, GROUP), lambda g: (0, g)),
            pl.BlockSpec((1, 27, GROUP), lambda g: (g, 0, 0)),
            pl.BlockSpec((GROUP_HEADS, 2, LANES), lambda g: (g, 0, 0)),
        ),
        scratch_shapes=[
            pltpu.VMEM((HEIGHT + 2, WIDTH + 2, FRAMES, GROUP), F32),
            pltpu.VMEM((HEIGHT + 2, WIDTH + 2, FRAMES, GROUP), F32),
            pltpu.VMEM((ROWS, GROUP), F32),
            pltpu.VMEM((27, FRAMES, GROUP), F32),
        ],
        compiler_params=params(),
        name="pool_back_%d" % kind,
    )(frames, grads_a, grads_b, vhat, mixed, taps, gain)


def project_grad_kernel(place_ref, normed_ref, dq_ref, dk_ref, dv_ref, one_ref, two_ref, full_ref):
    for kind, source_ref in enumerate((dq_ref, dk_ref, dv_ref)):
        grad = dot(normed_ref[...], source_ref[...], ((0,), (0,)))
        full_ref[:, kind * D : (kind + 1) * D] = grad.astype(BF16)
    half, columns = one_ref.shape[5:]
    for f in range(QKV // columns):

        @pl.loop(0, DP_BLOCKS)
        def _(d):
            bits = relative_bits(place_ref, d, f)
            lanes = slice(f * columns, (f + 1) * columns)
            at = pl.multiple_of(2 * d * half, half)
            one_ref[bits["c"], bits["x"], bits["y"], bits["z1"], bits["z2"]] = full_ref[pl.ds(at, half), lanes]
            at = pl.multiple_of((2 * d + 1) * half, half)
            two_ref[bits["c"], bits["y"], bits["x"], bits["z1"], bits["z2"]] = full_ref[pl.ds(at, half), lanes]


def project_grad(place, normed, dmixed, sides):
    vmem = pl.BlockSpec(memory_space=pltpu.VMEM)
    half = jax.ShapeDtypeStruct((2, 2, 2, 2, 2, D // DP_BLOCKS // 2, QKV // sides), BF16)
    return pl.pallas_call(
        project_grad_kernel,
        out_shape=(half, half),
        in_specs=[pl.BlockSpec(memory_space=pltpu.SMEM)] + [vmem] * 4,
        out_specs=(vmem, vmem),
        scratch_shapes=[pltpu.VMEM((D, QKV), BF16)],
        compiler_params=params(),
        name="project_grad",
    )(place, normed, *dmixed)


def project_back_kernel(
    dq_ref, dk_ref, dv_ref, weight_ref, x_ref, dmid_ref, g1_ref, gtok_ref, small_ref, dx_ref, wide_ref
):
    dy = None
    for kind, source_ref in enumerate((dq_ref, dk_ref, dv_ref)):
        term = dot(source_ref[...], weight_ref[:, kind * D : (kind + 1) * D], ((1,), (1,)))
        dy = term if dy is None else dy + term
    centred, rs = layer_stats(x_ref[...].astype(F32), D)
    vhat = centred * rs
    small_ref[0:1, :] = jnp.sum(dy * vhat, axis=0, keepdims=True)
    small_ref[1:2, :] = jnp.sum(dy, axis=0, keepdims=True)
    small_ref[2:8, :] = jnp.zeros((6, D), F32)
    scaled = dy * g1_ref[...]
    first = jnp.sum(scaled, axis=1, keepdims=True) * (1.0 / D)
    second = jnp.sum(scaled * vhat, axis=1, keepdims=True) * (1.0 / D)
    dx_ref[...] = dmid_ref[...] + rs * (scaled - first - vhat * second)

    @pl.loop(0, PLACES)
    def _(place):
        at = pl.multiple_of(place * FRAMES, FRAMES)
        write_place(wide_ref, place, dx_ref[pl.ds(at, FRAMES), :])

    for tile in range(D // LANES):
        gtok_ref[:, tile * LANES : (tile + 1) * LANES] = wide_ref[tile]


def project_back(dmixed, weight, x, dmid, g1):
    vmem = pl.BlockSpec(memory_space=pltpu.VMEM)
    return pl.pallas_call(
        project_back_kernel,
        out_shape=(jax.ShapeDtypeStruct((ROWS, D), F32), jax.ShapeDtypeStruct((8, D), F32)),
        in_specs=[vmem] * 7,
        out_specs=(vmem, vmem),
        scratch_shapes=[pltpu.VMEM((ROWS, D), F32), wide_scratch(D)],
        compiler_params=params(),
        name="project_back",
    )(*dmixed, weight, x, dmid, g1)


def row(vector):
    return vector.reshape(1, -1)


def tiled_lanes(array):
    return jnp.concatenate([array] * GROUP_HEADS, axis=-1)


def head_lanes(array):
    return jnp.pad(array, [(0, 0)] * (array.ndim - 1) + [(0, LANES - HEAD_DIM)])


DP_BLOCKS = 8
ROUTE_ONE = ("z2", "z1", "y", "x", "c")
ROUTE_TWO = ("z2", "z1", "x", "y", "c")
BIT = {"x": ("dp", 1), "z1": ("dp", 2), "z2": ("dp", 4), "y": ("fsdp", 2), "c": ("fsdp", 1)}


def swap(values, name, sizes):
    axis, bit = BIT[name]
    return lax.ppermute(values, axis, [(at, at ^ bit) for at in range(sizes[axis])])


def together(*values):
    return lax.optimization_barrier(values)


def flat_shard(one, two, proj):
    parts = tiles_of(one) + tiles_of(two.T)
    part = proj.shape[1]
    parts += [proj[:, :LANES], jnp.pad(proj[:, LANES:], ((0, 0), (0, 2 * LANES - part)))]
    return jnp.concatenate(parts, axis=0)


class Staged:
    def __init__(self):
        self.sizes = {"dp": 8, "fsdp": 4}

    def place(self):
        dp, fsdp = lax.axis_index("dp"), lax.axis_index("fsdp")
        return jnp.stack([dp & 1, (dp >> 1) & 1, (dp >> 2) & 1, (fsdp >> 1) & 1, fsdp & 1]).astype(jnp.int32)

    def first_weights(self, shard):
        half = shard.shape[0] // 2
        one, two = shard[None, :half], shard[None, half:]
        for a, b in zip(ROUTE_ONE, ROUTE_TWO):
            more_one, more_two = swap(one, a, self.sizes), swap(two, b, self.sizes)
            one, two = jnp.concatenate([one, more_one]), jnp.concatenate([two, more_two])
        return one, two

    def other_weights(self, one, two, proj, after):
        flat, _ = together(flat_shard(one, two, proj), after)
        return lax.all_gather(flat, ("dp", "fsdp"), axis=0, tiled=False).reshape((8, 4) + flat.shape)

    def halve(self, blocks, name):
        return blocks[0], swap(blocks[1], name, self.sizes)

    def total(self, vector):
        for name in ("c", "x", "y", "z1", "z2"):
            vector = vector + swap(vector, name, self.sizes)
        return vector


class Plain:
    def __init__(self, dp, fsdp):
        self.dp, self.fsdp = dp, fsdp

    def place(self):
        return jnp.zeros((5,), jnp.int32)

    def gather(self, shard):
        blocks = lax.all_gather(shard, ("dp", "fsdp"), axis=0, tiled=False)
        rows, columns = shard.shape
        joined = blocks.reshape(DP_BLOCKS, self.dp // DP_BLOCKS, self.fsdp, rows, columns).transpose(0, 2, 1, 3, 4)
        return joined.reshape(DP_BLOCKS, self.fsdp, self.dp // DP_BLOCKS * rows, columns)

    def first_weights(self, shard):
        blocks = self.gather(shard)
        half, columns = blocks.shape[2] // 2, blocks.shape[3]
        bits = blocks.reshape(2, 2, 2, 2, 2, 2, half, columns)
        at = {"z2": 0, "z1": 1, "x": 2, "y": 3, "c": 4}
        return tuple(
            bits.transpose([at[name] for name in reversed(route)] + [5, 6, 7])[:, :, :, :, :, side].reshape(
                32, half, columns
            )
            for side, route in enumerate((ROUTE_ONE, ROUTE_TWO))
        )

    def other_weights(self, one, two, proj, after):
        return jax.vmap(jax.vmap(flat_shard))(self.gather(one), self.gather(two), self.gather(proj))

    def scatter(self, blocks, route):
        at = {name: 4 - where for where, name in enumerate(route)}
        rows, columns = blocks.shape[5:]
        blocks = blocks.transpose([at[name] for name in ("z2", "z1", "x", "y", "c")] + [5, 6])
        split = blocks.reshape(DP_BLOCKS, self.fsdp, self.dp // DP_BLOCKS, rows * DP_BLOCKS // self.dp, columns)
        split = split.transpose(0, 2, 1, 3, 4).reshape(self.dp * self.fsdp, -1, columns)
        return lax.psum_scatter(split, ("dp", "fsdp"), scatter_dimension=0, tiled=False).astype(F32)

    def total(self, vector):
        return lax.psum(vector, ("dp", "fsdp"))


def run(
    comm, staged, tokens, prev_kv, memory, valid_frames, mem_len, ln1_gain, ln1_bias, w_qkv, qkv_bias, pool_conv, pool_gain,
    pool_bias, rel_time, rel_space, compress, w_proj, proj_bias, ln2_gain, ln2_bias, w_fc1, fc1_bias, w_fc2,
    fc2_bias, cotangent,
):
    place = comm.place()
    first, second = comm.first_weights(w_qkv)
    one_hot, own, fold, pick = (jnp.asarray(c, BF16) for c in constants())
    tables = jnp.concatenate([rel_time, rel_space[0], rel_space[1]], axis=0)
    tables = jnp.pad(tables, ((0, LANES - tables.shape[0]), (0, LANES - HEAD_DIM)))
    taps = jnp.broadcast_to(tiled_lanes(pool_conv)[:, :, None, :], (3, 27, 8, GROUP))
    gains, biases = head_lanes(pool_gain)[:, None], head_lanes(pool_bias)[:, None]
    x, normed, upstream, aug, table = prepare(
        valid_frames, mem_len, tokens, cotangent, row(ln1_gain), row(ln1_bias), one_hot, tables, pick
    )
    rest, parts = squeeze(prev_kv, memory, tiled_lanes(compress))
    flat = comm.other_weights(w_fc1, w_fc2, w_proj, first)
    heads, vhat, mixed, weight = query_key_value(
        valid_frames, place, normed, first, second, row(qkv_bias), taps, gains, biases
    )
    weights, pv, attended = attend(heads, rest, aug, table, own, fold)
    out, dmid, datt, gp, gw1, gw2, small_two, gb1 = feed_forward(
        place, attended, x, upstream, flat, row(proj_bias), row(ln2_gain), row(ln2_bias), row(fc1_bias), row(fc2_bias)
    )
    middle = {"proj": (gp, ROUTE_TWO), "one": (gw1, ROUTE_ONE), "two": (gw2, ROUTE_TWO)}
    big, routes = {k: v[0] for k, v in middle.items()}, {k: v[1] for k, v in middle.items()}

    def start(stage):
        return {k: comm.halve(big[k], routes[k][4 - stage]) for k in big} if staged else None

    def finish(moving, *after):
        if not staged:
            return after
        flying = [v for pair in moving.values() for v in pair]
        tied = together(*flying, *after)
        for at, k in enumerate(moving):
            big[k] = tied[2 * at] + tied[2 * at + 1]
        return tied[2 * len(moving) :]

    def back(start_head, datt):
        return attend_back(
            start_head, HEADS // 2, heads, rest, aug, table, own, fold, pick, weights, pv, datt, parts
        )

    moving = start(0)
    grads_a, gtable_a, gcompress_a = back(0, datt)
    (grads_a, datt) = finish(moving, grads_a, datt)
    moving = start(1)
    grads_b, gtable_b, gcompress_b = back(HEADS // 2, datt)
    (grads_a, grads_b) = finish(moving, grads_a, grads_b)
    dmixed, gbias, gtaps, gpool = [], [], [], []
    for kind in range(3):
        moving = start(2 + kind)
        pieces = pool_back(kind, valid_frames, grads_a, grads_b, vhat, mixed, taps, gains)
        (piece, grads_a) = finish(moving, pieces[0], grads_a)
        dmixed.append(piece)
        gbias.append(pieces[1])
        gtaps.append(pieces[2])
        gpool.append(pieces[3])
    qkv_one, qkv_two = project_grad(place, normed, dmixed, QKV // w_qkv.shape[1])
    if staged:
        for stage in range(5):
            kept_one, more_one = comm.halve(qkv_one, ROUTE_ONE[4 - stage])
            kept_two, more_two = comm.halve(qkv_two, ROUTE_TWO[4 - stage])
            qkv_one, qkv_two = kept_one + more_one, kept_two + more_two
    gtok, small_one = project_back(dmixed, weight, x, dmid, row(ln1_gain))
    gconv = jnp.sum(jnp.stack(gtaps).reshape(3, 2, 27, GROUP_HEADS, HEAD_DIM), axis=(1, 3))
    gpool = jnp.sum(jnp.stack(gpool), axis=1)[:, :, :HEAD_DIM]
    gtable, gcompress = gtable_a + gtable_b, gcompress_a + gcompress_b
    smalls = (
        small_one[0], small_one[1], jnp.concatenate(gbias, axis=1)[0], gconv, gpool[:, 0], gpool[:, 1],
        gtable[:15, :HEAD_DIM], gtable[15:53, :HEAD_DIM].reshape(2, 19, HEAD_DIM), gcompress[:, :, :HEAD_DIM],
        small_two[0], small_two[1], small_two[2], gb1[0], small_two[3],
    )
    vector = comm.total(jnp.concatenate([s.reshape(-1) for s in smalls]))
    totals, at = [], 0
    for s in smalls:
        totals.append(vector[at : at + s.size].reshape(s.shape))
        at += s.size
    if staged:
        qkv = jnp.concatenate([qkv_one, qkv_two], axis=0).astype(F32)
        sums = [qkv] + [big[k].astype(F32) for k in ("proj", "one", "two")]
    else:
        qkv_one = comm.scatter(jnp.concatenate([qkv_one, jnp.moveaxis(qkv_two, 1, 2)], axis=5), ROUTE_ONE)
        sums = [qkv_one] + [comm.scatter(big[k], routes[k]) for k in ("proj", "one", "two")]
    return (
        out, gtok, totals[0], totals[1], sums[0], totals[2], totals[3], totals[4], totals[5], totals[6],
        totals[7], totals[8], sums[1], totals[9], totals[10], totals[11], sums[2], totals[12], sums[3], totals[13],
    )


def solution(mesh):
    both = P(("dp", "fsdp"))
    rows = P(("dp", "fsdp"), None)
    second = P(None, ("dp", "fsdp"), None)
    blocks = P("dp", "fsdp")
    none = P()
    dp, fsdp = mesh.shape["dp"], mesh.shape["fsdp"]
    staged = (dp, fsdp) == (8, 4)
    return jax.shard_map(
        functools.partial(run, Staged() if staged else Plain(dp, fsdp), staged),
        mesh=mesh,
        in_specs=(
            rows, second, second, both, both, none, none, blocks, none, none, none, none, none, none, none, blocks,
            none, none, none, blocks, none, blocks, none, rows,
        ),
        out_specs=(
            rows, rows, none, none, blocks, none, none, none, none, none, none, none, blocks, none, none, none,
            blocks, none, blocks, none,
        ),
        check_vma=False,
    )
```

```python
import functools

import jax
import jax.numpy as jnp
import numpy as np
from jax import lax
from jax.experimental import pallas as pl
from jax.experimental.pallas import tpu as pltpu
from jax.sharding import PartitionSpec as P

D = 768
FF = 3072
HEADS = 8
HEAD_DIM = 96
LANES = 128
FRAMES = 8
HEIGHT = 10
WIDTH = 10
PLACES = HEIGHT * WIDTH
ROWS = 800
MEM = 200
GROUP = 384
GROUP_HEADS = 4
QKV = 3 * D
KEY_ROWS = 1280
MEM_AT = 800
SQUEEZE_AT = 1024
REST = KEY_ROWS - ROWS
TABLE = 384
EPSILON = 1e-06
SCALE = HEAD_DIM**-0.5
ROOT = HEAD_DIM**0.5
LOG2E = 1.4426950408889634
MASKED = -1e9
MASK_LANE = 124
ROW_BLOCK = 160
BF16 = jnp.bfloat16
F32 = jnp.float32
VMEM_LIMIT = 60 * 1024 * 1024


def constants():
    place = np.arange(PLACES).repeat(FRAMES)
    row_t = np.tile(np.arange(FRAMES), PLACES)
    row_i, row_j = place // WIDTH, place % WIDTH
    one_hot = np.zeros((KEY_ROWS, LANES), np.float32)
    rows = np.arange(ROWS)
    one_hot[rows, 96 + row_t] = 1
    one_hot[rows, 104 + row_i] = 1
    one_hot[rows, 114 + row_j] = 1
    own = np.zeros((ROWS, TABLE), np.float32)
    fold = np.zeros((TABLE, LANES), np.float32)
    pick = np.zeros((TABLE, LANES), np.float32)
    for base, length, row_at, lane, offset in (
        (0, FRAMES, row_t, 96, 0),
        (64, HEIGHT, row_i, 104, 15),
        (164, WIDTH, row_j, 114, 34),
    ):
        for a in range(length):
            for b in range(length):
                column = base + a * length + b
                own[:, column] = row_at == a
                fold[column, lane + b] = 1
                pick[column, offset + a - b + length - 1] = 1
    return one_hot, own, fold, pick


def lane_index(shape):
    return lax.broadcasted_iota(jnp.int32, shape, len(shape) - 1)


def dot(a, b, contract=((1,), (0,)), precision=None):
    return lax.dot_general(a, b, (contract, ((), ())), preferred_element_type=F32, precision=precision)


def layer_stats(values, width):
    average = jnp.sum(values, axis=-1, keepdims=True) * (1.0 / width)
    centred = values - average
    variance = jnp.sum(centred * centred, axis=-1, keepdims=True) * (1.0 / width)
    return centred, lax.rsqrt(variance + EPSILON)


def params(**more):
    return pltpu.CompilerParams(vmem_limit_bytes=VMEM_LIMIT, **more)


def whole(shape):
    return pl.BlockSpec(shape, lambda *_: (0,) * len(shape))


def tiles_of(values):
    return [values[:, at : at + LANES] for at in range(0, values.shape[1], LANES)]


def flat_pieces(one, two, proj):
    at = 0
    for part in tiles_of(one) + tiles_of(two.T) + tiles_of(proj):
        yield at, part
        at += part.shape[0]


def read_place(wide_ref, place, tiles=D // LANES):
    parts = [wide_ref[tile, pl.ds(place, FRAMES, stride=PLACES), :] for tile in range(tiles)]
    return jnp.concatenate(parts, axis=1)


def write_place(wide_ref, place, values):
    for tile, part in enumerate(tiles_of(values)):
        wide_ref[tile, pl.ds(place, FRAMES, stride=PLACES), :] = part


def wide_scratch(columns):
    return pltpu.VMEM((columns // LANES, ROWS, LANES), F32)


PARTS = 3
MESH = pl.DeviceIdType.MESH


class Gather:
    def __init__(self, shard_ref, all_ref, own_sem, send_sem, recv_sem):
        dp, fsdp = lax.axis_index("dp"), lax.axis_index("fsdp")
        self.z, self.x = dp // 2, dp % 2
        self.y, self.c = fsdp // 2, fsdp % 2
        self.shard_ref, self.all_ref = shard_ref, all_ref
        self.own_sem, self.send_sem, self.recv_sem = own_sem, send_sem, recv_sem
        self.rows = shard_ref.shape[0] // (2 * PARTS)
        self.copies = {}

    def device(self, z, x, y, c):
        return (2 * z + x, 2 * y + c)

    def partners(self):
        z, x, y, c = self.z, self.x, self.y, self.c
        along = [self.device((z + k) % 4, x, y, c) for k in (1, 2, 3)]
        return along + [self.device(z, 1 - x, y, c), self.device(z, x, 1 - y, c), self.device(z, x, y, 1 - c)]

    def begin(self):
        barrier = pltpu.get_barrier_semaphore()
        for partner in self.partners():
            pl.semaphore_signal(barrier, inc=1, device_id=partner, device_id_type=MESH)
        self.own = pltpu.make_async_copy(self.shard_ref, self.all_ref.at[self.z, self.x, self.y, self.c], self.own_sem)
        self.own.start()
        pl.semaphore_wait(barrier, 6)
        for part in range(PARTS):
            for route in range(2):
                for k in (1, 2, 3):
                    self.send(part, route, k - 1)

    def send(self, part, route, stage):
        z, x, y, c = self.z, self.x, self.y, self.c
        rows = pl.ds((2 * part + route) * self.rows, self.rows)
        partner = self.partners()[stage if stage < 3 or stage == 5 else 3 + (stage - 3 + route) % 2]
        every = slice(None)
        if stage < 3:
            place = (z, x, y, c)
        elif stage == 3:
            place = (every, x, y, c)
        elif stage == 4:
            place = (every, every, y, c) if route == 0 else (every, x, every, c)
        else:
            place = (every, every, every, c)
        target = self.all_ref.at[(*place, rows)]
        source = self.shard_ref.at[rows] if stage < 3 else target
        at = (2 * part + route) * 6 + stage
        copy = pltpu.make_async_remote_copy(
            src_ref=source,
            dst_ref=target,
            send_sem=self.send_sem.at[at],
            recv_sem=self.recv_sem.at[at],
            device_id=partner,
            device_id_type=MESH,
        )
        copy.start()
        self.copies[part, route, stage] = copy

    def advance(self, part, level):
        if level == 0 and part == 0:
            self.own.wait()
        for route in range(2):
            for stage in ((0, 1, 2), (3,), (4,), (5,))[level]:
                self.copies[part, route, stage].wait_recv()
        if level < 3:
            for route in range(2):
                self.send(part, route, 3 + level)

    def steps(self):
        order = []
        for turn in range(PARTS + 3):
            for level in reversed(range(4)):
                if 0 <= turn - level < PARTS:
                    order.append((turn - level, level))
        return [functools.partial(self.advance, *step) for step in order]

    def end(self):
        for copy in self.copies.values():
            copy.wait_send()


def prepare_kernel(
    communicate, frames_ref, length_ref, tokens_ref, cot_ref, gain_ref, bias_ref, one_hot_ref, time_ref, space_ref,
    pick_ref, prev_ref, mem_ref, taps_ref, *refs,
):
    if communicate:
        shard_ref, one_ref, two_ref, proj_ref, all_ref, flat_ref = refs[:6]
        refs = refs[6:]
    x_ref, normed_ref, upstream_ref, aug_ref, table_ref, rest_ref, tap_ref, wide_ref, sums_ref, parts_ref = refs[:10]
    tables_ref = refs[10]
    steps = []
    if communicate:
        gather = Gather(shard_ref, all_ref, *refs[11:])
        gather.begin()
        steps = gather.steps()

    def advance(count=1):
        for _ in range(min(count, len(steps))):
            steps.pop(0)()

    def permute(source_ref, target_ref):
        for tile, part in enumerate(tiles_of(source_ref[...])):
            wide_ref[tile] = part.astype(F32)

        @pl.loop(0, PLACES // 2)
        def _(pair):
            first = read_place(wide_ref, 2 * pair)
            second = read_place(wide_ref, 2 * pair + 1)
            at = pl.multiple_of(pair * 16, 16)
            target_ref[pl.ds(at, 16), :] = jnp.concatenate([first, second], axis=0).astype(BF16)

    if communicate:
        for at, part in flat_pieces(one_ref[...], two_ref[...], proj_ref[...]):
            flat_ref[at : at + part.shape[0], : part.shape[1]] = part
    permute(cot_ref, upstream_ref)
    permute(tokens_ref, x_ref)
    advance()
    centred, rs = layer_stats(x_ref[...].astype(F32), D)
    normed_ref[...] = (centred * rs * gain_ref[...].reshape(1, D) + bias_ref[...].reshape(1, D)).astype(BF16)
    row = lax.broadcasted_iota(jnp.int32, (KEY_ROWS, LANES), 0)
    frames, length = frames_ref[0], length_ref[0]
    place = jnp.where(row < MEM_AT, row & 7, jnp.where(row < SQUEEZE_AT, row - MEM_AT, row - SQUEEZE_AT))
    limit = jnp.where(row < MEM_AT, frames, jnp.where(row < SQUEEZE_AT, length, MEM))
    off = jnp.where(place >= limit, jnp.where(lane_index((KEY_ROWS, LANES)) == MASK_LANE, MASKED, 0.0), 0.0)
    aug_ref[...] = (one_hot_ref[...].astype(F32) + off).astype(BF16)
    tables_ref[...] = jnp.zeros((LANES, LANES), F32)
    spans = 2 * HEIGHT - 1
    tables_ref[0 : 2 * FRAMES - 1, :HEAD_DIM] = time_ref[...]
    tables_ref[15 : 15 + spans, :HEAD_DIM] = space_ref[0]
    tables_ref[15 + spans : 15 + 2 * spans, :HEAD_DIM] = space_ref[1]
    table_ref[...] = dot(pick_ref[...], tables_ref[...].astype(BF16)).astype(BF16)
    advance()

    def head_of(values, head):
        return values[:, HEAD_DIM * head : HEAD_DIM * head + HEAD_DIM]

    for s in range(2):
        for group in range(2):
            columns = slice(group * GROUP, (group + 1) * GROUP)
            for tile, part in enumerate(tiles_of(prev_ref[s, :, columns])):
                wide_ref[tile] = part.astype(F32)

            taps = [tiled_lanes(taps_ref[s, tap : tap + 1, :]) for tap in range(4)]

            @pl.loop(0, HEIGHT // 2)
            def _(i):
                for j in range(WIDTH // 2):
                    total = None
                    at = pl.multiple_of((i * (WIDTH // 2) + j) * FRAMES, FRAMES)
                    for tap in range(4):
                        place = (2 * i + tap // 2) * WIDTH + 2 * j + tap % 2
                        part = read_place(wide_ref, place, GROUP // LANES)
                        parts_ref[tap, pl.ds(at, FRAMES), :] = part
                        term = part * taps[tap]
                        total = term if total is None else total + term
                    sums_ref[pl.ds(at, FRAMES), :] = total

            old = mem_ref[s, :, columns].astype(F32)
            for head in range(GROUP_HEADS):
                rest = jnp.concatenate(
                    [
                        head_of(old, head),
                        jnp.zeros((SQUEEZE_AT - MEM_AT - MEM, HEAD_DIM), F32),
                        head_of(sums_ref[...], head),
                        jnp.zeros((KEY_ROWS - SQUEEZE_AT - MEM, HEAD_DIM), F32),
                    ],
                    axis=0,
                )
                rest = jnp.concatenate([rest, jnp.zeros((REST, LANES - HEAD_DIM), F32)], axis=1)
                rest_ref[s, group * GROUP_HEADS + head] = rest.astype(BF16)
                for tap in range(4):
                    part = jnp.concatenate([head_of(parts_ref[tap], head), jnp.zeros((8, HEAD_DIM), F32)], axis=0)
                    part = jnp.concatenate([part, jnp.zeros((208, LANES - HEAD_DIM), F32)], axis=1)
                    tap_ref[s, group * GROUP_HEADS + head, tap] = part.astype(BF16)
            advance(3 if group + s else 2)
    advance(len(steps))
    if communicate:
        gather.end()


def prepare(frames, length, tokens, cot, gain, bias, one_hot, rel_time, rel_space, pick, prev, memory, taps, shards=None):
    smem = pl.BlockSpec(memory_space=pltpu.SMEM)
    vmem = pl.BlockSpec(memory_space=pltpu.VMEM)
    communicate = shards is not None
    out_shape = [
        jax.ShapeDtypeStruct((ROWS, D), BF16),
        jax.ShapeDtypeStruct((ROWS, D), BF16),
        jax.ShapeDtypeStruct((ROWS, D), BF16),
        jax.ShapeDtypeStruct((KEY_ROWS, LANES), BF16),
        jax.ShapeDtypeStruct((TABLE, LANES), BF16),
        jax.ShapeDtypeStruct((2, HEADS, REST, LANES), BF16),
        jax.ShapeDtypeStruct((2, HEADS, 4, 208, LANES), BF16),
    ]
    in_specs, out_specs = [smem, smem] + [vmem] * 11, [vmem] * 7
    operands = [frames, length, tokens, cot, gain, bias, one_hot, rel_time, rel_space, pick, prev, memory, taps]
    scratch = [
        wide_scratch(D),
        pltpu.VMEM((MEM, GROUP), F32),
        pltpu.VMEM((4, MEM, GROUP), F32),
        pltpu.VMEM((LANES, LANES), F32),
    ]
    more = {}
    if communicate:
        anywhere = pl.BlockSpec(memory_space=pl.ANY)
        shard, one, two, proj = shards
        rows = (one.size + two.size) // LANES + 2 * proj.shape[0]
        out_shape = [
            jax.ShapeDtypeStruct((4, 2, 2, 2) + shard.shape, BF16),
            jax.ShapeDtypeStruct((rows, LANES), BF16),
        ] + out_shape
        in_specs += [anywhere, vmem, vmem, vmem]
        out_specs = [anywhere, vmem] + out_specs
        operands += shards
        count = 2 * PARTS * 6
        scratch += [pltpu.SemaphoreType.DMA, pltpu.SemaphoreType.DMA((count,)), pltpu.SemaphoreType.DMA((count,))]
        more = {"collective_id": 0, "has_side_effects": True}
    return pl.pallas_call(
        functools.partial(prepare_kernel, communicate),
        out_shape=tuple(out_shape),
        in_specs=in_specs,
        out_specs=tuple(out_specs),
        scratch_shapes=scratch,
        compiler_params=params(**more),
        name="prepare",
    )(*operands)


def shift_frames(values, step):
    frame = lax.broadcasted_iota(jnp.int32, values.shape, values.ndim - 2)
    moved = pltpu.roll(values, step % FRAMES, values.ndim - 2)
    edge = 0 if step == 1 else FRAMES - 1
    return jnp.where(frame == edge, 0.0, moved)


def convolve(grid_ref, taps_ref, flip, i, lanes):
    sums = [None, None, None]
    for b in range(3):
        for e in range(3):
            window = grid_ref[i + b, e : e + WIDTH, :, lanes]
            for a in range(3):
                tap = 9 * a + 3 * b + e
                term = window * taps_ref[26 - tap if flip else tap, :, lanes][None]
                sums[a] = term if sums[a] is None else sums[a] + term
    return sums[1] + shift_frames(sums[0], 1) + shift_frames(sums[2], -1)


def spread_taps(raw_ref, taps_ref):
    for tap in range(27):
        line = tiled_lanes(raw_ref[0, tap : tap + 1, :])
        taps_ref[tap] = jnp.broadcast_to(line, (FRAMES, GROUP))


def clear_border(grid_ref):
    grid_ref[...] = jnp.zeros(grid_ref.shape, grid_ref.dtype)


def relative_bits(place_ref, d, f):
    return {
        "x": (d & 1) ^ place_ref[0],
        "z1": ((d >> 1) & 1) ^ place_ref[1],
        "z2": ((d >> 2) & 1) ^ place_ref[2],
        "y": ((f >> 1) & 1) ^ place_ref[3],
        "c": (f & 1) ^ place_ref[4],
    }


def slot(bits, order):
    return sum(bits[name] << at for at, name in enumerate(order))


def qkv_kernel(
    frames_ref, normed_ref, shards_ref, qkv_bias_ref, taps_raw_ref, gain_ref, bias_ref,
    heads_ref, vhat_ref, mixed_ref, weight_ref, grid_ref, pooled_ref, taps_ref,
):
    step = pl.program_id(0)

    @pl.when(step == 0)
    def _():
        clear_border(grid_ref)
        depth, columns = shards_ref.shape[2:]
        for f in range(QKV // columns):
            for d in range(DP_BLOCKS):
                weight_ref[d * depth : (d + 1) * depth, f * columns : (f + 1) * columns] = shards_ref[d, f]

    @pl.when(step % 2 == 0)
    def _():
        spread_taps(taps_raw_ref, taps_ref)

    at = pl.multiple_of(step * GROUP, LANES)
    mixed = dot(normed_ref[...], weight_ref[:, pl.ds(at, GROUP)]) + qkv_bias_ref[...]
    row = lax.broadcasted_iota(jnp.int32, (ROWS, GROUP), 0)
    mixed = jnp.where((row & 7) < frames_ref[0], mixed, 0.0)
    mixed_ref[...] = mixed.astype(BF16)
    grid_ref[1 : HEIGHT + 1, 1 : WIDTH + 1] = mixed.reshape(HEIGHT, WIDTH, FRAMES, GROUP)

    @pl.loop(0, HEIGHT)
    def _(i):
        for tile in range(GROUP // LANES):
            lanes = slice(tile * LANES, tile * LANES + LANES)
            line = convolve(grid_ref, taps_ref, False, i, lanes)
            at = pl.multiple_of(i * WIDTH * FRAMES, WIDTH * FRAMES)
            pooled_ref[pl.ds(at, WIDTH * FRAMES), lanes] = line.reshape(WIDTH * FRAMES, LANES)

    lane = lane_index((ROWS, LANES))
    for head in range(GROUP_HEADS):
        values = pooled_ref[:, HEAD_DIM * head : HEAD_DIM * head + LANES]
        values = jnp.where(lane < HEAD_DIM, values, 0.0)
        average = jnp.sum(values, axis=-1, keepdims=True) * (1.0 / HEAD_DIM)
        centred = jnp.where(lane < HEAD_DIM, values - average, 0.0)
        variance = jnp.sum(centred * centred, axis=-1, keepdims=True) * (1.0 / HEAD_DIM)
        rs = lax.rsqrt(variance + EPSILON)
        vhat = centred * rs
        heads_ref[head] = (vhat * gain_ref[0] + bias_ref[0]).astype(BF16)
        high = rs.astype(BF16).astype(F32)
        extra = jnp.where(lane == HEAD_DIM, high, jnp.where(lane == HEAD_DIM + 1, rs - high, 0.0))
        vhat_ref[head] = (vhat + extra).astype(BF16)


def query_key_value(frames, normed, shards, qkv_bias, taps, gain, bias):
    smem = pl.BlockSpec(memory_space=pltpu.SMEM)
    return pl.pallas_call(
        qkv_kernel,
        grid=(6,),
        out_shape=(
            jax.ShapeDtypeStruct((3 * HEADS, ROWS, LANES), BF16),
            jax.ShapeDtypeStruct((3 * HEADS, ROWS, LANES), BF16),
            jax.ShapeDtypeStruct((ROWS, QKV), BF16),
            jax.ShapeDtypeStruct((D, QKV), BF16),
        ),
        in_specs=[
            smem,
            whole((ROWS, D)),
            whole(shards.shape),
            pl.BlockSpec((1, GROUP), lambda g: (0, g)),
            pl.BlockSpec((1, 27, HEAD_DIM), lambda g: (g // 2, 0, 0)),
            pl.BlockSpec((1, 1, LANES), lambda g: (g // 2, 0, 0)),
            pl.BlockSpec((1, 1, LANES), lambda g: (g // 2, 0, 0)),
        ],
        out_specs=(
            pl.BlockSpec((GROUP_HEADS, ROWS, LANES), lambda g: (g, 0, 0)),
            pl.BlockSpec((GROUP_HEADS, ROWS, LANES), lambda g: (g, 0, 0)),
            pl.BlockSpec((ROWS, GROUP), lambda g: (0, g)),
            whole((D, QKV)),
        ),
        scratch_shapes=[
            pltpu.VMEM((HEIGHT + 2, WIDTH + 2, FRAMES, GROUP), F32),
            pltpu.VMEM((ROWS, GROUP + LANES), F32),
            pltpu.VMEM((27, FRAMES, GROUP), F32),
        ],
        compiler_params=params(),
        name="query_key_value",
    )(frames, normed, shards, qkv_bias, taps, gain, bias)


def attend_kernel(
    q_ref, k_ref, v_ref, krest_ref, vrest_ref, aug_ref, table_ref, own_ref, fold_ref,
    weights_ref, pv_ref, out_ref, keys_ref, vals_ref, query_ref,
):
    lane = lane_index((KEY_ROWS, LANES))
    keys_ref[:ROWS] = k_ref[0] + aug_ref[:ROWS]
    keys_ref[ROWS:] = krest_ref[0, 0] + aug_ref[ROWS:]
    one = jnp.where(lane == HEAD_DIM, 1.0, 0.0).astype(BF16)
    vals_ref[:ROWS] = v_ref[0] + one[:ROWS]
    vals_ref[ROWS:] = vrest_ref[0, 0] + one[ROWS:]
    query = q_ref[0]
    every = (dot(query, table_ref[...], ((1,), (1,))) * ROOT).astype(BF16) * own_ref[...]
    relative = dot(every, fold_ref[...])
    marked = jnp.where(lane[:ROWS] == MASK_LANE, 1.0, relative)
    query_ref[...] = (query.astype(F32) + marked).astype(BF16)

    @pl.loop(0, ROWS // ROW_BLOCK)
    def _(block):
        rows = pl.ds(pl.multiple_of(block * ROW_BLOCK, ROW_BLOCK), ROW_BLOCK)
        scores = dot(query_ref[rows, :], keys_ref[...], ((1,), (1,)))
        largest = jnp.max(scores, axis=1, keepdims=True)
        weights = jnp.exp2((scores - largest) * (SCALE * LOG2E)).astype(BF16)
        weights_ref[0, rows, :] = weights
        total = dot(weights, vals_ref[...])
        inverse = 1.0 / total[:, HEAD_DIM : HEAD_DIM + 1]
        lane = lane_index((ROW_BLOCK, LANES))
        pv = jnp.where(lane < HEAD_DIM, total * inverse, 0.0)
        out_ref[0, rows, :] = (pv + q_ref[0, rows, :].astype(F32)).astype(BF16)
        high = inverse.astype(BF16).astype(F32)
        extra = jnp.where(lane == HEAD_DIM, high, jnp.where(lane == HEAD_DIM + 1, inverse - high, 0.0))
        pv_ref[0, rows, :] = (pv + extra).astype(BF16)


def attend(heads, rest, aug, table, own, fold):
    head = (1, ROWS, LANES)
    tail = (1, 1, REST, LANES)
    return pl.pallas_call(
        attend_kernel,
        grid=(HEADS,),
        out_shape=(
            jax.ShapeDtypeStruct((HEADS, ROWS, KEY_ROWS), BF16),
            jax.ShapeDtypeStruct((HEADS, ROWS, LANES), BF16),
            jax.ShapeDtypeStruct((HEADS, ROWS, LANES), BF16),
        ),
        in_specs=[
            pl.BlockSpec(head, lambda h: (h, 0, 0)),
            pl.BlockSpec(head, lambda h: (HEADS + h, 0, 0)),
            pl.BlockSpec(head, lambda h: (2 * HEADS + h, 0, 0)),
            pl.BlockSpec(tail, lambda h: (0, h, 0, 0)),
            pl.BlockSpec(tail, lambda h: (1, h, 0, 0)),
            whole((KEY_ROWS, LANES)),
            whole((TABLE, LANES)),
            whole((ROWS, TABLE)),
            whole((TABLE, LANES)),
        ],
        out_specs=(
            pl.BlockSpec((1, ROWS, KEY_ROWS), lambda h: (h, 0, 0)),
            pl.BlockSpec(head, lambda h: (h, 0, 0)),
            pl.BlockSpec(head, lambda h: (h, 0, 0)),
        ),
        scratch_shapes=[
            pltpu.VMEM((KEY_ROWS, LANES), BF16),
            pltpu.VMEM((KEY_ROWS, LANES), BF16),
            pltpu.VMEM((ROWS, LANES), BF16),
        ],
        compiler_params=params(),
        name="attend",
    )(heads, heads, heads, rest, rest, aug, table, own, fold)


CHUNK = 384
CHUNKS = FF // CHUNK


def middle_kernel(
    place_ref, att_ref, x_ref, up_ref, wp_ref, w1_ref, w2_ref, pb_ref, g2_ref, b2_ref, fb1_ref, fb2_ref,
    out_ref, dmid_ref, datt_ref, gp_ref, gw1_ref, gw2_ref, small_ref, gb1_ref,
    packed_ref, proj_ref, mid_ref, hidden_ref, total_ref, dhid_ref, wide_ref, w1_scr, w2_scr,
):
    step = pl.program_id(0)
    sides = wp_ref.shape[1]
    part = D // sides
    depth = D // DP_BLOCKS

    @pl.when(step == 0)
    def _():
        for head in range(HEADS):
            packed_ref[:, HEAD_DIM * head : HEAD_DIM * (head + 1)] = att_ref[head][:, :HEAD_DIM]
        for f in range(sides):
            for d in range(DP_BLOCKS):
                rows = slice(d * depth, (d + 1) * depth)
                proj_ref[rows, f * part : f * part + LANES] = wp_ref[d, f, :depth]
                proj_ref[rows, f * part + LANES : (f + 1) * part] = wp_ref[d, f, depth:, : part - LANES]
        middle = x_ref[...].astype(F32) + dot(packed_ref[...], proj_ref[...]) + pb_ref[...]
        mid_ref[...] = middle
        centred, rs = layer_stats(middle, D)
        hidden_ref[...] = (centred * rs * g2_ref[...] + b2_ref[...]).astype(BF16)
        total_ref[...] = middle + fb2_ref[...]
        dhid_ref[...] = jnp.zeros((ROWS, D), F32)

    for tile in range(CHUNK // LANES):
        lanes = slice(tile * LANES, (tile + 1) * LANES)
        for d in range(DP_BLOCKS):
            w1_scr[d * depth : (d + 1) * depth, lanes] = w1_ref[d, 0, tile * depth : (tile + 1) * depth]
        for f in range(sides):
            w2_scr[f * part : (f + 1) * part, lanes] = w2_ref[0, f, tile * part : (tile + 1) * part]
    w1, w2 = w1_scr[...], w2_scr[...]
    before = dot(hidden_ref[...], w1) + fb1_ref[...]
    erf = lax.erf(before * (2.0**-0.5))
    cdf = 0.5 * (1.0 + erf)
    activated = (before * cdf).astype(BF16)
    slope = cdf + before * (jnp.exp(before * before * -0.5) * 0.3989422804014327)
    dbefore = dot(up_ref[...], w2) * slope
    dbefore_low = dbefore.astype(BF16)
    gb1_ref[...] = jnp.sum(dbefore_low.astype(F32), axis=0, keepdims=True)
    total_ref[...] += dot(activated, w2, ((1,), (1,)))
    grad_two = dot(activated, up_ref[...], ((0,), (0,))).astype(BF16)
    for f in range(sides):
        bits = relative_bits(place_ref, 0, f)
        gw2_ref[bits["c"], bits["y"], 0, 0, 0] = grad_two[:, f * part : (f + 1) * part]
    dhid_ref[...] += dot(dbefore_low, w1, ((1,), (1,)))
    grad_one = dot(hidden_ref[...], dbefore_low, ((0,), (0,))).astype(BF16)
    for d in range(DP_BLOCKS):
        bits = relative_bits(place_ref, d, 0)
        gw1_ref[0, bits["x"], 0, bits["z1"], bits["z2"]] = grad_one[d * depth : (d + 1) * depth]

    @pl.when(step == CHUNKS - 1)
    def _():
        @pl.loop(0, PLACES)
        def _(place):
            at = pl.multiple_of(place * FRAMES, FRAMES)
            write_place(wide_ref, place, total_ref[pl.ds(at, FRAMES), :])

        for tile in range(D // LANES):
            out_ref[:, tile * LANES : (tile + 1) * LANES] = wide_ref[tile].astype(BF16)
        upstream = up_ref[...].astype(F32)
        dhidden = dhid_ref[...]
        centred, rs = layer_stats(mid_ref[...], D)
        vhat = centred * rs
        dgain = jnp.sum(dhidden * vhat, axis=0, keepdims=True)
        dbias = jnp.sum(dhidden, axis=0, keepdims=True)
        scaled = dhidden * g2_ref[...]
        first = jnp.sum(scaled, axis=1, keepdims=True) * (1.0 / D)
        second = jnp.sum(scaled * vhat, axis=1, keepdims=True) * (1.0 / D)
        dmiddle = upstream + rs * (scaled - first - vhat * second)
        dmid_ref[...] = dmiddle
        dproj = dmiddle.astype(BF16)
        small_ref[0:1, :] = jnp.sum(dproj.astype(F32), axis=0, keepdims=True)
        small_ref[1:2, :] = dgain
        small_ref[2:3, :] = dbias
        small_ref[3:4, :] = jnp.sum(upstream, axis=0, keepdims=True)
        small_ref[4:8, :] = jnp.zeros((4, D), F32)
        grad_proj = dot(packed_ref[...], dproj, ((0,), (0,))).astype(BF16)
        for d in range(DP_BLOCKS):
            for f in range(sides):
                bits = relative_bits(place_ref, d, f)
                block = grad_proj[d * depth : (d + 1) * depth, f * part : (f + 1) * part]
                gp_ref[bits["c"], bits["y"], bits["x"], bits["z1"], bits["z2"]] = block
        datt = dot(dproj, proj_ref[...], ((1,), (1,))).astype(BF16)
        for head in range(HEADS):
            datt_ref[head] = jnp.concatenate(
                [datt[:, HEAD_DIM * head : HEAD_DIM * (head + 1)], jnp.zeros((ROWS, LANES - HEAD_DIM), BF16)],
                axis=1,
            )


def feed_forward(place, att, x, up, flat, pb, g2, b2, fb1, fb2):
    once = pl.Buffered(1)
    sides = flat.shape[1]
    part, depth = D // sides, D // DP_BLOCKS

    def kept(shape):
        return pl.BlockSpec(shape, lambda *_: (0,) * len(shape), pipeline_mode=once)

    def one_place(c, place):
        return (place[4] ^ ((c // 2) & 1), 0, place[3] ^ (c // 4), 0, 0, 0, c % 2)

    def two_place(c, place):
        return (0, 0, place[0] ^ (c & 1), place[1] ^ ((c >> 1) & 1), place[2] ^ (c >> 2), 0, 0)

    def clear(c, place):
        return (0, c)

    return pl.pallas_call(
        middle_kernel,
        out_shape=(
            jax.ShapeDtypeStruct((ROWS, D), BF16),
            jax.ShapeDtypeStruct((ROWS, D), F32),
            jax.ShapeDtypeStruct((HEADS, ROWS, LANES), BF16),
            jax.ShapeDtypeStruct((2, 2, 2, 2, 2, depth, part), BF16),
            jax.ShapeDtypeStruct((2, 2, 2, 2, 2, depth, FF // sides), BF16),
            jax.ShapeDtypeStruct((2, 2, 2, 2, 2, FF // DP_BLOCKS, part), BF16),
            jax.ShapeDtypeStruct((8, D), F32),
            jax.ShapeDtypeStruct((1, FF), F32),
        ),
        grid_spec=pltpu.PrefetchScalarGridSpec(
            num_scalar_prefetch=1,
            grid=(CHUNKS,),
            in_specs=[
                kept((HEADS, ROWS, LANES)),
                kept((ROWS, D)),
                kept((ROWS, D)),
                pl.BlockSpec((DP_BLOCKS, sides, 2 * depth, LANES), lambda c, place: (0, 0, 6, 0), pipeline_mode=once),
                pl.BlockSpec((DP_BLOCKS, 1, 3 * depth, LANES), lambda c, place: (0, c // 2, c % 2, 0)),
                pl.BlockSpec((1, sides, 3 * part, LANES), lambda c, place: (c, 0, 1, 0)),
                kept((1, D)),
                kept((1, D)),
                kept((1, D)),
                pl.BlockSpec((1, CHUNK), clear),
                kept((1, D)),
            ],
            out_specs=(
                kept((ROWS, D)),
                kept((ROWS, D)),
                kept((HEADS, ROWS, LANES)),
                kept((2, 2, 2, 2, 2, depth, part)),
                pl.BlockSpec((1, 2, 1, 2, 2, depth, CHUNK), one_place),
                pl.BlockSpec((2, 2, 1, 1, 1, FF // DP_BLOCKS, part), two_place),
                kept((8, D)),
                pl.BlockSpec((1, CHUNK), clear),
            ),
            scratch_shapes=[
                pltpu.VMEM((ROWS, D), BF16),
                pltpu.VMEM((D, D), BF16),
                pltpu.VMEM((ROWS, D), F32),
                pltpu.VMEM((ROWS, D), BF16),
                pltpu.VMEM((ROWS, D), F32),
                pltpu.VMEM((ROWS, D), F32),
                wide_scratch(D),
                pltpu.VMEM((D, CHUNK), BF16),
                pltpu.VMEM((D, CHUNK), BF16),
            ],
        ),
        compiler_params=params(),
        name="feed_forward",
    )(place, att, x, up, flat, flat, flat, pb, g2, b2, fb1, fb2)


def attend_back_kernel(
    q_ref, k_ref, v_ref, krest_ref, vrest_ref, aug_ref, table_ref, own_ref, fold_ref, pick_ref,
    weights_ref, pv_ref, datt_ref, parts_ref,
    grads_ref, gtable_ref, gtaps_ref,
    keys_ref, vals_ref, up_ref, slopes_ref, gsum_ref,
):
    step = pl.program_id(0)
    lane = lane_index((KEY_ROWS, LANES))
    row_lane = lane[:ROWS]

    @pl.when(step == 0)
    def _():
        gsum_ref[...] = jnp.zeros((TABLE, LANES), F32)
        gtaps_ref[...] = jnp.zeros((2, 4, LANES), F32)

    keys_ref[:ROWS] = k_ref[0] + aug_ref[:ROWS]
    keys_ref[ROWS:] = krest_ref[0, 0] + aug_ref[ROWS:]
    one = jnp.where((lane >= HEAD_DIM) & (lane < HEAD_DIM + 3), 1.0, 0.0).astype(BF16)
    vals_ref[:ROWS] = v_ref[0] + one[:ROWS]
    vals_ref[ROWS:] = vrest_ref[0, 0] + one[ROWS:]
    pv = pv_ref[0].astype(F32)
    inverse = pv[:, HEAD_DIM : HEAD_DIM + 1] + pv[:, HEAD_DIM + 1 : HEAD_DIM + 2]
    datt = datt_ref[0].astype(F32)
    upstream = (datt * inverse).astype(BF16).astype(F32)
    mean = jnp.sum(upstream * pv, axis=1, keepdims=True)
    high = mean.astype(BF16).astype(F32)
    low = (mean - high).astype(BF16).astype(F32)
    least = mean - high - low
    extra = jnp.where(
        row_lane == HEAD_DIM,
        -high,
        jnp.where(row_lane == HEAD_DIM + 1, -low, jnp.where(row_lane == HEAD_DIM + 2, -least, 0.0)),
    )
    up_ref[...] = (upstream + extra).astype(BF16)

    @pl.loop(0, ROWS // ROW_BLOCK)
    def _(block):
        rows = pl.ds(pl.multiple_of(block * ROW_BLOCK, ROW_BLOCK), ROW_BLOCK)
        dprobs = dot(up_ref[rows, :], vals_ref[...], ((1,), (1,)))
        slopes_ref[rows, :] = (weights_ref[0, rows, :].astype(F32) * dprobs).astype(BF16)

    dvals = dot(weights_ref[0], up_ref[...], ((0,), (0,)))
    dkeys = dot(slopes_ref[...], q_ref[0], ((0,), (0,))) * SCALE
    dquery = dot(slopes_ref[...], keys_ref[...])
    spread = dot(dquery.astype(BF16), fold_ref[...], ((1,), (1,))).astype(BF16) * own_ref[...]
    gsum_ref[...] += dot(spread, q_ref[0], ((0,), (0,)))
    dquery = dquery * SCALE + datt + dot(spread, table_ref[...])
    grads_ref[0, 0] = dquery.astype(BF16)
    grads_ref[1, 0] = dkeys[:ROWS].astype(BF16)
    grads_ref[2, 0] = dvals[:ROWS].astype(BF16)
    for s, whole_grad in ((0, dkeys), (1, dvals)):
        piece = whole_grad[SQUEEZE_AT : SQUEEZE_AT + MEM]
        for tap in range(4):
            product = piece * parts_ref[s, 0, tap].astype(F32)[:MEM]
            gtaps_ref[s, tap : tap + 1, :] += jnp.sum(product, axis=0, keepdims=True)

    @pl.when(step == pl.num_programs(0) - 1)
    def _():
        gtable_ref[...] = dot(pick_ref[...], gsum_ref[...], ((0,), (0,)), lax.Precision.HIGHEST)


def attend_back(start, count, heads, rest, aug, table, own, fold, pick, weights, pv, datt, parts):
    head = (1, ROWS, LANES)
    tail = (1, 1, REST, LANES)
    own_head = pl.BlockSpec(head, lambda h: (start + h, 0, 0))
    return pl.pallas_call(
        attend_back_kernel,
        grid=(count,),
        out_shape=(
            jax.ShapeDtypeStruct((3, count, ROWS, LANES), BF16),
            jax.ShapeDtypeStruct((LANES, LANES), F32),
            jax.ShapeDtypeStruct((2, 4, LANES), F32),
        ),
        in_specs=[
            own_head,
            pl.BlockSpec(head, lambda h: (HEADS + start + h, 0, 0)),
            pl.BlockSpec(head, lambda h: (2 * HEADS + start + h, 0, 0)),
            pl.BlockSpec(tail, lambda h: (0, start + h, 0, 0)),
            pl.BlockSpec(tail, lambda h: (1, start + h, 0, 0)),
            whole((KEY_ROWS, LANES)),
            whole((TABLE, LANES)),
            whole((ROWS, TABLE)),
            whole((TABLE, LANES)),
            whole((TABLE, LANES)),
            pl.BlockSpec((1, ROWS, KEY_ROWS), lambda h: (start + h, 0, 0)),
            own_head,
            own_head,
            pl.BlockSpec((2, 1, 4, 208, LANES), lambda h: (0, start + h, 0, 0, 0)),
        ],
        out_specs=(
            pl.BlockSpec((3, 1, ROWS, LANES), lambda h: (0, h, 0, 0)),
            whole((LANES, LANES)),
            whole((2, 4, LANES)),
        ),
        scratch_shapes=[
            pltpu.VMEM((KEY_ROWS, LANES), BF16),
            pltpu.VMEM((KEY_ROWS, LANES), BF16),
            pltpu.VMEM((ROWS, LANES), BF16),
            pltpu.VMEM((ROWS, KEY_ROWS), BF16),
            pltpu.VMEM((TABLE, LANES), F32),
        ],
        compiler_params=params(),
        name="attend_back",
    )(heads, heads, heads, rest, rest, aug, table, own, fold, pick.astype(F32), weights, pv, datt, parts)


def pool_back_kernel(
    frames_ref, first_ref, second_ref, vhat_ref, mixed_ref, taps_raw_ref, gain_ref,
    dmix_ref, gbias_ref, gtaps_ref, gpool_ref,
    grid_ref, dgrid_ref, dpool_ref, sums_ref, taps_ref,
):
    step = pl.program_id(0)

    @pl.when(step == 0)
    def _():
        spread_taps(taps_raw_ref, taps_ref)
        clear_border(grid_ref)
        clear_border(dgrid_ref)

    lane = lane_index((ROWS, LANES))
    for head in range(GROUP_HEADS):
        dy = jnp.where(step == 0, first_ref[0, head].astype(F32), second_ref[0, head].astype(F32))
        dy = jnp.where(lane < HEAD_DIM, dy, 0.0)
        vhat = vhat_ref[head].astype(F32)
        rs = vhat[:, HEAD_DIM : HEAD_DIM + 1] + vhat[:, HEAD_DIM + 1 : HEAD_DIM + 2]
        product = dy * vhat
        gpool_ref[head, 0:1, :] = jnp.sum(product, axis=0, keepdims=True)
        gpool_ref[head, 1:2, :] = jnp.sum(dy, axis=0, keepdims=True)
        scaled = dy * gain_ref[0]
        first = jnp.sum(scaled, axis=1, keepdims=True) * (1.0 / HEAD_DIM)
        second = jnp.sum(product * gain_ref[0], axis=1, keepdims=True) * (1.0 / HEAD_DIM)
        dpool = rs * (scaled - first - vhat * second)
        dpool_ref[:, HEAD_DIM * head : HEAD_DIM * (head + 1)] = dpool[:, :HEAD_DIM]
    dgrid_ref[1 : HEIGHT + 1, 1 : WIDTH + 1] = dpool_ref[...].reshape(HEIGHT, WIDTH, FRAMES, GROUP)
    grid_ref[1 : HEIGHT + 1, 1 : WIDTH + 1] = mixed_ref[...].astype(F32).reshape(HEIGHT, WIDTH, FRAMES, GROUP)
    sums_ref[...] = jnp.zeros(sums_ref.shape, F32)

    @pl.loop(0, HEIGHT)
    def _(i):
        for tile in range(GROUP // LANES):
            lanes = slice(tile * LANES, tile * LANES + LANES)
            line = convolve(dgrid_ref, taps_ref, True, i, lanes)
            frame = lax.broadcasted_iota(jnp.int32, line.shape, 1)
            line = jnp.where(frame < frames_ref[0], line, 0.0)
            at = pl.multiple_of(i * WIDTH * FRAMES, WIDTH * FRAMES)
            dmix_ref[pl.ds(at, WIDTH * FRAMES), lanes] = line.reshape(WIDTH * FRAMES, LANES).astype(BF16)
            own = dgrid_ref[i + 1, 1 : WIDTH + 1, :, lanes]
            moved = (shift_frames(own, -1), own, shift_frames(own, 1))
            for b in range(3):
                for e in range(3):
                    window = grid_ref[i + b, e : e + WIDTH, :, lanes]
                    for a in range(3):
                        tap = 9 * a + 3 * b + e
                        sums_ref[tap, :, lanes] += jnp.sum(window * moved[a], axis=0)

    for tap in range(27):
        gtaps_ref[0, tap : tap + 1, :] = jnp.sum(sums_ref[tap], axis=0, keepdims=True)
    gbias_ref[...] = jnp.sum(dmix_ref[...].astype(F32), axis=0, keepdims=True)


def pool_back(kind, frames, grads_a, grads_b, vhat, mixed, taps, gain):
    smem = pl.BlockSpec(memory_space=pltpu.SMEM)
    return pl.pallas_call(
        pool_back_kernel,
        grid=(2,),
        out_shape=(
            jax.ShapeDtypeStruct((ROWS, D), BF16),
            jax.ShapeDtypeStruct((1, D), F32),
            jax.ShapeDtypeStruct((2, 27, GROUP), F32),
            jax.ShapeDtypeStruct((HEADS, 2, LANES), F32),
        ),
        in_specs=[
            smem,
            pl.BlockSpec((1, GROUP_HEADS, ROWS, LANES), lambda g: (kind, 0, 0, 0)),
            pl.BlockSpec((1, GROUP_HEADS, ROWS, LANES), lambda g: (kind, 0, 0, 0)),
            pl.BlockSpec((GROUP_HEADS, ROWS, LANES), lambda g: (2 * kind + g, 0, 0)),
            pl.BlockSpec((ROWS, GROUP), lambda g: (0, 2 * kind + g)),
            pl.BlockSpec((1, 27, HEAD_DIM), lambda g: (kind, 0, 0)),
            pl.BlockSpec((1, 1, LANES), lambda g: (kind, 0, 0)),
        ],
        out_specs=(
            pl.BlockSpec((ROWS, GROUP), lambda g: (0, g)),
            pl.BlockSpec((1, GROUP), lambda g: (0, g)),
            pl.BlockSpec((1, 27, GROUP), lambda g: (g, 0, 0)),
            pl.BlockSpec((GROUP_HEADS, 2, LANES), lambda g: (g, 0, 0)),
        ),
        scratch_shapes=[
            pltpu.VMEM((HEIGHT + 2, WIDTH + 2, FRAMES, GROUP), F32),
            pltpu.VMEM((HEIGHT + 2, WIDTH + 2, FRAMES, GROUP), F32),
            pltpu.VMEM((ROWS, GROUP), F32),
            pltpu.VMEM((27, FRAMES, GROUP), F32),
            pltpu.VMEM((27, FRAMES, GROUP), F32),
        ],
        compiler_params=params(),
        name="pool_back_%d" % kind,
    )(frames, grads_a, grads_b, vhat, mixed, taps, gain)


def project_grad_kernel(place_ref, normed_ref, dq_ref, dk_ref, dv_ref, one_ref, two_ref, full_ref):
    for kind, source_ref in enumerate((dq_ref, dk_ref, dv_ref)):
        grad = dot(normed_ref[...], source_ref[...], ((0,), (0,)))
        full_ref[:, kind * D : (kind + 1) * D] = grad.astype(BF16)
    half, columns = one_ref.shape[5:]
    for f in range(QKV // columns):

        @pl.loop(0, DP_BLOCKS)
        def _(d):
            bits = relative_bits(place_ref, d, f)
            lanes = slice(f * columns, (f + 1) * columns)
            at = pl.multiple_of(2 * d * half, half)
            one_ref[bits["c"], bits["x"], bits["y"], bits["z1"], bits["z2"]] = full_ref[pl.ds(at, half), lanes]
            at = pl.multiple_of((2 * d + 1) * half, half)
            two_ref[bits["c"], bits["y"], bits["x"], bits["z1"], bits["z2"]] = full_ref[pl.ds(at, half), lanes]


def project_grad(place, normed, dmixed, sides):
    vmem = pl.BlockSpec(memory_space=pltpu.VMEM)
    half = jax.ShapeDtypeStruct((2, 2, 2, 2, 2, D // DP_BLOCKS // 2, QKV // sides), BF16)
    return pl.pallas_call(
        project_grad_kernel,
        out_shape=(half, half),
        in_specs=[pl.BlockSpec(memory_space=pltpu.SMEM)] + [vmem] * 4,
        out_specs=(vmem, vmem),
        scratch_shapes=[pltpu.VMEM((D, QKV), BF16)],
        compiler_params=params(),
        name="project_grad",
    )(place, normed, *dmixed)


def project_back_kernel(
    dq_ref, dk_ref, dv_ref, weight_ref, x_ref, dmid_ref, g1_ref, gtok_ref, small_ref, dx_ref, wide_ref
):
    dy = None
    for kind, source_ref in enumerate((dq_ref, dk_ref, dv_ref)):
        term = dot(source_ref[...], weight_ref[:, kind * D : (kind + 1) * D], ((1,), (1,)))
        dy = term if dy is None else dy + term
    centred, rs = layer_stats(x_ref[...].astype(F32), D)
    vhat = centred * rs
    small_ref[0:1, :] = jnp.sum(dy * vhat, axis=0, keepdims=True)
    small_ref[1:2, :] = jnp.sum(dy, axis=0, keepdims=True)
    small_ref[2:8, :] = jnp.zeros((6, D), F32)
    scaled = dy * g1_ref[...]
    first = jnp.sum(scaled, axis=1, keepdims=True) * (1.0 / D)
    second = jnp.sum(scaled * vhat, axis=1, keepdims=True) * (1.0 / D)
    dx_ref[...] = dmid_ref[...] + rs * (scaled - first - vhat * second)

    @pl.loop(0, PLACES)
    def _(place):
        at = pl.multiple_of(place * FRAMES, FRAMES)
        write_place(wide_ref, place, dx_ref[pl.ds(at, FRAMES), :])

    for tile in range(D // LANES):
        gtok_ref[:, tile * LANES : (tile + 1) * LANES] = wide_ref[tile]


def project_back(dmixed, weight, x, dmid, g1):
    vmem = pl.BlockSpec(memory_space=pltpu.VMEM)
    return pl.pallas_call(
        project_back_kernel,
        out_shape=(jax.ShapeDtypeStruct((ROWS, D), F32), jax.ShapeDtypeStruct((8, D), F32)),
        in_specs=[vmem] * 7,
        out_specs=(vmem, vmem),
        scratch_shapes=[pltpu.VMEM((ROWS, D), F32), wide_scratch(D)],
        compiler_params=params(),
        name="project_back",
    )(*dmixed, weight, x, dmid, g1)


def row(vector):
    return vector.reshape(1, -1)


def tiled_lanes(array):
    return jnp.concatenate([array] * GROUP_HEADS, axis=-1)


def head_lanes(array):
    return jnp.pad(array, [(0, 0)] * (array.ndim - 1) + [(0, LANES - HEAD_DIM)])


DP_BLOCKS = 8
ROUTE_ONE = ("z2", "z1", "y", "x", "c")
ROUTE_TWO = ("z2", "z1", "x", "y", "c")
BIT = {"x": ("dp", 1), "z1": ("dp", 2), "z2": ("dp", 4), "y": ("fsdp", 2), "c": ("fsdp", 1)}


def swap(values, name, sizes):
    axis, bit = BIT[name]
    return lax.ppermute(values, axis, [(at, at ^ bit) for at in range(sizes[axis])])


def together(*values):
    return lax.optimization_barrier(values)


def flat_shard(one, two, proj):
    pieces = [part for _, part in flat_pieces(one, two, proj)]
    pieces[-1] = jnp.pad(pieces[-1], ((0, 0), (0, LANES - pieces[-1].shape[1])))
    return jnp.concatenate(pieces, axis=0)


class Staged:
    def __init__(self):
        self.sizes = {"dp": 8, "fsdp": 4}

    def place(self):
        dp, fsdp = lax.axis_index("dp"), lax.axis_index("fsdp")
        return jnp.stack([dp & 1, (dp >> 1) & 1, (dp >> 2) & 1, (fsdp >> 1) & 1, fsdp & 1]).astype(jnp.int32)

    def other_weights(self, flat):
        return lax.all_gather(flat, ("dp", "fsdp"), axis=0, tiled=False).reshape((8, 4) + flat.shape)

    def halve(self, blocks, name):
        return blocks[0], swap(blocks[1], name, self.sizes)

    def total(self, vector):
        for name in ("c", "x", "y", "z1", "z2"):
            vector = vector + swap(vector, name, self.sizes)
        return vector


class Plain:
    def __init__(self, dp, fsdp):
        self.dp, self.fsdp = dp, fsdp

    def place(self):
        return jnp.zeros((5,), jnp.int32)

    def gather(self, shard):
        blocks = lax.all_gather(shard, ("dp", "fsdp"), axis=0, tiled=False)
        rows, columns = shard.shape
        joined = blocks.reshape(DP_BLOCKS, self.dp // DP_BLOCKS, self.fsdp, rows, columns).transpose(0, 2, 1, 3, 4)
        return joined.reshape(DP_BLOCKS, self.fsdp, self.dp // DP_BLOCKS * rows, columns)

    def other_weights(self, one, two, proj):
        return jax.vmap(jax.vmap(flat_shard))(self.gather(one), self.gather(two), self.gather(proj))

    def scatter(self, blocks, route):
        at = {name: 4 - where for where, name in enumerate(route)}
        rows, columns = blocks.shape[5:]
        blocks = blocks.transpose([at[name] for name in ("z2", "z1", "x", "y", "c")] + [5, 6])
        split = blocks.reshape(DP_BLOCKS, self.fsdp, self.dp // DP_BLOCKS, rows * DP_BLOCKS // self.dp, columns)
        split = split.transpose(0, 2, 1, 3, 4).reshape(self.dp * self.fsdp, -1, columns)
        return lax.psum_scatter(split, ("dp", "fsdp"), scatter_dimension=0, tiled=False).astype(F32)

    def total(self, vector):
        return lax.psum(vector, ("dp", "fsdp"))


def run(
    comm, staged, tokens, prev_kv, memory, valid_frames, mem_len, ln1_gain, ln1_bias, w_qkv, qkv_bias, pool_conv, pool_gain,
    pool_bias, rel_time, rel_space, compress, w_proj, proj_bias, ln2_gain, ln2_bias, w_fc1, fc1_bias, w_fc2,
    fc2_bias, cotangent,
):
    place = comm.place()
    one_hot, own, fold, pick = (jnp.asarray(c, BF16) for c in constants())
    taps, gains, biases = pool_conv, head_lanes(pool_gain)[:, None], head_lanes(pool_bias)[:, None]
    prepared = prepare(
        valid_frames, mem_len, tokens, cotangent, ln1_gain, ln1_bias, one_hot, rel_time, rel_space, pick,
        prev_kv, memory, compress, [w_qkv, w_fc1, w_fc2, w_proj] if staged else None,
    )
    x, normed, upstream, aug, table, rest, parts = prepared[-7:]
    if staged:
        first, flat = prepared[0].reshape(8, 4, *w_qkv.shape), comm.other_weights(prepared[1])
    else:
        first, flat = comm.gather(w_qkv), comm.other_weights(w_fc1, w_fc2, w_proj)
    heads, vhat, mixed, weight = query_key_value(valid_frames, normed, first, row(qkv_bias), taps, gains, biases)
    weights, pv, attended = attend(heads, rest, aug, table, own, fold)
    out, dmid, datt, gp, gw1, gw2, small_two, gb1 = feed_forward(
        place, attended, x, upstream, flat, row(proj_bias), row(ln2_gain), row(ln2_bias), row(fc1_bias), row(fc2_bias)
    )
    middle = {"proj": (gp, ROUTE_TWO), "one": (gw1, ROUTE_ONE), "two": (gw2, ROUTE_TWO)}
    big, routes = {k: v[0] for k, v in middle.items()}, {k: v[1] for k, v in middle.items()}

    def start(stage):
        return {k: comm.halve(big[k], routes[k][4 - stage]) for k in big} if staged else None

    def finish(moving, *after):
        if not staged:
            return after
        flying = [v for pair in moving.values() for v in pair]
        tied = together(*flying, *after)
        for at, k in enumerate(moving):
            big[k] = tied[2 * at] + tied[2 * at + 1]
        return tied[2 * len(moving) :]

    def back(start_head, datt):
        return attend_back(
            start_head, HEADS // 2, heads, rest, aug, table, own, fold, pick, weights, pv, datt, parts
        )

    moving = start(0)
    grads_a, gtable_a, gcompress_a = back(0, datt)
    (grads_a, datt) = finish(moving, grads_a, datt)
    moving = start(1)
    grads_b, gtable_b, gcompress_b = back(HEADS // 2, datt)
    (grads_a, grads_b) = finish(moving, grads_a, grads_b)
    dmixed, gbias, gtaps, gpool = [], [], [], []
    for kind in range(3):
        moving = start(2 + kind)
        pieces = pool_back(kind, valid_frames, grads_a, grads_b, vhat, mixed, taps, gains)
        (piece, grads_a) = finish(moving, pieces[0], grads_a)
        dmixed.append(piece)
        gbias.append(pieces[1])
        gtaps.append(pieces[2])
        gpool.append(pieces[3])
    qkv_one, qkv_two = project_grad(place, normed, dmixed, QKV // w_qkv.shape[1])
    if staged:
        for stage in range(5):
            kept_one, more_one = comm.halve(qkv_one, ROUTE_ONE[4 - stage])
            kept_two, more_two = comm.halve(qkv_two, ROUTE_TWO[4 - stage])
            qkv_one, qkv_two = kept_one + more_one, kept_two + more_two
    gtok, small_one = project_back(dmixed, weight, x, dmid, row(ln1_gain))
    gconv = jnp.sum(jnp.stack(gtaps).reshape(3, 2, 27, GROUP_HEADS, HEAD_DIM), axis=(1, 3))
    gpool = jnp.sum(jnp.stack(gpool), axis=1)[:, :, :HEAD_DIM]
    gtable, gcompress = gtable_a + gtable_b, gcompress_a + gcompress_b
    smalls = (
        small_one[0], small_one[1], jnp.concatenate(gbias, axis=1)[0], gconv, gpool[:, 0], gpool[:, 1],
        gtable[:15, :HEAD_DIM], gtable[15:53, :HEAD_DIM].reshape(2, 19, HEAD_DIM), gcompress[:, :, :HEAD_DIM],
        small_two[0], small_two[1], small_two[2], gb1[0], small_two[3],
    )
    vector = comm.total(jnp.concatenate([s.reshape(-1) for s in smalls]))
    totals, at = [], 0
    for s in smalls:
        totals.append(vector[at : at + s.size].reshape(s.shape))
        at += s.size
    if staged:
        qkv = jnp.concatenate([qkv_one, qkv_two], axis=0).astype(F32)
        sums = [qkv] + [big[k].astype(F32) for k in ("proj", "one", "two")]
    else:
        qkv_one = comm.scatter(jnp.concatenate([qkv_one, jnp.moveaxis(qkv_two, 1, 2)], axis=5), ROUTE_ONE)
        sums = [qkv_one] + [comm.scatter(big[k], routes[k]) for k in ("proj", "one", "two")]
    return (
        out, gtok, totals[0], totals[1], sums[0], totals[2], totals[3], totals[4], totals[5], totals[6],
        totals[7], totals[8], sums[1], totals[9], totals[10], totals[11], sums[2], totals[12], sums[3], totals[13],
    )


def solution(mesh):
    both = P(("dp", "fsdp"))
    rows = P(("dp", "fsdp"), None)
    second = P(None, ("dp", "fsdp"), None)
    blocks = P("dp", "fsdp")
    none = P()
    dp, fsdp = mesh.shape["dp"], mesh.shape["fsdp"]
    staged = (dp, fsdp) == (8, 4)
    return jax.shard_map(
        functools.partial(run, Staged() if staged else Plain(dp, fsdp), staged),
        mesh=mesh,
        in_specs=(
            rows, second, second, both, both, none, none, blocks, none, none, none, none, none, none, none, blocks,
            none, none, none, blocks, none, blocks, none, rows,
        ),
        out_specs=(
            rows, rows, none, none, blocks, none, none, none, none, none, none, none, blocks, none, none, none,
            blocks, none, blocks, none,
        ),
        check_vma=False,
    )
```

```python
import functools

import jax
import jax.numpy as jnp
import numpy as np
from jax import lax
from jax.experimental import pallas as pl
from jax.experimental.pallas import tpu as pltpu
from jax.sharding import PartitionSpec as P

D = 768
FF = 3072
HEADS = 8
HEAD_DIM = 96
LANES = 128
FRAMES = 8
HEIGHT = 10
WIDTH = 10
PLACES = HEIGHT * WIDTH
ROWS = 800
MEM = 200
GROUP = 384
GROUP_HEADS = 4
QKV = 3 * D
KEY_ROWS = 1280
MEM_AT = 800
SQUEEZE_AT = 1024
REST = KEY_ROWS - ROWS
TABLE = 384
EPSILON = 1e-06
SCALE = HEAD_DIM**-0.5
ROOT = HEAD_DIM**0.5
LOG2E = 1.4426950408889634
MASKED = -1e9
MASK_LANE = 124
ROW_BLOCK = 400
BF16 = jnp.bfloat16
F32 = jnp.float32
VMEM_LIMIT = 60 * 1024 * 1024


def constants():
    place = np.arange(PLACES).repeat(FRAMES)
    row_t = np.tile(np.arange(FRAMES), PLACES)
    row_i, row_j = place // WIDTH, place % WIDTH
    one_hot = np.zeros((KEY_ROWS, LANES), np.float32)
    rows = np.arange(ROWS)
    one_hot[rows, 96 + row_t] = 1
    one_hot[rows, 104 + row_i] = 1
    one_hot[rows, 114 + row_j] = 1
    own = np.zeros((ROWS, TABLE), np.float32)
    fold = np.zeros((TABLE, LANES), np.float32)
    pick = np.zeros((TABLE, LANES), np.float32)
    for base, length, row_at, lane, offset in (
        (0, FRAMES, row_t, 96, 0),
        (64, HEIGHT, row_i, 104, 15),
        (164, WIDTH, row_j, 114, 34),
    ):
        for a in range(length):
            for b in range(length):
                column = base + a * length + b
                own[:, column] = row_at == a
                fold[column, lane + b] = 1
                pick[column, offset + a - b + length - 1] = 1
    lanes = np.arange(GROUP) // HEAD_DIM
    same = (lanes[:, None] == lanes[None, :]).astype(np.float32)
    return one_hot, own, fold, pick, same


def lane_index(shape):
    return lax.broadcasted_iota(jnp.int32, shape, len(shape) - 1)


def dot(a, b, contract=((1,), (0,)), precision=None):
    return lax.dot_general(a, b, (contract, ((), ())), preferred_element_type=F32, precision=precision)


def layer_stats(values, width):
    average = jnp.sum(values, axis=-1, keepdims=True) * (1.0 / width)
    centred = values - average
    variance = jnp.sum(centred * centred, axis=-1, keepdims=True) * (1.0 / width)
    return centred, lax.rsqrt(variance + EPSILON)


def params(**more):
    return pltpu.CompilerParams(vmem_limit_bytes=VMEM_LIMIT, **more)


def whole(shape):
    return pl.BlockSpec(shape, lambda *_: (0,) * len(shape))


def tiles_of(values):
    return [values[:, at : at + LANES] for at in range(0, values.shape[1], LANES)]


def flat_pieces(one, two, proj):
    at = 0
    for part in tiles_of(one) + tiles_of(two) + tiles_of(proj):
        yield at, part
        at += part.shape[0]


def read_place(wide_ref, place, tiles=D // LANES):
    parts = [wide_ref[tile, pl.ds(place, FRAMES, stride=PLACES), :] for tile in range(tiles)]
    return jnp.concatenate(parts, axis=1)


def write_place(wide_ref, place, values):
    for tile, part in enumerate(tiles_of(values)):
        wide_ref[tile, pl.ds(place, FRAMES, stride=PLACES), :] = part


def wide_scratch(columns):
    return pltpu.VMEM((columns // LANES, ROWS, LANES), F32)


PARTS = 3
MESH = pl.DeviceIdType.MESH


class Gather:
    def __init__(self, shard_ref, all_ref, own_sem, send_sem, recv_sem):
        dp, fsdp = lax.axis_index("dp"), lax.axis_index("fsdp")
        self.z, self.x = dp // 2, dp % 2
        self.y, self.c = fsdp // 2, fsdp % 2
        self.shard_ref, self.all_ref = shard_ref, all_ref
        self.own_sem, self.send_sem, self.recv_sem = own_sem, send_sem, recv_sem
        self.rows = shard_ref.shape[0] // (2 * PARTS)
        self.copies = {}

    def device(self, z, x, y, c):
        return (2 * z + x, 2 * y + c)

    def partners(self):
        z, x, y, c = self.z, self.x, self.y, self.c
        along = [self.device((z + k) % 4, x, y, c) for k in (1, 2, 3)]
        return along + [self.device(z, 1 - x, y, c), self.device(z, x, 1 - y, c), self.device(z, x, y, 1 - c)]

    def begin(self):
        barrier = pltpu.get_barrier_semaphore()
        for partner in self.partners():
            pl.semaphore_signal(barrier, inc=1, device_id=partner, device_id_type=MESH)
        self.own = pltpu.make_async_copy(self.shard_ref, self.all_ref.at[self.z, self.x, self.y, self.c], self.own_sem)
        self.own.start()
        pl.semaphore_wait(barrier, 6)
        self.send_along(0)

    def send_along(self, part):
        if part < PARTS:
            for route in range(2):
                for stage in range(3):
                    self.send(part, route, stage)

    def send(self, part, route, stage):
        z, x, y, c = self.z, self.x, self.y, self.c
        rows = pl.ds((2 * part + route) * self.rows, self.rows)
        partner = self.partners()[stage if stage < 3 or stage == 5 else 3 + (stage - 3 + route) % 2]
        every = slice(None)
        if stage < 3:
            place = (z, x, y, c)
        elif stage == 3:
            place = (every, x, y, c)
        elif stage == 4:
            place = (every, every, y, c) if route == 0 else (every, x, every, c)
        else:
            place = (every, every, every, c)
        target = self.all_ref.at[(*place, rows)]
        source = self.shard_ref.at[rows] if stage < 3 else target
        at = (2 * part + route) * 6 + stage
        copy = pltpu.make_async_remote_copy(
            src_ref=source,
            dst_ref=target,
            send_sem=self.send_sem.at[at],
            recv_sem=self.recv_sem.at[at],
            device_id=partner,
            device_id_type=MESH,
        )
        copy.start()
        self.copies[part, route, stage] = copy

    def advance(self, part, level):
        if level == 0 and part == 0:
            self.own.wait()
        for route in range(2):
            for stage in ((0, 1, 2), (3,), (4,), (5,))[level]:
                self.copies[part, route, stage].wait_recv()
        if level == 0:
            self.send_along(part + 1)
        if level < 3:
            for route in range(2):
                self.send(part, route, 3 + level)

    def steps(self):
        order = []
        for turn in range(PARTS + 3):
            for level in reversed(range(4)):
                if 0 <= turn - level < PARTS:
                    order.append((turn - level, level))
        return [functools.partial(self.advance, *step) for step in order]

    def end(self):
        for copy in self.copies.values():
            copy.wait_send()


def prepare_kernel(
    communicate, frames_ref, length_ref, tokens_ref, cot_ref, gain_ref, bias_ref, one_hot_ref, time_ref, space_ref,
    pick_ref, prev_ref, mem_ref, taps_ref, *refs,
):
    if communicate:
        shard_ref, all_ref = refs[:2]
        refs = refs[2:]
    x_ref, normed_ref, upstream_ref, aug_ref, table_ref, rest_ref, tap_ref, wide_ref, sums_ref, parts_ref = refs[:10]
    tables_ref = refs[10]
    steps = []
    if communicate:
        gather = Gather(shard_ref, all_ref, *refs[11:])
        gather.begin()
        steps = gather.steps()

    def advance(count=1):
        for _ in range(min(count, len(steps))):
            steps.pop(0)()

    def permute(source_ref, target_ref):
        for tile, part in enumerate(tiles_of(source_ref[...])):
            wide_ref[tile] = part.astype(F32)

        @pl.loop(0, PLACES // 2)
        def _(pair):
            first = read_place(wide_ref, 2 * pair)
            second = read_place(wide_ref, 2 * pair + 1)
            at = pl.multiple_of(pair * 16, 16)
            target_ref[pl.ds(at, 16), :] = jnp.concatenate([first, second], axis=0).astype(BF16)

    permute(cot_ref, upstream_ref)
    permute(tokens_ref, x_ref)
    advance()
    centred, rs = layer_stats(x_ref[...].astype(F32), D)
    normed_ref[...] = (centred * rs * gain_ref[...].reshape(1, D) + bias_ref[...].reshape(1, D)).astype(BF16)
    row = lax.broadcasted_iota(jnp.int32, (KEY_ROWS, LANES), 0)
    frames, length = frames_ref[0], length_ref[0]
    place = jnp.where(row < MEM_AT, row & 7, jnp.where(row < SQUEEZE_AT, row - MEM_AT, row - SQUEEZE_AT))
    limit = jnp.where(row < MEM_AT, frames, jnp.where(row < SQUEEZE_AT, length, MEM))
    off = jnp.where(place >= limit, jnp.where(lane_index((KEY_ROWS, LANES)) == MASK_LANE, MASKED, 0.0), 0.0)
    aug_ref[...] = (one_hot_ref[...].astype(F32) + off).astype(BF16)
    tables_ref[...] = jnp.zeros((LANES, LANES), F32)
    spans = 2 * HEIGHT - 1
    tables_ref[0 : 2 * FRAMES - 1, :HEAD_DIM] = time_ref[...]
    for s in range(2):
        tables_ref[15 + spans * s : 15 + spans * (s + 1), :HEAD_DIM] = space_ref[:, s]
    table_ref[...] = dot(pick_ref[...], tables_ref[...].astype(BF16)).astype(BF16)
    advance()

    def head_of(values, head):
        return values[:, HEAD_DIM * head : HEAD_DIM * head + HEAD_DIM]

    for s in range(2):
        for group in range(2):
            columns = slice(group * GROUP, (group + 1) * GROUP)
            for tile, part in enumerate(tiles_of(prev_ref[s, :, columns])):
                wide_ref[tile] = part.astype(F32)

            taps = [tiled_lanes(taps_ref[s, tap : tap + 1, :]) for tap in range(4)]

            @pl.loop(0, HEIGHT // 2)
            def _(i):
                for j in range(WIDTH // 2):
                    total = None
                    at = pl.multiple_of((i * (WIDTH // 2) + j) * FRAMES, FRAMES)
                    for tap in range(4):
                        place = (2 * i + tap // 2) * WIDTH + 2 * j + tap % 2
                        part = read_place(wide_ref, place, GROUP // LANES)
                        parts_ref[tap, pl.ds(at, FRAMES), :] = part
                        term = part * taps[tap]
                        total = term if total is None else total + term
                    sums_ref[pl.ds(at, FRAMES), :] = total

            old = mem_ref[s, :, columns].astype(F32)
            for head in range(GROUP_HEADS):
                rest = jnp.concatenate(
                    [
                        head_of(old, head),
                        jnp.zeros((SQUEEZE_AT - MEM_AT - MEM, HEAD_DIM), F32),
                        head_of(sums_ref[...], head),
                        jnp.zeros((KEY_ROWS - SQUEEZE_AT - MEM, HEAD_DIM), F32),
                    ],
                    axis=0,
                )
                rest = jnp.concatenate([rest, jnp.zeros((REST, LANES - HEAD_DIM), F32)], axis=1)
                rest_ref[s, group * GROUP_HEADS + head] = rest.astype(BF16)
                for tap in range(4):
                    part = jnp.concatenate([head_of(parts_ref[tap], head), jnp.zeros((8, HEAD_DIM), F32)], axis=0)
                    part = jnp.concatenate([part, jnp.zeros((208, LANES - HEAD_DIM), F32)], axis=1)
                    tap_ref[s, group * GROUP_HEADS + head, tap] = part.astype(BF16)
            advance(3 if group + s else 2)
    advance(len(steps))
    if communicate:
        gather.end()


def pack_kernel(one_ref, two_ref, proj_ref, flat_ref):
    for at, part in flat_pieces(one_ref[...], two_ref[...], proj_ref[...]):
        flat_ref[at : at + part.shape[0], : part.shape[1]] = part


def pack(one, two, proj):
    vmem = pl.BlockSpec(memory_space=pltpu.VMEM)
    rows = (one.size + two.size) // LANES + 2 * proj.shape[0]
    return pl.pallas_call(
        pack_kernel,
        out_shape=jax.ShapeDtypeStruct((rows, LANES), BF16),
        in_specs=[vmem] * 3,
        out_specs=vmem,
        compiler_params=params(),
        name="pack",
    )(one, two, proj)


def prepare(frames, length, tokens, cot, gain, bias, one_hot, rel_time, rel_space, pick, prev, memory, taps, shard=None):
    smem = pl.BlockSpec(memory_space=pltpu.SMEM)
    vmem = pl.BlockSpec(memory_space=pltpu.VMEM)
    communicate = shard is not None
    out_shape = [
        jax.ShapeDtypeStruct((ROWS, D), BF16),
        jax.ShapeDtypeStruct((ROWS, D), BF16),
        jax.ShapeDtypeStruct((ROWS, D), BF16),
        jax.ShapeDtypeStruct((KEY_ROWS, LANES), BF16),
        jax.ShapeDtypeStruct((TABLE, LANES), BF16),
        jax.ShapeDtypeStruct((2, HEADS, REST, LANES), BF16),
        jax.ShapeDtypeStruct((2, HEADS, 4, 208, LANES), BF16),
    ]
    in_specs, out_specs = [smem, smem] + [vmem] * 11, [vmem] * 7
    operands = [frames, length, tokens, cot, gain, bias, one_hot, rel_time, rel_space, pick, prev, memory, taps]
    scratch = [
        wide_scratch(D),
        pltpu.VMEM((MEM, GROUP), F32),
        pltpu.VMEM((4, MEM, GROUP), F32),
        pltpu.VMEM((LANES, LANES), F32),
    ]
    more = {}
    if communicate:
        anywhere = pl.BlockSpec(memory_space=pl.ANY)
        out_shape = [jax.ShapeDtypeStruct((4, 2, 2, 2) + shard.shape, BF16)] + out_shape
        in_specs.append(anywhere)
        out_specs = [anywhere] + out_specs
        operands.append(shard)
        count = 2 * PARTS * 6
        scratch += [pltpu.SemaphoreType.DMA, pltpu.SemaphoreType.DMA((count,)), pltpu.SemaphoreType.DMA((count,))]
        more = {"collective_id": 0, "has_side_effects": True}
    return pl.pallas_call(
        functools.partial(prepare_kernel, communicate),
        out_shape=tuple(out_shape),
        in_specs=in_specs,
        out_specs=tuple(out_specs),
        scratch_shapes=scratch,
        compiler_params=params(**more),
        name="prepare",
    )(*operands)


def shift_frames(values, step):
    frame = lax.broadcasted_iota(jnp.int32, values.shape, values.ndim - 2)
    moved = pltpu.roll(values, step % FRAMES, values.ndim - 2)
    edge = 0 if step == 1 else FRAMES - 1
    return jnp.where(frame == edge, 0.0, moved)


def convolve(grid_ref, taps_ref, flip, i, lanes):
    sums = [None, None, None]
    for b in range(3):
        for e in range(3):
            window = grid_ref[i + b, e : e + WIDTH, :, lanes]
            for a in range(3):
                tap = 9 * a + 3 * b + e
                term = window * taps_ref[26 - tap if flip else tap, :, lanes][None]
                sums[a] = term if sums[a] is None else sums[a] + term
    return sums[1] + shift_frames(sums[0], 1) + shift_frames(sums[2], -1)


def spread_taps(raw_ref, taps_ref):
    for tap in range(27):
        line = tiled_lanes(raw_ref[0, tap : tap + 1, :])
        taps_ref[tap] = jnp.broadcast_to(line, (FRAMES, GROUP))


def clear_border(grid_ref):
    grid_ref[...] = jnp.zeros(grid_ref.shape, grid_ref.dtype)


def relative_bits(place_ref, d, f):
    return {
        "x": (d & 1) ^ place_ref[0],
        "z1": ((d >> 1) & 1) ^ place_ref[1],
        "z2": ((d >> 2) & 1) ^ place_ref[2],
        "y": ((f >> 1) & 1) ^ place_ref[3],
        "c": (f & 1) ^ place_ref[4],
    }


def slot(bits, order):
    return sum(bits[name] << at for at, name in enumerate(order))


def qkv_kernel(
    frames_ref, normed_ref, shards_ref, qkv_bias_ref, taps_raw_ref, gain_ref, bias_ref, same_ref,
    heads_ref, vhat_ref, rs_ref, mixed_ref, weight_ref, grid_ref, pooled_ref, taps_ref, line_ref,
):
    step = pl.program_id(0)

    @pl.when(step == 0)
    def _():
        clear_border(grid_ref)
        line_ref[...] = qkv_bias_ref[...].reshape(1, QKV)
        depth, columns = shards_ref.shape[2:]
        for f in range(QKV // columns):
            for d in range(DP_BLOCKS):
                weight_ref[d * depth : (d + 1) * depth, f * columns : (f + 1) * columns] = shards_ref[d, f]

    @pl.when(step % 2 == 0)
    def _():
        spread_taps(taps_raw_ref, taps_ref)

    at = pl.multiple_of(step * GROUP, LANES)
    mixed = dot(normed_ref[...], weight_ref[:, pl.ds(at, GROUP)]) + line_ref[:, pl.ds(at, GROUP)]
    row = lax.broadcasted_iota(jnp.int32, (ROWS, GROUP), 0)
    mixed = jnp.where((row & 7) < frames_ref[0], mixed, 0.0)
    mixed_ref[...] = mixed.astype(BF16)
    grid_ref[1 : HEIGHT + 1, 1 : WIDTH + 1] = mixed.reshape(HEIGHT, WIDTH, FRAMES, GROUP)

    @pl.loop(0, HEIGHT)
    def _(i):
        for tile in range(GROUP // LANES):
            lanes = slice(tile * LANES, tile * LANES + LANES)
            line = convolve(grid_ref, taps_ref, False, i, lanes)
            at = pl.multiple_of(i * WIDTH * FRAMES, WIDTH * FRAMES)
            pooled_ref[pl.ds(at, WIDTH * FRAMES), lanes] = line.reshape(WIDTH * FRAMES, LANES)

    pooled = pooled_ref[...]
    high = pooled.astype(BF16)
    low = (pooled - high.astype(F32)).astype(BF16)
    centred = pooled - (dot(high, same_ref[...]) + dot(low, same_ref[...])) * (1.0 / HEAD_DIM)
    variance = dot((centred * centred).astype(BF16), same_ref[...]) * (1.0 / HEAD_DIM)
    rs = lax.rsqrt(variance + EPSILON)
    vhat = centred * rs
    rs_ref[...] = rs
    vhat_ref[...] = vhat.astype(BF16)
    kind = pl.ds(step // 2, 1)
    out = (vhat * tiled_lanes(gain_ref[kind, :]) + tiled_lanes(bias_ref[kind, :])).astype(BF16)
    for head in range(GROUP_HEADS):
        own = out[:, HEAD_DIM * head : HEAD_DIM * (head + 1)]
        heads_ref[head] = jnp.concatenate([own, jnp.zeros((ROWS, LANES - HEAD_DIM), BF16)], axis=1)


def query_key_value(frames, normed, shards, qkv_bias, taps, gain, bias, same):
    smem = pl.BlockSpec(memory_space=pltpu.SMEM)
    return pl.pallas_call(
        qkv_kernel,
        grid=(6,),
        out_shape=(
            jax.ShapeDtypeStruct((3 * HEADS, ROWS, LANES), BF16),
            jax.ShapeDtypeStruct((ROWS, QKV), BF16),
            jax.ShapeDtypeStruct((ROWS, QKV), F32),
            jax.ShapeDtypeStruct((ROWS, QKV), BF16),
            jax.ShapeDtypeStruct((D, QKV), BF16),
        ),
        in_specs=[
            smem,
            whole((ROWS, D)),
            whole(shards.shape),
            whole((QKV,)),
            pl.BlockSpec((1, 27, HEAD_DIM), lambda g: (g // 2, 0, 0)),
            whole((3, HEAD_DIM)),
            whole((3, HEAD_DIM)),
            whole((GROUP, GROUP)),
        ],
        out_specs=(
            pl.BlockSpec((GROUP_HEADS, ROWS, LANES), lambda g: (g, 0, 0)),
            pl.BlockSpec((ROWS, GROUP), lambda g: (0, g)),
            pl.BlockSpec((ROWS, GROUP), lambda g: (0, g)),
            pl.BlockSpec((ROWS, GROUP), lambda g: (0, g)),
            whole((D, QKV)),
        ),
        scratch_shapes=[
            pltpu.VMEM((HEIGHT + 2, WIDTH + 2, FRAMES, GROUP), F32),
            pltpu.VMEM((ROWS, GROUP), F32),
            pltpu.VMEM((27, FRAMES, GROUP), F32),
            pltpu.VMEM((1, QKV), F32),
        ],
        compiler_params=params(),
        name="query_key_value",
    )(frames, normed, shards, qkv_bias, taps, gain, bias, same)


def attend_kernel(
    q_ref, k_ref, v_ref, krest_ref, vrest_ref, aug_ref, table_ref, own_ref, fold_ref,
    weights_ref, pv_ref, out_ref, keys_ref, vals_ref, query_ref,
):
    lane = lane_index((KEY_ROWS, LANES))
    keys_ref[:ROWS] = k_ref[0] + aug_ref[:ROWS]
    keys_ref[ROWS:] = krest_ref[0, 0] + aug_ref[ROWS:]
    one = jnp.where(lane == HEAD_DIM, 1.0, 0.0).astype(BF16)
    vals_ref[:ROWS] = v_ref[0] + one[:ROWS]
    vals_ref[ROWS:] = vrest_ref[0, 0] + one[ROWS:]
    query = q_ref[0]
    every = (dot(query, table_ref[...], ((1,), (1,))) * ROOT).astype(BF16) * own_ref[...]
    relative = dot(every, fold_ref[...])
    marked = jnp.where(lane[:ROWS] == MASK_LANE, 1.0, relative)
    query_ref[...] = (query.astype(F32) + marked).astype(BF16)

    for block in range(ROWS // ROW_BLOCK):
        rows = slice(block * ROW_BLOCK, (block + 1) * ROW_BLOCK)
        scores = dot(query_ref[rows, :], keys_ref[...], ((1,), (1,)))
        largest = jnp.max(scores, axis=1, keepdims=True)
        weights = jnp.exp2((scores - largest) * (SCALE * LOG2E)).astype(BF16)
        weights_ref[0, rows, :] = weights
        total = dot(weights, vals_ref[...])
        inverse = 1.0 / total[:, HEAD_DIM : HEAD_DIM + 1]
        lane = lane_index((ROW_BLOCK, LANES))
        pv = jnp.where(lane < HEAD_DIM, total * inverse, 0.0)
        out_ref[0, rows, :] = (pv + q_ref[0, rows, :].astype(F32)).astype(BF16)
        high = inverse.astype(BF16).astype(F32)
        extra = jnp.where(lane == HEAD_DIM, high, jnp.where(lane == HEAD_DIM + 1, inverse - high, 0.0))
        pv_ref[0, rows, :] = (pv + extra).astype(BF16)


def attend(heads, rest, aug, table, own, fold):
    head = (1, ROWS, LANES)
    tail = (1, 1, REST, LANES)
    return pl.pallas_call(
        attend_kernel,
        grid=(HEADS,),
        out_shape=(
            jax.ShapeDtypeStruct((HEADS, ROWS, KEY_ROWS), BF16),
            jax.ShapeDtypeStruct((HEADS, ROWS, LANES), BF16),
            jax.ShapeDtypeStruct((HEADS, ROWS, LANES), BF16),
        ),
        in_specs=[
            pl.BlockSpec(head, lambda h: (h, 0, 0)),
            pl.BlockSpec(head, lambda h: (HEADS + h, 0, 0)),
            pl.BlockSpec(head, lambda h: (2 * HEADS + h, 0, 0)),
            pl.BlockSpec(tail, lambda h: (0, h, 0, 0)),
            pl.BlockSpec(tail, lambda h: (1, h, 0, 0)),
            whole((KEY_ROWS, LANES)),
            whole((TABLE, LANES)),
            whole((ROWS, TABLE)),
            whole((TABLE, LANES)),
        ],
        out_specs=(
            pl.BlockSpec((1, ROWS, KEY_ROWS), lambda h: (h, 0, 0)),
            pl.BlockSpec(head, lambda h: (h, 0, 0)),
            pl.BlockSpec(head, lambda h: (h, 0, 0)),
        ),
        scratch_shapes=[
            pltpu.VMEM((KEY_ROWS, LANES), BF16),
            pltpu.VMEM((KEY_ROWS, LANES), BF16),
            pltpu.VMEM((ROWS, LANES), BF16),
        ],
        compiler_params=params(),
        name="attend",
    )(heads, heads, heads, rest, rest, aug, table, own, fold)


CHUNK = 768
CHUNKS = FF // CHUNK
TILES = CHUNK // LANES


def middle_kernel(
    place_ref, att_ref, x_ref, up_ref, wp_ref, w1_ref, w2_ref, pb_ref, g2_ref, b2_ref, fb1_ref, fb2_ref,
    out_ref, dmid_ref, datt_ref, plow_ref, phigh_ref, low1_ref, high1_ref, low2_ref, high2_ref, small_ref, gb1_ref,
    packed_ref, proj_ref, mid_ref, hidden_ref, total_ref, dhid_ref, wide_ref, w1_scr, w2_scr, grad_ref,
    hiddent_ref, upt_ref,
):
    step = pl.program_id(0)
    sides = wp_ref.shape[1]
    part = D // sides
    depth = D // DP_BLOCKS
    inner = FF // DP_BLOCKS

    @pl.when(step == 0)
    def _():
        for head in range(HEADS):
            packed_ref[:, HEAD_DIM * head : HEAD_DIM * (head + 1)] = att_ref[head][:, :HEAD_DIM]
        for f in range(sides):
            for d in range(DP_BLOCKS):
                rows = slice(d * depth, (d + 1) * depth)
                proj_ref[rows, f * part : f * part + LANES] = wp_ref[d, f, :depth]
                proj_ref[rows, f * part + LANES : (f + 1) * part] = wp_ref[d, f, depth:, : part - LANES]
        middle = x_ref[...].astype(F32) + dot(packed_ref[...], proj_ref[...]) + pb_ref[...].reshape(1, D)
        mid_ref[...] = middle
        centred, rs = layer_stats(middle, D)
        hidden = centred * rs * g2_ref[...].reshape(1, D) + b2_ref[...].reshape(1, D)
        hidden_ref[...] = hidden.astype(BF16)
        hiddent_ref[...] = hidden.T.astype(BF16)
        upt_ref[...] = up_ref[...].T
        total_ref[...] = middle + fb2_ref[...].reshape(1, D).reshape(1, D)
        dhid_ref[...] = jnp.zeros((ROWS, D), F32)

    for tile in range(TILES):
        lanes = slice(tile * LANES, (tile + 1) * LANES)
        for d in range(DP_BLOCKS):
            w1_scr[d * depth : (d + 1) * depth, lanes] = w1_ref[d, 0, tile * depth : (tile + 1) * depth]
        side, at = divmod(tile, inner // LANES)
        for f in range(sides):
            w2_scr[f * part : (f + 1) * part, lanes] = w2_ref[side, f, at * part : (at + 1) * part]
    w1, w2 = w1_scr[...], w2_scr[...]
    before = dot(hidden_ref[...], w1) + fb1_ref[...]
    cdf = 0.5 + 0.5 * lax.erf(before * (2.0**-0.5))
    activated = (before * cdf).astype(BF16)
    slope = cdf + before * (jnp.exp(before * before * -0.5) * 0.3989422804014327)
    dbefore = dot(up_ref[...], w2) * slope
    dbefore_low = dbefore.astype(BF16)
    gb1_ref[...] = jnp.sum(dbefore_low.astype(F32), axis=0, keepdims=True)
    total_ref[...] += dot(activated, w2, ((1,), (1,)))
    dhid_ref[...] += dot(dbefore_low, w1, ((1,), (1,)))

    core = place_ref[4]
    grad_ref[...] = dot(upt_ref[...], activated).astype(BF16)
    for tile in range(TILES):
        lanes = slice(tile * LANES, (tile + 1) * LANES)
        side, at = divmod(tile, inner // LANES)
        rows = slice(at * part, (at + 1) * part)
        for y in range(sides // 2):
            bits = relative_bits(place_ref, side, 2 * y)
            for target_ref, c in ((low2_ref, core), (high2_ref, 1 - core)):
                start = pl.multiple_of((2 * y + c) * part, part)
                target_ref[bits["y"], bits["x"], 0, 0, rows] = grad_ref[pl.ds(start, part), lanes]
    grad_ref[...] = dot(hiddent_ref[...], dbefore_low).astype(BF16)

    def store_one(target_ref):
        for tile in range(TILES):
            lanes = slice(tile * LANES, (tile + 1) * LANES)
            for d in range(DP_BLOCKS):
                bits = relative_bits(place_ref, d, 0)
                block = grad_ref[d * depth : (d + 1) * depth, lanes]
                target_ref[bits["x"], 0, bits["z1"], bits["z2"], tile * depth : (tile + 1) * depth] = block

    @pl.when(step < CHUNKS // 2)
    def _():
        store_one(low1_ref)

    @pl.when(step >= CHUNKS // 2)
    def _():
        store_one(high1_ref)

    @pl.when(step == CHUNKS - 1)
    def _():
        @pl.loop(0, PLACES)
        def _(place):
            at = pl.multiple_of(place * FRAMES, FRAMES)
            write_place(wide_ref, place, total_ref[pl.ds(at, FRAMES), :])

        for tile in range(D // LANES):
            out_ref[:, tile * LANES : (tile + 1) * LANES] = wide_ref[tile].astype(BF16)
        upstream = up_ref[...].astype(F32)
        dhidden = dhid_ref[...]
        centred, rs = layer_stats(mid_ref[...], D)
        vhat = centred * rs
        dgain = jnp.sum(dhidden * vhat, axis=0, keepdims=True)
        dbias = jnp.sum(dhidden, axis=0, keepdims=True)
        scaled = dhidden * g2_ref[...].reshape(1, D)
        first = jnp.sum(scaled, axis=1, keepdims=True) * (1.0 / D)
        second = jnp.sum(scaled * vhat, axis=1, keepdims=True) * (1.0 / D)
        dmiddle = upstream + rs * (scaled - first - vhat * second)
        dmid_ref[...] = dmiddle
        dproj = dmiddle.astype(BF16)
        small_ref[0:1, :] = jnp.sum(dproj.astype(F32), axis=0, keepdims=True)
        small_ref[1:2, :] = dgain
        small_ref[2:3, :] = dbias
        small_ref[3:4, :] = jnp.sum(upstream, axis=0, keepdims=True)
        small_ref[4:8, :] = jnp.zeros((4, D), F32)
        grad_ref[...] = dot(packed_ref[...], dproj, ((0,), (0,))).astype(BF16)
        for d in range(DP_BLOCKS):
            rows = slice(d * depth, (d + 1) * depth)
            for y in range(sides // 2):
                bits = relative_bits(place_ref, d, 2 * y)
                where = (bits["y"], bits["x"], bits["z1"], bits["z2"])
                sides_of = [grad_ref[rows, f * part : (f + 1) * part] for f in (2 * y, 2 * y + 1)]
                for target_ref, c in ((plow_ref, core), (phigh_ref, 1 - core)):
                    block = jnp.where(c == 0, sides_of[0], sides_of[1])
                    target_ref[(*where, slice(0, depth))] = block[:, :LANES]
                    rest = jnp.concatenate([block[:, LANES:], jnp.zeros((depth, 2 * LANES - part), BF16)], axis=1)
                    target_ref[(*where, slice(depth, 2 * depth))] = rest
        datt = dot(dproj, proj_ref[...], ((1,), (1,))).astype(BF16)
        for head in range(HEADS):
            datt_ref[head] = jnp.concatenate(
                [datt[:, HEAD_DIM * head : HEAD_DIM * (head + 1)], jnp.zeros((ROWS, LANES - HEAD_DIM), BF16)],
                axis=1,
            )


def feed_forward(place, att, x, up, flat, pb, g2, b2, fb1, fb2):
    once = pl.Buffered(1)
    sides = flat.shape[1]
    part, depth = D // sides, D // DP_BLOCKS
    rows_one, rows_two = TILES * depth, FF // DP_BLOCKS // LANES * part

    def kept(shape):
        return pl.BlockSpec(shape, lambda *_: (0,) * len(shape), pipeline_mode=once)

    def side_of(s, place):
        return 2 * (place[3] ^ (s & 1)) + (place[4] ^ (s >> 1))

    def columns(s, place):
        return (0, side_of(s, place))

    def low_one(s, place):
        return (0, jnp.where(s < 2, s & 1, 1), 0, 0, 0, 0)

    def high_one(s, place):
        return (0, jnp.where(s < 2, 0, s & 1), 0, 0, 0, 0)

    def pair(s, place):
        side = side_of(s, place)
        return (0, 0, place[1] ^ (side & 1), place[2] ^ (side >> 1), 0, 0)

    bits = (2, 2, 2, 2)
    one, two, proj = bits + (rows_one, LANES), bits + (rows_two, LANES), bits + (2 * depth, LANES)
    return pl.pallas_call(
        middle_kernel,
        out_shape=(
            jax.ShapeDtypeStruct((ROWS, D), BF16),
            jax.ShapeDtypeStruct((ROWS, D), F32),
            jax.ShapeDtypeStruct((HEADS, ROWS, LANES), BF16),
            jax.ShapeDtypeStruct(proj, BF16),
            jax.ShapeDtypeStruct(proj, BF16),
            jax.ShapeDtypeStruct(one, BF16),
            jax.ShapeDtypeStruct(one, BF16),
            jax.ShapeDtypeStruct(two, BF16),
            jax.ShapeDtypeStruct(two, BF16),
            jax.ShapeDtypeStruct((8, D), F32),
            jax.ShapeDtypeStruct((1, FF), F32),
        ),
        grid_spec=pltpu.PrefetchScalarGridSpec(
            num_scalar_prefetch=1,
            grid=(CHUNKS,),
            in_specs=[
                kept((HEADS, ROWS, LANES)),
                kept((ROWS, D)),
                kept((ROWS, D)),
                pl.BlockSpec(
                    (DP_BLOCKS, sides, 2 * depth, LANES), lambda s, place: (0, 0, 6, 0), pipeline_mode=once
                ),
                pl.BlockSpec(
                    (DP_BLOCKS, 1, rows_one, LANES), lambda s, place: (0, side_of(s, place), 0, 0)
                ),
                pl.BlockSpec((2, sides, rows_two, LANES), lambda s, place: (side_of(s, place), 0, 1, 0)),
                kept((D,)),
                kept((D,)),
                kept((D,)),
                pl.BlockSpec((1, CHUNK), columns),
                kept((D,)),
            ],
            out_specs=(
                kept((ROWS, D)),
                kept((ROWS, D)),
                kept((HEADS, ROWS, LANES)),
                kept(proj),
                kept(proj),
                pl.BlockSpec((2, 1, 2, 2, rows_one, LANES), low_one),
                pl.BlockSpec((2, 1, 2, 2, rows_one, LANES), high_one),
                pl.BlockSpec((2, 2, 1, 1, rows_two, LANES), pair),
                pl.BlockSpec((2, 2, 1, 1, rows_two, LANES), pair),
                kept((8, D)),
                pl.BlockSpec((1, CHUNK), columns),
            ),
            scratch_shapes=[
                pltpu.VMEM((ROWS, D), BF16),
                pltpu.VMEM((D, D), BF16),
                pltpu.VMEM((ROWS, D), F32),
                pltpu.VMEM((ROWS, D), BF16),
                pltpu.VMEM((ROWS, D), F32),
                pltpu.VMEM((ROWS, D), F32),
                wide_scratch(D),
                pltpu.VMEM((D, CHUNK), BF16),
                pltpu.VMEM((D, CHUNK), BF16),
                pltpu.VMEM((D, CHUNK), BF16),
                pltpu.VMEM((D, ROWS), BF16),
                pltpu.VMEM((D, ROWS), BF16),
            ],
        ),
        compiler_params=params(),
        name="feed_forward",
    )(place, att, x, up, flat, flat, flat, pb, g2, b2, fb1, fb2)


def halve_kernel(counts, *refs):
    outs = refs[4 * sum(counts) :]
    refs = list(refs)
    for route, pieces in enumerate(counts):
        at = 0
        for _ in range(pieces):
            rows = refs[0].shape[1]
            for side in range(2):
                kept_ref, more_ref = refs.pop(0), refs.pop(0)
                outs[2 * route + side][:, at : at + rows] = kept_ref[...] + more_ref[...]
            at += rows


def halve_sum(routes, name):
    blocks = routes[0][0][0].shape[0]
    run = max(1, blocks // 4)
    steps = blocks // 2 // run
    in_specs, operands, shapes, out_specs = [], [], [], []
    for kept, more in routes:
        for k, m in zip(kept, more):
            for side in range(2):
                spec = pl.BlockSpec((run,) + k.shape[1:], lambda i, side=side: (i + side * steps, 0, 0))
                in_specs += [spec, spec]
                operands += [k, m]
        rows = sum(k.shape[1] for k in kept)
        shapes += [jax.ShapeDtypeStruct((blocks // 2, rows, LANES), BF16)] * 2
        out_specs += [pl.BlockSpec((run, rows, LANES), lambda i: (i, 0, 0))] * 2
    return pl.pallas_call(
        functools.partial(halve_kernel, [len(kept) for kept, _ in routes]),
        grid=(steps,),
        out_shape=tuple(shapes),
        in_specs=in_specs,
        out_specs=tuple(out_specs),
        compiler_params=params(),
        name=name,
    )(*operands)


def attend_back_kernel(
    q_ref, k_ref, v_ref, krest_ref, vrest_ref, aug_ref, table_ref, own_ref, fold_ref, pick_ref,
    weights_ref, pv_ref, datt_ref, parts_ref,
    grads_ref, gtable_ref, gtaps_ref,
    keys_ref, vals_ref, up_ref, gsum_ref,
):
    step = pl.program_id(0)
    lane = lane_index((KEY_ROWS, LANES))
    row_lane = lane[:ROWS]

    @pl.when(step == 0)
    def _():
        gsum_ref[...] = jnp.zeros((TABLE, LANES), F32)
        gtaps_ref[...] = jnp.zeros((2, 4, LANES), F32)

    keys_ref[:ROWS] = k_ref[0] + aug_ref[:ROWS]
    keys_ref[ROWS:] = krest_ref[0, 0] + aug_ref[ROWS:]
    one = jnp.where((lane >= HEAD_DIM) & (lane < HEAD_DIM + 3), 1.0, 0.0).astype(BF16)
    vals_ref[:ROWS] = v_ref[0] + one[:ROWS]
    vals_ref[ROWS:] = vrest_ref[0, 0] + one[ROWS:]
    pv = pv_ref[0].astype(F32)
    inverse = pv[:, HEAD_DIM : HEAD_DIM + 1] + pv[:, HEAD_DIM + 1 : HEAD_DIM + 2]
    datt = datt_ref[0].astype(F32)
    upstream = (datt * inverse).astype(BF16).astype(F32)
    mean = jnp.sum(upstream * pv, axis=1, keepdims=True)
    high = mean.astype(BF16).astype(F32)
    low = (mean - high).astype(BF16).astype(F32)
    least = mean - high - low
    extra = jnp.where(
        row_lane == HEAD_DIM,
        -high,
        jnp.where(row_lane == HEAD_DIM + 1, -low, jnp.where(row_lane == HEAD_DIM + 2, -least, 0.0)),
    )
    up_ref[...] = (upstream + extra).astype(BF16)

    dvals, dkeys, dquery = None, None, []
    for block in range(ROWS // ROW_BLOCK):
        rows = slice(block * ROW_BLOCK, (block + 1) * ROW_BLOCK)
        weights = weights_ref[0, rows, :]
        dprobs = dot(up_ref[rows, :], vals_ref[...], ((1,), (1,)))
        slopes = (weights.astype(F32) * dprobs).astype(BF16)
        dquery.append(dot(slopes, keys_ref[...]))
        more_vals = dot(up_ref[rows, :], weights, ((0,), (0,)))
        more_keys = dot(q_ref[0, rows, :], slopes, ((0,), (0,)))
        dvals = more_vals if dvals is None else dvals + more_vals
        dkeys = more_keys if dkeys is None else dkeys + more_keys
    dvals, dkeys = dvals.T, dkeys.T * SCALE
    dquery = jnp.concatenate(dquery, axis=0)
    spread = dot(dquery.astype(BF16), fold_ref[...], ((1,), (1,))).astype(BF16) * own_ref[...]
    gsum_ref[...] += dot(spread, q_ref[0], ((0,), (0,)))
    dquery = dquery * SCALE + datt + dot(spread, table_ref[...])
    grads_ref[0, 0] = dquery.astype(BF16)
    grads_ref[1, 0] = dkeys[:ROWS].astype(BF16)
    grads_ref[2, 0] = dvals[:ROWS].astype(BF16)
    for s, whole_grad in ((0, dkeys), (1, dvals)):
        piece = whole_grad[SQUEEZE_AT : SQUEEZE_AT + MEM]
        for tap in range(4):
            product = piece * parts_ref[s, 0, tap].astype(F32)[:MEM]
            gtaps_ref[s, tap : tap + 1, :] += jnp.sum(product, axis=0, keepdims=True)

    @pl.when(step == pl.num_programs(0) - 1)
    def _():
        gtable_ref[...] = dot(pick_ref[...].astype(F32), gsum_ref[...], ((0,), (0,)), lax.Precision.HIGHEST)


def attend_back(start, count, heads, rest, aug, table, own, fold, pick, weights, pv, datt, parts):
    head = (1, ROWS, LANES)
    tail = (1, 1, REST, LANES)
    own_head = pl.BlockSpec(head, lambda h: (start + h, 0, 0))
    return pl.pallas_call(
        attend_back_kernel,
        grid=(count,),
        out_shape=(
            jax.ShapeDtypeStruct((3, count, ROWS, LANES), BF16),
            jax.ShapeDtypeStruct((LANES, LANES), F32),
            jax.ShapeDtypeStruct((2, 4, LANES), F32),
        ),
        in_specs=[
            own_head,
            pl.BlockSpec(head, lambda h: (HEADS + start + h, 0, 0)),
            pl.BlockSpec(head, lambda h: (2 * HEADS + start + h, 0, 0)),
            pl.BlockSpec(tail, lambda h: (0, start + h, 0, 0)),
            pl.BlockSpec(tail, lambda h: (1, start + h, 0, 0)),
            whole((KEY_ROWS, LANES)),
            whole((TABLE, LANES)),
            whole((ROWS, TABLE)),
            whole((TABLE, LANES)),
            whole((TABLE, LANES)),
            pl.BlockSpec((1, ROWS, KEY_ROWS), lambda h: (start + h, 0, 0)),
            own_head,
            own_head,
            pl.BlockSpec((2, 1, 4, 208, LANES), lambda h: (0, start + h, 0, 0, 0)),
        ],
        out_specs=(
            pl.BlockSpec((3, 1, ROWS, LANES), lambda h: (0, h, 0, 0)),
            whole((LANES, LANES)),
            whole((2, 4, LANES)),
        ),
        scratch_shapes=[
            pltpu.VMEM((KEY_ROWS, LANES), BF16),
            pltpu.VMEM((KEY_ROWS, LANES), BF16),
            pltpu.VMEM((ROWS, LANES), BF16),
            pltpu.VMEM((TABLE, LANES), F32),
        ],
        compiler_params=params(),
        name="attend_back",
    )(heads, heads, heads, rest, rest, aug, table, own, fold, pick, weights, pv, datt, parts)


def pool_back_kernel(
    kind, frames_ref, first_ref, second_ref, third_ref, vhat_ref, rs_ref, mixed_ref, taps_raw_ref, gain_ref, same_ref,
    dmix_ref, small_ref,
    grid_ref, dgrid_ref, sums_ref, taps_ref,
):
    step = pl.program_id(0)

    @pl.when(step == 0)
    def _():
        spread_taps(taps_raw_ref, taps_ref)
        clear_border(grid_ref)
        clear_border(dgrid_ref)

    other = [(first_ref, 0), (first_ref, 1), (second_ref, 0), (second_ref, 1), (third_ref, 0), (third_ref, 1)]
    own = [
        jnp.where(step == 0, ref[0, at], other_ref[0, other_at])
        for (ref, at), (other_ref, other_at) in zip(other[:4], other[2:])
    ]
    dy = jnp.concatenate([values[:, :HEAD_DIM] for values in own], axis=1).astype(F32)
    vhat = vhat_ref[...].astype(F32)
    gain = tiled_lanes(gain_ref[kind : kind + 1, :])
    product = dy * vhat
    small_ref[0, 28:29, :] = jnp.sum(product, axis=0, keepdims=True)
    small_ref[0, 29:30, :] = jnp.sum(dy, axis=0, keepdims=True)
    small_ref[0, 30:32, :] = jnp.zeros((2, GROUP), F32)
    scaled = dy * gain
    first = dot(scaled.astype(BF16), same_ref[...]) * (1.0 / HEAD_DIM)
    second = dot((product * gain).astype(BF16), same_ref[...]) * (1.0 / HEAD_DIM)
    dpool = rs_ref[...] * (scaled - first - vhat * second)
    dgrid_ref[1 : HEIGHT + 1, 1 : WIDTH + 1] = dpool.reshape(HEIGHT, WIDTH, FRAMES, GROUP)
    grid_ref[1 : HEIGHT + 1, 1 : WIDTH + 1] = mixed_ref[...].astype(F32).reshape(HEIGHT, WIDTH, FRAMES, GROUP)
    sums_ref[...] = jnp.zeros(sums_ref.shape, F32)

    @pl.loop(0, HEIGHT)
    def _(i):
        for tile in range(GROUP // LANES):
            lanes = slice(tile * LANES, tile * LANES + LANES)
            line = convolve(dgrid_ref, taps_ref, True, i, lanes)
            frame = lax.broadcasted_iota(jnp.int32, line.shape, 1)
            line = jnp.where(frame < frames_ref[0], line, 0.0)
            at = pl.multiple_of(i * WIDTH * FRAMES, WIDTH * FRAMES)
            dmix_ref[pl.ds(at, WIDTH * FRAMES), lanes] = line.reshape(WIDTH * FRAMES, LANES).astype(BF16)
            own = dgrid_ref[i + 1, 1 : WIDTH + 1, :, lanes]
            moved = (shift_frames(own, -1), own, shift_frames(own, 1))
            for b in range(3):
                for e in range(3):
                    window = grid_ref[i + b, e : e + WIDTH, :, lanes]
                    for a in range(3):
                        tap = 9 * a + 3 * b + e
                        sums_ref[tap, :, lanes] += jnp.sum(window * moved[a], axis=0)

    for tap in range(27):
        small_ref[0, tap : tap + 1, :] = jnp.sum(sums_ref[tap], axis=0, keepdims=True)
    small_ref[0, 27:28, :] = jnp.sum(dmix_ref[...].astype(F32), axis=0, keepdims=True)


def pool_back(kind, frames, grads_a, grads_b, vhat, rs, mixed, taps, gain, same):
    smem = pl.BlockSpec(memory_space=pltpu.SMEM)
    group = pl.BlockSpec((ROWS, GROUP), lambda g: (0, 2 * kind + g))
    return pl.pallas_call(
        functools.partial(pool_back_kernel, kind),
        grid=(2,),
        out_shape=(
            jax.ShapeDtypeStruct((ROWS, D), BF16),
            jax.ShapeDtypeStruct((2, 32, GROUP), F32),
        ),
        in_specs=[
            smem,
            pl.BlockSpec((1, 2, ROWS, LANES), lambda g: (kind, 0, 0, 0)),
            pl.BlockSpec((1, 2, ROWS, LANES), lambda g: (kind, g, 0, 0)),
            pl.BlockSpec((1, 2, ROWS, LANES), lambda g: (kind, 2, 0, 0)),
            group,
            group,
            group,
            pl.BlockSpec((1, 27, HEAD_DIM), lambda g: (kind, 0, 0)),
            whole((3, HEAD_DIM)),
            whole((GROUP, GROUP)),
        ],
        out_specs=(
            pl.BlockSpec((ROWS, GROUP), lambda g: (0, g)),
            pl.BlockSpec((1, 32, GROUP), lambda g: (g, 0, 0)),
        ),
        scratch_shapes=[
            pltpu.VMEM((HEIGHT + 2, WIDTH + 2, FRAMES, GROUP), F32),
            pltpu.VMEM((HEIGHT + 2, WIDTH + 2, FRAMES, GROUP), F32),
            pltpu.VMEM((27, FRAMES, GROUP), F32),
            pltpu.VMEM((27, FRAMES, GROUP), F32),
        ],
        compiler_params=params(),
        name="pool_back_%d" % kind,
    )(frames, grads_a, grads_b, grads_b, vhat, rs, mixed, taps, gain, same)


def project_grad_kernel(place_ref, normed_ref, dq_ref, dk_ref, dv_ref, one_ref, two_ref, full_ref):
    for kind, source_ref in enumerate((dq_ref, dk_ref, dv_ref)):
        grad = dot(normed_ref[...], source_ref[...], ((0,), (0,)))
        full_ref[:, kind * D : (kind + 1) * D] = grad.astype(BF16)
    half, columns = one_ref.shape[5:]
    for f in range(QKV // columns):

        @pl.loop(0, DP_BLOCKS)
        def _(d):
            bits = relative_bits(place_ref, d, f)
            lanes = slice(f * columns, (f + 1) * columns)
            at = pl.multiple_of(2 * d * half, half)
            one_ref[bits["c"], bits["x"], bits["y"], bits["z1"], bits["z2"]] = full_ref[pl.ds(at, half), lanes]
            at = pl.multiple_of((2 * d + 1) * half, half)
            two_ref[bits["c"], bits["y"], bits["x"], bits["z1"], bits["z2"]] = full_ref[pl.ds(at, half), lanes]


def project_grad(place, normed, dmixed, sides):
    vmem = pl.BlockSpec(memory_space=pltpu.VMEM)
    half = jax.ShapeDtypeStruct((2, 2, 2, 2, 2, D // DP_BLOCKS // 2, QKV // sides), BF16)
    return pl.pallas_call(
        project_grad_kernel,
        out_shape=(half, half),
        in_specs=[pl.BlockSpec(memory_space=pltpu.SMEM)] + [vmem] * 4,
        out_specs=(vmem, vmem),
        scratch_shapes=[pltpu.VMEM((D, QKV), BF16)],
        compiler_params=params(),
        name="project_grad",
    )(place, normed, *dmixed)


def project_back_kernel(
    dq_ref, dk_ref, dv_ref, weight_ref, x_ref, dmid_ref, g1_ref, gtok_ref, small_ref, dx_ref, wide_ref
):
    dy = None
    for kind, source_ref in enumerate((dq_ref, dk_ref, dv_ref)):
        term = dot(source_ref[...], weight_ref[:, kind * D : (kind + 1) * D], ((1,), (1,)))
        dy = term if dy is None else dy + term
    centred, rs = layer_stats(x_ref[...].astype(F32), D)
    vhat = centred * rs
    small_ref[0:1, :] = jnp.sum(dy * vhat, axis=0, keepdims=True)
    small_ref[1:2, :] = jnp.sum(dy, axis=0, keepdims=True)
    small_ref[2:8, :] = jnp.zeros((6, D), F32)
    scaled = dy * g1_ref[...]
    first = jnp.sum(scaled, axis=1, keepdims=True) * (1.0 / D)
    second = jnp.sum(scaled * vhat, axis=1, keepdims=True) * (1.0 / D)
    dx_ref[...] = dmid_ref[...] + rs * (scaled - first - vhat * second)

    @pl.loop(0, PLACES)
    def _(place):
        at = pl.multiple_of(place * FRAMES, FRAMES)
        write_place(wide_ref, place, dx_ref[pl.ds(at, FRAMES), :])

    for tile in range(D // LANES):
        gtok_ref[:, tile * LANES : (tile + 1) * LANES] = wide_ref[tile]


def project_back(dmixed, weight, x, dmid, g1):
    vmem = pl.BlockSpec(memory_space=pltpu.VMEM)
    return pl.pallas_call(
        project_back_kernel,
        out_shape=(jax.ShapeDtypeStruct((ROWS, D), F32), jax.ShapeDtypeStruct((8, D), F32)),
        in_specs=[vmem] * 7,
        out_specs=(vmem, vmem),
        scratch_shapes=[pltpu.VMEM((ROWS, D), F32), wide_scratch(D)],
        compiler_params=params(),
        name="project_back",
    )(*dmixed, weight, x, dmid, g1)


VECTOR_ROWS = 256
TABLE_AT, COMPRESS_AT, WIDE_AT = 96, 152, 160


class Scatter:
    def __init__(self, blocks_ref, out_ref, vector_ref, from_core, from_first, from_second, from_z, sems):
        dp, fsdp = lax.axis_index("dp"), lax.axis_index("fsdp")
        self.z, self.x = dp // 2, dp % 2
        self.y, self.c = fsdp // 2, fsdp % 2
        self.blocks_ref, self.out_ref, self.vector_ref = blocks_ref, out_ref, vector_ref
        self.from_core, self.from_first, self.from_second, self.from_z = from_core, from_first, from_second, from_z
        self.send_sem, self.recv_sem, self.vector_send, self.vector_recv, self.vector_more = sems
        self.rows = blocks_ref.shape[4] // (2 * PARTS)
        self.copies = {}

    def device(self, z, x, y, c):
        return (2 * z + x, 2 * y + c)

    def begin(self):
        z, x, y, c = self.z, self.x, self.y, self.c
        self.along = [self.device((z + k) % 4, x, y, c) for k in (1, 2, 3)]
        self.over_x, self.over_y = self.device(z, 1 - x, y, c), self.device(z, x, 1 - y, c)
        self.over_c = self.device(z, x, y, 1 - c)
        barrier = pltpu.get_barrier_semaphore()
        for partner in self.along + [self.over_x, self.over_y, self.over_c]:
            pl.semaphore_signal(barrier, inc=1, device_id=partner, device_id_type=MESH)
        pl.semaphore_wait(barrier, 6)

    def copy(self, source, target, send_sem, recv_sem, partner):
        copy = pltpu.make_async_remote_copy(
            src_ref=source, dst_ref=target, send_sem=send_sem, recv_sem=recv_sem, device_id=partner, device_id_type=MESH
        )
        copy.start()
        return copy

    def span(self, part, route):
        return pl.ds((2 * part + route) * self.rows, self.rows)

    def send(self, part, level):
        z, x, y, c = self.z, self.x, self.y, self.c
        every = slice(None)
        blocks = self.blocks_ref
        for route in range(2):
            span = self.span(part, route)
            if level == 0:
                moves = [(blocks.at[every, every, every, 1 - c, span], self.from_core.at[every, every, every, span], self.over_c)]
            elif level == 1:
                where = (every, 1 - x, every, c, span) if route == 0 else (every, every, 1 - y, c, span)
                moves = [(blocks.at[where], self.from_first.at[every, every, span], self.over_y if route else self.over_x)]
            elif level == 2:
                where = (every, x, 1 - y, c, span) if route == 0 else (every, 1 - x, y, c, span)
                moves = [(blocks.at[where], self.from_second.at[every, span], self.over_x if route else self.over_y)]
            else:
                moves = [
                    (blocks.at[(z + k) % 4, x, y, c, span], self.from_z.at[k - 1, span], self.along[k - 1])
                    for k in (1, 2, 3)
                ]
            for at, (source, target, partner) in enumerate(moves):
                slot = (2 * part + route) * 6 + level + at
                self.copies[part, route, level, at] = self.copy(
                    source, target, self.send_sem.at[slot], self.recv_sem.at[slot], partner
                )

    def advance(self, part, level):
        z, x, y, c = self.z, self.x, self.y, self.c
        every = slice(None)
        blocks = self.blocks_ref
        for route in range(2):
            span = self.span(part, route)
            for at in range(3 if level == 3 else 1):
                self.copies[part, route, level, at].wait_recv()
            if level == 0:
                where, more = (every, every, every, c, span), self.from_core[:, :, :, span]
            elif level == 1:
                where = (every, x, every, c, span) if route == 0 else (every, every, y, c, span)
                more = self.from_first[:, :, span]
            elif level == 2:
                where, more = (every, x, y, c, span), self.from_second[:, span]
            if level < 3:
                blocks[where] = blocks[where] + more
            else:
                total = blocks[z, x, y, c, span].astype(F32)
                for k in range(3):
                    total = total + self.from_z[k, span].astype(F32)
                self.out_ref[span] = total
        if level < 3:
            self.send(part, level + 1)

    def steps(self):
        order = []
        for turn in range(PARTS + 3):
            for level in reversed(range(4)):
                if 0 <= turn - level < PARTS:
                    order.append((turn - level, level))
        return [functools.partial(self.advance, *step) for step in order]

    def send_vector(self, stage):
        z, x, y, c = self.z, self.x, self.y, self.c
        partner = (
            self.over_c, self.over_x, self.over_y, self.device(z + 1 - 2 * (z % 2), x, y, c), self.along[1]
        )[stage]
        self.copies["vector", stage] = self.copy(
            self.vector_ref.at[stage], self.vector_more.at[stage], self.vector_send.at[stage],
            self.vector_recv.at[stage], partner,
        )

    def advance_vector(self, stage):
        self.copies["vector", stage].wait_recv()
        self.vector_ref[stage + 1] = self.vector_ref[stage] + self.vector_more[stage]
        if stage < 4:
            self.send_vector(stage + 1)

    def end(self):
        for copy in self.copies.values():
            copy.wait_send()


def tail_kernel(
    normed_ref, dq_ref, dk_ref, dv_ref, weight_ref, x_ref, dmid_ref, g1_ref, pq_ref, pk_ref, pv_ref,
    ta_ref, tb_ref, ca_ref, cb_ref, two_ref, gb1_ref,
    gqkv_ref, dx_ref, done_ref,
    blocks_ref, vector_ref, from_core, from_first, from_second, from_z, *sems,
):
    scatter = Scatter(blocks_ref, gqkv_ref, vector_ref, from_core, from_first, from_second, from_z, sems)
    scatter.begin()
    depth, columns = blocks_ref.shape[4:]
    pieces = (dq_ref, dk_ref, dv_ref)
    normed = normed_ref[...]
    for kind, source_ref in enumerate(pieces):
        grad = dot(normed, source_ref[...], ((0,), (0,))).astype(BF16)
        for f in range(QKV // columns):
            start, stop = max(f * columns, kind * D), min((f + 1) * columns, (kind + 1) * D)
            if start < stop:
                for d in range(DP_BLOCKS):
                    block = grad[d * depth : (d + 1) * depth, start - kind * D : stop - kind * D]
                    blocks_ref[d // 2, d % 2, f // 2, f % 2, :, start - f * columns : stop - f * columns] = block
    for part in range(PARTS):
        scatter.send(part, 0)
    steps = scatter.steps()

    def advance(count):
        for _ in range(min(count, len(steps))):
            steps.pop(0)()

    dy = None
    for kind, source_ref in enumerate(pieces):
        term = dot(source_ref[...], weight_ref[:, kind * D : (kind + 1) * D], ((1,), (1,)))
        dy = term if dy is None else dy + term
    advance(1)
    centred, rs = layer_stats(x_ref[...].astype(F32), D)
    vhat = centred * rs
    vector_ref[0] = jnp.zeros((VECTOR_ROWS, LANES), F32)
    for kind, source_ref in enumerate((pq_ref, pk_ref, pv_ref)):
        sums = source_ref[0] + source_ref[1]
        total = sums[:, :HEAD_DIM]
        for head in range(1, GROUP_HEADS):
            total = total + sums[:, HEAD_DIM * head : HEAD_DIM * (head + 1)]
        vector_ref[0, 32 * kind : 32 * kind + 32, :HEAD_DIM] = total
    vector_ref[0, TABLE_AT:COMPRESS_AT] = (ta_ref[...] + tb_ref[...])[: COMPRESS_AT - TABLE_AT]
    for s in range(2):
        vector_ref[0, COMPRESS_AT + 4 * s : COMPRESS_AT + 4 * s + 4] = ca_ref[s] + cb_ref[s]
    lines = [two_ref[at : at + 1, :] for at in range(4)]
    lines += [jnp.sum(dy * vhat, axis=0, keepdims=True), jnp.sum(dy, axis=0, keepdims=True)]
    lines += [
        jnp.concatenate([ref[0, 27:28, :], ref[1, 27:28, :]], axis=1) for ref in (pq_ref, pk_ref, pv_ref)
    ]
    lines += [gb1_ref[:, at : at + D] for at in range(0, FF, D)]
    for tile in range(D // LANES):
        for at, line in enumerate(lines):
            vector_ref[0, WIDE_AT + 16 * tile + at : WIDE_AT + 16 * tile + at + 1] = line[:, tile * LANES : (tile + 1) * LANES]
    scatter.send_vector(0)
    advance(2)
    scatter.advance_vector(0)
    scaled = dy * g1_ref[...].reshape(1, D)
    first = jnp.sum(scaled, axis=1, keepdims=True) * (1.0 / D)
    second = jnp.sum(scaled * vhat, axis=1, keepdims=True) * (1.0 / D)
    dx_ref[...] = dmid_ref[...] + rs * (scaled - first - vhat * second)
    advance(2)
    scatter.advance_vector(1)

    advance(2)
    scatter.advance_vector(2)
    advance(2)
    scatter.advance_vector(3)
    advance(len(steps))
    scatter.advance_vector(4)
    done_ref[...] = vector_ref[5]
    scatter.end()


def tail(normed, dmixed, weight, x, dmid, g1, pools, tables, compresses, two, gb1, shard):
    vmem = pl.BlockSpec(memory_space=pltpu.VMEM)
    depth, columns = shard
    shapes = [shard, (ROWS, D), (VECTOR_ROWS, LANES)]
    count = 2 * PARTS * 6
    return pl.pallas_call(
        tail_kernel,
        out_shape=tuple(jax.ShapeDtypeStruct(shape, F32) for shape in shapes),
        in_specs=[vmem] * 17,
        out_specs=(vmem,) * len(shapes),
        scratch_shapes=[
            pltpu.VMEM((4, 2, 2, 2, depth, columns), BF16),
            pltpu.VMEM((6, VECTOR_ROWS, LANES), F32),
            pltpu.VMEM((4, 2, 2, depth, columns), BF16),
            pltpu.VMEM((4, 2, depth, columns), BF16),
            pltpu.VMEM((4, depth, columns), BF16),
            pltpu.VMEM((3, depth, columns), BF16),
            pltpu.SemaphoreType.DMA((count,)),
            pltpu.SemaphoreType.DMA((count,)),
            pltpu.SemaphoreType.DMA((5,)),
            pltpu.SemaphoreType.DMA((5,)),
            pltpu.VMEM((5, VECTOR_ROWS, LANES), F32),
        ],
        compiler_params=params(collective_id=1, has_side_effects=True),
        name="tail",
    )(normed, *dmixed, weight, x, dmid, g1, *pools, *tables, *compresses, two, gb1)


def finish_kernel(
    gqkv_ref, dx_ref, done_ref, one_ref, one_more_ref, two_ref, two_more_ref,
    gtok_ref, ln1g_ref, ln1b_ref, wqkv_ref, qkvb_ref, conv_ref, pgain_ref, pbias_ref, time_ref, space_ref, comp_ref,
    wp_ref, projb_ref, ln2g_ref, ln2b_ref, w1_ref, fc1b_ref, w2_ref, fc2b_ref, wide_ref,
):
    @pl.loop(0, PLACES)
    def _(place):
        at = pl.multiple_of(place * FRAMES, FRAMES)
        write_place(wide_ref, place, dx_ref[pl.ds(at, FRAMES), :])

    for tile in range(D // LANES):
        gtok_ref[:, tile * LANES : (tile + 1) * LANES] = wide_ref[tile]
    wqkv_ref[...] = gqkv_ref[...]
    one = one_ref[0].astype(F32) + one_more_ref[0].astype(F32)
    two = two_ref[0].astype(F32) + two_more_ref[0].astype(F32)
    depth, part = w1_ref.shape[0], wp_ref.shape[1]
    for tile in range(w1_ref.shape[1] // LANES):
        w1_ref[:, tile * LANES : (tile + 1) * LANES] = one[tile * depth : (tile + 1) * depth]
    tiles = w2_ref.shape[1] // LANES
    for tile in range(tiles):
        w2_ref[:, tile * LANES : (tile + 1) * LANES] = two[tile * part : (tile + 1) * part]
    at = tiles * part
    wp_ref[:, :LANES] = two[at : at + depth]
    wp_ref[:, LANES:] = two[at + depth : at + 2 * depth, : part - LANES]
    for kind in range(3):
        conv_ref[kind] = done_ref[32 * kind : 32 * kind + 27, :HEAD_DIM]
        pgain_ref[kind : kind + 1, :] = done_ref[32 * kind + 28 : 32 * kind + 29, :HEAD_DIM]
        pbias_ref[kind : kind + 1, :] = done_ref[32 * kind + 29 : 32 * kind + 30, :HEAD_DIM]
    spans = 2 * HEIGHT - 1
    time_ref[...] = done_ref[TABLE_AT : TABLE_AT + 15, :HEAD_DIM]
    for s in range(2):
        start = TABLE_AT + 15 + spans * s
        space_ref[:, s] = done_ref[start : start + spans, :HEAD_DIM]
        comp_ref[s] = done_ref[COMPRESS_AT + 4 * s : COMPRESS_AT + 4 * s + 4, :HEAD_DIM]

    def line_of(at):
        tiles = [done_ref[WIDE_AT + 16 * tile + at : WIDE_AT + 16 * tile + at + 1, :] for tile in range(D // LANES)]
        return jnp.concatenate(tiles, axis=1).reshape(D)

    for at, target_ref in enumerate((projb_ref, ln2g_ref, ln2b_ref, fc2b_ref, ln1g_ref, ln1b_ref)):
        target_ref[...] = line_of(at)
    for kind in range(3):
        qkvb_ref[kind * D : (kind + 1) * D] = line_of(6 + kind)
    for side in range(FF // D):
        fc1b_ref[side * D : (side + 1) * D] = line_of(9 + side)


def finish(operands, w_qkv, w_proj, w_fc1, w_fc2):
    vmem = pl.BlockSpec(memory_space=pltpu.VMEM)
    shapes = [
        (ROWS, D), (D,), (D,), w_qkv, (QKV,), (3, 27, HEAD_DIM), (3, HEAD_DIM), (3, HEAD_DIM), (15, HEAD_DIM),
        (2 * HEIGHT - 1, 2, HEAD_DIM), (2, 4, HEAD_DIM), w_proj, (D,), (D,), (D,), w_fc1, (FF,), w_fc2[::-1], (D,),
    ]
    done = pl.pallas_call(
        finish_kernel,
        out_shape=tuple(jax.ShapeDtypeStruct(shape, F32) for shape in shapes),
        in_specs=[vmem] * 7,
        out_specs=(vmem,) * len(shapes),
        scratch_shapes=[wide_scratch(D)],
        compiler_params=params(),
        name="finish",
    )(*operands)
    done = list(done)
    done[9], done[17] = done[9].transpose(1, 0, 2), done[17].T
    return done


def row(vector):
    return vector.reshape(1, -1)


def tiled_lanes(array):
    return jnp.concatenate([array] * GROUP_HEADS, axis=-1)


def head_lanes(array):
    return jnp.pad(array, [(0, 0)] * (array.ndim - 1) + [(0, LANES - HEAD_DIM)])


DP_BLOCKS = 8
ROUTE_ONE = ("z2", "z1", "y", "x", "c")
ROUTE_TWO = ("z2", "z1", "x", "y", "c")
BIT = {"x": ("dp", 1), "z1": ("dp", 2), "z2": ("dp", 4), "y": ("fsdp", 2), "c": ("fsdp", 1)}


def swap(values, name, sizes):
    axis, bit = BIT[name]
    return lax.ppermute(values, axis, [(at, at ^ bit) for at in range(sizes[axis])])


def together(*values):
    return lax.optimization_barrier(values)


def flat_shard(one, two, proj):
    pieces = [part for _, part in flat_pieces(one, two, proj)]
    pieces[-1] = jnp.pad(pieces[-1], ((0, 0), (0, LANES - pieces[-1].shape[1])))
    return jnp.concatenate(pieces, axis=0)


class Staged:
    def __init__(self):
        self.sizes = {"dp": 8, "fsdp": 4}

    def place(self):
        dp, fsdp = lax.axis_index("dp"), lax.axis_index("fsdp")
        return jnp.stack([dp & 1, (dp >> 1) & 1, (dp >> 2) & 1, (fsdp >> 1) & 1, fsdp & 1]).astype(jnp.int32)

    def other_weights(self, flat):
        return lax.all_gather(flat, ("dp", "fsdp"), axis=0, tiled=False).reshape((8, 4) + flat.shape)


class Plain:
    def __init__(self, dp, fsdp):
        self.dp, self.fsdp = dp, fsdp

    def place(self):
        return jnp.zeros((5,), jnp.int32)

    def gather(self, shard):
        blocks = lax.all_gather(shard, ("dp", "fsdp"), axis=0, tiled=False)
        rows, columns = shard.shape
        joined = blocks.reshape(DP_BLOCKS, self.dp // DP_BLOCKS, self.fsdp, rows, columns).transpose(0, 2, 1, 3, 4)
        return joined.reshape(DP_BLOCKS, self.fsdp, self.dp // DP_BLOCKS * rows, columns)

    def other_weights(self, one, two, proj):
        return jax.vmap(jax.vmap(flat_shard))(self.gather(one), jnp.swapaxes(self.gather(two), 2, 3), self.gather(proj))

    def scatter(self, blocks, route):
        at = {name: 4 - where for where, name in enumerate(route)}
        rows, columns = blocks.shape[5:]
        blocks = blocks.transpose([at[name] for name in ("z2", "z1", "x", "y", "c")] + [5, 6])
        split = blocks.reshape(DP_BLOCKS, self.fsdp, self.dp // DP_BLOCKS, rows * DP_BLOCKS // self.dp, columns)
        split = split.transpose(0, 2, 1, 3, 4).reshape(self.dp * self.fsdp, -1, columns)
        return lax.psum_scatter(split, ("dp", "fsdp"), scatter_dimension=0, tiled=False).astype(F32)

    def scatter_flat(self, low, high, route, unpack):
        blocks = jnp.concatenate([low[None], high[None]])
        blocks = jax.vmap(unpack)(blocks.reshape((32,) + blocks.shape[5:]))
        return self.scatter(blocks.reshape((2,) * 5 + blocks.shape[1:]), route)

    def total(self, vector):
        return lax.psum(vector, ("dp", "fsdp"))


def run(
    comm, staged, tokens, prev_kv, memory, valid_frames, mem_len, ln1_gain, ln1_bias, w_qkv, qkv_bias, pool_conv, pool_gain,
    pool_bias, rel_time, rel_space, compress, w_proj, proj_bias, ln2_gain, ln2_bias, w_fc1, fc1_bias, w_fc2,
    fc2_bias, cotangent,
):
    place = comm.place()
    fsdp = QKV // w_qkv.shape[1]
    one_hot, own, fold, pick, same = (jnp.asarray(c, BF16) for c in constants())
    taps, gains, biases = pool_conv, pool_gain, pool_bias
    if staged:
        flat = pack(w_fc1, w_fc2.T, w_proj)
        w_qkv, flat = together(w_qkv, flat)
        flat = comm.other_weights(flat)
    prepared = prepare(
        valid_frames, mem_len, tokens, cotangent, ln1_gain, ln1_bias, one_hot, rel_time, rel_space.transpose(1, 0, 2), pick,
        prev_kv, memory, compress, w_qkv if staged else None,
    )
    x, normed, upstream, aug, table, rest, parts = prepared[-7:]
    if staged:
        first = prepared[0].reshape(8, 4, *w_qkv.shape)
    else:
        first, flat = comm.gather(w_qkv), comm.other_weights(w_fc1, w_fc2, w_proj)
    heads, vhat, rs, mixed, weight = query_key_value(
        valid_frames, normed, first, qkv_bias, taps, gains, biases, same
    )
    weights, pv, attended = attend(heads, rest, aug, table, own, fold)
    out, dmid, datt, plow, phigh, low1, high1, low2, high2, small_two, gb1 = feed_forward(
        place, attended, x, upstream, flat, proj_bias, ln2_gain, ln2_bias, row(fc1_bias), fc2_bias
    )

    def back(start_head, count, datt):
        return attend_back(
            start_head, count, heads, rest, aug, table, own, fold, pick, weights, pv, datt, parts
        )

    def pool(kind, grads_a, grads_b):
        pieces = pool_back(kind, valid_frames, grads_a, grads_b, vhat, rs, mixed, taps, gains, same)
        for target, piece in zip((dmixed, pools), pieces):
            target.append(piece)
        return pieces[0]

    dmixed, pools = [], []
    if staged:
        def blocks(values):
            return values.reshape(-1, *values.shape[-2:])

        def stage(one, two, names, step, *tied):
            keep_one, send_one = one
            keep_two, send_two = two
            more_one = swap(send_one, names[0], comm.sizes)
            more_two = [swap(send, names[1], comm.sizes) for send in send_two]
            result = step(*tied)
            more_one, *more_two = together(more_one, *more_two, result[0])[:-1]
            return keep_one, more_one, keep_two, more_two, result

        one = blocks(low1), blocks(high1)
        two = [blocks(low2), blocks(plow)], [blocks(high2), blocks(phigh)]
        *sums, (grads_a, gtable_a, gcompress_a) = stage(one, two, ("c", "c"), lambda datt: back(0, 2, datt), datt)
        for names, step in (
            (("x", "y"), "attend"),
            (("y", "x"), 0),
            (("z1", "z1"), 1),
            (("z2", "z2"), 2),
        ):
            low_one, high_one, low, high = halve_sum((([sums[0]], [sums[1]]), (sums[2], sums[3])), "halve")
            one, two = (low_one, high_one), ([low], [high])
            if step == "attend":
                datt, *_ = together(datt, grads_a, one[1], high)
                *sums, (grads_b, gtable_b, gcompress_b) = stage(one, two, names, lambda datt: back(2, 6, datt), datt)
            else:
                grads_b, *_ = together(grads_b, one[1], high)
                *sums, _ = stage(one, two, names, lambda grads: (pool(step, grads_a, grads),), grads_b)
    else:
        grads_a, gtable_a, gcompress_a = back(0, 2, datt)
        grads_b, gtable_b, gcompress_b = back(2, 6, datt)
        for kind in range(3):
            pool(kind, grads_a, grads_b)
        depth, part = D // DP_BLOCKS, D // fsdp

        def unpack_one(block):
            return jnp.concatenate(list(block.reshape(-1, depth, LANES)), axis=1)

        def unpack_two(block):
            return jnp.concatenate(list(block.reshape(-1, part, LANES)), axis=1).T

        def unpack_proj(block):
            return jnp.concatenate([block[:depth], block[depth:, : part - LANES]], axis=1)

        w1_sum = comm.scatter_flat(low1, high1, ROUTE_ONE, unpack_one)
        w2_sum = comm.scatter_flat(low2, high2, ROUTE_TWO, unpack_two)
        wp_sum = comm.scatter_flat(plow, phigh, ROUTE_TWO, unpack_proj)
    if staged:
        ended = tail(
            normed, dmixed, weight, x, dmid, ln1_gain, pools, (gtable_a, gtable_b), (gcompress_a, gcompress_b),
            small_two, gb1, w_qkv.shape,
        )
        last = (sums[0], sums[1], sums[2][0], sums[3][0])
        return (out, *finish((*ended, *last), w_qkv.shape, w_proj.shape, w_fc1.shape, w_fc2.shape))
    qkv_one, qkv_two = project_grad(place, normed, dmixed, fsdp)
    gtok, small_one = project_back(dmixed, weight, x, dmid, row(ln1_gain))
    pools = jnp.stack(pools)
    gbias = pools[:, :, 27].reshape(QKV)
    pools = jnp.sum(pools.reshape(3, 2, 32, GROUP_HEADS, HEAD_DIM), axis=(1, 3))
    gconv, gpool = pools[:, :27], pools[:, 28:30]
    gtable, gcompress = gtable_a + gtable_b, gcompress_a + gcompress_b
    smalls = (
        small_one[0], small_one[1], gbias, gconv, gpool[:, 0], gpool[:, 1],
        gtable[:15, :HEAD_DIM], gtable[15:53, :HEAD_DIM].reshape(2, 19, HEAD_DIM), gcompress[:, :, :HEAD_DIM],
        small_two[0], small_two[1], small_two[2], gb1[0], small_two[3],
    )
    vector = comm.total(jnp.concatenate([s.reshape(-1) for s in smalls]))
    totals, at = [], 0
    for s in smalls:
        totals.append(vector[at : at + s.size].reshape(s.shape))
        at += s.size
    qkv = comm.scatter(jnp.concatenate([qkv_one, jnp.moveaxis(qkv_two, 1, 2)], axis=5), ROUTE_ONE)
    sums = [qkv, wp_sum, w1_sum, w2_sum]
    return (
        out, gtok, totals[0], totals[1], sums[0], totals[2], totals[3], totals[4], totals[5], totals[6],
        totals[7], totals[8], sums[1], totals[9], totals[10], totals[11], sums[2], totals[12], sums[3], totals[13],
    )


def solution(mesh):
    both = P(("dp", "fsdp"))
    rows = P(("dp", "fsdp"), None)
    second = P(None, ("dp", "fsdp"), None)
    blocks = P("dp", "fsdp")
    none = P()
    dp, fsdp = mesh.shape["dp"], mesh.shape["fsdp"]
    staged = (dp, fsdp) == (8, 4)
    return jax.shard_map(
        functools.partial(run, Staged() if staged else Plain(dp, fsdp), staged),
        mesh=mesh,
        in_specs=(
            rows, second, second, both, both, none, none, blocks, none, none, none, none, none, none, none, blocks,
            none, none, none, blocks, none, blocks, none, rows,
        ),
        out_specs=(
            rows, rows, none, none, blocks, none, none, none, none, none, none, none, blocks, none, none, none,
            blocks, none, blocks, none,
        ),
        check_vma=False,
    )
```

```python
import functools

import jax
import jax.numpy as jnp
import numpy as np
from jax import lax
from jax.experimental import pallas as pl
from jax.experimental.pallas import tpu as pltpu
from jax.sharding import PartitionSpec as P

D = 768
FF = 3072
HEADS = 8
HEAD_DIM = 96
LANES = 128
FRAMES = 8
HEIGHT = 10
WIDTH = 10
PLACES = HEIGHT * WIDTH
ROWS = 800
MEM = 200
GROUP = 384
GROUP_HEADS = 4
QKV = 3 * D
KEY_ROWS = 1280
MEM_AT = 800
SQUEEZE_AT = 1024
REST = KEY_ROWS - ROWS
TABLE = 384
EPSILON = 1e-06
SCALE = HEAD_DIM**-0.5
ROOT = HEAD_DIM**0.5
LOG2E = 1.4426950408889634
MASKED = -1e9
MASK_LANE = 124
ROW_BLOCK = 400
BF16 = jnp.bfloat16
F32 = jnp.float32
VMEM_LIMIT = 60 * 1024 * 1024


def constants():
    place = np.arange(PLACES).repeat(FRAMES)
    row_t = np.tile(np.arange(FRAMES), PLACES)
    row_i, row_j = place // WIDTH, place % WIDTH
    one_hot = np.zeros((KEY_ROWS, LANES), np.float32)
    rows = np.arange(ROWS)
    one_hot[rows, 96 + row_t] = 1
    one_hot[rows, 104 + row_i] = 1
    one_hot[rows, 114 + row_j] = 1
    own = np.zeros((ROWS, TABLE), np.float32)
    fold = np.zeros((TABLE, LANES), np.float32)
    pick = np.zeros((TABLE, LANES), np.float32)
    for base, length, row_at, lane, offset in (
        (0, FRAMES, row_t, 96, 0),
        (64, HEIGHT, row_i, 104, 15),
        (164, WIDTH, row_j, 114, 34),
    ):
        for a in range(length):
            for b in range(length):
                column = base + a * length + b
                own[:, column] = row_at == a
                fold[column, lane + b] = 1
                pick[column, offset + a - b + length - 1] = 1
    lanes = np.arange(GROUP) // HEAD_DIM
    same = (lanes[:, None] == lanes[None, :]).astype(np.float32)
    return one_hot, own, fold, pick, same


def lane_index(shape):
    return lax.broadcasted_iota(jnp.int32, shape, len(shape) - 1)


def dot(a, b, contract=((1,), (0,)), precision=None):
    return lax.dot_general(a, b, (contract, ((), ())), preferred_element_type=F32, precision=precision)


def layer_stats(values, width):
    average = jnp.sum(values, axis=-1, keepdims=True) * (1.0 / width)
    centred = values - average
    variance = jnp.sum(centred * centred, axis=-1, keepdims=True) * (1.0 / width)
    return centred, lax.rsqrt(variance + EPSILON)


def params(**more):
    return pltpu.CompilerParams(vmem_limit_bytes=VMEM_LIMIT, **more)


def whole(shape):
    return pl.BlockSpec(shape, lambda *_: (0,) * len(shape))


def tiles_of(values):
    return [values[:, at : at + LANES] for at in range(0, values.shape[1], LANES)]


def flat_pieces(one, two, proj):
    at = 0
    for part in tiles_of(one) + tiles_of(two) + tiles_of(proj):
        yield at, part
        at += part.shape[0]


def read_place(wide_ref, place, tiles=D // LANES):
    parts = [wide_ref[tile, pl.ds(place, FRAMES, stride=PLACES), :] for tile in range(tiles)]
    return jnp.concatenate(parts, axis=1)


def write_place(wide_ref, place, values):
    for tile, part in enumerate(tiles_of(values)):
        wide_ref[tile, pl.ds(place, FRAMES, stride=PLACES), :] = part


def wide_scratch(columns):
    return pltpu.VMEM((columns // LANES, ROWS, LANES), F32)


PARTS = 3
MESH = pl.DeviceIdType.MESH


class Neighbours:
    def __init__(self):
        dp, fsdp = lax.axis_index("dp"), lax.axis_index("fsdp")
        z, x, y, c = dp // 2, dp % 2, fsdp // 2, fsdp % 2
        self.over = {
            "c": (dp, 2 * y + 1 - c),
            "x": (2 * z + 1 - x, fsdp),
            "y": (dp, 2 * (1 - y) + c),
            "z1": (2 * (z + 1 - 2 * (z % 2)) + x, fsdp),
            "z2": (2 * ((z + 2) % 4) + x, fsdp),
        }

    def greet(self, names):
        barrier = pltpu.get_barrier_semaphore()
        for name in names:
            pl.semaphore_signal(barrier, inc=1, device_id=self.over[name], device_id_type=MESH)
        pl.semaphore_wait(barrier, len(names))

    def copy(self, name, source, target, sems, at):
        return pltpu.make_async_remote_copy(
            src_ref=source,
            dst_ref=target,
            send_sem=sems[0].at[at],
            recv_sem=sems[1].at[at],
            device_id=self.over[name],
            device_id_type=MESH,
        )


class Gather:
    def __init__(self, shard_ref, all_ref, own_sem, send_sem, recv_sem):
        dp, fsdp = lax.axis_index("dp"), lax.axis_index("fsdp")
        self.z, self.x = dp // 2, dp % 2
        self.y, self.c = fsdp // 2, fsdp % 2
        self.shard_ref, self.all_ref = shard_ref, all_ref
        self.own_sem, self.send_sem, self.recv_sem = own_sem, send_sem, recv_sem
        self.rows = shard_ref.shape[0] // (2 * PARTS)
        self.copies = {}

    def device(self, z, x, y, c):
        return (2 * z + x, 2 * y + c)

    def partners(self):
        z, x, y, c = self.z, self.x, self.y, self.c
        along = [self.device((z + k) % 4, x, y, c) for k in (1, 2, 3)]
        return along + [self.device(z, 1 - x, y, c), self.device(z, x, 1 - y, c), self.device(z, x, y, 1 - c)]

    def begin(self):
        barrier = pltpu.get_barrier_semaphore()
        for partner in self.partners():
            pl.semaphore_signal(barrier, inc=1, device_id=partner, device_id_type=MESH)
        self.own = pltpu.make_async_copy(self.shard_ref, self.all_ref.at[self.z, self.x, self.y, self.c], self.own_sem)
        self.own.start()
        pl.semaphore_wait(barrier, 6)
        self.send_along(0)

    def send_along(self, part):
        if part < PARTS:
            for route in range(2):
                for stage in range(3):
                    self.send(part, route, stage)

    def send(self, part, route, stage):
        z, x, y, c = self.z, self.x, self.y, self.c
        rows = pl.ds((2 * part + route) * self.rows, self.rows)
        partner = self.partners()[stage if stage < 3 or stage == 5 else 3 + (stage - 3 + route) % 2]
        every = slice(None)
        if stage < 3:
            place = (z, x, y, c)
        elif stage == 3:
            place = (every, x, y, c)
        elif stage == 4:
            place = (every, every, y, c) if route == 0 else (every, x, every, c)
        else:
            place = (every, every, every, c)
        target = self.all_ref.at[(*place, rows)]
        source = self.shard_ref.at[rows] if stage < 3 else target
        at = (2 * part + route) * 6 + stage
        copy = pltpu.make_async_remote_copy(
            src_ref=source,
            dst_ref=target,
            send_sem=self.send_sem.at[at],
            recv_sem=self.recv_sem.at[at],
            device_id=partner,
            device_id_type=MESH,
        )
        copy.start()
        self.copies[part, route, stage] = copy

    def advance(self, part, level):
        if level == 0 and part == 0:
            self.own.wait()
        for route in range(2):
            for stage in ((0, 1, 2), (3,), (4,), (5,))[level]:
                self.copies[part, route, stage].wait_recv()
        if level == 0:
            self.send_along(part + 1)
        if level < 3:
            for route in range(2):
                self.send(part, route, 3 + level)

    def steps(self):
        order = []
        for turn in range(PARTS + 3):
            for level in reversed(range(4)):
                if 0 <= turn - level < PARTS:
                    order.append((turn - level, level))
        return [functools.partial(self.advance, *step) for step in order]

    def end(self):
        for copy in self.copies.values():
            copy.wait_send()


def prepare_kernel(
    communicate, frames_ref, length_ref, tokens_ref, cot_ref, gain_ref, bias_ref, one_hot_ref, time_ref, space_ref,
    pick_ref, prev_ref, mem_ref, taps_ref, *refs,
):
    if communicate:
        shard_ref, all_ref = refs[:2]
        refs = refs[2:]
    x_ref, normed_ref, turned_ref, upstream_ref, aug_ref, table_ref, rest_ref, tap_ref = refs[:8]
    wide_ref, sums_ref, parts_ref, tables_ref = refs[8:12]
    steps = []
    if communicate:
        gather = Gather(shard_ref, all_ref, *refs[12:])
        gather.begin()
        steps = gather.steps()

    def advance(count=1):
        for _ in range(min(count, len(steps))):
            steps.pop(0)()

    def permute(source_ref, target_ref):
        for tile, part in enumerate(tiles_of(source_ref[...])):
            wide_ref[tile] = part.astype(F32)

        @pl.loop(0, PLACES // 2)
        def _(pair):
            first = read_place(wide_ref, 2 * pair)
            second = read_place(wide_ref, 2 * pair + 1)
            at = pl.multiple_of(pair * 16, 16)
            target_ref[pl.ds(at, 16), :] = jnp.concatenate([first, second], axis=0).astype(BF16)

    permute(cot_ref, upstream_ref)
    permute(tokens_ref, x_ref)
    advance()
    centred, rs = layer_stats(x_ref[...].astype(F32), D)
    normed_ref[...] = (centred * rs * gain_ref[...].reshape(1, D) + bias_ref[...].reshape(1, D)).astype(BF16)
    turned_ref[...] = normed_ref[...].T
    row = lax.broadcasted_iota(jnp.int32, (KEY_ROWS, LANES), 0)
    frames, length = frames_ref[0], length_ref[0]
    place = jnp.where(row < MEM_AT, row & 7, jnp.where(row < SQUEEZE_AT, row - MEM_AT, row - SQUEEZE_AT))
    limit = jnp.where(row < MEM_AT, frames, jnp.where(row < SQUEEZE_AT, length, MEM))
    off = jnp.where(place >= limit, jnp.where(lane_index((KEY_ROWS, LANES)) == MASK_LANE, MASKED, 0.0), 0.0)
    aug_ref[...] = (one_hot_ref[...].astype(F32) + off).astype(BF16)
    tables_ref[...] = jnp.zeros((LANES, LANES), F32)
    spans = 2 * HEIGHT - 1
    tables_ref[0 : 2 * FRAMES - 1, :HEAD_DIM] = time_ref[...]
    for s in range(2):
        tables_ref[15 + spans * s : 15 + spans * (s + 1), :HEAD_DIM] = space_ref[:, s]
    table_ref[...] = dot(pick_ref[...], tables_ref[...].astype(BF16)).astype(BF16)
    advance()

    def head_of(values, head):
        return values[:, HEAD_DIM * head : HEAD_DIM * head + HEAD_DIM]

    for s in range(2):
        for group in range(2):
            columns = slice(group * GROUP, (group + 1) * GROUP)
            for tile, part in enumerate(tiles_of(prev_ref[s, :, columns])):
                wide_ref[tile] = part.astype(F32)

            taps = [tiled_lanes(taps_ref[s, tap : tap + 1, :]) for tap in range(4)]

            @pl.loop(0, HEIGHT // 2)
            def _(i):
                for j in range(WIDTH // 2):
                    total = None
                    at = pl.multiple_of((i * (WIDTH // 2) + j) * FRAMES, FRAMES)
                    for tap in range(4):
                        place = (2 * i + tap // 2) * WIDTH + 2 * j + tap % 2
                        part = read_place(wide_ref, place, GROUP // LANES)
                        parts_ref[tap, pl.ds(at, FRAMES), :] = part
                        term = part * taps[tap]
                        total = term if total is None else total + term
                    sums_ref[pl.ds(at, FRAMES), :] = total

            old = mem_ref[s, :, columns].astype(F32)
            for head in range(GROUP_HEADS):
                rest = jnp.concatenate(
                    [
                        head_of(old, head),
                        jnp.zeros((SQUEEZE_AT - MEM_AT - MEM, HEAD_DIM), F32),
                        head_of(sums_ref[...], head),
                        jnp.zeros((KEY_ROWS - SQUEEZE_AT - MEM, HEAD_DIM), F32),
                    ],
                    axis=0,
                )
                rest = jnp.concatenate([rest, jnp.zeros((REST, LANES - HEAD_DIM), F32)], axis=1)
                rest_ref[s, group * GROUP_HEADS + head] = rest.astype(BF16)
                for tap in range(4):
                    part = jnp.concatenate([head_of(parts_ref[tap], head), jnp.zeros((8, HEAD_DIM), F32)], axis=0)
                    part = jnp.concatenate([part, jnp.zeros((208, LANES - HEAD_DIM), F32)], axis=1)
                    tap_ref[s, group * GROUP_HEADS + head, tap] = part.astype(BF16)
            advance(3 if group + s else 2)
    advance(len(steps))
    if communicate:
        gather.end()


def pack_kernel(one_ref, two_ref, proj_ref, flat_ref):
    for at, part in flat_pieces(one_ref[...], two_ref[...], proj_ref[...]):
        flat_ref[at : at + part.shape[0], : part.shape[1]] = part


def pack(one, two, proj):
    vmem = pl.BlockSpec(memory_space=pltpu.VMEM)
    rows = (one.size + two.size) // LANES + 2 * proj.shape[0]
    return pl.pallas_call(
        pack_kernel,
        out_shape=jax.ShapeDtypeStruct((rows, LANES), BF16),
        in_specs=[vmem] * 3,
        out_specs=vmem,
        compiler_params=params(),
        name="pack",
    )(one, two, proj)


def prepare(frames, length, tokens, cot, gain, bias, one_hot, rel_time, rel_space, pick, prev, memory, taps, shard=None):
    smem = pl.BlockSpec(memory_space=pltpu.SMEM)
    vmem = pl.BlockSpec(memory_space=pltpu.VMEM)
    communicate = shard is not None
    out_shape = [
        jax.ShapeDtypeStruct((ROWS, D), BF16),
        jax.ShapeDtypeStruct((ROWS, D), BF16),
        jax.ShapeDtypeStruct((D, ROWS), BF16),
        jax.ShapeDtypeStruct((ROWS, D), BF16),
        jax.ShapeDtypeStruct((KEY_ROWS, LANES), BF16),
        jax.ShapeDtypeStruct((TABLE, LANES), BF16),
        jax.ShapeDtypeStruct((2, HEADS, REST, LANES), BF16),
        jax.ShapeDtypeStruct((2, HEADS, 4, 208, LANES), BF16),
    ]
    in_specs, out_specs = [smem, smem] + [vmem] * 11, [vmem] * 8
    operands = [frames, length, tokens, cot, gain, bias, one_hot, rel_time, rel_space, pick, prev, memory, taps]
    scratch = [
        wide_scratch(D),
        pltpu.VMEM((MEM, GROUP), F32),
        pltpu.VMEM((4, MEM, GROUP), F32),
        pltpu.VMEM((LANES, LANES), F32),
    ]
    more = {}
    if communicate:
        anywhere = pl.BlockSpec(memory_space=pl.ANY)
        out_shape = [jax.ShapeDtypeStruct((4, 2, 2, 2) + shard.shape, BF16)] + out_shape
        in_specs.append(anywhere)
        out_specs = [anywhere] + out_specs
        operands.append(shard)
        count = 2 * PARTS * 6
        scratch += [pltpu.SemaphoreType.DMA, pltpu.SemaphoreType.DMA((count,)), pltpu.SemaphoreType.DMA((count,))]
        more = {"collective_id": 0, "has_side_effects": True}
    return pl.pallas_call(
        functools.partial(prepare_kernel, communicate),
        out_shape=tuple(out_shape),
        in_specs=in_specs,
        out_specs=tuple(out_specs),
        scratch_shapes=scratch,
        compiler_params=params(**more),
        name="prepare",
    )(*operands)


def shift_frames(values, step):
    frame = lax.broadcasted_iota(jnp.int32, values.shape, values.ndim - 2)
    moved = pltpu.roll(values, step % FRAMES, values.ndim - 2)
    edge = 0 if step == 1 else FRAMES - 1
    return jnp.where(frame == edge, 0.0, moved)


def convolve(grid_ref, taps_ref, flip, i, lanes):
    sums = [None, None, None]
    for b in range(3):
        for e in range(3):
            window = grid_ref[i + b, e : e + WIDTH, :, lanes]
            for a in range(3):
                tap = 9 * a + 3 * b + e
                term = window * taps_ref[26 - tap if flip else tap, :, lanes][None]
                sums[a] = term if sums[a] is None else sums[a] + term
    return sums[1] + shift_frames(sums[0], 1) + shift_frames(sums[2], -1)


def spread_taps(raw_ref, taps_ref):
    for tap in range(27):
        line = tiled_lanes(raw_ref[0, tap : tap + 1, :])
        taps_ref[tap] = jnp.broadcast_to(line, (FRAMES, GROUP))


def clear_border(grid_ref):
    grid_ref[...] = jnp.zeros(grid_ref.shape, grid_ref.dtype)


def relative_bits(place_ref, d, f):
    return {
        "x": (d & 1) ^ place_ref[0],
        "z1": ((d >> 1) & 1) ^ place_ref[1],
        "z2": ((d >> 2) & 1) ^ place_ref[2],
        "y": ((f >> 1) & 1) ^ place_ref[3],
        "c": (f & 1) ^ place_ref[4],
    }


def slot(bits, order):
    return sum(bits[name] << at for at, name in enumerate(order))


def qkv_kernel(
    frames_ref, normed_ref, shards_ref, qkv_bias_ref, taps_raw_ref, gain_ref, bias_ref, same_ref,
    heads_ref, vhat_ref, rs_ref, mixed_ref, weight_ref, grid_ref, pooled_ref, taps_ref, line_ref,
):
    step = pl.program_id(0)

    @pl.when(step == 0)
    def _():
        clear_border(grid_ref)
        line_ref[...] = qkv_bias_ref[...].reshape(1, QKV)
        depth, columns = shards_ref.shape[2:]
        for f in range(QKV // columns):
            for d in range(DP_BLOCKS):
                weight_ref[d * depth : (d + 1) * depth, f * columns : (f + 1) * columns] = shards_ref[d, f]

    @pl.when(step % 2 == 0)
    def _():
        spread_taps(taps_raw_ref, taps_ref)

    at = pl.multiple_of(step * GROUP, LANES)
    mixed = dot(normed_ref[...], weight_ref[:, pl.ds(at, GROUP)]) + line_ref[:, pl.ds(at, GROUP)]
    row = lax.broadcasted_iota(jnp.int32, (ROWS, GROUP), 0)
    mixed = jnp.where((row & 7) < frames_ref[0], mixed, 0.0)
    mixed_ref[...] = mixed.astype(BF16)
    grid_ref[1 : HEIGHT + 1, 1 : WIDTH + 1] = mixed.reshape(HEIGHT, WIDTH, FRAMES, GROUP)

    @pl.loop(0, HEIGHT)
    def _(i):
        for tile in range(GROUP // LANES):
            lanes = slice(tile * LANES, tile * LANES + LANES)
            line = convolve(grid_ref, taps_ref, False, i, lanes)
            at = pl.multiple_of(i * WIDTH * FRAMES, WIDTH * FRAMES)
            pooled_ref[pl.ds(at, WIDTH * FRAMES), lanes] = line.reshape(WIDTH * FRAMES, LANES)

    pooled = pooled_ref[...]
    high = pooled.astype(BF16)
    low = (pooled - high.astype(F32)).astype(BF16)
    centred = pooled - (dot(high, same_ref[...]) + dot(low, same_ref[...])) * (1.0 / HEAD_DIM)
    variance = dot((centred * centred).astype(BF16), same_ref[...]) * (1.0 / HEAD_DIM)
    rs = lax.rsqrt(variance + EPSILON)
    vhat = centred * rs
    rs_ref[...] = rs
    vhat_ref[...] = vhat.astype(BF16)
    kind = pl.ds(step // 2, 1)
    out = (vhat * tiled_lanes(gain_ref[kind, :]) + tiled_lanes(bias_ref[kind, :])).astype(BF16)
    for head in range(GROUP_HEADS):
        own = out[:, HEAD_DIM * head : HEAD_DIM * (head + 1)]
        heads_ref[head] = jnp.concatenate([own, jnp.zeros((ROWS, LANES - HEAD_DIM), BF16)], axis=1)


def query_key_value(frames, normed, shards, qkv_bias, taps, gain, bias, same):
    smem = pl.BlockSpec(memory_space=pltpu.SMEM)
    return pl.pallas_call(
        qkv_kernel,
        grid=(6,),
        out_shape=(
            jax.ShapeDtypeStruct((3 * HEADS, ROWS, LANES), BF16),
            jax.ShapeDtypeStruct((ROWS, QKV), BF16),
            jax.ShapeDtypeStruct((ROWS, QKV), F32),
            jax.ShapeDtypeStruct((ROWS, QKV), BF16),
            jax.ShapeDtypeStruct((D, QKV), BF16),
        ),
        in_specs=[
            smem,
            whole((ROWS, D)),
            whole(shards.shape),
            whole((QKV,)),
            pl.BlockSpec((1, 27, HEAD_DIM), lambda g: (g // 2, 0, 0)),
            whole((3, HEAD_DIM)),
            whole((3, HEAD_DIM)),
            whole((GROUP, GROUP)),
        ],
        out_specs=(
            pl.BlockSpec((GROUP_HEADS, ROWS, LANES), lambda g: (g, 0, 0)),
            pl.BlockSpec((ROWS, GROUP), lambda g: (0, g)),
            pl.BlockSpec((ROWS, GROUP), lambda g: (0, g)),
            pl.BlockSpec((ROWS, GROUP), lambda g: (0, g)),
            whole((D, QKV)),
        ),
        scratch_shapes=[
            pltpu.VMEM((HEIGHT + 2, WIDTH + 2, FRAMES, GROUP), F32),
            pltpu.VMEM((ROWS, GROUP), F32),
            pltpu.VMEM((27, FRAMES, GROUP), F32),
            pltpu.VMEM((1, QKV), F32),
        ],
        compiler_params=params(),
        name="query_key_value",
    )(frames, normed, shards, qkv_bias, taps, gain, bias, same)


def attend_kernel(
    q_ref, k_ref, v_ref, krest_ref, vrest_ref, aug_ref, table_ref, own_ref, fold_ref,
    weights_ref, pv_ref, out_ref, keys_ref, vals_ref, query_ref,
):
    lane = lane_index((KEY_ROWS, LANES))
    keys_ref[:ROWS] = k_ref[0] + aug_ref[:ROWS]
    keys_ref[ROWS:] = krest_ref[0, 0] + aug_ref[ROWS:]
    one = jnp.where(lane == HEAD_DIM, 1.0, 0.0).astype(BF16)
    vals_ref[:ROWS] = v_ref[0] + one[:ROWS]
    vals_ref[ROWS:] = vrest_ref[0, 0] + one[ROWS:]
    query = q_ref[0]
    every = (dot(query, table_ref[...], ((1,), (1,))) * ROOT).astype(BF16) * own_ref[...]
    relative = dot(every, fold_ref[...])
    marked = jnp.where(lane[:ROWS] == MASK_LANE, 1.0, relative)
    query_ref[...] = (query.astype(F32) + marked).astype(BF16)

    for block in range(ROWS // ROW_BLOCK):
        rows = slice(block * ROW_BLOCK, (block + 1) * ROW_BLOCK)
        scores = dot(query_ref[rows, :], keys_ref[...], ((1,), (1,)))
        largest = jnp.max(scores, axis=1, keepdims=True)
        weights = jnp.exp2((scores - largest) * (SCALE * LOG2E)).astype(BF16)
        weights_ref[0, rows, :] = weights
        total = dot(weights, vals_ref[...])
        inverse = 1.0 / total[:, HEAD_DIM : HEAD_DIM + 1]
        lane = lane_index((ROW_BLOCK, LANES))
        pv = jnp.where(lane < HEAD_DIM, total * inverse, 0.0)
        out_ref[0, rows, :] = (pv + q_ref[0, rows, :].astype(F32)).astype(BF16)
        high = inverse.astype(BF16).astype(F32)
        extra = jnp.where(lane == HEAD_DIM, high, jnp.where(lane == HEAD_DIM + 1, inverse - high, 0.0))
        pv_ref[0, rows, :] = (pv + extra).astype(BF16)


def attend(heads, rest, aug, table, own, fold):
    head = (1, ROWS, LANES)
    tail = (1, 1, REST, LANES)
    return pl.pallas_call(
        attend_kernel,
        grid=(HEADS,),
        out_shape=(
            jax.ShapeDtypeStruct((HEADS, ROWS, KEY_ROWS), BF16),
            jax.ShapeDtypeStruct((HEADS, ROWS, LANES), BF16),
            jax.ShapeDtypeStruct((HEADS, ROWS, LANES), BF16),
        ),
        in_specs=[
            pl.BlockSpec(head, lambda h: (h, 0, 0)),
            pl.BlockSpec(head, lambda h: (HEADS + h, 0, 0)),
            pl.BlockSpec(head, lambda h: (2 * HEADS + h, 0, 0)),
            pl.BlockSpec(tail, lambda h: (0, h, 0, 0)),
            pl.BlockSpec(tail, lambda h: (1, h, 0, 0)),
            whole((KEY_ROWS, LANES)),
            whole((TABLE, LANES)),
            whole((ROWS, TABLE)),
            whole((TABLE, LANES)),
        ],
        out_specs=(
            pl.BlockSpec((1, ROWS, KEY_ROWS), lambda h: (h, 0, 0)),
            pl.BlockSpec(head, lambda h: (h, 0, 0)),
            pl.BlockSpec(head, lambda h: (h, 0, 0)),
        ),
        scratch_shapes=[
            pltpu.VMEM((KEY_ROWS, LANES), BF16),
            pltpu.VMEM((KEY_ROWS, LANES), BF16),
            pltpu.VMEM((ROWS, LANES), BF16),
        ],
        compiler_params=params(),
        name="attend",
    )(heads, heads, heads, rest, rest, aug, table, own, fold)


CHUNK = 768
CHUNKS = FF // CHUNK
TILES = CHUNK // LANES


def middle_kernel(
    place_ref, att_ref, x_ref, up_ref, wp_ref, w1_ref, w2_ref, pb_ref, g2_ref, b2_ref, fb1_ref, fb2_ref,
    out_ref, dmid_ref, datt_ref, plow_ref, phigh_ref, low1_ref, high1_ref, low2_ref, high2_ref, small_ref, gb1_ref,
    packed_ref, proj_ref, mid_ref, hidden_ref, total_ref, dhid_ref, wide_ref, w1_scr, w2_scr, grad_ref,
    hiddent_ref, upt_ref,
):
    step = pl.program_id(0)
    sides = wp_ref.shape[1]
    part = D // sides
    depth = D // DP_BLOCKS
    inner = FF // DP_BLOCKS

    @pl.when(step == 0)
    def _():
        for head in range(HEADS):
            packed_ref[:, HEAD_DIM * head : HEAD_DIM * (head + 1)] = att_ref[head][:, :HEAD_DIM]
        for f in range(sides):
            for d in range(DP_BLOCKS):
                rows = slice(d * depth, (d + 1) * depth)
                proj_ref[rows, f * part : f * part + LANES] = wp_ref[d, f, :depth]
                proj_ref[rows, f * part + LANES : (f + 1) * part] = wp_ref[d, f, depth:, : part - LANES]
        middle = x_ref[...].astype(F32) + dot(packed_ref[...], proj_ref[...]) + pb_ref[...].reshape(1, D)
        mid_ref[...] = middle
        centred, rs = layer_stats(middle, D)
        hidden = centred * rs * g2_ref[...].reshape(1, D) + b2_ref[...].reshape(1, D)
        hidden_ref[...] = hidden.astype(BF16)
        hiddent_ref[...] = hidden.T.astype(BF16)
        upt_ref[...] = up_ref[...].T
        total_ref[...] = middle + fb2_ref[...].reshape(1, D).reshape(1, D)
        dhid_ref[...] = jnp.zeros((ROWS, D), F32)

    for tile in range(TILES):
        lanes = slice(tile * LANES, (tile + 1) * LANES)
        for d in range(DP_BLOCKS):
            w1_scr[d * depth : (d + 1) * depth, lanes] = w1_ref[d, 0, tile * depth : (tile + 1) * depth]
        side, at = divmod(tile, inner // LANES)
        for f in range(sides):
            w2_scr[f * part : (f + 1) * part, lanes] = w2_ref[side, f, at * part : (at + 1) * part]
    w1, w2 = w1_scr[...], w2_scr[...]
    before = dot(hidden_ref[...], w1) + fb1_ref[...]
    cdf = 0.5 + 0.5 * lax.erf(before * (2.0**-0.5))
    activated = (before * cdf).astype(BF16)
    slope = cdf + before * (jnp.exp(before * before * -0.5) * 0.3989422804014327)
    dbefore = dot(up_ref[...], w2) * slope
    dbefore_low = dbefore.astype(BF16)
    gb1_ref[...] = jnp.sum(dbefore_low.astype(F32), axis=0, keepdims=True)
    total_ref[...] += dot(activated, w2, ((1,), (1,)))
    dhid_ref[...] += dot(dbefore_low, w1, ((1,), (1,)))

    core = place_ref[4]
    grad_ref[...] = dot(upt_ref[...], activated).astype(BF16)
    for tile in range(TILES):
        lanes = slice(tile * LANES, (tile + 1) * LANES)
        side, at = divmod(tile, inner // LANES)
        rows = slice(at * part, (at + 1) * part)
        for y in range(sides // 2):
            bits = relative_bits(place_ref, side, 2 * y)
            for target_ref, c in ((low2_ref, core), (high2_ref, 1 - core)):
                start = pl.multiple_of((2 * y + c) * part, part)
                target_ref[bits["y"], bits["x"], 0, 0, rows] = grad_ref[pl.ds(start, part), lanes]
    grad_ref[...] = dot(hiddent_ref[...], dbefore_low).astype(BF16)

    def store_one(target_ref):
        for tile in range(TILES):
            lanes = slice(tile * LANES, (tile + 1) * LANES)
            for d in range(DP_BLOCKS):
                bits = relative_bits(place_ref, d, 0)
                block = grad_ref[d * depth : (d + 1) * depth, lanes]
                target_ref[bits["x"], 0, bits["z1"], bits["z2"], tile * depth : (tile + 1) * depth] = block

    @pl.when(step < CHUNKS // 2)
    def _():
        store_one(low1_ref)

    @pl.when(step >= CHUNKS // 2)
    def _():
        store_one(high1_ref)

    @pl.when(step == CHUNKS - 1)
    def _():
        @pl.loop(0, PLACES)
        def _(place):
            at = pl.multiple_of(place * FRAMES, FRAMES)
            write_place(wide_ref, place, total_ref[pl.ds(at, FRAMES), :])

        for tile in range(D // LANES):
            out_ref[:, tile * LANES : (tile + 1) * LANES] = wide_ref[tile].astype(BF16)
        upstream = up_ref[...].astype(F32)
        dhidden = dhid_ref[...]
        centred, rs = layer_stats(mid_ref[...], D)
        vhat = centred * rs
        dgain = jnp.sum(dhidden * vhat, axis=0, keepdims=True)
        dbias = jnp.sum(dhidden, axis=0, keepdims=True)
        scaled = dhidden * g2_ref[...].reshape(1, D)
        first = jnp.sum(scaled, axis=1, keepdims=True) * (1.0 / D)
        second = jnp.sum(scaled * vhat, axis=1, keepdims=True) * (1.0 / D)
        dmiddle = upstream + rs * (scaled - first - vhat * second)
        dmid_ref[...] = dmiddle
        dproj = dmiddle.astype(BF16)
        small_ref[0:1, :] = jnp.sum(dproj.astype(F32), axis=0, keepdims=True)
        small_ref[1:2, :] = dgain
        small_ref[2:3, :] = dbias
        small_ref[3:4, :] = jnp.sum(upstream, axis=0, keepdims=True)
        small_ref[4:8, :] = jnp.zeros((4, D), F32)
        grad_ref[...] = dot(packed_ref[...], dproj, ((0,), (0,))).astype(BF16)
        for d in range(DP_BLOCKS):
            rows = slice(d * depth, (d + 1) * depth)
            for y in range(sides // 2):
                bits = relative_bits(place_ref, d, 2 * y)
                where = (bits["y"], bits["x"], bits["z1"], bits["z2"])
                sides_of = [grad_ref[rows, f * part : (f + 1) * part] for f in (2 * y, 2 * y + 1)]
                for target_ref, c in ((plow_ref, core), (phigh_ref, 1 - core)):
                    block = jnp.where(c == 0, sides_of[0], sides_of[1])
                    target_ref[(*where, slice(0, depth))] = block[:, :LANES]
                    rest = jnp.concatenate([block[:, LANES:], jnp.zeros((depth, 2 * LANES - part), BF16)], axis=1)
                    target_ref[(*where, slice(depth, 2 * depth))] = rest
        datt = dot(dproj, proj_ref[...], ((1,), (1,))).astype(BF16)
        for head in range(HEADS):
            datt_ref[head] = jnp.concatenate(
                [datt[:, HEAD_DIM * head : HEAD_DIM * (head + 1)], jnp.zeros((ROWS, LANES - HEAD_DIM), BF16)],
                axis=1,
            )


def feed_forward(place, att, x, up, flat, pb, g2, b2, fb1, fb2):
    once = pl.Buffered(1)
    sides = flat.shape[1]
    part, depth = D // sides, D // DP_BLOCKS
    rows_one, rows_two = TILES * depth, FF // DP_BLOCKS // LANES * part

    def kept(shape):
        return pl.BlockSpec(shape, lambda *_: (0,) * len(shape), pipeline_mode=once)

    def side_of(s, place):
        return 2 * (place[3] ^ (s & 1)) + (place[4] ^ (s >> 1))

    def columns(s, place):
        return (0, side_of(s, place))

    def low_one(s, place):
        return (0, jnp.where(s < 2, s & 1, 1), 0, 0, 0, 0)

    def high_one(s, place):
        return (0, jnp.where(s < 2, 0, s & 1), 0, 0, 0, 0)

    def pair(s, place):
        side = side_of(s, place)
        return (0, 0, place[1] ^ (side & 1), place[2] ^ (side >> 1), 0, 0)

    bits = (2, 2, 2, 2)
    one, two, proj = bits + (rows_one, LANES), bits + (rows_two, LANES), bits + (2 * depth, LANES)
    return pl.pallas_call(
        middle_kernel,
        out_shape=(
            jax.ShapeDtypeStruct((ROWS, D), BF16),
            jax.ShapeDtypeStruct((ROWS, D), F32),
            jax.ShapeDtypeStruct((HEADS, ROWS, LANES), BF16),
            jax.ShapeDtypeStruct(proj, BF16),
            jax.ShapeDtypeStruct(proj, BF16),
            jax.ShapeDtypeStruct(one, BF16),
            jax.ShapeDtypeStruct(one, BF16),
            jax.ShapeDtypeStruct(two, BF16),
            jax.ShapeDtypeStruct(two, BF16),
            jax.ShapeDtypeStruct((8, D), F32),
            jax.ShapeDtypeStruct((1, FF), F32),
        ),
        grid_spec=pltpu.PrefetchScalarGridSpec(
            num_scalar_prefetch=1,
            grid=(CHUNKS,),
            in_specs=[
                kept((HEADS, ROWS, LANES)),
                kept((ROWS, D)),
                kept((ROWS, D)),
                pl.BlockSpec(
                    (DP_BLOCKS, sides, 2 * depth, LANES), lambda s, place: (0, 0, 6, 0), pipeline_mode=once
                ),
                pl.BlockSpec(
                    (DP_BLOCKS, 1, rows_one, LANES), lambda s, place: (0, side_of(s, place), 0, 0)
                ),
                pl.BlockSpec((2, sides, rows_two, LANES), lambda s, place: (side_of(s, place), 0, 1, 0)),
                kept((D,)),
                kept((D,)),
                kept((D,)),
                pl.BlockSpec((1, CHUNK), columns),
                kept((D,)),
            ],
            out_specs=(
                kept((ROWS, D)),
                kept((ROWS, D)),
                kept((HEADS, ROWS, LANES)),
                kept(proj),
                kept(proj),
                pl.BlockSpec((2, 1, 2, 2, rows_one, LANES), low_one),
                pl.BlockSpec((2, 1, 2, 2, rows_one, LANES), high_one),
                pl.BlockSpec((2, 2, 1, 1, rows_two, LANES), pair),
                pl.BlockSpec((2, 2, 1, 1, rows_two, LANES), pair),
                kept((8, D)),
                pl.BlockSpec((1, CHUNK), columns),
            ),
            scratch_shapes=[
                pltpu.VMEM((ROWS, D), BF16),
                pltpu.VMEM((D, D), BF16),
                pltpu.VMEM((ROWS, D), F32),
                pltpu.VMEM((ROWS, D), BF16),
                pltpu.VMEM((ROWS, D), F32),
                pltpu.VMEM((ROWS, D), F32),
                wide_scratch(D),
                pltpu.VMEM((D, CHUNK), BF16),
                pltpu.VMEM((D, CHUNK), BF16),
                pltpu.VMEM((D, CHUNK), BF16),
                pltpu.VMEM((D, ROWS), BF16),
                pltpu.VMEM((D, ROWS), BF16),
            ],
        ),
        compiler_params=params(),
        name="feed_forward",
    )(place, att, x, up, flat, flat, flat, pb, g2, b2, fb1, fb2)


SPLIT = 128
ONE_DIMS, TWO_DIMS = ("x", "y", "z1", "z2"), ("y", "x", "z1", "z2")
LINE_X, LINE_Y = ("z1", "x", "y", "z2"), ("z1", "y", "x", "z2")
PIECES = (
    (0, ONE_DIMS, ONE_DIMS),
    (1, TWO_DIMS, TWO_DIMS),
    (0, ONE_DIMS, LINE_X),
    (1, TWO_DIMS, LINE_X),
    (2, TWO_DIMS, LINE_Y),
)


def piece_rows(rows_one, rows_two, rows_proj):
    one, two = rows_one - SPLIT, rows_two - SPLIT
    return (0, one), (0, two), (one, SPLIT), (two, SPLIT), (0, rows_proj)


def pick_blocks(dims, **fixed):
    return tuple(fixed.get(name, slice(None)) for name in dims)


def without(dims, *names):
    return tuple(name for name in dims if name not in names)


def first_halving(sent, sums, kept, got, more, *sems):
    step = pl.program_id(0)
    own_sem, *sems = sems
    near = Neighbours()
    spans = piece_rows(sent[0].shape[4], sent[2].shape[4], sent[4].shape[4])
    every = range(len(PIECES))

    def own():
        copies = []
        for p in every:
            array, dims, _ = PIECES[p]
            source = sent[2 * array].at[(*pick_blocks(dims), pl.ds(*spans[p]))]
            copies.append(pltpu.make_async_copy(source, kept[p], own_sem.at[p]))
        return copies

    def over_core(part):
        copies = []
        for p in every:
            array, dims, route = PIECES[p]
            where = pick_blocks(dims, **{route[0]: 1 - part})
            source = sent[2 * array + 1].at[(*where, pl.ds(*spans[p]))]
            copies.append(near.copy("c", source, got[p].at[where], sems, 2 * p + part))
        return copies

    def onward():
        copies = []
        for p in every:
            _, dims, route = PIECES[p]
            source = kept[p].at[pick_blocks(dims, **{route[0]: 1})]
            copies.append(near.copy(route[0], source, more[p], sems, 10 + p))
        return copies

    def arrive(part):
        for copy in over_core(part):
            copy.wait_recv()
        for p in every:
            _, dims, route = PIECES[p]
            where = pick_blocks(dims, **{route[0]: 1 - part})
            kept[p][where] = kept[p][where] + got[p][where]

    @pl.when(step == 0)
    def _():
        near.greet(("c", "x", "y", "z1"))
        for copy in over_core(0) + over_core(1) + own():
            copy.start()

    @pl.when(step == 1)
    def _():
        for copy in own():
            copy.wait()
        arrive(0)
        for copy in onward():
            copy.start()

    @pl.when(step == 2)
    def _():
        arrive(1)

    @pl.when(step == pl.num_programs(0) - 1)
    def _():
        for copy in onward():
            copy.wait_recv()
        for p in every:
            _, dims, route = PIECES[p]
            sums[p][...] = kept[p][pick_blocks(dims, **{route[0]: 0})] + more[p][...]
        for copy in over_core(0) + over_core(1) + onward():
            copy.wait_send()


def attend_back_kernel(
    q_ref, k_ref, v_ref, krest_ref, vrest_ref, aug_ref, table_ref, own_ref, fold_ref, pick_ref,
    weights_ref, pv_ref, datt_ref, parts_ref, *refs,
):
    communicate = len(refs) > 7
    if communicate:
        sent, (grads_ref, gtable_ref, gtaps_ref), sums = refs[:6], refs[6:9], refs[9:14]
        keys_ref, vals_ref, up_ref, gsum_ref = refs[14:18]
        first_halving(sent, sums, refs[18:23], refs[23:28], refs[28:33], *refs[33:])
    else:
        grads_ref, gtable_ref, gtaps_ref, keys_ref, vals_ref, up_ref, gsum_ref = refs
    step = pl.program_id(0)
    lane = lane_index((KEY_ROWS, LANES))
    row_lane = lane[:ROWS]

    @pl.when(step == 0)
    def _():
        gsum_ref[...] = jnp.zeros((TABLE, LANES), F32)
        gtaps_ref[...] = jnp.zeros((2, 4, LANES), F32)

    keys_ref[:ROWS] = k_ref[0] + aug_ref[:ROWS]
    keys_ref[ROWS:] = krest_ref[0, 0] + aug_ref[ROWS:]
    one = jnp.where((lane >= HEAD_DIM) & (lane < HEAD_DIM + 3), 1.0, 0.0).astype(BF16)
    vals_ref[:ROWS] = v_ref[0] + one[:ROWS]
    vals_ref[ROWS:] = vrest_ref[0, 0] + one[ROWS:]
    pv = pv_ref[0].astype(F32)
    inverse = pv[:, HEAD_DIM : HEAD_DIM + 1] + pv[:, HEAD_DIM + 1 : HEAD_DIM + 2]
    datt = datt_ref[0].astype(F32)
    upstream = (datt * inverse).astype(BF16).astype(F32)
    mean = jnp.sum(upstream * pv, axis=1, keepdims=True)
    high = mean.astype(BF16).astype(F32)
    low = (mean - high).astype(BF16).astype(F32)
    least = mean - high - low
    extra = jnp.where(
        row_lane == HEAD_DIM,
        -high,
        jnp.where(row_lane == HEAD_DIM + 1, -low, jnp.where(row_lane == HEAD_DIM + 2, -least, 0.0)),
    )
    up_ref[...] = (upstream + extra).astype(BF16)

    dvals, dkeys, dquery = None, None, []
    for block in range(ROWS // ROW_BLOCK):
        rows = slice(block * ROW_BLOCK, (block + 1) * ROW_BLOCK)
        weights = weights_ref[0, rows, :]
        dprobs = dot(up_ref[rows, :], vals_ref[...], ((1,), (1,)))
        slopes = (weights.astype(F32) * dprobs).astype(BF16)
        dquery.append(dot(slopes, keys_ref[...]))
        more_vals = dot(up_ref[rows, :], weights, ((0,), (0,)))
        more_keys = dot(q_ref[0, rows, :], slopes, ((0,), (0,)))
        dvals = more_vals if dvals is None else dvals + more_vals
        dkeys = more_keys if dkeys is None else dkeys + more_keys
    dvals, dkeys = dvals.T, dkeys.T * SCALE
    dquery = jnp.concatenate(dquery, axis=0)
    spread = dot(dquery.astype(BF16), fold_ref[...], ((1,), (1,))).astype(BF16) * own_ref[...]
    gsum_ref[...] += dot(spread, q_ref[0], ((0,), (0,)))
    dquery = dquery * SCALE + datt + dot(spread, table_ref[...])
    grads_ref[0, 0] = dquery.astype(BF16)
    grads_ref[1, 0] = dkeys[:ROWS].astype(BF16)
    grads_ref[2, 0] = dvals[:ROWS].astype(BF16)
    for s, whole_grad in ((0, dkeys), (1, dvals)):
        piece = whole_grad[SQUEEZE_AT : SQUEEZE_AT + MEM]
        for tap in range(4):
            product = piece * parts_ref[s, 0, tap].astype(F32)[:MEM]
            gtaps_ref[s, tap : tap + 1, :] += jnp.sum(product, axis=0, keepdims=True)

    @pl.when(step == pl.num_programs(0) - 1)
    def _():
        gtable_ref[...] = dot(pick_ref[...].astype(F32), gsum_ref[...], ((0,), (0,)), lax.Precision.HIGHEST)


def attend_back(sent, heads, rest, aug, table, own, fold, pick, weights, pv, datt, parts):
    head = (1, ROWS, LANES)
    tail = (1, 1, REST, LANES)
    own_head = pl.BlockSpec(head, lambda h: (h, 0, 0))
    out_shape = [
        jax.ShapeDtypeStruct((3, HEADS, ROWS, LANES), BF16),
        jax.ShapeDtypeStruct((LANES, LANES), F32),
        jax.ShapeDtypeStruct((2, 4, LANES), F32),
    ]
    out_specs = [pl.BlockSpec((3, 1, ROWS, LANES), lambda h: (0, h, 0, 0)), whole((LANES, LANES)), whole((2, 4, LANES))]
    scratch = [
        pltpu.VMEM((KEY_ROWS, LANES), BF16),
        pltpu.VMEM((KEY_ROWS, LANES), BF16),
        pltpu.VMEM((ROWS, LANES), BF16),
        pltpu.VMEM((TABLE, LANES), F32),
    ]
    more = {}
    if sent:
        spans = piece_rows(sent[0].shape[4], sent[2].shape[4], sent[4].shape[4])
        for _, rows in spans:
            out_shape.append(jax.ShapeDtypeStruct((2, 2, 2, rows, LANES), BF16))
            out_specs.append(whole((2, 2, 2, rows, LANES)))
        scratch += [pltpu.VMEM((2,) * bits + (rows, LANES), BF16) for bits in (4, 4, 3) for _, rows in spans]
        scratch += [pltpu.SemaphoreType.DMA((5,)), pltpu.SemaphoreType.DMA((15,)), pltpu.SemaphoreType.DMA((15,))]
        more = {"collective_id": 2, "has_side_effects": True}
    return pl.pallas_call(
        attend_back_kernel,
        grid=(HEADS,),
        out_shape=tuple(out_shape),
        in_specs=[
            own_head,
            pl.BlockSpec(head, lambda h: (HEADS + h, 0, 0)),
            pl.BlockSpec(head, lambda h: (2 * HEADS + h, 0, 0)),
            pl.BlockSpec(tail, lambda h: (0, h, 0, 0)),
            pl.BlockSpec(tail, lambda h: (1, h, 0, 0)),
            whole((KEY_ROWS, LANES)),
            whole((TABLE, LANES)),
            whole((ROWS, TABLE)),
            whole((TABLE, LANES)),
            whole((TABLE, LANES)),
            pl.BlockSpec((1, ROWS, KEY_ROWS), lambda h: (h, 0, 0)),
            own_head,
            own_head,
            pl.BlockSpec((2, 1, 4, 208, LANES), lambda h: (0, h, 0, 0, 0)),
        ]
        + [pl.BlockSpec(memory_space=pl.ANY)] * len(sent),
        out_specs=tuple(out_specs),
        scratch_shapes=scratch,
        compiler_params=params(**more),
        name="attend_back",
    )(heads, heads, heads, rest, rest, aug, table, own, fold, pick, weights, pv, datt, parts, *sent)


def last_halving(ins, outs, got, kept, sems):
    step = pl.program_id(0)
    near = Neighbours()
    pieces = len(PIECES)
    first, second, third = got[:pieces], got[pieces : 2 * pieces], got[2 * pieces :]
    fours, twos = kept[:pieces], kept[pieces:]
    plane, line = (0, 1), (2, 3, 4)

    def copy(p, stage, part):
        _, dims, route = PIECES[p]
        dims = without(dims, *route[:stage])
        at = 5 * p + 2 * (stage - 1) + part
        fixed = {route[stage]: 1}
        if stage < 3:
            fixed[route[stage + 1]] = 1 - part
        source = (ins, fours, twos)[stage - 1][p].at[pick_blocks(dims, **fixed)]
        target = (first, second, third)[stage - 1][p]
        if stage < 3:
            target = target.at[pick_blocks(without(dims, route[stage]), **fixed)]
        return near.copy(route[stage], source, target, sems, at)

    def start(group, stage):
        for p in group:
            for part in range(2 if stage < 3 else 1):
                copy(p, stage, part).start()

    def arrive(group, stage, part):
        for p in group:
            copy(p, stage, part).wait_recv()
            _, dims, route = PIECES[p]
            dims = without(dims, *route[:stage])
            fixed = {route[stage + 1]: 1 - part}
            here = pick_blocks(dims, **{route[stage]: 0}, **fixed)
            there = pick_blocks(without(dims, route[stage]), **fixed)
            source = (ins, fours)[stage - 1][p]
            (fours, twos)[stage - 1][p][there] = source[here] + (first, second)[stage - 1][p][there]

    @pl.when(step == 0)
    def _():
        near.greet(("c", "x", "y", "z1", "z2"))
        start(plane + line, 1)

    @pl.when(step == 1)
    def _():
        arrive(plane, 1, 0)
        start(plane, 2)

    @pl.when(step == 2)
    def _():
        arrive(plane, 1, 1)
        arrive(line, 1, 0)
        start(line, 2)

    @pl.when(step == 3)
    def _():
        arrive(plane, 2, 0)
        start(plane, 3)

    @pl.when(step == 4)
    def _():
        arrive(plane, 2, 1)
        arrive(line, 1, 1)
        arrive(line, 2, 0)
        start(line, 3)

    def end():
        arrive(line, 2, 1)
        for p in range(pieces):
            copy(p, 3, 0).wait_recv()
            outs[p][...] = twos[p][0].astype(F32) + third[p][...].astype(F32)
        for p in range(pieces):
            for stage in (1, 2, 3):
                for part in range(2 if stage < 3 else 1):
                    copy(p, stage, part).wait_send()

    return near, end


EARLY_ROWS = 112
EARLY_COMPRESS, EARLY_WIDE = 56, 64
DOUBLINGS = ("c", "x", "y", "z1", "z2")


def early_sums(near, table_ref, comp_ref, two_ref, gb1_ref, out_ref, vector_ref, more_ref, sems):
    step = pl.program_id(0)

    def move(stage):
        return near.copy(DOUBLINGS[stage], vector_ref.at[stage], more_ref.at[stage], sems, stage)

    @pl.when(step == 0)
    def _():
        vector_ref[0, :EARLY_COMPRESS] = table_ref[:EARLY_COMPRESS]
        for s in range(2):
            vector_ref[0, EARLY_COMPRESS + 4 * s : EARLY_COMPRESS + 4 * s + 4] = comp_ref[s]
        lines = [two_ref[at : at + 1, :] for at in range(4)] + [gb1_ref[:, at : at + D] for at in range(0, FF, D)]
        for tile in range(D // LANES):
            for at, line in enumerate(lines):
                row = EARLY_WIDE + 8 * tile + at
                vector_ref[0, row : row + 1] = line[:, tile * LANES : (tile + 1) * LANES]
        move(0).start()

    for stage in range(1, 5):

        @pl.when(step == stage)
        def _():
            move(stage - 1).wait_recv()
            vector_ref[stage] = vector_ref[stage - 1] + more_ref[stage - 1]
            move(stage).start()

    def end():
        move(4).wait_recv()
        out_ref[...] = vector_ref[4] + more_ref[4]
        for stage in range(5):
            move(stage).wait_send()

    return end


def pool_back_kernel(
    frames_ref, grads_ref, vhat_ref, rs_ref, mixed_ref, taps_raw_ref, gain_ref, same_ref, *refs,
):
    communicate = len(refs) > 6
    if communicate:
        dmix_ref, small_ref, grid_ref, dgrid_ref, sums_ref, taps_ref = (*refs[9:11], *refs[17:21])
        near, end_halving = last_halving(refs[:5], refs[11:16], refs[21:36], refs[36:46], refs[46:48])
        end_early = early_sums(near, *refs[5:9], refs[16], *refs[48:50], refs[50:52])
    else:
        dmix_ref, small_ref, grid_ref, dgrid_ref, sums_ref, taps_ref = refs
    step = pl.program_id(0)

    @pl.when(step == 0)
    def _():
        clear_border(grid_ref)
        clear_border(dgrid_ref)

    @pl.when(step % 2 == 0)
    def _():
        spread_taps(taps_raw_ref, taps_ref)

    dy = jnp.concatenate([grads_ref[0, head][:, :HEAD_DIM] for head in range(GROUP_HEADS)], axis=1).astype(F32)
    vhat = vhat_ref[...].astype(F32)
    gain = tiled_lanes(gain_ref[pl.ds(step // 2, 1), :])
    product = dy * vhat
    small_ref[0, 28:29, :] = jnp.sum(product, axis=0, keepdims=True)
    small_ref[0, 29:30, :] = jnp.sum(dy, axis=0, keepdims=True)
    small_ref[0, 30:32, :] = jnp.zeros((2, GROUP), F32)
    scaled = dy * gain
    first = dot(scaled.astype(BF16), same_ref[...]) * (1.0 / HEAD_DIM)
    second = dot((product * gain).astype(BF16), same_ref[...]) * (1.0 / HEAD_DIM)
    dpool = rs_ref[...] * (scaled - first - vhat * second)
    dgrid_ref[1 : HEIGHT + 1, 1 : WIDTH + 1] = dpool.reshape(HEIGHT, WIDTH, FRAMES, GROUP)
    grid_ref[1 : HEIGHT + 1, 1 : WIDTH + 1] = mixed_ref[...].astype(F32).reshape(HEIGHT, WIDTH, FRAMES, GROUP)
    sums_ref[...] = jnp.zeros(sums_ref.shape, F32)

    @pl.loop(0, HEIGHT)
    def _(i):
        for tile in range(GROUP // LANES):
            lanes = slice(tile * LANES, tile * LANES + LANES)
            line = convolve(dgrid_ref, taps_ref, True, i, lanes)
            frame = lax.broadcasted_iota(jnp.int32, line.shape, 1)
            line = jnp.where(frame < frames_ref[0], line, 0.0)
            at = pl.multiple_of(i * WIDTH * FRAMES, WIDTH * FRAMES)
            dmix_ref[pl.ds(at, WIDTH * FRAMES), lanes] = line.reshape(WIDTH * FRAMES, LANES).astype(BF16)
            own = dgrid_ref[i + 1, 1 : WIDTH + 1, :, lanes]
            moved = (shift_frames(own, -1), own, shift_frames(own, 1))
            for b in range(3):
                for e in range(3):
                    window = grid_ref[i + b, e : e + WIDTH, :, lanes]
                    for a in range(3):
                        tap = 9 * a + 3 * b + e
                        sums_ref[tap, :, lanes] += jnp.sum(window * moved[a], axis=0)

    for tap in range(27):
        small_ref[0, tap : tap + 1, :] = jnp.sum(sums_ref[tap], axis=0, keepdims=True)
    small_ref[0, 27:28, :] = jnp.sum(dmix_ref[...].astype(F32), axis=0, keepdims=True)
    if communicate:

        @pl.when(step == 5)
        def _():
            end_halving()
            end_early()


def pool_back(sums, smalls, frames, grads, vhat, rs, mixed, taps, gain, same):
    smem = pl.BlockSpec(memory_space=pltpu.SMEM)
    group = pl.BlockSpec((ROWS, GROUP), lambda g: (0, g))
    out_shape = [jax.ShapeDtypeStruct((ROWS, QKV), BF16), jax.ShapeDtypeStruct((6, 32, GROUP), F32)]
    out_specs = [group, pl.BlockSpec((1, 32, GROUP), lambda g: (g, 0, 0))]
    scratch = [
        pltpu.VMEM((HEIGHT + 2, WIDTH + 2, FRAMES, GROUP), F32),
        pltpu.VMEM((HEIGHT + 2, WIDTH + 2, FRAMES, GROUP), F32),
        pltpu.VMEM((27, FRAMES, GROUP), F32),
        pltpu.VMEM((27, FRAMES, GROUP), F32),
    ]
    more = {}
    if sums:
        rows = [total.shape[3] for total in sums]
        for count in (*rows, EARLY_ROWS):
            out_shape.append(jax.ShapeDtypeStruct((count, LANES), F32))
            out_specs.append(whole((count, LANES)))
        for shape in ((2, 2), (2,), (), (2, 2), (2,)):
            scratch += [pltpu.VMEM((*shape, count, LANES), BF16) for count in rows]
        scratch += [pltpu.SemaphoreType.DMA((25,))] * 2
        scratch += [pltpu.VMEM((5, EARLY_ROWS, LANES), F32)] * 2
        scratch += [pltpu.SemaphoreType.DMA((5,))] * 2
        more = {"collective_id": 3, "has_side_effects": True}
    return pl.pallas_call(
        pool_back_kernel,
        grid=(6,),
        out_shape=tuple(out_shape),
        in_specs=[
            smem,
            pl.BlockSpec((1, GROUP_HEADS, ROWS, LANES), lambda g: (g // 2, g % 2, 0, 0)),
            group,
            group,
            group,
            pl.BlockSpec((1, 27, HEAD_DIM), lambda g: (g // 2, 0, 0)),
            whole((3, HEAD_DIM)),
            whole((GROUP, GROUP)),
        ]
        + [whole(value.shape) for value in (*sums, *smalls)],
        out_specs=tuple(out_specs),
        scratch_shapes=scratch,
        compiler_params=params(**more),
        name="pool_back",
    )(frames, grads, vhat, rs, mixed, taps, gain, same, *sums, *smalls)


def project_grad_kernel(place_ref, normed_ref, dmixed_ref, one_ref, two_ref, full_ref):
    for kind in range(3):
        grad = dot(normed_ref[...], dmixed_ref[:, kind * D : (kind + 1) * D], ((0,), (0,)))
        full_ref[:, kind * D : (kind + 1) * D] = grad.astype(BF16)
    half, columns = one_ref.shape[5:]
    for f in range(QKV // columns):

        @pl.loop(0, DP_BLOCKS)
        def _(d):
            bits = relative_bits(place_ref, d, f)
            lanes = slice(f * columns, (f + 1) * columns)
            at = pl.multiple_of(2 * d * half, half)
            one_ref[bits["c"], bits["x"], bits["y"], bits["z1"], bits["z2"]] = full_ref[pl.ds(at, half), lanes]
            at = pl.multiple_of((2 * d + 1) * half, half)
            two_ref[bits["c"], bits["y"], bits["x"], bits["z1"], bits["z2"]] = full_ref[pl.ds(at, half), lanes]


def project_grad(place, normed, dmixed, sides):
    vmem = pl.BlockSpec(memory_space=pltpu.VMEM)
    half = jax.ShapeDtypeStruct((2, 2, 2, 2, 2, D // DP_BLOCKS // 2, QKV // sides), BF16)
    return pl.pallas_call(
        project_grad_kernel,
        out_shape=(half, half),
        in_specs=[pl.BlockSpec(memory_space=pltpu.SMEM)] + [vmem] * 2,
        out_specs=(vmem, vmem),
        scratch_shapes=[pltpu.VMEM((D, QKV), BF16)],
        compiler_params=params(),
        name="project_grad",
    )(place, normed, dmixed)


def project_back_kernel(dmixed_ref, weight_ref, x_ref, dmid_ref, g1_ref, gtok_ref, small_ref, dx_ref, wide_ref):
    dy = dot(dmixed_ref[...], weight_ref[...], ((1,), (1,)))
    centred, rs = layer_stats(x_ref[...].astype(F32), D)
    vhat = centred * rs
    small_ref[0:1, :] = jnp.sum(dy * vhat, axis=0, keepdims=True)
    small_ref[1:2, :] = jnp.sum(dy, axis=0, keepdims=True)
    small_ref[2:8, :] = jnp.zeros((6, D), F32)
    scaled = dy * g1_ref[...]
    first = jnp.sum(scaled, axis=1, keepdims=True) * (1.0 / D)
    second = jnp.sum(scaled * vhat, axis=1, keepdims=True) * (1.0 / D)
    dx_ref[...] = dmid_ref[...] + rs * (scaled - first - vhat * second)

    @pl.loop(0, PLACES)
    def _(place):
        at = pl.multiple_of(place * FRAMES, FRAMES)
        write_place(wide_ref, place, dx_ref[pl.ds(at, FRAMES), :])

    for tile in range(D // LANES):
        gtok_ref[:, tile * LANES : (tile + 1) * LANES] = wide_ref[tile]


def project_back(dmixed, weight, x, dmid, g1):
    vmem = pl.BlockSpec(memory_space=pltpu.VMEM)
    return pl.pallas_call(
        project_back_kernel,
        out_shape=(jax.ShapeDtypeStruct((ROWS, D), F32), jax.ShapeDtypeStruct((8, D), F32)),
        in_specs=[vmem] * 5,
        out_specs=(vmem, vmem),
        scratch_shapes=[pltpu.VMEM((ROWS, D), F32), wide_scratch(D)],
        compiler_params=params(),
        name="project_back",
    )(dmixed, weight, x, dmid, g1)


VECTOR_ROWS = 144
WIDE_AT = 96


class Scatter:
    def __init__(self, blocks_ref, out_ref, vector_ref, from_core, from_first, from_second, from_z, sems):
        dp, fsdp = lax.axis_index("dp"), lax.axis_index("fsdp")
        self.z, self.x = dp // 2, dp % 2
        self.y, self.c = fsdp // 2, fsdp % 2
        self.blocks_ref, self.out_ref, self.vector_ref = blocks_ref, out_ref, vector_ref
        self.from_core, self.from_first, self.from_second, self.from_z = from_core, from_first, from_second, from_z
        self.send_sem, self.recv_sem, self.vector_send, self.vector_recv, self.vector_more = sems
        self.rows = blocks_ref.shape[4] // (2 * PARTS)
        self.copies = {}

    def device(self, z, x, y, c):
        return (2 * z + x, 2 * y + c)

    def begin(self):
        z, x, y, c = self.z, self.x, self.y, self.c
        self.along = [self.device((z + k) % 4, x, y, c) for k in (1, 2, 3)]
        self.over_x, self.over_y = self.device(z, 1 - x, y, c), self.device(z, x, 1 - y, c)
        self.over_c = self.device(z, x, y, 1 - c)
        barrier = pltpu.get_barrier_semaphore()
        for partner in self.along + [self.over_x, self.over_y, self.over_c]:
            pl.semaphore_signal(barrier, inc=1, device_id=partner, device_id_type=MESH)
        pl.semaphore_wait(barrier, 6)

    def copy(self, source, target, send_sem, recv_sem, partner):
        copy = pltpu.make_async_remote_copy(
            src_ref=source, dst_ref=target, send_sem=send_sem, recv_sem=recv_sem, device_id=partner, device_id_type=MESH
        )
        copy.start()
        return copy

    def span(self, part, route):
        return pl.ds((2 * part + route) * self.rows, self.rows)

    def send(self, part, level):
        z, x, y, c = self.z, self.x, self.y, self.c
        every = slice(None)
        blocks = self.blocks_ref
        for route in range(2):
            span = self.span(part, route)
            if level == 0:
                moves = [(blocks.at[every, every, every, 1 - c, span], self.from_core.at[every, every, every, span], self.over_c)]
            elif level == 1:
                where = (every, 1 - x, every, c, span) if route == 0 else (every, every, 1 - y, c, span)
                moves = [(blocks.at[where], self.from_first.at[every, every, span], self.over_y if route else self.over_x)]
            elif level == 2:
                where = (every, x, 1 - y, c, span) if route == 0 else (every, 1 - x, y, c, span)
                moves = [(blocks.at[where], self.from_second.at[every, span], self.over_x if route else self.over_y)]
            else:
                moves = [
                    (blocks.at[(z + k) % 4, x, y, c, span], self.from_z.at[k - 1, span], self.along[k - 1])
                    for k in (1, 2, 3)
                ]
            for at, (source, target, partner) in enumerate(moves):
                slot = (2 * part + route) * 6 + level + at
                self.copies[part, route, level, at] = self.copy(
                    source, target, self.send_sem.at[slot], self.recv_sem.at[slot], partner
                )

    def advance(self, part, level):
        z, x, y, c = self.z, self.x, self.y, self.c
        every = slice(None)
        blocks = self.blocks_ref
        for route in range(2):
            span = self.span(part, route)
            for at in range(3 if level == 3 else 1):
                self.copies[part, route, level, at].wait_recv()
            if level == 0:
                where, more = (every, every, every, c, span), self.from_core[:, :, :, span]
            elif level == 1:
                where = (every, x, every, c, span) if route == 0 else (every, every, y, c, span)
                more = self.from_first[:, :, span]
            elif level == 2:
                where, more = (every, x, y, c, span), self.from_second[:, span]
            if level < 3:
                blocks[where] = blocks[where] + more
            else:
                total = blocks[z, x, y, c, span].astype(F32)
                for k in range(3):
                    total = total + self.from_z[k, span].astype(F32)
                self.out_ref[span] = total
        if level < 3:
            self.send(part, level + 1)

    def steps(self):
        order = []
        for turn in range(PARTS + 3):
            for level in reversed(range(4)):
                if 0 <= turn - level < PARTS:
                    order.append((turn - level, level))
        return [functools.partial(self.advance, *step) for step in order]

    def send_vector(self, stage):
        z, x, y, c = self.z, self.x, self.y, self.c
        partner = (
            self.over_c, self.over_x, self.over_y, self.device(z + 1 - 2 * (z % 2), x, y, c), self.along[1]
        )[stage]
        self.copies["vector", stage] = self.copy(
            self.vector_ref.at[stage], self.vector_more.at[stage], self.vector_send.at[stage],
            self.vector_recv.at[stage], partner,
        )

    def advance_vector(self, stage):
        self.copies["vector", stage].wait_recv()
        self.vector_ref[stage + 1] = self.vector_ref[stage] + self.vector_more[stage]
        if stage < 4:
            self.send_vector(stage + 1)

    def end(self):
        for copy in self.copies.values():
            copy.wait_send()


def tail_kernel(
    turned_ref, dmixed_ref, weight_ref, x_ref, dmid_ref, g1_ref, pools_ref,
    gqkv_ref, dx_ref, done_ref,
    blocks_ref, vector_ref, from_core, from_first, from_second, from_z, *sems,
):
    scatter = Scatter(blocks_ref, gqkv_ref, vector_ref, from_core, from_first, from_second, from_z, sems)
    scatter.begin()
    steps = scatter.steps()

    def advance(count):
        for _ in range(min(count, len(steps))):
            steps.pop(0)()

    depth, columns = blocks_ref.shape[4:]
    rows = depth // PARTS
    for part in range(PARTS):
        turned = [turned_ref[d * depth + part * rows : d * depth + (part + 1) * rows] for d in range(DP_BLOCKS)]
        grad = dot(jnp.concatenate(turned, axis=0), dmixed_ref[...]).astype(BF16)
        for f in range(QKV // columns):
            for d in range(DP_BLOCKS):
                block = grad[d * rows : (d + 1) * rows, f * columns : (f + 1) * columns]
                blocks_ref[d // 2, d % 2, f // 2, f % 2, part * rows : (part + 1) * rows] = block
        scatter.send(part, 0)
        advance(part)
    dy = dot(dmixed_ref[...], weight_ref[...], ((1,), (1,)))
    advance(3)
    centred, rs = layer_stats(x_ref[...].astype(F32), D)
    vhat = centred * rs
    vector_ref[0] = jnp.zeros((VECTOR_ROWS, LANES), F32)
    for kind in range(3):
        sums = pools_ref[2 * kind] + pools_ref[2 * kind + 1]
        total = sums[:, :HEAD_DIM]
        for head in range(1, GROUP_HEADS):
            total = total + sums[:, HEAD_DIM * head : HEAD_DIM * (head + 1)]
        vector_ref[0, 32 * kind : 32 * kind + 32, :HEAD_DIM] = total
    lines = [jnp.sum(dy * vhat, axis=0, keepdims=True), jnp.sum(dy, axis=0, keepdims=True)]
    lines += [
        jnp.concatenate([pools_ref[2 * kind, 27:28, :], pools_ref[2 * kind + 1, 27:28, :]], axis=1)
        for kind in range(3)
    ]
    for tile in range(D // LANES):
        for at, line in enumerate(lines):
            vector_ref[0, WIDE_AT + 8 * tile + at : WIDE_AT + 8 * tile + at + 1] = line[:, tile * LANES : (tile + 1) * LANES]
    scatter.send_vector(0)
    advance(2)
    scatter.advance_vector(0)
    scaled = dy * g1_ref[...].reshape(1, D)
    first = jnp.sum(scaled, axis=1, keepdims=True) * (1.0 / D)
    second = jnp.sum(scaled * vhat, axis=1, keepdims=True) * (1.0 / D)
    dx_ref[...] = dmid_ref[...] + rs * (scaled - first - vhat * second)
    advance(2)
    scatter.advance_vector(1)

    advance(2)
    scatter.advance_vector(2)
    advance(2)
    scatter.advance_vector(3)
    advance(len(steps))
    scatter.advance_vector(4)
    done_ref[...] = vector_ref[5]
    scatter.end()


def tail(turned, dmixed, weight, x, dmid, g1, pools, shard):
    vmem = pl.BlockSpec(memory_space=pltpu.VMEM)
    depth, columns = shard
    shapes = [shard, (ROWS, D), (VECTOR_ROWS, LANES)]
    count = 2 * PARTS * 6
    return pl.pallas_call(
        tail_kernel,
        out_shape=tuple(jax.ShapeDtypeStruct(shape, F32) for shape in shapes),
        in_specs=[vmem] * 7,
        out_specs=(vmem,) * len(shapes),
        scratch_shapes=[
            pltpu.VMEM((4, 2, 2, 2, depth, columns), BF16),
            pltpu.VMEM((6, VECTOR_ROWS, LANES), F32),
            pltpu.VMEM((4, 2, 2, depth, columns), BF16),
            pltpu.VMEM((4, 2, depth, columns), BF16),
            pltpu.VMEM((4, depth, columns), BF16),
            pltpu.VMEM((3, depth, columns), BF16),
            pltpu.SemaphoreType.DMA((count,)),
            pltpu.SemaphoreType.DMA((count,)),
            pltpu.SemaphoreType.DMA((5,)),
            pltpu.SemaphoreType.DMA((5,)),
            pltpu.VMEM((5, VECTOR_ROWS, LANES), F32),
        ],
        compiler_params=params(collective_id=1, has_side_effects=True),
        name="tail",
    )(turned, dmixed, weight, x, dmid, g1, pools)


def finish_kernel(
    gqkv_ref, dx_ref, done_ref, one_ref, two_ref, one_rest_ref, two_rest_ref, proj_ref, early_ref,
    gtok_ref, ln1g_ref, ln1b_ref, wqkv_ref, qkvb_ref, conv_ref, pgain_ref, pbias_ref, time_ref, space_ref, comp_ref,
    wp_ref, projb_ref, ln2g_ref, ln2b_ref, w1_ref, fc1b_ref, w2_ref, fc2b_ref, wide_ref,
):
    @pl.loop(0, PLACES)
    def _(place):
        at = pl.multiple_of(place * FRAMES, FRAMES)
        write_place(wide_ref, place, dx_ref[pl.ds(at, FRAMES), :])

    for tile in range(D // LANES):
        gtok_ref[:, tile * LANES : (tile + 1) * LANES] = wide_ref[tile]
    wqkv_ref[...] = gqkv_ref[...]
    one = jnp.concatenate([one_ref[...], one_rest_ref[...]], axis=0)
    two = jnp.concatenate([two_ref[...], two_rest_ref[...]], axis=0)
    depth, part = w1_ref.shape[0], wp_ref.shape[1]
    for tile in range(w1_ref.shape[1] // LANES):
        w1_ref[:, tile * LANES : (tile + 1) * LANES] = one[tile * depth : (tile + 1) * depth]
    tiles = w2_ref.shape[1] // LANES
    for tile in range(tiles):
        w2_ref[:, tile * LANES : (tile + 1) * LANES] = two[tile * part : (tile + 1) * part]
    wp_ref[:, :LANES] = proj_ref[:depth]
    wp_ref[:, LANES:] = proj_ref[depth:, : part - LANES]
    for kind in range(3):
        conv_ref[kind] = done_ref[32 * kind : 32 * kind + 27, :HEAD_DIM]
        pgain_ref[kind : kind + 1, :] = done_ref[32 * kind + 28 : 32 * kind + 29, :HEAD_DIM]
        pbias_ref[kind : kind + 1, :] = done_ref[32 * kind + 29 : 32 * kind + 30, :HEAD_DIM]
    spans = 2 * HEIGHT - 1
    time_ref[...] = early_ref[:15, :HEAD_DIM]
    for s in range(2):
        start = 15 + spans * s
        space_ref[:, s] = early_ref[start : start + spans, :HEAD_DIM]
        comp_ref[s] = early_ref[EARLY_COMPRESS + 4 * s : EARLY_COMPRESS + 4 * s + 4, :HEAD_DIM]

    def line_of(source_ref, base, at):
        rows = [base + 8 * tile + at for tile in range(D // LANES)]
        return jnp.concatenate([source_ref[row : row + 1, :] for row in rows], axis=1).reshape(D)

    for at, target_ref in enumerate((projb_ref, ln2g_ref, ln2b_ref, fc2b_ref)):
        target_ref[...] = line_of(early_ref, EARLY_WIDE, at)
    for side in range(FF // D):
        fc1b_ref[side * D : (side + 1) * D] = line_of(early_ref, EARLY_WIDE, 4 + side)
    for at, target_ref in enumerate((ln1g_ref, ln1b_ref)):
        target_ref[...] = line_of(done_ref, WIDE_AT, at)
    for kind in range(3):
        qkvb_ref[kind * D : (kind + 1) * D] = line_of(done_ref, WIDE_AT, 2 + kind)


def finish(operands, w_qkv, w_proj, w_fc1, w_fc2):
    vmem = pl.BlockSpec(memory_space=pltpu.VMEM)
    shapes = [
        (ROWS, D), (D,), (D,), w_qkv, (QKV,), (3, 27, HEAD_DIM), (3, HEAD_DIM), (3, HEAD_DIM), (15, HEAD_DIM),
        (2 * HEIGHT - 1, 2, HEAD_DIM), (2, 4, HEAD_DIM), w_proj, (D,), (D,), (D,), w_fc1, (FF,), w_fc2[::-1], (D,),
    ]
    done = pl.pallas_call(
        finish_kernel,
        out_shape=tuple(jax.ShapeDtypeStruct(shape, F32) for shape in shapes),
        in_specs=[vmem] * 9,
        out_specs=(vmem,) * len(shapes),
        scratch_shapes=[wide_scratch(D)],
        compiler_params=params(),
        name="finish",
    )(*operands)
    done = list(done)
    done[9], done[17] = done[9].transpose(1, 0, 2), done[17].T
    return done


def row(vector):
    return vector.reshape(1, -1)


def tiled_lanes(array):
    return jnp.concatenate([array] * GROUP_HEADS, axis=-1)


def head_lanes(array):
    return jnp.pad(array, [(0, 0)] * (array.ndim - 1) + [(0, LANES - HEAD_DIM)])


DP_BLOCKS = 8
ROUTE_ONE = ("z2", "z1", "y", "x", "c")
ROUTE_TWO = ("z2", "z1", "x", "y", "c")


def together(*values):
    return lax.optimization_barrier(values)


def flat_shard(one, two, proj):
    pieces = [part for _, part in flat_pieces(one, two, proj)]
    pieces[-1] = jnp.pad(pieces[-1], ((0, 0), (0, LANES - pieces[-1].shape[1])))
    return jnp.concatenate(pieces, axis=0)


class Staged:
    def place(self):
        dp, fsdp = lax.axis_index("dp"), lax.axis_index("fsdp")
        return jnp.stack([dp & 1, (dp >> 1) & 1, (dp >> 2) & 1, (fsdp >> 1) & 1, fsdp & 1]).astype(jnp.int32)

    def other_weights(self, flat):
        return lax.all_gather(flat, ("dp", "fsdp"), axis=0, tiled=False).reshape((8, 4) + flat.shape)


class Plain:
    def __init__(self, dp, fsdp):
        self.dp, self.fsdp = dp, fsdp

    def place(self):
        return jnp.zeros((5,), jnp.int32)

    def gather(self, shard):
        blocks = lax.all_gather(shard, ("dp", "fsdp"), axis=0, tiled=False)
        rows, columns = shard.shape
        joined = blocks.reshape(DP_BLOCKS, self.dp // DP_BLOCKS, self.fsdp, rows, columns).transpose(0, 2, 1, 3, 4)
        return joined.reshape(DP_BLOCKS, self.fsdp, self.dp // DP_BLOCKS * rows, columns)

    def other_weights(self, one, two, proj):
        return jax.vmap(jax.vmap(flat_shard))(self.gather(one), jnp.swapaxes(self.gather(two), 2, 3), self.gather(proj))

    def scatter(self, blocks, route):
        at = {name: 4 - where for where, name in enumerate(route)}
        rows, columns = blocks.shape[5:]
        blocks = blocks.transpose([at[name] for name in ("z2", "z1", "x", "y", "c")] + [5, 6])
        split = blocks.reshape(DP_BLOCKS, self.fsdp, self.dp // DP_BLOCKS, rows * DP_BLOCKS // self.dp, columns)
        split = split.transpose(0, 2, 1, 3, 4).reshape(self.dp * self.fsdp, -1, columns)
        return lax.psum_scatter(split, ("dp", "fsdp"), scatter_dimension=0, tiled=False).astype(F32)

    def scatter_flat(self, low, high, route, unpack):
        blocks = jnp.concatenate([low[None], high[None]])
        blocks = jax.vmap(unpack)(blocks.reshape((32,) + blocks.shape[5:]))
        return self.scatter(blocks.reshape((2,) * 5 + blocks.shape[1:]), route)

    def total(self, vector):
        return lax.psum(vector, ("dp", "fsdp"))


def run(
    comm, staged, tokens, prev_kv, memory, valid_frames, mem_len, ln1_gain, ln1_bias, w_qkv, qkv_bias, pool_conv, pool_gain,
    pool_bias, rel_time, rel_space, compress, w_proj, proj_bias, ln2_gain, ln2_bias, w_fc1, fc1_bias, w_fc2,
    fc2_bias, cotangent,
):
    place = comm.place()
    fsdp = QKV // w_qkv.shape[1]
    one_hot, own, fold, pick, same = (jnp.asarray(c, BF16) for c in constants())
    taps, gains, biases = pool_conv, pool_gain, pool_bias
    if staged:
        flat = pack(w_fc1, w_fc2.T, w_proj)
        w_qkv, flat = together(w_qkv, flat)
        flat = comm.other_weights(flat)
    prepared = prepare(
        valid_frames, mem_len, tokens, cotangent, ln1_gain, ln1_bias, one_hot, rel_time, rel_space.transpose(1, 0, 2), pick,
        prev_kv, memory, compress, w_qkv if staged else None,
    )
    x, normed, turned, upstream, aug, table, rest, parts = prepared[-8:]
    if staged:
        first = prepared[0].reshape(8, 4, *w_qkv.shape)
    else:
        first, flat = comm.gather(w_qkv), comm.other_weights(w_fc1, w_fc2, w_proj)
    heads, vhat, rs, mixed, weight = query_key_value(
        valid_frames, normed, first, qkv_bias, taps, gains, biases, same
    )
    weights, pv, attended = attend(heads, rest, aug, table, own, fold)
    out, dmid, datt, plow, phigh, low1, high1, low2, high2, small_two, gb1 = feed_forward(
        place, attended, x, upstream, flat, proj_bias, ln2_gain, ln2_bias, row(fc1_bias), fc2_bias
    )

    sent = [low1, high1, low2, high2, plow, phigh] if staged else []
    grads, gtable, gcompress, *sums = attend_back(
        sent, heads, rest, aug, table, own, fold, pick, weights, pv, datt, parts
    )
    smalls = [gtable, gcompress, small_two, gb1] if staged else []
    dmixed, pools, *sums = pool_back(sums, smalls, valid_frames, grads, vhat, rs, mixed, taps, gains, same)
    if staged:
        ended = tail(turned, dmixed, weight, x, dmid, ln1_gain, pools, w_qkv.shape)
        return (out, *finish((*ended, *sums), w_qkv.shape, w_proj.shape, w_fc1.shape, w_fc2.shape))
    depth, part = D // DP_BLOCKS, D // fsdp

    def unpack_one(block):
        return jnp.concatenate(list(block.reshape(-1, depth, LANES)), axis=1)

    def unpack_two(block):
        return jnp.concatenate(list(block.reshape(-1, part, LANES)), axis=1).T

    def unpack_proj(block):
        return jnp.concatenate([block[:depth], block[depth:, : part - LANES]], axis=1)

    w1_sum = comm.scatter_flat(low1, high1, ROUTE_ONE, unpack_one)
    w2_sum = comm.scatter_flat(low2, high2, ROUTE_TWO, unpack_two)
    wp_sum = comm.scatter_flat(plow, phigh, ROUTE_TWO, unpack_proj)
    qkv_one, qkv_two = project_grad(place, normed, dmixed, fsdp)
    gtok, small_one = project_back(dmixed, weight, x, dmid, row(ln1_gain))
    gbias = pools[:, 27].reshape(QKV)
    pools = jnp.sum(pools.reshape(3, 2, 32, GROUP_HEADS, HEAD_DIM), axis=(1, 3))
    gconv, gpool = pools[:, :27], pools[:, 28:30]
    smalls = (
        small_one[0], small_one[1], gbias, gconv, gpool[:, 0], gpool[:, 1],
        gtable[:15, :HEAD_DIM], gtable[15:53, :HEAD_DIM].reshape(2, 19, HEAD_DIM), gcompress[:, :, :HEAD_DIM],
        small_two[0], small_two[1], small_two[2], gb1[0], small_two[3],
    )
    vector = comm.total(jnp.concatenate([s.reshape(-1) for s in smalls]))
    totals, at = [], 0
    for s in smalls:
        totals.append(vector[at : at + s.size].reshape(s.shape))
        at += s.size
    qkv = comm.scatter(jnp.concatenate([qkv_one, jnp.moveaxis(qkv_two, 1, 2)], axis=5), ROUTE_ONE)
    sums = [qkv, wp_sum, w1_sum, w2_sum]
    return (
        out, gtok, totals[0], totals[1], sums[0], totals[2], totals[3], totals[4], totals[5], totals[6],
        totals[7], totals[8], sums[1], totals[9], totals[10], totals[11], sums[2], totals[12], sums[3], totals[13],
    )


def solution(mesh):
    both = P(("dp", "fsdp"))
    rows = P(("dp", "fsdp"), None)
    second = P(None, ("dp", "fsdp"), None)
    blocks = P("dp", "fsdp")
    none = P()
    dp, fsdp = mesh.shape["dp"], mesh.shape["fsdp"]
    staged = (dp, fsdp) == (8, 4)
    return jax.shard_map(
        functools.partial(run, Staged() if staged else Plain(dp, fsdp), staged),
        mesh=mesh,
        in_specs=(
            rows, second, second, both, both, none, none, blocks, none, none, none, none, none, none, none, blocks,
            none, none, none, blocks, none, blocks, none, rows,
        ),
        out_specs=(
            rows, rows, none, none, blocks, none, none, none, none, none, none, none, blocks, none, none, none,
            blocks, none, blocks, none,
        ),
        check_vma=False,
    )
```

```python
import functools

import jax
import jax.numpy as jnp
import numpy as np
from jax import lax
from jax.experimental import pallas as pl
from jax.experimental.pallas import tpu as pltpu
from jax.sharding import PartitionSpec as P

D = 768
FF = 3072
HEADS = 8
HEAD_DIM = 96
LANES = 128
FRAMES = 8
HEIGHT = 10
WIDTH = 10
PLACES = HEIGHT * WIDTH
ROWS = 800
MEM = 200
GROUP = 384
GROUP_HEADS = 4
QKV = 3 * D
KEY_ROWS = 1280
MEM_AT = 800
SQUEEZE_AT = 1024
REST = KEY_ROWS - ROWS
TABLE = 384
EPSILON = 1e-06
SCALE = HEAD_DIM**-0.5
ROOT = HEAD_DIM**0.5
LOG2E = 1.4426950408889634
MASKED = -1e9
MASK_LANE = 124
ROW_BLOCK = 400
BF16 = jnp.bfloat16
F32 = jnp.float32
VMEM_LIMIT = 60 * 1024 * 1024


def constants():
    place = np.arange(PLACES).repeat(FRAMES)
    row_t = np.tile(np.arange(FRAMES), PLACES)
    row_i, row_j = place // WIDTH, place % WIDTH
    one_hot = np.zeros((KEY_ROWS, LANES), np.float32)
    rows = np.arange(ROWS)
    one_hot[rows, 96 + row_t] = 1
    one_hot[rows, 104 + row_i] = 1
    one_hot[rows, 114 + row_j] = 1
    own = np.zeros((ROWS, TABLE), np.float32)
    fold = np.zeros((TABLE, LANES), np.float32)
    pick = np.zeros((TABLE, LANES), np.float32)
    for base, length, row_at, lane, offset in (
        (0, FRAMES, row_t, 96, 0),
        (64, HEIGHT, row_i, 104, 15),
        (164, WIDTH, row_j, 114, 34),
    ):
        for a in range(length):
            for b in range(length):
                column = base + a * length + b
                own[:, column] = row_at == a
                fold[column, lane + b] = 1
                pick[column, offset + a - b + length - 1] = 1
    lanes = np.arange(GROUP) // HEAD_DIM
    same = (lanes[:, None] == lanes[None, :]).astype(np.float32)
    return one_hot, own, fold, pick, same


def lane_index(shape):
    return lax.broadcasted_iota(jnp.int32, shape, len(shape) - 1)


def dot(a, b, contract=((1,), (0,)), precision=None):
    return lax.dot_general(a, b, (contract, ((), ())), preferred_element_type=F32, precision=precision)


def layer_stats(values, width):
    average = jnp.sum(values, axis=-1, keepdims=True) * (1.0 / width)
    centred = values - average
    variance = jnp.sum(centred * centred, axis=-1, keepdims=True) * (1.0 / width)
    return centred, lax.rsqrt(variance + EPSILON)


def params(**more):
    return pltpu.CompilerParams(vmem_limit_bytes=VMEM_LIMIT, **more)


def whole(shape):
    return pl.BlockSpec(shape, lambda *_: (0,) * len(shape))


def tiles_of(values):
    return [values[:, at : at + LANES] for at in range(0, values.shape[1], LANES)]


def flat_pieces(one, two, proj):
    at = 0
    for part in tiles_of(one) + tiles_of(two) + tiles_of(proj):
        yield at, part
        at += part.shape[0]


def read_place(wide_ref, place, tiles=D // LANES):
    parts = [wide_ref[tile, pl.ds(place, FRAMES, stride=PLACES), :] for tile in range(tiles)]
    return jnp.concatenate(parts, axis=1)


def write_place(wide_ref, place, values):
    for tile, part in enumerate(tiles_of(values)):
        wide_ref[tile, pl.ds(place, FRAMES, stride=PLACES), :] = part


def wide_scratch(columns):
    return pltpu.VMEM((columns // LANES, ROWS, LANES), F32)


PARTS = 3
WALL_AFTER = 6
MESH = pl.DeviceIdType.MESH


class Neighbours:
    def __init__(self):
        dp, fsdp = lax.axis_index("dp"), lax.axis_index("fsdp")
        z, x, y, c = dp // 2, dp % 2, fsdp // 2, fsdp % 2
        self.over = {
            "c": (dp, 2 * y + 1 - c),
            "x": (2 * z + 1 - x, fsdp),
            "y": (dp, 2 * (1 - y) + c),
            "z1": (2 * (z + 1 - 2 * (z % 2)) + x, fsdp),
            "z2": (2 * ((z + 2) % 4) + x, fsdp),
        }

    def greet(self, names):
        barrier = pltpu.get_barrier_semaphore()
        for name in names:
            pl.semaphore_signal(barrier, inc=1, device_id=self.over[name], device_id_type=MESH)
        pl.semaphore_wait(barrier, len(names))

    def copy(self, name, source, target, sems, at):
        return pltpu.make_async_remote_copy(
            src_ref=source,
            dst_ref=target,
            send_sem=sems[0].at[at],
            recv_sem=sems[1].at[at],
            device_id=self.over[name],
            device_id_type=MESH,
        )


PLACE_DIMS = ("z2", "z1", "x", "y", "c")
WALL_ROUTES = (
    ("z2", "z1", "y", "x", "c"),
    ("z2", "z1", "x", "y", "c"),
    ("z2", "y", "x", "z1", "c"),
    ("z2", "x", "y", "z1", "c"),
)


class Doubling:
    def __init__(self, near, wall_ref, sems):
        dp, fsdp = lax.axis_index("dp"), lax.axis_index("fsdp")
        self.mine = {"z2": dp // 4, "z1": dp // 2 % 2, "x": dp % 2, "y": fsdp // 2, "c": fsdp % 2}
        self.near, self.wall_ref, self.sems = near, wall_ref, sems
        rows = wall_ref.shape[5]
        third = rows // 3
        self.spans = ((0, third), (third, third), (2 * third, third // 2), (2 * third + third // 2, third // 2))
        self.made = {}

    def region(self, piece, free, other=()):
        where = [
            slice(None) if name in free else (1 - self.mine[name] if name in other else self.mine[name])
            for name in PLACE_DIMS
        ]
        return self.wall_ref.at[(*where, pl.ds(*self.spans[piece]))]

    def plan(self, *key):
        self.made[key] = functools.partial(self.make, *key, len(self.made))

    def make(self, piece, stage, part, at):
        route = WALL_ROUTES[piece]
        if stage < 4:
            free = route[: max(stage - 1, 0)]
            place = self.region(piece, free, route[stage - 1 : stage] if part else ())
        else:
            free, other = ((route[:3], ()), (route[:2], (route[3],)), (route[:2], (route[3], route[2])))[part]
            place = self.region(piece, free, other)
        return self.near.copy(route[stage], place, place, self.sems, at)

    def start(self, *keys):
        for key in keys:
            self.made[key]().start()

    def arrive(self, *keys):
        for key in keys:
            self.made[key]().wait_recv()

    def end(self):
        for make in self.made.values():
            make().wait_send()


FLAT, UPRIGHT, EVERY_PIECE = (0, 1), (2, 3), (0, 1, 2, 3)


def keys_of(pieces, stage, *parts):
    return [(piece, stage, part) for piece in pieces for part in parts]


def doubling_in_queries(wall_ref, sems):
    step = pl.program_id(0)
    doubling = Doubling(Neighbours(), wall_ref, sems)
    early = keys_of(FLAT, 1, 1) + keys_of(FLAT, 2, 0) + keys_of(UPRIGHT, 1, 0, 1) + keys_of(UPRIGHT, 2, 0)
    later = keys_of(EVERY_PIECE, 2, 1) + keys_of(EVERY_PIECE, 3, 0)
    for key in early + later:
        doubling.plan(*key)

    @pl.when(step == 0)
    def _():
        doubling.near.greet(("x", "y", "z1"))
        doubling.start(*early)

    @pl.when(step == 2)
    def _():
        doubling.arrive(*keys_of(FLAT, 1, 1), *keys_of(UPRIGHT, 1, 0, 1))
        doubling.start(*later)

    def end():
        @pl.when(step == 5)
        def _():
            doubling.arrive(*keys_of(EVERY_PIECE, 2, 0, 1), *keys_of(EVERY_PIECE, 3, 0))
            doubling.end()

    return end


def doubling_in_attention(wall_ref, sems):
    step = pl.program_id(0)
    doubling = Doubling(Neighbours(), wall_ref, sems)
    early = keys_of(EVERY_PIECE, 3, 1) + keys_of(EVERY_PIECE, 4, 0, 1)
    later = keys_of(EVERY_PIECE, 4, 2)
    for key in early + later:
        doubling.plan(*key)

    @pl.when(step == 0)
    def _():
        doubling.near.greet(("x", "y", "z1", "c"))
        doubling.start(*early)

    @pl.when(step == 5)
    def _():
        doubling.arrive(*keys_of(EVERY_PIECE, 3, 1))
        doubling.start(*later)

    def end():
        @pl.when(step == HEADS - 1)
        def _():
            doubling.arrive(*keys_of(EVERY_PIECE, 4, 0, 1, 2))
            doubling.end()

    return end


class Gather:
    def __init__(self, shard_ref, all_ref, own_sem, send_sem, recv_sem):
        dp, fsdp = lax.axis_index("dp"), lax.axis_index("fsdp")
        self.z, self.x = dp // 2, dp % 2
        self.y, self.c = fsdp // 2, fsdp % 2
        self.shard_ref, self.all_ref = shard_ref, all_ref
        self.own_sem, self.send_sem, self.recv_sem = own_sem, send_sem, recv_sem
        self.rows = shard_ref.shape[0] // (2 * PARTS)
        self.copies = {}

    def device(self, z, x, y, c):
        return (2 * z + x, 2 * y + c)

    def partners(self):
        z, x, y, c = self.z, self.x, self.y, self.c
        along = [self.device((z + k) % 4, x, y, c) for k in (1, 2, 3)]
        return along + [self.device(z, 1 - x, y, c), self.device(z, x, 1 - y, c), self.device(z, x, y, 1 - c)]

    def begin(self):
        barrier = pltpu.get_barrier_semaphore()
        for partner in self.partners():
            pl.semaphore_signal(barrier, inc=1, device_id=partner, device_id_type=MESH)
        self.own = pltpu.make_async_copy(self.shard_ref, self.all_ref.at[self.z, self.x, self.y, self.c], self.own_sem)
        self.own.start()
        pl.semaphore_wait(barrier, 6)
        self.send_along(0)

    def send_along(self, part):
        if part < PARTS:
            for route in range(2):
                for stage in range(3):
                    self.send(part, route, stage)

    def send(self, part, route, stage):
        z, x, y, c = self.z, self.x, self.y, self.c
        rows = pl.ds((2 * part + route) * self.rows, self.rows)
        partner = self.partners()[stage if stage < 3 or stage == 5 else 3 + (stage - 3 + route) % 2]
        every = slice(None)
        if stage < 3:
            place = (z, x, y, c)
        elif stage == 3:
            place = (every, x, y, c)
        elif stage == 4:
            place = (every, every, y, c) if route == 0 else (every, x, every, c)
        else:
            place = (every, every, every, c)
        target = self.all_ref.at[(*place, rows)]
        source = self.shard_ref.at[rows] if stage < 3 else target
        at = (2 * part + route) * 6 + stage
        copy = pltpu.make_async_remote_copy(
            src_ref=source,
            dst_ref=target,
            send_sem=self.send_sem.at[at],
            recv_sem=self.recv_sem.at[at],
            device_id=partner,
            device_id_type=MESH,
        )
        copy.start()
        self.copies[part, route, stage] = copy

    def advance(self, part, level):
        if level == 0 and part == 0:
            self.own.wait()
        for route in range(2):
            for stage in ((0, 1, 2), (3,), (4,), (5,))[level]:
                self.copies[part, route, stage].wait_recv()
        if level == 0:
            self.send_along(part + 1)
        if level < 3:
            for route in range(2):
                self.send(part, route, 3 + level)

    def steps(self):
        order = []
        for turn in range(PARTS + 3):
            for level in reversed(range(4)):
                if 0 <= turn - level < PARTS:
                    order.append((turn - level, level))
        return [functools.partial(self.advance, *step) for step in order]

    def end(self):
        for copy in self.copies.values():
            copy.wait_send()


def prepare_kernel(
    communicate, frames_ref, length_ref, tokens_ref, cot_ref, gain_ref, bias_ref, one_hot_ref, time_ref, space_ref,
    pick_ref, prev_ref, mem_ref, taps_ref, *refs,
):
    if communicate:
        shard_ref, one_ref, two_ref, proj_ref, all_ref, wall_ref = refs[:6]
        refs = refs[6:]
    x_ref, normed_ref, turned_ref, upstream_ref, aug_ref, table_ref, rest_ref, tap_ref = refs[:8]
    wide_ref, sums_ref, parts_ref, tables_ref = refs[8:12]
    steps = []
    if communicate:
        flat_ref, wall_own_sem, wall_send_sem, wall_recv_sem = refs[12:16]
        gather = Gather(shard_ref, all_ref, *refs[16:])
        gather.begin()
        for at, part in flat_pieces(one_ref[...], two_ref[...], proj_ref[...]):
            short = jnp.zeros((part.shape[0], LANES - part.shape[1]), BF16)
            flat_ref[at : at + part.shape[0]] = jnp.concatenate([part, short], axis=1) if short.size else part
        doubling = Doubling(Neighbours(), wall_ref, (wall_send_sem, wall_recv_sem))
        first_stage = keys_of(EVERY_PIECE, 0, 0) + keys_of(FLAT, 1, 0)
        for key in first_stage:
            doubling.plan(*key)
        here = tuple(doubling.mine[name] for name in PLACE_DIMS)
        own = pltpu.make_async_copy(flat_ref, wall_ref.at[here], wall_own_sem)
        own.start()

        def first_doubling():
            own.wait()
            doubling.start(*first_stage)

        steps = gather.steps()
        steps.insert(WALL_AFTER, first_doubling)

    def advance(count=1):
        for _ in range(min(count, len(steps))):
            steps.pop(0)()

    def permute(source_ref, target_ref):
        for tile, part in enumerate(tiles_of(source_ref[...])):
            wide_ref[tile] = part.astype(F32)

        @pl.loop(0, PLACES // 2)
        def _(pair):
            first = read_place(wide_ref, 2 * pair)
            second = read_place(wide_ref, 2 * pair + 1)
            at = pl.multiple_of(pair * 16, 16)
            target_ref[pl.ds(at, 16), :] = jnp.concatenate([first, second], axis=0).astype(BF16)

    permute(cot_ref, upstream_ref)
    permute(tokens_ref, x_ref)
    advance()
    centred, rs = layer_stats(x_ref[...].astype(F32), D)
    normed_ref[...] = (centred * rs * gain_ref[...].reshape(1, D) + bias_ref[...].reshape(1, D)).astype(BF16)
    turned_ref[...] = normed_ref[...].T
    row = lax.broadcasted_iota(jnp.int32, (KEY_ROWS, LANES), 0)
    frames, length = frames_ref[0], length_ref[0]
    place = jnp.where(row < MEM_AT, row & 7, jnp.where(row < SQUEEZE_AT, row - MEM_AT, row - SQUEEZE_AT))
    limit = jnp.where(row < MEM_AT, frames, jnp.where(row < SQUEEZE_AT, length, MEM))
    off = jnp.where(place >= limit, jnp.where(lane_index((KEY_ROWS, LANES)) == MASK_LANE, MASKED, 0.0), 0.0)
    aug_ref[...] = (one_hot_ref[...].astype(F32) + off).astype(BF16)
    tables_ref[...] = jnp.zeros((LANES, LANES), F32)
    spans = 2 * HEIGHT - 1
    tables_ref[0 : 2 * FRAMES - 1, :HEAD_DIM] = time_ref[...]
    for s in range(2):
        tables_ref[15 + spans * s : 15 + spans * (s + 1), :HEAD_DIM] = space_ref[:, s]
    table_ref[...] = dot(pick_ref[...], tables_ref[...].astype(BF16)).astype(BF16)
    advance()

    def head_of(values, head):
        return values[:, HEAD_DIM * head : HEAD_DIM * head + HEAD_DIM]

    for s in range(2):
        for group in range(2):
            columns = slice(group * GROUP, (group + 1) * GROUP)
            for tile, part in enumerate(tiles_of(prev_ref[s, :, columns])):
                wide_ref[tile] = part.astype(F32)

            taps = [tiled_lanes(taps_ref[s, tap : tap + 1, :]) for tap in range(4)]

            @pl.loop(0, HEIGHT // 2)
            def _(i):
                for j in range(WIDTH // 2):
                    total = None
                    at = pl.multiple_of((i * (WIDTH // 2) + j) * FRAMES, FRAMES)
                    for tap in range(4):
                        place = (2 * i + tap // 2) * WIDTH + 2 * j + tap % 2
                        part = read_place(wide_ref, place, GROUP // LANES)
                        parts_ref[tap, pl.ds(at, FRAMES), :] = part
                        term = part * taps[tap]
                        total = term if total is None else total + term
                    sums_ref[pl.ds(at, FRAMES), :] = total

            old = mem_ref[s, :, columns].astype(F32)
            for head in range(GROUP_HEADS):
                rest = jnp.concatenate(
                    [
                        head_of(old, head),
                        jnp.zeros((SQUEEZE_AT - MEM_AT - MEM, HEAD_DIM), F32),
                        head_of(sums_ref[...], head),
                        jnp.zeros((KEY_ROWS - SQUEEZE_AT - MEM, HEAD_DIM), F32),
                    ],
                    axis=0,
                )
                rest = jnp.concatenate([rest, jnp.zeros((REST, LANES - HEAD_DIM), F32)], axis=1)
                rest_ref[s, group * GROUP_HEADS + head] = rest.astype(BF16)
                for tap in range(4):
                    part = jnp.concatenate([head_of(parts_ref[tap], head), jnp.zeros((8, HEAD_DIM), F32)], axis=0)
                    part = jnp.concatenate([part, jnp.zeros((208, LANES - HEAD_DIM), F32)], axis=1)
                    tap_ref[s, group * GROUP_HEADS + head, tap] = part.astype(BF16)
            advance(3 if group + s else 2)
    advance(len(steps))
    if communicate:
        doubling.arrive(*first_stage)
        doubling.end()
        gather.end()


def prepare(frames, length, tokens, cot, gain, bias, one_hot, rel_time, rel_space, pick, prev, memory, taps, shards=None):
    smem = pl.BlockSpec(memory_space=pltpu.SMEM)
    vmem = pl.BlockSpec(memory_space=pltpu.VMEM)
    communicate = shards is not None
    out_shape = [
        jax.ShapeDtypeStruct((ROWS, D), BF16),
        jax.ShapeDtypeStruct((ROWS, D), BF16),
        jax.ShapeDtypeStruct((D, ROWS), BF16),
        jax.ShapeDtypeStruct((ROWS, D), BF16),
        jax.ShapeDtypeStruct((KEY_ROWS, LANES), BF16),
        jax.ShapeDtypeStruct((TABLE, LANES), BF16),
        jax.ShapeDtypeStruct((2, HEADS, REST, LANES), BF16),
        jax.ShapeDtypeStruct((2, HEADS, 4, 208, LANES), BF16),
    ]
    in_specs, out_specs = [smem, smem] + [vmem] * 11, [vmem] * 8
    operands = [frames, length, tokens, cot, gain, bias, one_hot, rel_time, rel_space, pick, prev, memory, taps]
    scratch = [
        wide_scratch(D),
        pltpu.VMEM((MEM, GROUP), F32),
        pltpu.VMEM((4, MEM, GROUP), F32),
        pltpu.VMEM((LANES, LANES), F32),
    ]
    more = {}
    if communicate:
        anywhere = pl.BlockSpec(memory_space=pl.ANY)
        shard, one, two, proj = shards
        rows = (one.size + two.size) // LANES + 2 * proj.shape[0]
        out_shape = [
            jax.ShapeDtypeStruct((4, 2, 2, 2) + shard.shape, BF16),
            jax.ShapeDtypeStruct((2, 2, 2, 2, 2, rows, LANES), BF16),
        ] + out_shape
        in_specs += [anywhere, vmem, vmem, vmem]
        out_specs = [anywhere, anywhere] + out_specs
        operands += shards
        count = 2 * PARTS * 6
        scratch += [pltpu.VMEM((rows, LANES), BF16), pltpu.SemaphoreType.DMA]
        scratch += [pltpu.SemaphoreType.DMA((6,)), pltpu.SemaphoreType.DMA((6,))]
        scratch += [pltpu.SemaphoreType.DMA, pltpu.SemaphoreType.DMA((count,)), pltpu.SemaphoreType.DMA((count,))]
        more = {"collective_id": 0, "has_side_effects": True}
    return pl.pallas_call(
        functools.partial(prepare_kernel, communicate),
        out_shape=tuple(out_shape),
        in_specs=in_specs,
        out_specs=tuple(out_specs),
        scratch_shapes=scratch,
        compiler_params=params(**more),
        name="prepare",
    )(*operands)


def shift_frames(values, step):
    frame = lax.broadcasted_iota(jnp.int32, values.shape, values.ndim - 2)
    moved = pltpu.roll(values, step % FRAMES, values.ndim - 2)
    edge = 0 if step == 1 else FRAMES - 1
    return jnp.where(frame == edge, 0.0, moved)


def convolve(grid_ref, taps_ref, flip, i, lanes):
    sums = [None, None, None]
    for b in range(3):
        for e in range(3):
            window = grid_ref[i + b, e : e + WIDTH, :, lanes]
            for a in range(3):
                tap = 9 * a + 3 * b + e
                term = window * taps_ref[26 - tap if flip else tap, :, lanes][None]
                sums[a] = term if sums[a] is None else sums[a] + term
    return sums[1] + shift_frames(sums[0], 1) + shift_frames(sums[2], -1)


def spread_taps(raw_ref, taps_ref):
    for tap in range(27):
        line = tiled_lanes(raw_ref[0, tap : tap + 1, :])
        taps_ref[tap] = jnp.broadcast_to(line, (FRAMES, GROUP))


def clear_border(grid_ref):
    grid_ref[...] = jnp.zeros(grid_ref.shape, grid_ref.dtype)


def relative_bits(place_ref, d, f):
    return {
        "x": (d & 1) ^ place_ref[0],
        "z1": ((d >> 1) & 1) ^ place_ref[1],
        "z2": ((d >> 2) & 1) ^ place_ref[2],
        "y": ((f >> 1) & 1) ^ place_ref[3],
        "c": (f & 1) ^ place_ref[4],
    }


def slot(bits, order):
    return sum(bits[name] << at for at, name in enumerate(order))


def qkv_kernel(
    frames_ref, normed_ref, shards_ref, qkv_bias_ref, taps_raw_ref, gain_ref, bias_ref, same_ref, *refs,
):
    communicate = len(refs) > 9
    if communicate:
        refs, end = (*refs[1:6], *refs[7:11]), doubling_in_queries(refs[6], refs[11:])
    heads_ref, vhat_ref, rs_ref, mixed_ref, weight_ref, grid_ref, pooled_ref, taps_ref, line_ref = refs
    step = pl.program_id(0)

    @pl.when(step == 0)
    def _():
        clear_border(grid_ref)
        line_ref[...] = qkv_bias_ref[...].reshape(1, QKV)
        depth, columns = shards_ref.shape[2:]
        for f in range(QKV // columns):
            for d in range(DP_BLOCKS):
                weight_ref[d * depth : (d + 1) * depth, f * columns : (f + 1) * columns] = shards_ref[d, f]

    @pl.when(step % 2 == 0)
    def _():
        spread_taps(taps_raw_ref, taps_ref)

    at = pl.multiple_of(step * GROUP, LANES)
    mixed = dot(normed_ref[...], weight_ref[:, pl.ds(at, GROUP)]) + line_ref[:, pl.ds(at, GROUP)]
    row = lax.broadcasted_iota(jnp.int32, (ROWS, GROUP), 0)
    mixed = jnp.where((row & 7) < frames_ref[0], mixed, 0.0)
    mixed_ref[...] = mixed.astype(BF16)
    grid_ref[1 : HEIGHT + 1, 1 : WIDTH + 1] = mixed.reshape(HEIGHT, WIDTH, FRAMES, GROUP)

    @pl.loop(0, HEIGHT)
    def _(i):
        for tile in range(GROUP // LANES):
            lanes = slice(tile * LANES, tile * LANES + LANES)
            line = convolve(grid_ref, taps_ref, False, i, lanes)
            at = pl.multiple_of(i * WIDTH * FRAMES, WIDTH * FRAMES)
            pooled_ref[pl.ds(at, WIDTH * FRAMES), lanes] = line.reshape(WIDTH * FRAMES, LANES)

    pooled = pooled_ref[...]
    high = pooled.astype(BF16)
    low = (pooled - high.astype(F32)).astype(BF16)
    centred = pooled - (dot(high, same_ref[...]) + dot(low, same_ref[...])) * (1.0 / HEAD_DIM)
    variance = dot((centred * centred).astype(BF16), same_ref[...]) * (1.0 / HEAD_DIM)
    rs = lax.rsqrt(variance + EPSILON)
    vhat = centred * rs
    rs_ref[...] = rs
    vhat_ref[...] = vhat.astype(BF16)
    kind = pl.ds(step // 2, 1)
    out = (vhat * tiled_lanes(gain_ref[kind, :]) + tiled_lanes(bias_ref[kind, :])).astype(BF16)
    for head in range(GROUP_HEADS):
        own = out[:, HEAD_DIM * head : HEAD_DIM * (head + 1)]
        heads_ref[head] = jnp.concatenate([own, jnp.zeros((ROWS, LANES - HEAD_DIM), BF16)], axis=1)
    if communicate:
        end()


def wall_more(wall, out_shape, out_specs, scratch, operands, collective_id):
    if wall is None:
        return {}, {}
    anywhere = pl.BlockSpec(memory_space=pl.ANY)
    out_shape.append(jax.ShapeDtypeStruct(wall.shape, wall.dtype))
    out_specs.append(anywhere)
    scratch += [pltpu.SemaphoreType.DMA((18,)), pltpu.SemaphoreType.DMA((18,))]
    operands.append(wall)
    return {"collective_id": collective_id, "has_side_effects": True}, {len(operands) - 1: len(out_shape) - 1}


def query_key_value(frames, normed, shards, qkv_bias, taps, gain, bias, same, wall=None):
    smem = pl.BlockSpec(memory_space=pltpu.SMEM)
    group = pl.BlockSpec((ROWS, GROUP), lambda g: (0, g))
    out_shape = [
        jax.ShapeDtypeStruct((3 * HEADS, ROWS, LANES), BF16),
        jax.ShapeDtypeStruct((ROWS, QKV), BF16),
        jax.ShapeDtypeStruct((ROWS, QKV), F32),
        jax.ShapeDtypeStruct((ROWS, QKV), BF16),
        jax.ShapeDtypeStruct((D, QKV), BF16),
    ]
    out_specs = [
        pl.BlockSpec((GROUP_HEADS, ROWS, LANES), lambda g: (g, 0, 0)), group, group, group, whole((D, QKV))
    ]
    scratch = [
        pltpu.VMEM((HEIGHT + 2, WIDTH + 2, FRAMES, GROUP), F32),
        pltpu.VMEM((ROWS, GROUP), F32),
        pltpu.VMEM((27, FRAMES, GROUP), F32),
        pltpu.VMEM((1, QKV), F32),
    ]
    operands = [frames, normed, shards, qkv_bias, taps, gain, bias, same]
    in_specs = [
        smem,
        whole((ROWS, D)),
        whole(shards.shape),
        whole((QKV,)),
        pl.BlockSpec((1, 27, HEAD_DIM), lambda g: (g // 2, 0, 0)),
        whole((3, HEAD_DIM)),
        whole((3, HEAD_DIM)),
        whole((GROUP, GROUP)),
    ]
    more, aliases = wall_more(wall, out_shape, out_specs, scratch, operands, 4)
    return pl.pallas_call(
        qkv_kernel,
        grid=(6,),
        out_shape=tuple(out_shape),
        in_specs=in_specs + [pl.BlockSpec(memory_space=pl.ANY)] * len(aliases),
        out_specs=tuple(out_specs),
        scratch_shapes=scratch,
        input_output_aliases=aliases,
        compiler_params=params(**more),
        name="query_key_value",
    )(*operands)


def attend_kernel(
    q_ref, k_ref, v_ref, krest_ref, vrest_ref, aug_ref, table_ref, own_ref, fold_ref, *refs,
):
    communicate = len(refs) > 6
    if communicate:
        refs, end = (*refs[1:4], *refs[5:8]), doubling_in_attention(refs[4], refs[8:])
    weights_ref, pv_ref, out_ref, keys_ref, vals_ref, query_ref = refs
    lane = lane_index((KEY_ROWS, LANES))
    keys_ref[:ROWS] = k_ref[0] + aug_ref[:ROWS]
    keys_ref[ROWS:] = krest_ref[0, 0] + aug_ref[ROWS:]
    one = jnp.where(lane == HEAD_DIM, 1.0, 0.0).astype(BF16)
    vals_ref[:ROWS] = v_ref[0] + one[:ROWS]
    vals_ref[ROWS:] = vrest_ref[0, 0] + one[ROWS:]
    query = q_ref[0]
    every = (dot(query, table_ref[...], ((1,), (1,))) * ROOT).astype(BF16) * own_ref[...]
    relative = dot(every, fold_ref[...])
    marked = jnp.where(lane[:ROWS] == MASK_LANE, 1.0, relative)
    query_ref[...] = (query.astype(F32) + marked).astype(BF16)

    for block in range(ROWS // ROW_BLOCK):
        rows = slice(block * ROW_BLOCK, (block + 1) * ROW_BLOCK)
        scores = dot(query_ref[rows, :], keys_ref[...], ((1,), (1,)))
        largest = jnp.max(scores, axis=1, keepdims=True)
        weights = jnp.exp2((scores - largest) * (SCALE * LOG2E)).astype(BF16)
        weights_ref[0, rows, :] = weights
        total = dot(weights, vals_ref[...])
        inverse = 1.0 / total[:, HEAD_DIM : HEAD_DIM + 1]
        lane = lane_index((ROW_BLOCK, LANES))
        pv = jnp.where(lane < HEAD_DIM, total * inverse, 0.0)
        out_ref[0, rows, :] = (pv + q_ref[0, rows, :].astype(F32)).astype(BF16)
        high = inverse.astype(BF16).astype(F32)
        extra = jnp.where(lane == HEAD_DIM, high, jnp.where(lane == HEAD_DIM + 1, inverse - high, 0.0))
        pv_ref[0, rows, :] = (pv + extra).astype(BF16)
    if communicate:
        end()


def attend(heads, rest, aug, table, own, fold, wall=None):
    head = (1, ROWS, LANES)
    tail = (1, 1, REST, LANES)
    out_shape = [
        jax.ShapeDtypeStruct((HEADS, ROWS, KEY_ROWS), BF16),
        jax.ShapeDtypeStruct((HEADS, ROWS, LANES), BF16),
        jax.ShapeDtypeStruct((HEADS, ROWS, LANES), BF16),
    ]
    out_specs = [
        pl.BlockSpec((1, ROWS, KEY_ROWS), lambda h: (h, 0, 0)),
        pl.BlockSpec(head, lambda h: (h, 0, 0)),
        pl.BlockSpec(head, lambda h: (h, 0, 0)),
    ]
    scratch = [
        pltpu.VMEM((KEY_ROWS, LANES), BF16),
        pltpu.VMEM((KEY_ROWS, LANES), BF16),
        pltpu.VMEM((ROWS, LANES), BF16),
    ]
    operands = [heads, heads, heads, rest, rest, aug, table, own, fold]
    in_specs = [
        pl.BlockSpec(head, lambda h: (h, 0, 0)),
        pl.BlockSpec(head, lambda h: (HEADS + h, 0, 0)),
        pl.BlockSpec(head, lambda h: (2 * HEADS + h, 0, 0)),
        pl.BlockSpec(tail, lambda h: (0, h, 0, 0)),
        pl.BlockSpec(tail, lambda h: (1, h, 0, 0)),
        whole((KEY_ROWS, LANES)),
        whole((TABLE, LANES)),
        whole((ROWS, TABLE)),
        whole((TABLE, LANES)),
    ]
    more, aliases = wall_more(wall, out_shape, out_specs, scratch, operands, 5)
    return pl.pallas_call(
        attend_kernel,
        grid=(HEADS,),
        out_shape=tuple(out_shape),
        in_specs=in_specs + [pl.BlockSpec(memory_space=pl.ANY)] * len(aliases),
        out_specs=tuple(out_specs),
        scratch_shapes=scratch,
        input_output_aliases=aliases,
        compiler_params=params(**more),
        name="attend",
    )(*operands)


CHUNK = 768
CHUNKS = FF // CHUNK
TILES = CHUNK // LANES


def middle_kernel(
    place_ref, att_ref, x_ref, up_ref, wp_ref, w1_ref, w2_ref, pb_ref, g2_ref, b2_ref, fb1_ref, fb2_ref,
    out_ref, dmid_ref, datt_ref, plow_ref, phigh_ref, low1_ref, high1_ref, low2_ref, high2_ref, small_ref, gb1_ref,
    packed_ref, proj_ref, mid_ref, hidden_ref, total_ref, dhid_ref, wide_ref, w1_scr, w2_scr, grad_ref,
    hiddent_ref, upt_ref,
):
    step = pl.program_id(0)
    sides = wp_ref.shape[1]
    part = D // sides
    depth = D // DP_BLOCKS
    inner = FF // DP_BLOCKS

    @pl.when(step == 0)
    def _():
        for head in range(HEADS):
            packed_ref[:, HEAD_DIM * head : HEAD_DIM * (head + 1)] = att_ref[head][:, :HEAD_DIM]
        for f in range(sides):
            for d in range(DP_BLOCKS):
                rows = slice(d * depth, (d + 1) * depth)
                proj_ref[rows, f * part : f * part + LANES] = wp_ref[d, f, :depth]
                proj_ref[rows, f * part + LANES : (f + 1) * part] = wp_ref[d, f, depth:, : part - LANES]
        middle = x_ref[...].astype(F32) + dot(packed_ref[...], proj_ref[...]) + pb_ref[...].reshape(1, D)
        mid_ref[...] = middle
        centred, rs = layer_stats(middle, D)
        hidden = centred * rs * g2_ref[...].reshape(1, D) + b2_ref[...].reshape(1, D)
        hidden_ref[...] = hidden.astype(BF16)
        hiddent_ref[...] = hidden.T.astype(BF16)
        upt_ref[...] = up_ref[...].T
        total_ref[...] = middle + fb2_ref[...].reshape(1, D).reshape(1, D)
        dhid_ref[...] = jnp.zeros((ROWS, D), F32)

    for tile in range(TILES):
        lanes = slice(tile * LANES, (tile + 1) * LANES)
        for d in range(DP_BLOCKS):
            w1_scr[d * depth : (d + 1) * depth, lanes] = w1_ref[d, 0, tile * depth : (tile + 1) * depth]
        side, at = divmod(tile, inner // LANES)
        for f in range(sides):
            w2_scr[f * part : (f + 1) * part, lanes] = w2_ref[side, f, at * part : (at + 1) * part]
    w1, w2 = w1_scr[...], w2_scr[...]
    before = dot(hidden_ref[...], w1) + fb1_ref[...]
    cdf = 0.5 + 0.5 * lax.erf(before * (2.0**-0.5))
    activated = (before * cdf).astype(BF16)
    slope = cdf + before * (jnp.exp(before * before * -0.5) * 0.3989422804014327)
    dbefore = dot(up_ref[...], w2) * slope
    dbefore_low = dbefore.astype(BF16)
    gb1_ref[...] = jnp.sum(dbefore_low.astype(F32), axis=0, keepdims=True)
    total_ref[...] += dot(activated, w2, ((1,), (1,)))
    dhid_ref[...] += dot(dbefore_low, w1, ((1,), (1,)))

    core = place_ref[4]
    grad_ref[...] = dot(upt_ref[...], activated).astype(BF16)
    for tile in range(TILES):
        lanes = slice(tile * LANES, (tile + 1) * LANES)
        side, at = divmod(tile, inner // LANES)
        rows = slice(at * part, (at + 1) * part)
        for y in range(sides // 2):
            bits = relative_bits(place_ref, side, 2 * y)
            for target_ref, c in ((low2_ref, core), (high2_ref, 1 - core)):
                start = pl.multiple_of((2 * y + c) * part, part)
                target_ref[bits["y"], bits["x"], 0, 0, rows] = grad_ref[pl.ds(start, part), lanes]
    grad_ref[...] = dot(hiddent_ref[...], dbefore_low).astype(BF16)

    def store_one(target_ref):
        for tile in range(TILES):
            lanes = slice(tile * LANES, (tile + 1) * LANES)
            for d in range(DP_BLOCKS):
                bits = relative_bits(place_ref, d, 0)
                block = grad_ref[d * depth : (d + 1) * depth, lanes]
                target_ref[bits["x"], 0, bits["z1"], bits["z2"], tile * depth : (tile + 1) * depth] = block

    @pl.when(step < CHUNKS // 2)
    def _():
        store_one(low1_ref)

    @pl.when(step >= CHUNKS // 2)
    def _():
        store_one(high1_ref)

    @pl.when(step == CHUNKS - 1)
    def _():
        @pl.loop(0, PLACES)
        def _(place):
            at = pl.multiple_of(place * FRAMES, FRAMES)
            write_place(wide_ref, place, total_ref[pl.ds(at, FRAMES), :])

        for tile in range(D // LANES):
            out_ref[:, tile * LANES : (tile + 1) * LANES] = wide_ref[tile].astype(BF16)
        upstream = up_ref[...].astype(F32)
        dhidden = dhid_ref[...]
        centred, rs = layer_stats(mid_ref[...], D)
        vhat = centred * rs
        dgain = jnp.sum(dhidden * vhat, axis=0, keepdims=True)
        dbias = jnp.sum(dhidden, axis=0, keepdims=True)
        scaled = dhidden * g2_ref[...].reshape(1, D)
        first = jnp.sum(scaled, axis=1, keepdims=True) * (1.0 / D)
        second = jnp.sum(scaled * vhat, axis=1, keepdims=True) * (1.0 / D)
        dmiddle = upstream + rs * (scaled - first - vhat * second)
        dmid_ref[...] = dmiddle
        dproj = dmiddle.astype(BF16)
        small_ref[0:1, :] = jnp.sum(dproj.astype(F32), axis=0, keepdims=True)
        small_ref[1:2, :] = dgain
        small_ref[2:3, :] = dbias
        small_ref[3:4, :] = jnp.sum(upstream, axis=0, keepdims=True)
        small_ref[4:8, :] = jnp.zeros((4, D), F32)
        grad_ref[...] = dot(packed_ref[...], dproj, ((0,), (0,))).astype(BF16)
        for d in range(DP_BLOCKS):
            rows = slice(d * depth, (d + 1) * depth)
            for y in range(sides // 2):
                bits = relative_bits(place_ref, d, 2 * y)
                where = (bits["y"], bits["x"], bits["z1"], bits["z2"])
                sides_of = [grad_ref[rows, f * part : (f + 1) * part] for f in (2 * y, 2 * y + 1)]
                for target_ref, c in ((plow_ref, core), (phigh_ref, 1 - core)):
                    block = jnp.where(c == 0, sides_of[0], sides_of[1])
                    target_ref[(*where, slice(0, depth))] = block[:, :LANES]
                    rest = jnp.concatenate([block[:, LANES:], jnp.zeros((depth, 2 * LANES - part), BF16)], axis=1)
                    target_ref[(*where, slice(depth, 2 * depth))] = rest
        datt = dot(dproj, proj_ref[...], ((1,), (1,))).astype(BF16)
        for head in range(HEADS):
            datt_ref[head] = jnp.concatenate(
                [datt[:, HEAD_DIM * head : HEAD_DIM * (head + 1)], jnp.zeros((ROWS, LANES - HEAD_DIM), BF16)],
                axis=1,
            )


def feed_forward(place, att, x, up, flat, pb, g2, b2, fb1, fb2):
    once = pl.Buffered(1)
    sides = flat.shape[1]
    part, depth = D // sides, D // DP_BLOCKS
    rows_one, rows_two = TILES * depth, FF // DP_BLOCKS // LANES * part

    def kept(shape):
        return pl.BlockSpec(shape, lambda *_: (0,) * len(shape), pipeline_mode=once)

    def side_of(s, place):
        return 2 * (place[3] ^ (s & 1)) + (place[4] ^ (s >> 1))

    def columns(s, place):
        return (0, side_of(s, place))

    def low_one(s, place):
        return (0, jnp.where(s < 2, s & 1, 1), 0, 0, 0, 0)

    def high_one(s, place):
        return (0, jnp.where(s < 2, 0, s & 1), 0, 0, 0, 0)

    def pair(s, place):
        side = side_of(s, place)
        return (0, 0, place[1] ^ (side & 1), place[2] ^ (side >> 1), 0, 0)

    bits = (2, 2, 2, 2)
    one, two, proj = bits + (rows_one, LANES), bits + (rows_two, LANES), bits + (2 * depth, LANES)
    return pl.pallas_call(
        middle_kernel,
        out_shape=(
            jax.ShapeDtypeStruct((ROWS, D), BF16),
            jax.ShapeDtypeStruct((ROWS, D), F32),
            jax.ShapeDtypeStruct((HEADS, ROWS, LANES), BF16),
            jax.ShapeDtypeStruct(proj, BF16),
            jax.ShapeDtypeStruct(proj, BF16),
            jax.ShapeDtypeStruct(one, BF16),
            jax.ShapeDtypeStruct(one, BF16),
            jax.ShapeDtypeStruct(two, BF16),
            jax.ShapeDtypeStruct(two, BF16),
            jax.ShapeDtypeStruct((8, D), F32),
            jax.ShapeDtypeStruct((1, FF), F32),
        ),
        grid_spec=pltpu.PrefetchScalarGridSpec(
            num_scalar_prefetch=1,
            grid=(CHUNKS,),
            in_specs=[
                kept((HEADS, ROWS, LANES)),
                kept((ROWS, D)),
                kept((ROWS, D)),
                pl.BlockSpec(
                    (DP_BLOCKS, sides, 2 * depth, LANES), lambda s, place: (0, 0, 6, 0), pipeline_mode=once
                ),
                pl.BlockSpec(
                    (DP_BLOCKS, 1, rows_one, LANES), lambda s, place: (0, side_of(s, place), 0, 0)
                ),
                pl.BlockSpec((2, sides, rows_two, LANES), lambda s, place: (side_of(s, place), 0, 1, 0)),
                kept((D,)),
                kept((D,)),
                kept((D,)),
                pl.BlockSpec((1, CHUNK), columns),
                kept((D,)),
            ],
            out_specs=(
                kept((ROWS, D)),
                kept((ROWS, D)),
                kept((HEADS, ROWS, LANES)),
                kept(proj),
                kept(proj),
                pl.BlockSpec((2, 1, 2, 2, rows_one, LANES), low_one),
                pl.BlockSpec((2, 1, 2, 2, rows_one, LANES), high_one),
                pl.BlockSpec((2, 2, 1, 1, rows_two, LANES), pair),
                pl.BlockSpec((2, 2, 1, 1, rows_two, LANES), pair),
                kept((8, D)),
                pl.BlockSpec((1, CHUNK), columns),
            ),
            scratch_shapes=[
                pltpu.VMEM((ROWS, D), BF16),
                pltpu.VMEM((D, D), BF16),
                pltpu.VMEM((ROWS, D), F32),
                pltpu.VMEM((ROWS, D), BF16),
                pltpu.VMEM((ROWS, D), F32),
                pltpu.VMEM((ROWS, D), F32),
                wide_scratch(D),
                pltpu.VMEM((D, CHUNK), BF16),
                pltpu.VMEM((D, CHUNK), BF16),
                pltpu.VMEM((D, CHUNK), BF16),
                pltpu.VMEM((D, ROWS), BF16),
                pltpu.VMEM((D, ROWS), BF16),
            ],
        ),
        compiler_params=params(),
        name="feed_forward",
    )(place, att, x, up, flat, flat, flat, pb, g2, b2, fb1, fb2)


SPLIT = 128
ONE_DIMS, TWO_DIMS = ("x", "y", "z1", "z2"), ("y", "x", "z1", "z2")
LINE_X, LINE_Y = ("z1", "x", "y", "z2"), ("z1", "y", "x", "z2")
PIECES = (
    (0, ONE_DIMS, ONE_DIMS),
    (1, TWO_DIMS, TWO_DIMS),
    (0, ONE_DIMS, LINE_X),
    (1, TWO_DIMS, LINE_X),
    (2, TWO_DIMS, LINE_Y),
)


def piece_rows(rows_one, rows_two, rows_proj):
    one, two = rows_one - SPLIT, rows_two - SPLIT
    return (0, one), (0, two), (one, SPLIT), (two, SPLIT), (0, rows_proj)


def pick_blocks(dims, **fixed):
    return tuple(fixed.get(name, slice(None)) for name in dims)


def without(dims, *names):
    return tuple(name for name in dims if name not in names)


def first_halving(sent, sums, kept, got, more, *sems):
    step = pl.program_id(0)
    own_sem, *sems = sems
    near = Neighbours()
    spans = piece_rows(sent[0].shape[4], sent[2].shape[4], sent[4].shape[4])
    every = range(len(PIECES))

    def own():
        copies = []
        for p in every:
            array, dims, _ = PIECES[p]
            source = sent[2 * array].at[(*pick_blocks(dims), pl.ds(*spans[p]))]
            copies.append(pltpu.make_async_copy(source, kept[p], own_sem.at[p]))
        return copies

    def over_core(part):
        copies = []
        for p in every:
            array, dims, route = PIECES[p]
            where = pick_blocks(dims, **{route[0]: 1 - part})
            source = sent[2 * array + 1].at[(*where, pl.ds(*spans[p]))]
            copies.append(near.copy("c", source, got[p].at[where], sems, 2 * p + part))
        return copies

    def onward():
        copies = []
        for p in every:
            _, dims, route = PIECES[p]
            source = kept[p].at[pick_blocks(dims, **{route[0]: 1})]
            copies.append(near.copy(route[0], source, more[p], sems, 10 + p))
        return copies

    def arrive(part):
        for copy in over_core(part):
            copy.wait_recv()
        for p in every:
            _, dims, route = PIECES[p]
            where = pick_blocks(dims, **{route[0]: 1 - part})
            kept[p][where] = kept[p][where] + got[p][where]

    @pl.when(step == 0)
    def _():
        near.greet(("c", "x", "y", "z1"))
        for copy in over_core(0) + over_core(1) + own():
            copy.start()

    @pl.when(step == 1)
    def _():
        for copy in own():
            copy.wait()
        arrive(0)
        for copy in onward():
            copy.start()

    @pl.when(step == 2)
    def _():
        arrive(1)

    @pl.when(step == pl.num_programs(0) - 1)
    def _():
        for copy in onward():
            copy.wait_recv()
        for p in every:
            _, dims, route = PIECES[p]
            sums[p][...] = kept[p][pick_blocks(dims, **{route[0]: 0})] + more[p][...]
        for copy in over_core(0) + over_core(1) + onward():
            copy.wait_send()


def attend_back_kernel(
    q_ref, k_ref, v_ref, krest_ref, vrest_ref, aug_ref, table_ref, own_ref, fold_ref, pick_ref,
    weights_ref, pv_ref, datt_ref, parts_ref, *refs,
):
    communicate = len(refs) > 7
    if communicate:
        sent, (grads_ref, gtable_ref, gtaps_ref), sums = refs[:6], refs[6:9], refs[9:14]
        keys_ref, vals_ref, up_ref, gsum_ref = refs[14:18]
        first_halving(sent, sums, refs[18:23], refs[23:28], refs[28:33], *refs[33:])
    else:
        grads_ref, gtable_ref, gtaps_ref, keys_ref, vals_ref, up_ref, gsum_ref = refs
    step = pl.program_id(0)
    lane = lane_index((KEY_ROWS, LANES))
    row_lane = lane[:ROWS]

    @pl.when(step == 0)
    def _():
        gsum_ref[...] = jnp.zeros((TABLE, LANES), F32)
        gtaps_ref[...] = jnp.zeros((2, 4, LANES), F32)

    keys_ref[:ROWS] = k_ref[0] + aug_ref[:ROWS]
    keys_ref[ROWS:] = krest_ref[0, 0] + aug_ref[ROWS:]
    one = jnp.where((lane >= HEAD_DIM) & (lane < HEAD_DIM + 3), 1.0, 0.0).astype(BF16)
    vals_ref[:ROWS] = v_ref[0] + one[:ROWS]
    vals_ref[ROWS:] = vrest_ref[0, 0] + one[ROWS:]
    pv = pv_ref[0].astype(F32)
    inverse = pv[:, HEAD_DIM : HEAD_DIM + 1] + pv[:, HEAD_DIM + 1 : HEAD_DIM + 2]
    datt = datt_ref[0].astype(F32)
    upstream = (datt * inverse).astype(BF16).astype(F32)
    mean = jnp.sum(upstream * pv, axis=1, keepdims=True)
    high = mean.astype(BF16).astype(F32)
    low = (mean - high).astype(BF16).astype(F32)
    least = mean - high - low
    extra = jnp.where(
        row_lane == HEAD_DIM,
        -high,
        jnp.where(row_lane == HEAD_DIM + 1, -low, jnp.where(row_lane == HEAD_DIM + 2, -least, 0.0)),
    )
    up_ref[...] = (upstream + extra).astype(BF16)

    dvals, dkeys, dquery = None, None, []
    for block in range(ROWS // ROW_BLOCK):
        rows = slice(block * ROW_BLOCK, (block + 1) * ROW_BLOCK)
        weights = weights_ref[0, rows, :]
        dprobs = dot(up_ref[rows, :], vals_ref[...], ((1,), (1,)))
        slopes = (weights.astype(F32) * dprobs).astype(BF16)
        dquery.append(dot(slopes, keys_ref[...]))
        more_vals = dot(up_ref[rows, :], weights, ((0,), (0,)))
        more_keys = dot(q_ref[0, rows, :], slopes, ((0,), (0,)))
        dvals = more_vals if dvals is None else dvals + more_vals
        dkeys = more_keys if dkeys is None else dkeys + more_keys
    dvals, dkeys = dvals.T, dkeys.T * SCALE
    dquery = jnp.concatenate(dquery, axis=0)
    spread = dot(dquery.astype(BF16), fold_ref[...], ((1,), (1,))).astype(BF16) * own_ref[...]
    gsum_ref[...] += dot(spread, q_ref[0], ((0,), (0,)))
    dquery = dquery * SCALE + datt + dot(spread, table_ref[...])
    grads_ref[0, 0] = dquery.astype(BF16)
    grads_ref[1, 0] = dkeys[:ROWS].astype(BF16)
    grads_ref[2, 0] = dvals[:ROWS].astype(BF16)
    for s, whole_grad in ((0, dkeys), (1, dvals)):
        piece = whole_grad[SQUEEZE_AT : SQUEEZE_AT + MEM]
        for tap in range(4):
            product = piece * parts_ref[s, 0, tap].astype(F32)[:MEM]
            gtaps_ref[s, tap : tap + 1, :] += jnp.sum(product, axis=0, keepdims=True)

    @pl.when(step == pl.num_programs(0) - 1)
    def _():
        gtable_ref[...] = dot(pick_ref[...].astype(F32), gsum_ref[...], ((0,), (0,)), lax.Precision.HIGHEST)


def attend_back(sent, heads, rest, aug, table, own, fold, pick, weights, pv, datt, parts):
    head = (1, ROWS, LANES)
    tail = (1, 1, REST, LANES)
    own_head = pl.BlockSpec(head, lambda h: (h, 0, 0))
    out_shape = [
        jax.ShapeDtypeStruct((3, HEADS, ROWS, LANES), BF16),
        jax.ShapeDtypeStruct((LANES, LANES), F32),
        jax.ShapeDtypeStruct((2, 4, LANES), F32),
    ]
    out_specs = [pl.BlockSpec((3, 1, ROWS, LANES), lambda h: (0, h, 0, 0)), whole((LANES, LANES)), whole((2, 4, LANES))]
    scratch = [
        pltpu.VMEM((KEY_ROWS, LANES), BF16),
        pltpu.VMEM((KEY_ROWS, LANES), BF16),
        pltpu.VMEM((ROWS, LANES), BF16),
        pltpu.VMEM((TABLE, LANES), F32),
    ]
    more = {}
    if sent:
        spans = piece_rows(sent[0].shape[4], sent[2].shape[4], sent[4].shape[4])
        for _, rows in spans:
            out_shape.append(jax.ShapeDtypeStruct((2, 2, 2, rows, LANES), BF16))
            out_specs.append(whole((2, 2, 2, rows, LANES)))
        scratch += [pltpu.VMEM((2,) * bits + (rows, LANES), BF16) for bits in (4, 4, 3) for _, rows in spans]
        scratch += [pltpu.SemaphoreType.DMA((5,)), pltpu.SemaphoreType.DMA((15,)), pltpu.SemaphoreType.DMA((15,))]
        more = {"collective_id": 2, "has_side_effects": True}
    return pl.pallas_call(
        attend_back_kernel,
        grid=(HEADS,),
        out_shape=tuple(out_shape),
        in_specs=[
            own_head,
            pl.BlockSpec(head, lambda h: (HEADS + h, 0, 0)),
            pl.BlockSpec(head, lambda h: (2 * HEADS + h, 0, 0)),
            pl.BlockSpec(tail, lambda h: (0, h, 0, 0)),
            pl.BlockSpec(tail, lambda h: (1, h, 0, 0)),
            whole((KEY_ROWS, LANES)),
            whole((TABLE, LANES)),
            whole((ROWS, TABLE)),
            whole((TABLE, LANES)),
            whole((TABLE, LANES)),
            pl.BlockSpec((1, ROWS, KEY_ROWS), lambda h: (h, 0, 0)),
            own_head,
            own_head,
            pl.BlockSpec((2, 1, 4, 208, LANES), lambda h: (0, h, 0, 0, 0)),
        ]
        + [pl.BlockSpec(memory_space=pl.ANY)] * len(sent),
        out_specs=tuple(out_specs),
        scratch_shapes=scratch,
        compiler_params=params(**more),
        name="attend_back",
    )(heads, heads, heads, rest, rest, aug, table, own, fold, pick, weights, pv, datt, parts, *sent)


def last_halving(ins, outs, got, kept, sems):
    step = pl.program_id(0)
    near = Neighbours()
    pieces = len(PIECES)
    first, second, third = got[:pieces], got[pieces : 2 * pieces], got[2 * pieces :]
    fours, twos = kept[:pieces], kept[pieces:]
    plane, line = (0, 1), (2, 3, 4)

    def copy(p, stage, part):
        _, dims, route = PIECES[p]
        dims = without(dims, *route[:stage])
        at = 5 * p + 2 * (stage - 1) + part
        fixed = {route[stage]: 1}
        if stage < 3:
            fixed[route[stage + 1]] = 1 - part
        source = (ins, fours, twos)[stage - 1][p].at[pick_blocks(dims, **fixed)]
        target = (first, second, third)[stage - 1][p]
        if stage < 3:
            target = target.at[pick_blocks(without(dims, route[stage]), **fixed)]
        return near.copy(route[stage], source, target, sems, at)

    def start(group, stage):
        for p in group:
            for part in range(2 if stage < 3 else 1):
                copy(p, stage, part).start()

    def arrive(group, stage, part):
        for p in group:
            copy(p, stage, part).wait_recv()
            _, dims, route = PIECES[p]
            dims = without(dims, *route[:stage])
            fixed = {route[stage + 1]: 1 - part}
            here = pick_blocks(dims, **{route[stage]: 0}, **fixed)
            there = pick_blocks(without(dims, route[stage]), **fixed)
            source = (ins, fours)[stage - 1][p]
            (fours, twos)[stage - 1][p][there] = source[here] + (first, second)[stage - 1][p][there]

    @pl.when(step == 0)
    def _():
        near.greet(("c", "x", "y", "z1", "z2"))
        start(plane + line, 1)

    @pl.when(step == 1)
    def _():
        arrive(plane, 1, 0)
        start(plane, 2)

    @pl.when(step == 2)
    def _():
        arrive(plane, 1, 1)
        arrive(line, 1, 0)
        start(line, 2)

    @pl.when(step == 3)
    def _():
        arrive(plane, 2, 0)
        start(plane, 3)

    @pl.when(step == 4)
    def _():
        arrive(plane, 2, 1)
        arrive(line, 1, 1)
        arrive(line, 2, 0)
        start(line, 3)

    def end():
        arrive(line, 2, 1)
        for p in range(pieces):
            copy(p, 3, 0).wait_recv()
            outs[p][...] = twos[p][0].astype(F32) + third[p][...].astype(F32)
        for p in range(pieces):
            for stage in (1, 2, 3):
                for part in range(2 if stage < 3 else 1):
                    copy(p, stage, part).wait_send()

    return near, end


EARLY_ROWS = 112
EARLY_COMPRESS, EARLY_WIDE = 56, 64
DOUBLINGS = ("c", "x", "y", "z1", "z2")


def early_sums(near, table_ref, comp_ref, two_ref, gb1_ref, out_ref, vector_ref, more_ref, sems):
    step = pl.program_id(0)

    def move(stage):
        return near.copy(DOUBLINGS[stage], vector_ref.at[stage], more_ref.at[stage], sems, stage)

    @pl.when(step == 0)
    def _():
        vector_ref[0, :EARLY_COMPRESS] = table_ref[:EARLY_COMPRESS]
        for s in range(2):
            vector_ref[0, EARLY_COMPRESS + 4 * s : EARLY_COMPRESS + 4 * s + 4] = comp_ref[s]
        lines = [two_ref[at : at + 1, :] for at in range(4)] + [gb1_ref[:, at : at + D] for at in range(0, FF, D)]
        for tile in range(D // LANES):
            for at, line in enumerate(lines):
                row = EARLY_WIDE + 8 * tile + at
                vector_ref[0, row : row + 1] = line[:, tile * LANES : (tile + 1) * LANES]
        move(0).start()

    for stage in range(1, 5):

        @pl.when(step == stage)
        def _():
            move(stage - 1).wait_recv()
            vector_ref[stage] = vector_ref[stage - 1] + more_ref[stage - 1]
            move(stage).start()

    def end():
        move(4).wait_recv()
        out_ref[...] = vector_ref[4] + more_ref[4]
        for stage in range(5):
            move(stage).wait_send()

    return end


def pool_back_kernel(
    frames_ref, grads_ref, vhat_ref, rs_ref, mixed_ref, taps_raw_ref, gain_ref, same_ref, *refs,
):
    communicate = len(refs) > 6
    if communicate:
        dmix_ref, small_ref, grid_ref, dgrid_ref, sums_ref, taps_ref = (*refs[9:11], *refs[17:21])
        near, end_halving = last_halving(refs[:5], refs[11:16], refs[21:36], refs[36:46], refs[46:48])
        end_early = early_sums(near, *refs[5:9], refs[16], *refs[48:50], refs[50:52])
    else:
        dmix_ref, small_ref, grid_ref, dgrid_ref, sums_ref, taps_ref = refs
    step = pl.program_id(0)

    @pl.when(step == 0)
    def _():
        clear_border(grid_ref)
        clear_border(dgrid_ref)

    @pl.when(step % 2 == 0)
    def _():
        spread_taps(taps_raw_ref, taps_ref)

    dy = jnp.concatenate([grads_ref[0, head][:, :HEAD_DIM] for head in range(GROUP_HEADS)], axis=1).astype(F32)
    vhat = vhat_ref[...].astype(F32)
    gain = tiled_lanes(gain_ref[pl.ds(step // 2, 1), :])
    product = dy * vhat
    small_ref[0, 28:29, :] = jnp.sum(product, axis=0, keepdims=True)
    small_ref[0, 29:30, :] = jnp.sum(dy, axis=0, keepdims=True)
    small_ref[0, 30:32, :] = jnp.zeros((2, GROUP), F32)
    scaled = dy * gain
    first = dot(scaled.astype(BF16), same_ref[...]) * (1.0 / HEAD_DIM)
    second = dot((product * gain).astype(BF16), same_ref[...]) * (1.0 / HEAD_DIM)
    dpool = rs_ref[...] * (scaled - first - vhat * second)
    dgrid_ref[1 : HEIGHT + 1, 1 : WIDTH + 1] = dpool.reshape(HEIGHT, WIDTH, FRAMES, GROUP)
    grid_ref[1 : HEIGHT + 1, 1 : WIDTH + 1] = mixed_ref[...].astype(F32).reshape(HEIGHT, WIDTH, FRAMES, GROUP)
    sums_ref[...] = jnp.zeros(sums_ref.shape, F32)

    @pl.loop(0, HEIGHT)
    def _(i):
        for tile in range(GROUP // LANES):
            lanes = slice(tile * LANES, tile * LANES + LANES)
            line = convolve(dgrid_ref, taps_ref, True, i, lanes)
            frame = lax.broadcasted_iota(jnp.int32, line.shape, 1)
            line = jnp.where(frame < frames_ref[0], line, 0.0)
            at = pl.multiple_of(i * WIDTH * FRAMES, WIDTH * FRAMES)
            dmix_ref[pl.ds(at, WIDTH * FRAMES), lanes] = line.reshape(WIDTH * FRAMES, LANES).astype(BF16)
            own = dgrid_ref[i + 1, 1 : WIDTH + 1, :, lanes]
            moved = (shift_frames(own, -1), own, shift_frames(own, 1))
            for b in range(3):
                for e in range(3):
                    window = grid_ref[i + b, e : e + WIDTH, :, lanes]
                    for a in range(3):
                        tap = 9 * a + 3 * b + e
                        sums_ref[tap, :, lanes] += jnp.sum(window * moved[a], axis=0)

    for tap in range(27):
        small_ref[0, tap : tap + 1, :] = jnp.sum(sums_ref[tap], axis=0, keepdims=True)
    small_ref[0, 27:28, :] = jnp.sum(dmix_ref[...].astype(F32), axis=0, keepdims=True)
    if communicate:

        @pl.when(step == 5)
        def _():
            end_halving()
            end_early()


def pool_back(sums, smalls, frames, grads, vhat, rs, mixed, taps, gain, same):
    smem = pl.BlockSpec(memory_space=pltpu.SMEM)
    group = pl.BlockSpec((ROWS, GROUP), lambda g: (0, g))
    out_shape = [jax.ShapeDtypeStruct((ROWS, QKV), BF16), jax.ShapeDtypeStruct((6, 32, GROUP), F32)]
    out_specs = [group, pl.BlockSpec((1, 32, GROUP), lambda g: (g, 0, 0))]
    scratch = [
        pltpu.VMEM((HEIGHT + 2, WIDTH + 2, FRAMES, GROUP), F32),
        pltpu.VMEM((HEIGHT + 2, WIDTH + 2, FRAMES, GROUP), F32),
        pltpu.VMEM((27, FRAMES, GROUP), F32),
        pltpu.VMEM((27, FRAMES, GROUP), F32),
    ]
    more = {}
    if sums:
        rows = [total.shape[3] for total in sums]
        for count in (*rows, EARLY_ROWS):
            out_shape.append(jax.ShapeDtypeStruct((count, LANES), F32))
            out_specs.append(whole((count, LANES)))
        for shape in ((2, 2), (2,), (), (2, 2), (2,)):
            scratch += [pltpu.VMEM((*shape, count, LANES), BF16) for count in rows]
        scratch += [pltpu.SemaphoreType.DMA((25,))] * 2
        scratch += [pltpu.VMEM((5, EARLY_ROWS, LANES), F32)] * 2
        scratch += [pltpu.SemaphoreType.DMA((5,))] * 2
        more = {"collective_id": 3, "has_side_effects": True}
    return pl.pallas_call(
        pool_back_kernel,
        grid=(6,),
        out_shape=tuple(out_shape),
        in_specs=[
            smem,
            pl.BlockSpec((1, GROUP_HEADS, ROWS, LANES), lambda g: (g // 2, g % 2, 0, 0)),
            group,
            group,
            group,
            pl.BlockSpec((1, 27, HEAD_DIM), lambda g: (g // 2, 0, 0)),
            whole((3, HEAD_DIM)),
            whole((GROUP, GROUP)),
        ]
        + [whole(value.shape) for value in (*sums, *smalls)],
        out_specs=tuple(out_specs),
        scratch_shapes=scratch,
        compiler_params=params(**more),
        name="pool_back",
    )(frames, grads, vhat, rs, mixed, taps, gain, same, *sums, *smalls)


def project_grad_kernel(place_ref, normed_ref, dmixed_ref, one_ref, two_ref, full_ref):
    for kind in range(3):
        grad = dot(normed_ref[...], dmixed_ref[:, kind * D : (kind + 1) * D], ((0,), (0,)))
        full_ref[:, kind * D : (kind + 1) * D] = grad.astype(BF16)
    half, columns = one_ref.shape[5:]
    for f in range(QKV // columns):

        @pl.loop(0, DP_BLOCKS)
        def _(d):
            bits = relative_bits(place_ref, d, f)
            lanes = slice(f * columns, (f + 1) * columns)
            at = pl.multiple_of(2 * d * half, half)
            one_ref[bits["c"], bits["x"], bits["y"], bits["z1"], bits["z2"]] = full_ref[pl.ds(at, half), lanes]
            at = pl.multiple_of((2 * d + 1) * half, half)
            two_ref[bits["c"], bits["y"], bits["x"], bits["z1"], bits["z2"]] = full_ref[pl.ds(at, half), lanes]


def project_grad(place, normed, dmixed, sides):
    vmem = pl.BlockSpec(memory_space=pltpu.VMEM)
    half = jax.ShapeDtypeStruct((2, 2, 2, 2, 2, D // DP_BLOCKS // 2, QKV // sides), BF16)
    return pl.pallas_call(
        project_grad_kernel,
        out_shape=(half, half),
        in_specs=[pl.BlockSpec(memory_space=pltpu.SMEM)] + [vmem] * 2,
        out_specs=(vmem, vmem),
        scratch_shapes=[pltpu.VMEM((D, QKV), BF16)],
        compiler_params=params(),
        name="project_grad",
    )(place, normed, dmixed)


def project_back_kernel(dmixed_ref, weight_ref, x_ref, dmid_ref, g1_ref, gtok_ref, small_ref, dx_ref, wide_ref):
    dy = dot(dmixed_ref[...], weight_ref[...], ((1,), (1,)))
    centred, rs = layer_stats(x_ref[...].astype(F32), D)
    vhat = centred * rs
    small_ref[0:1, :] = jnp.sum(dy * vhat, axis=0, keepdims=True)
    small_ref[1:2, :] = jnp.sum(dy, axis=0, keepdims=True)
    small_ref[2:8, :] = jnp.zeros((6, D), F32)
    scaled = dy * g1_ref[...]
    first = jnp.sum(scaled, axis=1, keepdims=True) * (1.0 / D)
    second = jnp.sum(scaled * vhat, axis=1, keepdims=True) * (1.0 / D)
    dx_ref[...] = dmid_ref[...] + rs * (scaled - first - vhat * second)

    @pl.loop(0, PLACES)
    def _(place):
        at = pl.multiple_of(place * FRAMES, FRAMES)
        write_place(wide_ref, place, dx_ref[pl.ds(at, FRAMES), :])

    for tile in range(D // LANES):
        gtok_ref[:, tile * LANES : (tile + 1) * LANES] = wide_ref[tile]


def project_back(dmixed, weight, x, dmid, g1):
    vmem = pl.BlockSpec(memory_space=pltpu.VMEM)
    return pl.pallas_call(
        project_back_kernel,
        out_shape=(jax.ShapeDtypeStruct((ROWS, D), F32), jax.ShapeDtypeStruct((8, D), F32)),
        in_specs=[vmem] * 5,
        out_specs=(vmem, vmem),
        scratch_shapes=[pltpu.VMEM((ROWS, D), F32), wide_scratch(D)],
        compiler_params=params(),
        name="project_back",
    )(dmixed, weight, x, dmid, g1)


VECTOR_ROWS = 144
WIDE_AT = 96


class Scatter:
    def __init__(self, blocks_ref, out_ref, vector_ref, from_core, from_first, from_second, from_z, sems):
        dp, fsdp = lax.axis_index("dp"), lax.axis_index("fsdp")
        self.z, self.x = dp // 2, dp % 2
        self.y, self.c = fsdp // 2, fsdp % 2
        self.blocks_ref, self.out_ref, self.vector_ref = blocks_ref, out_ref, vector_ref
        self.from_core, self.from_first, self.from_second, self.from_z = from_core, from_first, from_second, from_z
        self.send_sem, self.recv_sem, self.vector_send, self.vector_recv, self.vector_more = sems
        self.rows = blocks_ref.shape[4] // (2 * PARTS)
        self.copies = {}

    def device(self, z, x, y, c):
        return (2 * z + x, 2 * y + c)

    def begin(self):
        z, x, y, c = self.z, self.x, self.y, self.c
        self.along = [self.device((z + k) % 4, x, y, c) for k in (1, 2, 3)]
        self.over_x, self.over_y = self.device(z, 1 - x, y, c), self.device(z, x, 1 - y, c)
        self.over_c = self.device(z, x, y, 1 - c)
        barrier = pltpu.get_barrier_semaphore()
        for partner in self.along + [self.over_x, self.over_y, self.over_c]:
            pl.semaphore_signal(barrier, inc=1, device_id=partner, device_id_type=MESH)
        pl.semaphore_wait(barrier, 6)

    def copy(self, source, target, send_sem, recv_sem, partner):
        copy = pltpu.make_async_remote_copy(
            src_ref=source, dst_ref=target, send_sem=send_sem, recv_sem=recv_sem, device_id=partner, device_id_type=MESH
        )
        copy.start()
        return copy

    def span(self, part, route):
        return pl.ds((2 * part + route) * self.rows, self.rows)

    def send(self, part, level):
        z, x, y, c = self.z, self.x, self.y, self.c
        every = slice(None)
        blocks = self.blocks_ref
        for route in range(2):
            span = self.span(part, route)
            if level == 0:
                moves = [(blocks.at[every, every, every, 1 - c, span], self.from_core.at[every, every, every, span], self.over_c)]
            elif level == 1:
                where = (every, 1 - x, every, c, span) if route == 0 else (every, every, 1 - y, c, span)
                moves = [(blocks.at[where], self.from_first.at[every, every, span], self.over_y if route else self.over_x)]
            elif level == 2:
                where = (every, x, 1 - y, c, span) if route == 0 else (every, 1 - x, y, c, span)
                moves = [(blocks.at[where], self.from_second.at[every, span], self.over_x if route else self.over_y)]
            else:
                moves = [
                    (blocks.at[(z + k) % 4, x, y, c, span], self.from_z.at[k - 1, span], self.along[k - 1])
                    for k in (1, 2, 3)
                ]
            for at, (source, target, partner) in enumerate(moves):
                slot = (2 * part + route) * 6 + level + at
                self.copies[part, route, level, at] = self.copy(
                    source, target, self.send_sem.at[slot], self.recv_sem.at[slot], partner
                )

    def advance(self, part, level):
        z, x, y, c = self.z, self.x, self.y, self.c
        every = slice(None)
        blocks = self.blocks_ref
        for route in range(2):
            span = self.span(part, route)
            for at in range(3 if level == 3 else 1):
                self.copies[part, route, level, at].wait_recv()
            if level == 0:
                where, more = (every, every, every, c, span), self.from_core[:, :, :, span]
            elif level == 1:
                where = (every, x, every, c, span) if route == 0 else (every, every, y, c, span)
                more = self.from_first[:, :, span]
            elif level == 2:
                where, more = (every, x, y, c, span), self.from_second[:, span]
            if level < 3:
                blocks[where] = blocks[where] + more
            else:
                total = blocks[z, x, y, c, span].astype(F32)
                for k in range(3):
                    total = total + self.from_z[k, span].astype(F32)
                self.out_ref[span] = total
        if level < 3:
            self.send(part, level + 1)

    def steps(self):
        order = []
        for turn in range(PARTS + 3):
            for level in reversed(range(4)):
                if 0 <= turn - level < PARTS:
                    order.append((turn - level, level))
        return [functools.partial(self.advance, *step) for step in order]

    def send_vector(self, stage):
        z, x, y, c = self.z, self.x, self.y, self.c
        partner = (
            self.over_c, self.over_x, self.over_y, self.device(z + 1 - 2 * (z % 2), x, y, c), self.along[1]
        )[stage]
        self.copies["vector", stage] = self.copy(
            self.vector_ref.at[stage], self.vector_more.at[stage], self.vector_send.at[stage],
            self.vector_recv.at[stage], partner,
        )

    def advance_vector(self, stage):
        self.copies["vector", stage].wait_recv()
        self.vector_ref[stage + 1] = self.vector_ref[stage] + self.vector_more[stage]
        if stage < 4:
            self.send_vector(stage + 1)

    def end(self):
        for copy in self.copies.values():
            copy.wait_send()


def tail_kernel(
    turned_ref, dmixed_ref, weight_ref, x_ref, dmid_ref, g1_ref, pools_ref,
    gqkv_ref, dx_ref, done_ref,
    blocks_ref, vector_ref, from_core, from_first, from_second, from_z, *sems,
):
    scatter = Scatter(blocks_ref, gqkv_ref, vector_ref, from_core, from_first, from_second, from_z, sems)
    scatter.begin()
    steps = scatter.steps()

    def advance(count):
        for _ in range(min(count, len(steps))):
            steps.pop(0)()

    depth, columns = blocks_ref.shape[4:]
    rows = depth // PARTS
    for part in range(PARTS):
        turned = [turned_ref[d * depth + part * rows : d * depth + (part + 1) * rows] for d in range(DP_BLOCKS)]
        grad = dot(jnp.concatenate(turned, axis=0), dmixed_ref[...]).astype(BF16)
        for f in range(QKV // columns):
            for d in range(DP_BLOCKS):
                block = grad[d * rows : (d + 1) * rows, f * columns : (f + 1) * columns]
                blocks_ref[d // 2, d % 2, f // 2, f % 2, part * rows : (part + 1) * rows] = block
        scatter.send(part, 0)
        advance(part)
    dy = dot(dmixed_ref[...], weight_ref[...], ((1,), (1,)))
    advance(3)
    centred, rs = layer_stats(x_ref[...].astype(F32), D)
    vhat = centred * rs
    vector_ref[0] = jnp.zeros((VECTOR_ROWS, LANES), F32)
    for kind in range(3):
        sums = pools_ref[2 * kind] + pools_ref[2 * kind + 1]
        total = sums[:, :HEAD_DIM]
        for head in range(1, GROUP_HEADS):
            total = total + sums[:, HEAD_DIM * head : HEAD_DIM * (head + 1)]
        vector_ref[0, 32 * kind : 32 * kind + 32, :HEAD_DIM] = total
    lines = [jnp.sum(dy * vhat, axis=0, keepdims=True), jnp.sum(dy, axis=0, keepdims=True)]
    lines += [
        jnp.concatenate([pools_ref[2 * kind, 27:28, :], pools_ref[2 * kind + 1, 27:28, :]], axis=1)
        for kind in range(3)
    ]
    for tile in range(D // LANES):
        for at, line in enumerate(lines):
            vector_ref[0, WIDE_AT + 8 * tile + at : WIDE_AT + 8 * tile + at + 1] = line[:, tile * LANES : (tile + 1) * LANES]
    scatter.send_vector(0)
    advance(2)
    scatter.advance_vector(0)
    scaled = dy * g1_ref[...].reshape(1, D)
    first = jnp.sum(scaled, axis=1, keepdims=True) * (1.0 / D)
    second = jnp.sum(scaled * vhat, axis=1, keepdims=True) * (1.0 / D)
    dx_ref[...] = dmid_ref[...] + rs * (scaled - first - vhat * second)
    advance(2)
    scatter.advance_vector(1)

    advance(2)
    scatter.advance_vector(2)
    advance(2)
    scatter.advance_vector(3)
    advance(len(steps))
    scatter.advance_vector(4)
    done_ref[...] = vector_ref[5]
    scatter.end()


def tail(turned, dmixed, weight, x, dmid, g1, pools, shard):
    vmem = pl.BlockSpec(memory_space=pltpu.VMEM)
    depth, columns = shard
    shapes = [shard, (ROWS, D), (VECTOR_ROWS, LANES)]
    count = 2 * PARTS * 6
    return pl.pallas_call(
        tail_kernel,
        out_shape=tuple(jax.ShapeDtypeStruct(shape, F32) for shape in shapes),
        in_specs=[vmem] * 7,
        out_specs=(vmem,) * len(shapes),
        scratch_shapes=[
            pltpu.VMEM((4, 2, 2, 2, depth, columns), BF16),
            pltpu.VMEM((6, VECTOR_ROWS, LANES), F32),
            pltpu.VMEM((4, 2, 2, depth, columns), BF16),
            pltpu.VMEM((4, 2, depth, columns), BF16),
            pltpu.VMEM((4, depth, columns), BF16),
            pltpu.VMEM((3, depth, columns), BF16),
            pltpu.SemaphoreType.DMA((count,)),
            pltpu.SemaphoreType.DMA((count,)),
            pltpu.SemaphoreType.DMA((5,)),
            pltpu.SemaphoreType.DMA((5,)),
            pltpu.VMEM((5, VECTOR_ROWS, LANES), F32),
        ],
        compiler_params=params(collective_id=1, has_side_effects=True),
        name="tail",
    )(turned, dmixed, weight, x, dmid, g1, pools)


def finish_kernel(
    gqkv_ref, dx_ref, done_ref, one_ref, two_ref, one_rest_ref, two_rest_ref, proj_ref, early_ref,
    gtok_ref, ln1g_ref, ln1b_ref, wqkv_ref, qkvb_ref, conv_ref, pgain_ref, pbias_ref, time_ref, space_ref, comp_ref,
    wp_ref, projb_ref, ln2g_ref, ln2b_ref, w1_ref, fc1b_ref, w2_ref, fc2b_ref, wide_ref,
):
    @pl.loop(0, PLACES)
    def _(place):
        at = pl.multiple_of(place * FRAMES, FRAMES)
        write_place(wide_ref, place, dx_ref[pl.ds(at, FRAMES), :])

    for tile in range(D // LANES):
        gtok_ref[:, tile * LANES : (tile + 1) * LANES] = wide_ref[tile]
    wqkv_ref[...] = gqkv_ref[...]
    one = jnp.concatenate([one_ref[...], one_rest_ref[...]], axis=0)
    two = jnp.concatenate([two_ref[...], two_rest_ref[...]], axis=0)
    depth, part = w1_ref.shape[0], wp_ref.shape[1]
    for tile in range(w1_ref.shape[1] // LANES):
        w1_ref[:, tile * LANES : (tile + 1) * LANES] = one[tile * depth : (tile + 1) * depth]
    tiles = w2_ref.shape[1] // LANES
    for tile in range(tiles):
        w2_ref[:, tile * LANES : (tile + 1) * LANES] = two[tile * part : (tile + 1) * part]
    wp_ref[:, :LANES] = proj_ref[:depth]
    wp_ref[:, LANES:] = proj_ref[depth:, : part - LANES]
    for kind in range(3):
        conv_ref[kind] = done_ref[32 * kind : 32 * kind + 27, :HEAD_DIM]
        pgain_ref[kind : kind + 1, :] = done_ref[32 * kind + 28 : 32 * kind + 29, :HEAD_DIM]
        pbias_ref[kind : kind + 1, :] = done_ref[32 * kind + 29 : 32 * kind + 30, :HEAD_DIM]
    spans = 2 * HEIGHT - 1
    time_ref[...] = early_ref[:15, :HEAD_DIM]
    for s in range(2):
        start = 15 + spans * s
        space_ref[:, s] = early_ref[start : start + spans, :HEAD_DIM]
        comp_ref[s] = early_ref[EARLY_COMPRESS + 4 * s : EARLY_COMPRESS + 4 * s + 4, :HEAD_DIM]

    def line_of(source_ref, base, at):
        rows = [base + 8 * tile + at for tile in range(D // LANES)]
        return jnp.concatenate([source_ref[row : row + 1, :] for row in rows], axis=1).reshape(D)

    for at, target_ref in enumerate((projb_ref, ln2g_ref, ln2b_ref, fc2b_ref)):
        target_ref[...] = line_of(early_ref, EARLY_WIDE, at)
    for side in range(FF // D):
        fc1b_ref[side * D : (side + 1) * D] = line_of(early_ref, EARLY_WIDE, 4 + side)
    for at, target_ref in enumerate((ln1g_ref, ln1b_ref)):
        target_ref[...] = line_of(done_ref, WIDE_AT, at)
    for kind in range(3):
        qkvb_ref[kind * D : (kind + 1) * D] = line_of(done_ref, WIDE_AT, 2 + kind)


def finish(operands, w_qkv, w_proj, w_fc1, w_fc2):
    vmem = pl.BlockSpec(memory_space=pltpu.VMEM)
    shapes = [
        (ROWS, D), (D,), (D,), w_qkv, (QKV,), (3, 27, HEAD_DIM), (3, HEAD_DIM), (3, HEAD_DIM), (15, HEAD_DIM),
        (2 * HEIGHT - 1, 2, HEAD_DIM), (2, 4, HEAD_DIM), w_proj, (D,), (D,), (D,), w_fc1, (FF,), w_fc2[::-1], (D,),
    ]
    done = pl.pallas_call(
        finish_kernel,
        out_shape=tuple(jax.ShapeDtypeStruct(shape, F32) for shape in shapes),
        in_specs=[vmem] * 9,
        out_specs=(vmem,) * len(shapes),
        scratch_shapes=[wide_scratch(D)],
        compiler_params=params(),
        name="finish",
    )(*operands)
    done = list(done)
    done[9], done[17] = done[9].transpose(1, 0, 2), done[17].T
    return done


def row(vector):
    return vector.reshape(1, -1)


def tiled_lanes(array):
    return jnp.concatenate([array] * GROUP_HEADS, axis=-1)


def head_lanes(array):
    return jnp.pad(array, [(0, 0)] * (array.ndim - 1) + [(0, LANES - HEAD_DIM)])


DP_BLOCKS = 8
ROUTE_ONE = ("z2", "z1", "y", "x", "c")
ROUTE_TWO = ("z2", "z1", "x", "y", "c")


def together(*values):
    return lax.optimization_barrier(values)


def flat_shard(one, two, proj):
    pieces = [part for _, part in flat_pieces(one, two, proj)]
    pieces[-1] = jnp.pad(pieces[-1], ((0, 0), (0, LANES - pieces[-1].shape[1])))
    return jnp.concatenate(pieces, axis=0)


class Staged:
    def place(self):
        dp, fsdp = lax.axis_index("dp"), lax.axis_index("fsdp")
        return jnp.stack([dp & 1, (dp >> 1) & 1, (dp >> 2) & 1, (fsdp >> 1) & 1, fsdp & 1]).astype(jnp.int32)


class Plain:
    def __init__(self, dp, fsdp):
        self.dp, self.fsdp = dp, fsdp

    def place(self):
        return jnp.zeros((5,), jnp.int32)

    def gather(self, shard):
        blocks = lax.all_gather(shard, ("dp", "fsdp"), axis=0, tiled=False)
        rows, columns = shard.shape
        joined = blocks.reshape(DP_BLOCKS, self.dp // DP_BLOCKS, self.fsdp, rows, columns).transpose(0, 2, 1, 3, 4)
        return joined.reshape(DP_BLOCKS, self.fsdp, self.dp // DP_BLOCKS * rows, columns)

    def other_weights(self, one, two, proj):
        return jax.vmap(jax.vmap(flat_shard))(self.gather(one), jnp.swapaxes(self.gather(two), 2, 3), self.gather(proj))

    def scatter(self, blocks, route):
        at = {name: 4 - where for where, name in enumerate(route)}
        rows, columns = blocks.shape[5:]
        blocks = blocks.transpose([at[name] for name in ("z2", "z1", "x", "y", "c")] + [5, 6])
        split = blocks.reshape(DP_BLOCKS, self.fsdp, self.dp // DP_BLOCKS, rows * DP_BLOCKS // self.dp, columns)
        split = split.transpose(0, 2, 1, 3, 4).reshape(self.dp * self.fsdp, -1, columns)
        return lax.psum_scatter(split, ("dp", "fsdp"), scatter_dimension=0, tiled=False).astype(F32)

    def scatter_flat(self, low, high, route, unpack):
        blocks = jnp.concatenate([low[None], high[None]])
        blocks = jax.vmap(unpack)(blocks.reshape((32,) + blocks.shape[5:]))
        return self.scatter(blocks.reshape((2,) * 5 + blocks.shape[1:]), route)

    def total(self, vector):
        return lax.psum(vector, ("dp", "fsdp"))


def run(
    comm, staged, tokens, prev_kv, memory, valid_frames, mem_len, ln1_gain, ln1_bias, w_qkv, qkv_bias, pool_conv, pool_gain,
    pool_bias, rel_time, rel_space, compress, w_proj, proj_bias, ln2_gain, ln2_bias, w_fc1, fc1_bias, w_fc2,
    fc2_bias, cotangent,
):
    place = comm.place()
    fsdp = QKV // w_qkv.shape[1]
    one_hot, own, fold, pick, same = (jnp.asarray(c, BF16) for c in constants())
    taps, gains, biases = pool_conv, pool_gain, pool_bias
    prepared = prepare(
        valid_frames, mem_len, tokens, cotangent, ln1_gain, ln1_bias, one_hot, rel_time, rel_space.transpose(1, 0, 2), pick,
        prev_kv, memory, compress, [w_qkv, w_fc1, w_fc2.T, w_proj] if staged else None,
    )
    x, normed, turned, upstream, aug, table, rest, parts = prepared[-8:]
    if staged:
        first, wall = prepared[0].reshape(8, 4, *w_qkv.shape), prepared[1]
    else:
        first, wall = comm.gather(w_qkv), None
    heads, vhat, rs, mixed, weight, *wall = query_key_value(
        valid_frames, normed, first, qkv_bias, taps, gains, biases, same, wall
    )
    weights, pv, attended, *wall = attend(heads, rest, aug, table, own, fold, *wall)
    if staged:
        flat = wall[0].reshape(8, 4, *wall[0].shape[5:])
    else:
        flat = comm.other_weights(w_fc1, w_fc2, w_proj)
    out, dmid, datt, plow, phigh, low1, high1, low2, high2, small_two, gb1 = feed_forward(
        place, attended, x, upstream, flat, proj_bias, ln2_gain, ln2_bias, row(fc1_bias), fc2_bias
    )

    sent = [low1, high1, low2, high2, plow, phigh] if staged else []
    grads, gtable, gcompress, *sums = attend_back(
        sent, heads, rest, aug, table, own, fold, pick, weights, pv, datt, parts
    )
    smalls = [gtable, gcompress, small_two, gb1] if staged else []
    dmixed, pools, *sums = pool_back(sums, smalls, valid_frames, grads, vhat, rs, mixed, taps, gains, same)
    if staged:
        ended = tail(turned, dmixed, weight, x, dmid, ln1_gain, pools, w_qkv.shape)
        return (out, *finish((*ended, *sums), w_qkv.shape, w_proj.shape, w_fc1.shape, w_fc2.shape))
    depth, part = D // DP_BLOCKS, D // fsdp

    def unpack_one(block):
        return jnp.concatenate(list(block.reshape(-1, depth, LANES)), axis=1)

    def unpack_two(block):
        return jnp.concatenate(list(block.reshape(-1, part, LANES)), axis=1).T

    def unpack_proj(block):
        return jnp.concatenate([block[:depth], block[depth:, : part - LANES]], axis=1)

    w1_sum = comm.scatter_flat(low1, high1, ROUTE_ONE, unpack_one)
    w2_sum = comm.scatter_flat(low2, high2, ROUTE_TWO, unpack_two)
    wp_sum = comm.scatter_flat(plow, phigh, ROUTE_TWO, unpack_proj)
    qkv_one, qkv_two = project_grad(place, normed, dmixed, fsdp)
    gtok, small_one = project_back(dmixed, weight, x, dmid, row(ln1_gain))
    gbias = pools[:, 27].reshape(QKV)
    pools = jnp.sum(pools.reshape(3, 2, 32, GROUP_HEADS, HEAD_DIM), axis=(1, 3))
    gconv, gpool = pools[:, :27], pools[:, 28:30]
    smalls = (
        small_one[0], small_one[1], gbias, gconv, gpool[:, 0], gpool[:, 1],
        gtable[:15, :HEAD_DIM], gtable[15:53, :HEAD_DIM].reshape(2, 19, HEAD_DIM), gcompress[:, :, :HEAD_DIM],
        small_two[0], small_two[1], small_two[2], gb1[0], small_two[3],
    )
    vector = comm.total(jnp.concatenate([s.reshape(-1) for s in smalls]))
    totals, at = [], 0
    for s in smalls:
        totals.append(vector[at : at + s.size].reshape(s.shape))
        at += s.size
    qkv = comm.scatter(jnp.concatenate([qkv_one, jnp.moveaxis(qkv_two, 1, 2)], axis=5), ROUTE_ONE)
    sums = [qkv, wp_sum, w1_sum, w2_sum]
    return (
        out, gtok, totals[0], totals[1], sums[0], totals[2], totals[3], totals[4], totals[5], totals[6],
        totals[7], totals[8], sums[1], totals[9], totals[10], totals[11], sums[2], totals[12], sums[3], totals[13],
    )


def solution(mesh):
    both = P(("dp", "fsdp"))
    rows = P(("dp", "fsdp"), None)
    second = P(None, ("dp", "fsdp"), None)
    blocks = P("dp", "fsdp")
    none = P()
    dp, fsdp = mesh.shape["dp"], mesh.shape["fsdp"]
    staged = (dp, fsdp) == (8, 4)
    return jax.shard_map(
        functools.partial(run, Staged() if staged else Plain(dp, fsdp), staged),
        mesh=mesh,
        in_specs=(
            rows, second, second, both, both, none, none, blocks, none, none, none, none, none, none, none, blocks,
            none, none, none, blocks, none, blocks, none, rows,
        ),
        out_specs=(
            rows, rows, none, none, blocks, none, none, none, none, none, none, none, blocks, none, none, none,
            blocks, none, blocks, none,
        ),
        check_vma=False,
    )
```

```python
import functools

import jax
import jax.numpy as jnp
import numpy as np
from jax import lax
from jax.experimental import pallas as pl
from jax.experimental.pallas import tpu as pltpu
from jax.sharding import PartitionSpec as P

D = 768
FF = 3072
HEADS = 8
HEAD_DIM = 96
LANES = 128
FRAMES = 8
HEIGHT = 10
WIDTH = 10
PLACES = HEIGHT * WIDTH
ROWS = 800
MEM = 200
GROUP = 384
GROUP_HEADS = 4
QKV = 3 * D
KEY_ROWS = 1280
MEM_AT = 800
SQUEEZE_AT = 1024
REST = KEY_ROWS - ROWS
TABLE = 384
EPSILON = 1e-06
SCALE = HEAD_DIM**-0.5
ROOT = HEAD_DIM**0.5
LOG2E = 1.4426950408889634
MASKED = -1e9
MASK_LANE = 124
FORWARD_ROWS = (slice(0, 272), slice(272, 544), slice(544, 800))
BACKWARD_ROWS = (slice(0, 208), slice(208, 400), slice(400, 608), slice(608, 800))
BF16 = jnp.bfloat16
F32 = jnp.float32
VMEM_LIMIT = 60 * 1024 * 1024


def constants():
    place = np.arange(PLACES).repeat(FRAMES)
    row_t = np.tile(np.arange(FRAMES), PLACES)
    row_i, row_j = place // WIDTH, place % WIDTH
    one_hot = np.zeros((KEY_ROWS, LANES), np.float32)
    rows = np.arange(ROWS)
    one_hot[rows, 96 + row_t] = 1
    one_hot[rows, 104 + row_i] = 1
    one_hot[rows, 114 + row_j] = 1
    own = np.zeros((ROWS, TABLE), np.float32)
    fold = np.zeros((TABLE, LANES), np.float32)
    pick = np.zeros((TABLE, LANES), np.float32)
    for base, length, row_at, lane, offset in (
        (0, FRAMES, row_t, 96, 0),
        (64, HEIGHT, row_i, 104, 15),
        (164, WIDTH, row_j, 114, 34),
    ):
        for a in range(length):
            for b in range(length):
                column = base + a * length + b
                own[:, column] = row_at == a
                fold[column, lane + b] = 1
                pick[column, offset + a - b + length - 1] = 1
    lanes = np.arange(GROUP) // HEAD_DIM
    same = (lanes[:, None] == lanes[None, :]).astype(np.float32)
    return one_hot, own, fold, pick, same


def lane_index(shape):
    return lax.broadcasted_iota(jnp.int32, shape, len(shape) - 1)


def dot(a, b, contract=((1,), (0,)), precision=None):
    return lax.dot_general(a, b, (contract, ((), ())), preferred_element_type=F32, precision=precision)


def layer_stats(values, width):
    average = jnp.sum(values, axis=-1, keepdims=True) * (1.0 / width)
    centred = values - average
    variance = jnp.sum(centred * centred, axis=-1, keepdims=True) * (1.0 / width)
    return centred, lax.rsqrt(variance + EPSILON)


def params(**more):
    return pltpu.CompilerParams(vmem_limit_bytes=VMEM_LIMIT, **more)


def whole(shape):
    return pl.BlockSpec(shape, lambda *_: (0,) * len(shape))


def tiles_of(values):
    return [values[:, at : at + LANES] for at in range(0, values.shape[1], LANES)]


def flat_pieces(one, two, proj):
    at = 0
    for part in tiles_of(one) + tiles_of(two) + tiles_of(proj):
        yield at, part
        at += part.shape[0]


def read_place(wide_ref, place, tiles=D // LANES):
    parts = [wide_ref[tile, pl.ds(place, FRAMES, stride=PLACES), :] for tile in range(tiles)]
    return jnp.concatenate(parts, axis=1)


def write_place(wide_ref, place, values):
    for tile, part in enumerate(tiles_of(values)):
        wide_ref[tile, pl.ds(place, FRAMES, stride=PLACES), :] = part


def wide_scratch(columns):
    return pltpu.VMEM((columns // LANES, ROWS, LANES), F32)


PARTS = 3
WALL_AFTER = 6
MESH = pl.DeviceIdType.MESH


class Neighbours:
    def __init__(self):
        dp, fsdp = lax.axis_index("dp"), lax.axis_index("fsdp")
        z, x, y, c = dp // 2, dp % 2, fsdp // 2, fsdp % 2
        self.over = {
            "c": (dp, 2 * y + 1 - c),
            "x": (2 * z + 1 - x, fsdp),
            "y": (dp, 2 * (1 - y) + c),
            "z1": (2 * (z + 1 - 2 * (z % 2)) + x, fsdp),
            "z2": (2 * ((z + 2) % 4) + x, fsdp),
        }

    def greet(self, names):
        barrier = pltpu.get_barrier_semaphore()
        for name in names:
            pl.semaphore_signal(barrier, inc=1, device_id=self.over[name], device_id_type=MESH)
        pl.semaphore_wait(barrier, len(names))

    def copy(self, name, source, target, sems, at):
        return pltpu.make_async_remote_copy(
            src_ref=source,
            dst_ref=target,
            send_sem=sems[0].at[at],
            recv_sem=sems[1].at[at],
            device_id=self.over[name],
            device_id_type=MESH,
        )


PLACE_DIMS = ("z2", "z1", "x", "y", "c")
WALL_ROUTES = (
    ("z2", "z1", "y", "x", "c"),
    ("z2", "z1", "x", "y", "c"),
    ("z2", "y", "x", "z1", "c"),
    ("z2", "x", "y", "z1", "c"),
)


class Doubling:
    def __init__(self, near, wall_ref, sems):
        dp, fsdp = lax.axis_index("dp"), lax.axis_index("fsdp")
        self.mine = {"z2": dp // 4, "z1": dp // 2 % 2, "x": dp % 2, "y": fsdp // 2, "c": fsdp % 2}
        self.near, self.wall_ref, self.sems = near, wall_ref, sems
        rows = wall_ref.shape[5]
        third = rows // 3
        self.spans = ((0, third), (third, third), (2 * third, third // 2), (2 * third + third // 2, third // 2))
        self.made = {}

    def region(self, piece, free, other=()):
        where = [
            slice(None) if name in free else (1 - self.mine[name] if name in other else self.mine[name])
            for name in PLACE_DIMS
        ]
        return self.wall_ref.at[(*where, pl.ds(*self.spans[piece]))]

    def plan(self, *key):
        self.made[key] = functools.partial(self.make, *key, len(self.made))

    def make(self, piece, stage, part, at):
        route = WALL_ROUTES[piece]
        if stage < 4:
            free = route[: max(stage - 1, 0)]
            place = self.region(piece, free, route[stage - 1 : stage] if part else ())
        else:
            free, other = ((route[:3], ()), (route[:2], (route[3],)), (route[:2], (route[3], route[2])))[part]
            place = self.region(piece, free, other)
        return self.near.copy(route[stage], place, place, self.sems, at)

    def start(self, *keys):
        for key in keys:
            self.made[key]().start()

    def arrive(self, *keys):
        for key in keys:
            self.made[key]().wait_recv()

    def end(self):
        for make in self.made.values():
            make().wait_send()


FLAT, UPRIGHT, EVERY_PIECE = (0, 1), (2, 3), (0, 1, 2, 3)


def keys_of(pieces, stage, *parts):
    return [(piece, stage, part) for piece in pieces for part in parts]


def doubling_in_queries(wall_ref, sems):
    step = pl.program_id(0)
    doubling = Doubling(Neighbours(), wall_ref, sems)
    early = keys_of(FLAT, 1, 1) + keys_of(FLAT, 2, 0) + keys_of(UPRIGHT, 1, 0, 1) + keys_of(UPRIGHT, 2, 0)
    later = keys_of(EVERY_PIECE, 2, 1) + keys_of(EVERY_PIECE, 3, 0)
    for key in early + later:
        doubling.plan(*key)

    @pl.when(step == 0)
    def _():
        doubling.near.greet(("x", "y", "z1"))
        doubling.start(*early)

    @pl.when(step == 2)
    def _():
        doubling.arrive(*keys_of(FLAT, 1, 1), *keys_of(UPRIGHT, 1, 0, 1))
        doubling.start(*later)

    def end():
        @pl.when(step == 5)
        def _():
            doubling.arrive(*keys_of(EVERY_PIECE, 2, 0, 1), *keys_of(EVERY_PIECE, 3, 0))
            doubling.end()

    return end


def doubling_in_attention(wall_ref, sems):
    step = pl.program_id(0)
    doubling = Doubling(Neighbours(), wall_ref, sems)
    early = keys_of(EVERY_PIECE, 3, 1) + keys_of(EVERY_PIECE, 4, 0, 1)
    later = keys_of(EVERY_PIECE, 4, 2)
    for key in early + later:
        doubling.plan(*key)

    @pl.when(step == 0)
    def _():
        doubling.near.greet(("x", "y", "z1", "c"))
        doubling.start(*early)

    @pl.when(step == 5)
    def _():
        doubling.arrive(*keys_of(EVERY_PIECE, 3, 1))
        doubling.start(*later)

    def end():
        @pl.when(step == HEADS - 1)
        def _():
            doubling.arrive(*keys_of(EVERY_PIECE, 4, 0, 1, 2))
            doubling.end()

    return end


class Gather:
    def __init__(self, shard_ref, all_ref, own_sem, send_sem, recv_sem):
        dp, fsdp = lax.axis_index("dp"), lax.axis_index("fsdp")
        self.z, self.x = dp // 2, dp % 2
        self.y, self.c = fsdp // 2, fsdp % 2
        self.shard_ref, self.all_ref = shard_ref, all_ref
        self.own_sem, self.send_sem, self.recv_sem = own_sem, send_sem, recv_sem
        self.rows = shard_ref.shape[0] // (2 * PARTS)
        self.copies = {}

    def device(self, z, x, y, c):
        return (2 * z + x, 2 * y + c)

    def partners(self):
        z, x, y, c = self.z, self.x, self.y, self.c
        along = [self.device((z + k) % 4, x, y, c) for k in (1, 2, 3)]
        return along + [self.device(z, 1 - x, y, c), self.device(z, x, 1 - y, c), self.device(z, x, y, 1 - c)]

    def begin(self):
        barrier = pltpu.get_barrier_semaphore()
        for partner in self.partners():
            pl.semaphore_signal(barrier, inc=1, device_id=partner, device_id_type=MESH)
        self.own = pltpu.make_async_copy(self.shard_ref, self.all_ref.at[self.z, self.x, self.y, self.c], self.own_sem)
        self.own.start()
        pl.semaphore_wait(barrier, 6)
        self.send_along(0)

    def send_along(self, part):
        if part < PARTS:
            for route in range(2):
                for stage in range(3):
                    self.send(part, route, stage)

    def send(self, part, route, stage):
        z, x, y, c = self.z, self.x, self.y, self.c
        rows = pl.ds((2 * part + route) * self.rows, self.rows)
        partner = self.partners()[stage if stage < 3 or stage == 5 else 3 + (stage - 3 + route) % 2]
        every = slice(None)
        if stage < 3:
            place = (z, x, y, c)
        elif stage == 3:
            place = (every, x, y, c)
        elif stage == 4:
            place = (every, every, y, c) if route == 0 else (every, x, every, c)
        else:
            place = (every, every, every, c)
        target = self.all_ref.at[(*place, rows)]
        source = self.shard_ref.at[rows] if stage < 3 else target
        at = (2 * part + route) * 6 + stage
        copy = pltpu.make_async_remote_copy(
            src_ref=source,
            dst_ref=target,
            send_sem=self.send_sem.at[at],
            recv_sem=self.recv_sem.at[at],
            device_id=partner,
            device_id_type=MESH,
        )
        copy.start()
        self.copies[part, route, stage] = copy

    def advance(self, part, level):
        if level == 0 and part == 0:
            self.own.wait()
        for route in range(2):
            for stage in ((0, 1, 2), (3,), (4,), (5,))[level]:
                self.copies[part, route, stage].wait_recv()
        if level == 0:
            self.send_along(part + 1)
        if level < 3:
            for route in range(2):
                self.send(part, route, 3 + level)

    def steps(self):
        order = []
        for turn in range(PARTS + 3):
            for level in reversed(range(4)):
                if 0 <= turn - level < PARTS:
                    order.append((turn - level, level))
        return [functools.partial(self.advance, *step) for step in order]

    def end(self):
        for copy in self.copies.values():
            copy.wait_send()


def prepare_kernel(
    communicate, frames_ref, length_ref, tokens_hbm, cot_hbm, gain_ref, bias_ref, one_hot_ref, time_ref, space_ref,
    pick_ref, prev_hbm, mem_hbm, taps_ref, *refs,
):
    if communicate:
        shard_ref, one_ref, two_ref, proj_ref, all_ref, wall_ref = refs[:6]
        refs = refs[6:]
    x_hbm, normed_hbm, turned_hbm, upstream_hbm, aug_ref, table_ref, rest_hbm, tap_hbm = refs[:8]
    wide_ref, sums_ref, parts_ref, tables_ref = refs[8:12]
    tokens_ref, cot_ref, prev_ref, mem_ref, x_ref, normed_ref, turned_ref, upstream_ref, rest_ref, tap_ref = refs[12:22]
    in_sem, out_sem, refs = refs[22], refs[23], refs[24:]
    loads = [
        pltpu.make_async_copy(source, target, in_sem.at[at])
        for at, (source, target) in enumerate(
            ((cot_hbm, cot_ref), (tokens_hbm, tokens_ref), (prev_hbm, prev_ref), (mem_hbm, mem_ref))
        )
    ]
    for load in loads:
        load.start()
    saves = []

    def save(source, target):
        saves.append(pltpu.make_async_copy(source, target, out_sem.at[len(saves)]))
        saves[-1].start()

    steps = []
    if communicate:
        flat_ref, wall_own_sem, wall_send_sem, wall_recv_sem = refs[:4]
        gather = Gather(shard_ref, all_ref, *refs[4:])
        gather.begin()
        for at, part in flat_pieces(one_ref[...], two_ref[...], proj_ref[...]):
            short = jnp.zeros((part.shape[0], LANES - part.shape[1]), BF16)
            flat_ref[at : at + part.shape[0]] = jnp.concatenate([part, short], axis=1) if short.size else part
        doubling = Doubling(Neighbours(), wall_ref, (wall_send_sem, wall_recv_sem))
        first_stage = keys_of(EVERY_PIECE, 0, 0) + keys_of(FLAT, 1, 0)
        for key in first_stage:
            doubling.plan(*key)
        here = tuple(doubling.mine[name] for name in PLACE_DIMS)
        own = pltpu.make_async_copy(flat_ref, wall_ref.at[here], wall_own_sem)
        own.start()

        def first_doubling():
            own.wait()
            doubling.start(*first_stage)

        steps = gather.steps()
        steps.insert(WALL_AFTER, first_doubling)

    def advance(count=1):
        for _ in range(min(count, len(steps))):
            steps.pop(0)()

    def permute(source_ref, target_ref):
        for tile, part in enumerate(tiles_of(source_ref[...])):
            wide_ref[tile] = part.astype(F32)

        @pl.loop(0, PLACES // 2)
        def _(pair):
            first = read_place(wide_ref, 2 * pair)
            second = read_place(wide_ref, 2 * pair + 1)
            at = pl.multiple_of(pair * 16, 16)
            target_ref[pl.ds(at, 16), :] = jnp.concatenate([first, second], axis=0).astype(BF16)

    loads[0].wait()
    permute(cot_ref, upstream_ref)
    save(upstream_ref, upstream_hbm)
    loads[1].wait()
    permute(tokens_ref, x_ref)
    save(x_ref, x_hbm)
    advance()
    centred, rs = layer_stats(x_ref[...].astype(F32), D)
    normed_ref[...] = (centred * rs * gain_ref[...].reshape(1, D) + bias_ref[...].reshape(1, D)).astype(BF16)
    turned_ref[...] = normed_ref[...].T
    save(normed_ref, normed_hbm)
    save(turned_ref, turned_hbm)
    row = lax.broadcasted_iota(jnp.int32, (KEY_ROWS, LANES), 0)
    frames, length = frames_ref[0], length_ref[0]
    place = jnp.where(row < MEM_AT, row & 7, jnp.where(row < SQUEEZE_AT, row - MEM_AT, row - SQUEEZE_AT))
    limit = jnp.where(row < MEM_AT, frames, jnp.where(row < SQUEEZE_AT, length, MEM))
    off = jnp.where(place >= limit, jnp.where(lane_index((KEY_ROWS, LANES)) == MASK_LANE, MASKED, 0.0), 0.0)
    aug_ref[...] = (one_hot_ref[...].astype(F32) + off).astype(BF16)
    tables_ref[...] = jnp.zeros((LANES, LANES), F32)
    spans = 2 * HEIGHT - 1
    tables_ref[0 : 2 * FRAMES - 1, :HEAD_DIM] = time_ref[...]
    for s in range(2):
        tables_ref[15 + spans * s : 15 + spans * (s + 1), :HEAD_DIM] = space_ref[:, s]
    table_ref[...] = dot(pick_ref[...], tables_ref[...].astype(BF16)).astype(BF16)
    advance()

    def head_of(values, head):
        return values[:, HEAD_DIM * head : HEAD_DIM * head + HEAD_DIM]

    loads[2].wait()
    loads[3].wait()
    for s in range(2):
        for group in range(2):
            columns = slice(group * GROUP, (group + 1) * GROUP)
            for tile, part in enumerate(tiles_of(prev_ref[s, :, columns])):
                wide_ref[tile] = part.astype(F32)

            taps = [tiled_lanes(taps_ref[s, tap : tap + 1, :]) for tap in range(4)]

            @pl.loop(0, HEIGHT // 2)
            def _(i):
                for j in range(WIDTH // 2):
                    total = None
                    at = pl.multiple_of((i * (WIDTH // 2) + j) * FRAMES, FRAMES)
                    for tap in range(4):
                        place = (2 * i + tap // 2) * WIDTH + 2 * j + tap % 2
                        part = read_place(wide_ref, place, GROUP // LANES)
                        parts_ref[tap, pl.ds(at, FRAMES), :] = part
                        term = part * taps[tap]
                        total = term if total is None else total + term
                    sums_ref[pl.ds(at, FRAMES), :] = total

            old = mem_ref[s, :, columns].astype(F32)
            for head in range(GROUP_HEADS):
                rest = jnp.concatenate(
                    [
                        head_of(old, head),
                        jnp.zeros((SQUEEZE_AT - MEM_AT - MEM, HEAD_DIM), F32),
                        head_of(sums_ref[...], head),
                        jnp.zeros((KEY_ROWS - SQUEEZE_AT - MEM, HEAD_DIM), F32),
                    ],
                    axis=0,
                )
                rest = jnp.concatenate([rest, jnp.zeros((REST, LANES - HEAD_DIM), F32)], axis=1)
                rest_ref[s, group * GROUP_HEADS + head] = rest.astype(BF16)
                for tap in range(4):
                    part = jnp.concatenate([head_of(parts_ref[tap], head), jnp.zeros((8, HEAD_DIM), F32)], axis=0)
                    part = jnp.concatenate([part, jnp.zeros((208, LANES - HEAD_DIM), F32)], axis=1)
                    tap_ref[s, group * GROUP_HEADS + head, tap] = part.astype(BF16)
            heads = pl.ds(group * GROUP_HEADS, GROUP_HEADS)
            save(rest_ref.at[s, heads], rest_hbm.at[s, heads])
            save(tap_ref.at[s, heads], tap_hbm.at[s, heads])
            advance(3 if group + s else 2)
    advance(len(steps))
    for saved in saves:
        saved.wait()
    if communicate:
        doubling.arrive(*first_stage)
        doubling.end()
        gather.end()


def prepare(frames, length, tokens, cot, gain, bias, one_hot, rel_time, rel_space, pick, prev, memory, taps, shards=None):
    smem = pl.BlockSpec(memory_space=pltpu.SMEM)
    vmem = pl.BlockSpec(memory_space=pltpu.VMEM)
    communicate = shards is not None
    out_shape = [
        jax.ShapeDtypeStruct((ROWS, D), BF16),
        jax.ShapeDtypeStruct((ROWS, D), BF16),
        jax.ShapeDtypeStruct((D, ROWS), BF16),
        jax.ShapeDtypeStruct((ROWS, D), BF16),
        jax.ShapeDtypeStruct((KEY_ROWS, LANES), BF16),
        jax.ShapeDtypeStruct((TABLE, LANES), BF16),
        jax.ShapeDtypeStruct((2, HEADS, REST, LANES), BF16),
        jax.ShapeDtypeStruct((2, HEADS, 4, 208, LANES), BF16),
    ]
    anywhere = pl.BlockSpec(memory_space=pl.ANY)
    in_specs = [smem, smem, anywhere, anywhere] + [vmem] * 6 + [anywhere, anywhere, vmem]
    out_specs = [anywhere] * 4 + [vmem] * 2 + [anywhere] * 2
    operands = [frames, length, tokens, cot, gain, bias, one_hot, rel_time, rel_space, pick, prev, memory, taps]
    scratch = [
        wide_scratch(D),
        pltpu.VMEM((MEM, GROUP), F32),
        pltpu.VMEM((4, MEM, GROUP), F32),
        pltpu.VMEM((LANES, LANES), F32),
    ]
    scratch += [pltpu.VMEM(value.shape, value.dtype) for value in (tokens, cot, prev, memory)]
    scratch += [pltpu.VMEM(out_shape[at].shape, BF16) for at in (0, 1, 2, 3, 6, 7)]
    scratch += [pltpu.SemaphoreType.DMA((4,)), pltpu.SemaphoreType.DMA((12,))]
    more = {}
    if communicate:
        shard, one, two, proj = shards
        rows = (one.size + two.size) // LANES + 2 * proj.shape[0]
        out_shape = [
            jax.ShapeDtypeStruct((4, 2, 2, 2) + shard.shape, BF16),
            jax.ShapeDtypeStruct((2, 2, 2, 2, 2, rows, LANES), BF16),
        ] + out_shape
        in_specs += [anywhere, vmem, vmem, vmem]
        out_specs = [anywhere, anywhere] + out_specs
        operands += shards
        count = 2 * PARTS * 6
        scratch += [pltpu.VMEM((rows, LANES), BF16), pltpu.SemaphoreType.DMA]
        scratch += [pltpu.SemaphoreType.DMA((6,)), pltpu.SemaphoreType.DMA((6,))]
        scratch += [pltpu.SemaphoreType.DMA, pltpu.SemaphoreType.DMA((count,)), pltpu.SemaphoreType.DMA((count,))]
        more = {"collective_id": 0, "has_side_effects": True}
    return pl.pallas_call(
        functools.partial(prepare_kernel, communicate),
        out_shape=tuple(out_shape),
        in_specs=in_specs,
        out_specs=tuple(out_specs),
        scratch_shapes=scratch,
        compiler_params=params(**more),
        name="prepare",
    )(*operands)


def shift_frames(values, step):
    frame = lax.broadcasted_iota(jnp.int32, values.shape, values.ndim - 2)
    moved = pltpu.roll(values, step % FRAMES, values.ndim - 2)
    edge = 0 if step == 1 else FRAMES - 1
    return jnp.where(frame == edge, 0.0, moved)


def convolve(grid_ref, taps_ref, flip, i, lanes):
    sums = [None, None, None]
    for b in range(3):
        for e in range(3):
            window = grid_ref[i + b, e : e + WIDTH, :, lanes]
            for a in range(3):
                tap = 9 * a + 3 * b + e
                term = window * taps_ref[26 - tap if flip else tap, :, lanes][None]
                sums[a] = term if sums[a] is None else sums[a] + term
    return sums[1] + shift_frames(sums[0], 1) + shift_frames(sums[2], -1)


def spread_taps(raw_ref, taps_ref):
    for tap in range(27):
        line = tiled_lanes(raw_ref[0, tap : tap + 1, :])
        taps_ref[tap] = jnp.broadcast_to(line, (FRAMES, GROUP))


def clear_border(grid_ref):
    grid_ref[...] = jnp.zeros(grid_ref.shape, grid_ref.dtype)


def relative_bits(place_ref, d, f):
    return {
        "x": (d & 1) ^ place_ref[0],
        "z1": ((d >> 1) & 1) ^ place_ref[1],
        "z2": ((d >> 2) & 1) ^ place_ref[2],
        "y": ((f >> 1) & 1) ^ place_ref[3],
        "c": (f & 1) ^ place_ref[4],
    }


def slot(bits, order):
    return sum(bits[name] << at for at, name in enumerate(order))


def qkv_kernel(
    frames_ref, normed_ref, shards_ref, qkv_bias_ref, taps_raw_ref, gain_ref, bias_ref, same_ref, *refs,
):
    communicate = len(refs) > 9
    if communicate:
        refs, end = (*refs[1:6], *refs[7:11]), doubling_in_queries(refs[6], refs[11:])
    heads_ref, vhat_ref, rs_ref, mixed_ref, weight_ref, grid_ref, pooled_ref, taps_ref, line_ref = refs
    step = pl.program_id(0)

    @pl.when(step == 0)
    def _():
        clear_border(grid_ref)
        line_ref[...] = qkv_bias_ref[...].reshape(1, QKV)
        depth, columns = shards_ref.shape[2:]
        for f in range(QKV // columns):
            for d in range(DP_BLOCKS):
                weight_ref[d * depth : (d + 1) * depth, f * columns : (f + 1) * columns] = shards_ref[d, f]

    @pl.when(step % 2 == 0)
    def _():
        spread_taps(taps_raw_ref, taps_ref)

    at = pl.multiple_of(step * GROUP, LANES)
    mixed = dot(normed_ref[...], weight_ref[:, pl.ds(at, GROUP)]) + line_ref[:, pl.ds(at, GROUP)]
    row = lax.broadcasted_iota(jnp.int32, (ROWS, GROUP), 0)
    mixed = jnp.where((row & 7) < frames_ref[0], mixed, 0.0)
    mixed_ref[...] = mixed.astype(BF16)
    grid_ref[1 : HEIGHT + 1, 1 : WIDTH + 1] = mixed.reshape(HEIGHT, WIDTH, FRAMES, GROUP)

    @pl.loop(0, HEIGHT)
    def _(i):
        for tile in range(GROUP // LANES):
            lanes = slice(tile * LANES, tile * LANES + LANES)
            line = convolve(grid_ref, taps_ref, False, i, lanes)
            at = pl.multiple_of(i * WIDTH * FRAMES, WIDTH * FRAMES)
            pooled_ref[pl.ds(at, WIDTH * FRAMES), lanes] = line.reshape(WIDTH * FRAMES, LANES)

    pooled = pooled_ref[...]
    high = pooled.astype(BF16)
    low = (pooled - high.astype(F32)).astype(BF16)
    centred = pooled - (dot(high, same_ref[...]) + dot(low, same_ref[...])) * (1.0 / HEAD_DIM)
    variance = dot((centred * centred).astype(BF16), same_ref[...]) * (1.0 / HEAD_DIM)
    rs = lax.rsqrt(variance + EPSILON)
    vhat = centred * rs
    rs_ref[...] = rs
    vhat_ref[...] = vhat.astype(BF16)
    kind = pl.ds(step // 2, 1)
    out = (vhat * tiled_lanes(gain_ref[kind, :]) + tiled_lanes(bias_ref[kind, :])).astype(BF16)
    for head in range(GROUP_HEADS):
        own = out[:, HEAD_DIM * head : HEAD_DIM * (head + 1)]
        heads_ref[head] = jnp.concatenate([own, jnp.zeros((ROWS, LANES - HEAD_DIM), BF16)], axis=1)
    if communicate:
        end()


def wall_more(wall, out_shape, out_specs, scratch, operands, collective_id):
    if wall is None:
        return {}, {}
    anywhere = pl.BlockSpec(memory_space=pl.ANY)
    out_shape.append(jax.ShapeDtypeStruct(wall.shape, wall.dtype))
    out_specs.append(anywhere)
    scratch += [pltpu.SemaphoreType.DMA((18,)), pltpu.SemaphoreType.DMA((18,))]
    operands.append(wall)
    return {"collective_id": collective_id, "has_side_effects": True}, {len(operands) - 1: len(out_shape) - 1}


def query_key_value(frames, normed, shards, qkv_bias, taps, gain, bias, same, wall=None):
    smem = pl.BlockSpec(memory_space=pltpu.SMEM)
    group = pl.BlockSpec((ROWS, GROUP), lambda g: (0, g))
    out_shape = [
        jax.ShapeDtypeStruct((3 * HEADS, ROWS, LANES), BF16),
        jax.ShapeDtypeStruct((ROWS, QKV), BF16),
        jax.ShapeDtypeStruct((ROWS, QKV), F32),
        jax.ShapeDtypeStruct((ROWS, QKV), BF16),
        jax.ShapeDtypeStruct((D, QKV), BF16),
    ]
    out_specs = [
        pl.BlockSpec((GROUP_HEADS, ROWS, LANES), lambda g: (g, 0, 0)), group, group, group, whole((D, QKV))
    ]
    scratch = [
        pltpu.VMEM((HEIGHT + 2, WIDTH + 2, FRAMES, GROUP), F32),
        pltpu.VMEM((ROWS, GROUP), F32),
        pltpu.VMEM((27, FRAMES, GROUP), F32),
        pltpu.VMEM((1, QKV), F32),
    ]
    operands = [frames, normed, shards, qkv_bias, taps, gain, bias, same]
    in_specs = [
        smem,
        whole((ROWS, D)),
        whole(shards.shape),
        whole((QKV,)),
        pl.BlockSpec((1, 27, HEAD_DIM), lambda g: (g // 2, 0, 0)),
        whole((3, HEAD_DIM)),
        whole((3, HEAD_DIM)),
        whole((GROUP, GROUP)),
    ]
    more, aliases = wall_more(wall, out_shape, out_specs, scratch, operands, 4)
    return pl.pallas_call(
        qkv_kernel,
        grid=(6,),
        out_shape=tuple(out_shape),
        in_specs=in_specs + [pl.BlockSpec(memory_space=pl.ANY)] * len(aliases),
        out_specs=tuple(out_specs),
        scratch_shapes=scratch,
        input_output_aliases=aliases,
        compiler_params=params(**more),
        name="query_key_value",
    )(*operands)


def attend_kernel(
    q_ref, k_ref, v_ref, krest_ref, vrest_ref, aug_ref, table_ref, own_ref, fold_ref, *refs,
):
    communicate = len(refs) > 6
    if communicate:
        refs, end = (*refs[1:4], *refs[5:8]), doubling_in_attention(refs[4], refs[8:])
    weights_ref, pv_ref, out_ref, keys_ref, vals_ref, query_ref = refs
    lane = lane_index((KEY_ROWS, LANES))
    keys_ref[:ROWS] = k_ref[0] + aug_ref[:ROWS]
    keys_ref[ROWS:] = krest_ref[0, 0] + aug_ref[ROWS:]
    one = jnp.where(lane == HEAD_DIM, 1.0, 0.0).astype(BF16)
    vals_ref[:ROWS] = v_ref[0] + one[:ROWS]
    vals_ref[ROWS:] = vrest_ref[0, 0] + one[ROWS:]
    query = q_ref[0]
    every = (dot(query, table_ref[...], ((1,), (1,))) * ROOT).astype(BF16) * own_ref[...]
    relative = dot(every, fold_ref[...])
    marked = jnp.where(lane[:ROWS] == MASK_LANE, 1.0, relative)
    query_ref[...] = (query.astype(F32) + marked).astype(BF16)

    for rows in FORWARD_ROWS:
        scores = dot(query_ref[rows, :], keys_ref[...], ((1,), (1,)))
        largest = jnp.max(scores, axis=1, keepdims=True)
        weights = jnp.exp2((scores - largest) * (SCALE * LOG2E)).astype(BF16)
        weights_ref[0, rows, :] = weights
        total = dot(weights, vals_ref[...])
        inverse = 1.0 / total[:, HEAD_DIM : HEAD_DIM + 1]
        lane = lane_index((rows.stop - rows.start, LANES))
        pv = jnp.where(lane < HEAD_DIM, total * inverse, 0.0)
        out_ref[0, rows, :] = (pv + q_ref[0, rows, :].astype(F32)).astype(BF16)
        high = inverse.astype(BF16).astype(F32)
        extra = jnp.where(lane == HEAD_DIM, high, jnp.where(lane == HEAD_DIM + 1, inverse - high, 0.0))
        pv_ref[0, rows, :] = (pv + extra).astype(BF16)
    if communicate:
        end()


def attend(heads, rest, aug, table, own, fold, wall=None):
    head = (1, ROWS, LANES)
    tail = (1, 1, REST, LANES)
    out_shape = [
        jax.ShapeDtypeStruct((HEADS, ROWS, KEY_ROWS), BF16),
        jax.ShapeDtypeStruct((HEADS, ROWS, LANES), BF16),
        jax.ShapeDtypeStruct((HEADS, ROWS, LANES), BF16),
    ]
    out_specs = [
        pl.BlockSpec((1, ROWS, KEY_ROWS), lambda h: (h, 0, 0)),
        pl.BlockSpec(head, lambda h: (h, 0, 0)),
        pl.BlockSpec(head, lambda h: (h, 0, 0)),
    ]
    scratch = [
        pltpu.VMEM((KEY_ROWS, LANES), BF16),
        pltpu.VMEM((KEY_ROWS, LANES), BF16),
        pltpu.VMEM((ROWS, LANES), BF16),
    ]
    operands = [heads, heads, heads, rest, rest, aug, table, own, fold]
    in_specs = [
        pl.BlockSpec(head, lambda h: (h, 0, 0)),
        pl.BlockSpec(head, lambda h: (HEADS + h, 0, 0)),
        pl.BlockSpec(head, lambda h: (2 * HEADS + h, 0, 0)),
        pl.BlockSpec(tail, lambda h: (0, h, 0, 0)),
        pl.BlockSpec(tail, lambda h: (1, h, 0, 0)),
        whole((KEY_ROWS, LANES)),
        whole((TABLE, LANES)),
        whole((ROWS, TABLE)),
        whole((TABLE, LANES)),
    ]
    more, aliases = wall_more(wall, out_shape, out_specs, scratch, operands, 5)
    return pl.pallas_call(
        attend_kernel,
        grid=(HEADS,),
        out_shape=tuple(out_shape),
        in_specs=in_specs + [pl.BlockSpec(memory_space=pl.ANY)] * len(aliases),
        out_specs=tuple(out_specs),
        scratch_shapes=scratch,
        input_output_aliases=aliases,
        compiler_params=params(**more),
        name="attend",
    )(*operands)


CHUNK = 768
CHUNKS = FF // CHUNK
TILES = CHUNK // LANES


def middle_kernel(
    place_ref, att_ref, x_ref, up_ref, wp_ref, w1_ref, w2_ref, pb_ref, g2_ref, b2_ref, fb1_ref, fb2_ref,
    out_ref, dmid_ref, datt_ref, plow_ref, phigh_ref, low1_ref, high1_ref, low2_ref, high2_ref, small_ref, gb1_ref,
    packed_ref, proj_ref, mid_ref, hidden_ref, total_ref, dhid_ref, wide_ref, w1_scr, w2_scr, grad_ref,
    hiddent_ref, upt_ref,
):
    step = pl.program_id(0)
    sides = wp_ref.shape[1]
    part = D // sides
    depth = D // DP_BLOCKS
    inner = FF // DP_BLOCKS

    @pl.when(step == 0)
    def _():
        for head in range(HEADS):
            packed_ref[:, HEAD_DIM * head : HEAD_DIM * (head + 1)] = att_ref[head][:, :HEAD_DIM]
        for f in range(sides):
            for d in range(DP_BLOCKS):
                rows = slice(d * depth, (d + 1) * depth)
                proj_ref[rows, f * part : f * part + LANES] = wp_ref[d, f, :depth]
                proj_ref[rows, f * part + LANES : (f + 1) * part] = wp_ref[d, f, depth:, : part - LANES]
        middle = x_ref[...].astype(F32) + dot(packed_ref[...], proj_ref[...]) + pb_ref[...].reshape(1, D)
        mid_ref[...] = middle
        centred, rs = layer_stats(middle, D)
        hidden = centred * rs * g2_ref[...].reshape(1, D) + b2_ref[...].reshape(1, D)
        hidden_ref[...] = hidden.astype(BF16)
        hiddent_ref[...] = hidden.T.astype(BF16)
        upt_ref[...] = up_ref[...].T
        total_ref[...] = middle + fb2_ref[...].reshape(1, D).reshape(1, D)
        dhid_ref[...] = jnp.zeros((ROWS, D), F32)

    for tile in range(TILES):
        lanes = slice(tile * LANES, (tile + 1) * LANES)
        for d in range(DP_BLOCKS):
            w1_scr[d * depth : (d + 1) * depth, lanes] = w1_ref[d, 0, tile * depth : (tile + 1) * depth]
        side, at = divmod(tile, inner // LANES)
        for f in range(sides):
            w2_scr[f * part : (f + 1) * part, lanes] = w2_ref[side, f, at * part : (at + 1) * part]
    w1, w2 = w1_scr[...], w2_scr[...]
    before = dot(hidden_ref[...], w1) + fb1_ref[...]
    cdf = 0.5 + 0.5 * lax.erf(before * (2.0**-0.5))
    activated = (before * cdf).astype(BF16)
    slope = cdf + before * (jnp.exp(before * before * -0.5) * 0.3989422804014327)
    dbefore = dot(up_ref[...], w2) * slope
    dbefore_low = dbefore.astype(BF16)
    gb1_ref[...] = jnp.sum(dbefore_low.astype(F32), axis=0, keepdims=True)
    total_ref[...] += dot(activated, w2, ((1,), (1,)))
    dhid_ref[...] += dot(dbefore_low, w1, ((1,), (1,)))

    core = place_ref[4]
    grad_ref[...] = dot(upt_ref[...], activated).astype(BF16)
    for tile in range(TILES):
        lanes = slice(tile * LANES, (tile + 1) * LANES)
        side, at = divmod(tile, inner // LANES)
        rows = slice(at * part, (at + 1) * part)
        for y in range(sides // 2):
            bits = relative_bits(place_ref, side, 2 * y)
            for target_ref, c in ((low2_ref, core), (high2_ref, 1 - core)):
                start = pl.multiple_of((2 * y + c) * part, part)
                target_ref[bits["y"], bits["x"], 0, 0, rows] = grad_ref[pl.ds(start, part), lanes]
    grad_ref[...] = dot(hiddent_ref[...], dbefore_low).astype(BF16)

    def store_one(target_ref):
        for tile in range(TILES):
            lanes = slice(tile * LANES, (tile + 1) * LANES)
            for d in range(DP_BLOCKS):
                bits = relative_bits(place_ref, d, 0)
                block = grad_ref[d * depth : (d + 1) * depth, lanes]
                target_ref[bits["x"], 0, bits["z1"], bits["z2"], tile * depth : (tile + 1) * depth] = block

    @pl.when(step < CHUNKS // 2)
    def _():
        store_one(low1_ref)

    @pl.when(step >= CHUNKS // 2)
    def _():
        store_one(high1_ref)

    @pl.when(step == CHUNKS - 1)
    def _():
        @pl.loop(0, PLACES)
        def _(place):
            at = pl.multiple_of(place * FRAMES, FRAMES)
            write_place(wide_ref, place, total_ref[pl.ds(at, FRAMES), :])

        for tile in range(D // LANES):
            out_ref[:, tile * LANES : (tile + 1) * LANES] = wide_ref[tile].astype(BF16)
        upstream = up_ref[...].astype(F32)
        dhidden = dhid_ref[...]
        centred, rs = layer_stats(mid_ref[...], D)
        vhat = centred * rs
        dgain = jnp.sum(dhidden * vhat, axis=0, keepdims=True)
        dbias = jnp.sum(dhidden, axis=0, keepdims=True)
        scaled = dhidden * g2_ref[...].reshape(1, D)
        first = jnp.sum(scaled, axis=1, keepdims=True) * (1.0 / D)
        second = jnp.sum(scaled * vhat, axis=1, keepdims=True) * (1.0 / D)
        dmiddle = upstream + rs * (scaled - first - vhat * second)
        dmid_ref[...] = dmiddle
        dproj = dmiddle.astype(BF16)
        small_ref[0:1, :] = jnp.sum(dproj.astype(F32), axis=0, keepdims=True)
        small_ref[1:2, :] = dgain
        small_ref[2:3, :] = dbias
        small_ref[3:4, :] = jnp.sum(upstream, axis=0, keepdims=True)
        small_ref[4:8, :] = jnp.zeros((4, D), F32)
        grad_ref[...] = dot(packed_ref[...], dproj, ((0,), (0,))).astype(BF16)
        for d in range(DP_BLOCKS):
            rows = slice(d * depth, (d + 1) * depth)
            for y in range(sides // 2):
                bits = relative_bits(place_ref, d, 2 * y)
                where = (bits["y"], bits["x"], bits["z1"], bits["z2"])
                sides_of = [grad_ref[rows, f * part : (f + 1) * part] for f in (2 * y, 2 * y + 1)]
                for target_ref, c in ((plow_ref, core), (phigh_ref, 1 - core)):
                    block = jnp.where(c == 0, sides_of[0], sides_of[1])
                    target_ref[(*where, slice(0, depth))] = block[:, :LANES]
                    rest = jnp.concatenate([block[:, LANES:], jnp.zeros((depth, 2 * LANES - part), BF16)], axis=1)
                    target_ref[(*where, slice(depth, 2 * depth))] = rest
        datt = dot(dproj, proj_ref[...], ((1,), (1,))).astype(BF16)
        for head in range(HEADS):
            datt_ref[head] = jnp.concatenate(
                [datt[:, HEAD_DIM * head : HEAD_DIM * (head + 1)], jnp.zeros((ROWS, LANES - HEAD_DIM), BF16)],
                axis=1,
            )


def feed_forward(place, att, x, up, flat, pb, g2, b2, fb1, fb2):
    once = pl.Buffered(1)
    sides = flat.shape[1]
    part, depth = D // sides, D // DP_BLOCKS
    rows_one, rows_two = TILES * depth, FF // DP_BLOCKS // LANES * part

    def kept(shape):
        return pl.BlockSpec(shape, lambda *_: (0,) * len(shape), pipeline_mode=once)

    def side_of(s, place):
        return 2 * (place[3] ^ (s & 1)) + (place[4] ^ (s >> 1))

    def columns(s, place):
        return (0, side_of(s, place))

    def low_one(s, place):
        return (0, jnp.where(s < 2, s & 1, 1), 0, 0, 0, 0)

    def high_one(s, place):
        return (0, jnp.where(s < 2, 0, s & 1), 0, 0, 0, 0)

    def pair(s, place):
        side = side_of(s, place)
        return (0, 0, place[1] ^ (side & 1), place[2] ^ (side >> 1), 0, 0)

    bits = (2, 2, 2, 2)
    one, two, proj = bits + (rows_one, LANES), bits + (rows_two, LANES), bits + (2 * depth, LANES)
    return pl.pallas_call(
        middle_kernel,
        out_shape=(
            jax.ShapeDtypeStruct((ROWS, D), BF16),
            jax.ShapeDtypeStruct((ROWS, D), F32),
            jax.ShapeDtypeStruct((HEADS, ROWS, LANES), BF16),
            jax.ShapeDtypeStruct(proj, BF16),
            jax.ShapeDtypeStruct(proj, BF16),
            jax.ShapeDtypeStruct(one, BF16),
            jax.ShapeDtypeStruct(one, BF16),
            jax.ShapeDtypeStruct(two, BF16),
            jax.ShapeDtypeStruct(two, BF16),
            jax.ShapeDtypeStruct((8, D), F32),
            jax.ShapeDtypeStruct((1, FF), F32),
        ),
        grid_spec=pltpu.PrefetchScalarGridSpec(
            num_scalar_prefetch=1,
            grid=(CHUNKS,),
            in_specs=[
                kept((HEADS, ROWS, LANES)),
                kept((ROWS, D)),
                kept((ROWS, D)),
                pl.BlockSpec(
                    (DP_BLOCKS, sides, 2 * depth, LANES), lambda s, place: (0, 0, 6, 0), pipeline_mode=once
                ),
                pl.BlockSpec(
                    (DP_BLOCKS, 1, rows_one, LANES), lambda s, place: (0, side_of(s, place), 0, 0)
                ),
                pl.BlockSpec((2, sides, rows_two, LANES), lambda s, place: (side_of(s, place), 0, 1, 0)),
                kept((D,)),
                kept((D,)),
                kept((D,)),
                pl.BlockSpec((1, CHUNK), columns),
                kept((D,)),
            ],
            out_specs=(
                kept((ROWS, D)),
                kept((ROWS, D)),
                kept((HEADS, ROWS, LANES)),
                kept(proj),
                kept(proj),
                pl.BlockSpec((2, 1, 2, 2, rows_one, LANES), low_one),
                pl.BlockSpec((2, 1, 2, 2, rows_one, LANES), high_one),
                pl.BlockSpec((2, 2, 1, 1, rows_two, LANES), pair),
                pl.BlockSpec((2, 2, 1, 1, rows_two, LANES), pair),
                kept((8, D)),
                pl.BlockSpec((1, CHUNK), columns),
            ),
            scratch_shapes=[
                pltpu.VMEM((ROWS, D), BF16),
                pltpu.VMEM((D, D), BF16),
                pltpu.VMEM((ROWS, D), F32),
                pltpu.VMEM((ROWS, D), BF16),
                pltpu.VMEM((ROWS, D), F32),
                pltpu.VMEM((ROWS, D), F32),
                wide_scratch(D),
                pltpu.VMEM((D, CHUNK), BF16),
                pltpu.VMEM((D, CHUNK), BF16),
                pltpu.VMEM((D, CHUNK), BF16),
                pltpu.VMEM((D, ROWS), BF16),
                pltpu.VMEM((D, ROWS), BF16),
            ],
        ),
        compiler_params=params(),
        name="feed_forward",
    )(place, att, x, up, flat, flat, flat, pb, g2, b2, fb1, fb2)


SPLIT = 128
ONE_DIMS, TWO_DIMS = ("x", "y", "z1", "z2"), ("y", "x", "z1", "z2")
LINE_X, LINE_Y = ("z1", "x", "y", "z2"), ("z1", "y", "x", "z2")
PIECES = (
    (0, ONE_DIMS, ONE_DIMS),
    (1, TWO_DIMS, TWO_DIMS),
    (0, ONE_DIMS, LINE_X),
    (1, TWO_DIMS, LINE_X),
    (2, TWO_DIMS, LINE_Y),
)


def piece_rows(rows_one, rows_two, rows_proj):
    one, two = rows_one - SPLIT, rows_two - SPLIT
    return (0, one), (0, two), (one, SPLIT), (two, SPLIT), (0, rows_proj)


def pick_blocks(dims, **fixed):
    return tuple(fixed.get(name, slice(None)) for name in dims)


def without(dims, *names):
    return tuple(name for name in dims if name not in names)


def first_halving(sent, sums, kept, got, more, *sems):
    step = pl.program_id(0)
    own_sem, *sems = sems
    near = Neighbours()
    spans = piece_rows(sent[0].shape[4], sent[2].shape[4], sent[4].shape[4])
    every = range(len(PIECES))

    def own():
        copies = []
        for p in every:
            array, dims, _ = PIECES[p]
            source = sent[2 * array].at[(*pick_blocks(dims), pl.ds(*spans[p]))]
            copies.append(pltpu.make_async_copy(source, kept[p], own_sem.at[p]))
        return copies

    def fixed(route, part):
        return ({route[0]: 1, route[1]: 1}, {route[0]: 1, route[1]: 0}, {route[0]: 0})[part]

    def over_core(part):
        copies = []
        for p in every:
            array, dims, route = PIECES[p]
            where = pick_blocks(dims, **fixed(route, part))
            source = sent[2 * array + 1].at[(*where, pl.ds(*spans[p]))]
            copies.append(near.copy("c", source, got[p].at[where], sems, 3 * p + part))
        return copies

    def onward(part):
        copies = []
        for p in every:
            _, dims, route = PIECES[p]
            source = kept[p].at[pick_blocks(dims, **fixed(route, part))]
            target = more[p].at[pick_blocks(without(dims, route[0]), **{route[1]: 1 - part})]
            copies.append(near.copy(route[0], source, target, sems, 15 + 2 * p + part))
        return copies

    def arrive(part):
        for copy in over_core(part):
            copy.wait_recv()
        for p in every:
            _, dims, route = PIECES[p]
            where = pick_blocks(dims, **fixed(route, part))
            kept[p][where] = kept[p][where] + got[p][where]

    @pl.when(step == 0)
    def _():
        near.greet(("c", "x", "y", "z1"))
        for copy in over_core(0) + over_core(1) + over_core(2) + own():
            copy.start()

    @pl.when(step == 1)
    def _():
        for copy in own():
            copy.wait()
        arrive(0)
        for copy in onward(0):
            copy.start()

    @pl.when(step == 2)
    def _():
        arrive(1)
        for copy in onward(1):
            copy.start()

    @pl.when(step == 4)
    def _():
        arrive(2)

    def end():
        @pl.when(step == pl.num_programs(0) - 1)
        def _():
            for copy in onward(0) + onward(1):
                copy.wait_recv()
            for p in every:
                _, dims, route = PIECES[p]
                sums[p][...] = kept[p][pick_blocks(dims, **{route[0]: 0})] + more[p][...]
            for copy in over_core(0) + over_core(1) + over_core(2) + onward(0) + onward(1):
                copy.wait_send()

    return end


def attend_back_kernel(
    q_ref, k_ref, v_ref, krest_ref, vrest_ref, aug_ref, table_ref, own_ref, fold_ref, pick_ref,
    weights_ref, pv_ref, datt_ref, parts_ref, *refs,
):
    communicate = len(refs) > 7
    if communicate:
        sent, (grads_ref, gtable_ref, gtaps_ref), sums = refs[:6], refs[6:9], refs[9:14]
        keys_ref, vals_ref, up_ref, gsum_ref = refs[14:18]
        end = first_halving(sent, sums, refs[18:23], refs[23:28], refs[28:33], *refs[33:])
    else:
        grads_ref, gtable_ref, gtaps_ref, keys_ref, vals_ref, up_ref, gsum_ref = refs
    step = pl.program_id(0)
    lane = lane_index((KEY_ROWS, LANES))
    row_lane = lane[:ROWS]

    @pl.when(step == 0)
    def _():
        gsum_ref[...] = jnp.zeros((TABLE, LANES), F32)
        gtaps_ref[...] = jnp.zeros((2, 4, LANES), F32)

    keys_ref[:ROWS] = k_ref[0] + aug_ref[:ROWS]
    keys_ref[ROWS:] = krest_ref[0, 0] + aug_ref[ROWS:]
    one = jnp.where((lane >= HEAD_DIM) & (lane < HEAD_DIM + 3), 1.0, 0.0).astype(BF16)
    vals_ref[:ROWS] = v_ref[0] + one[:ROWS]
    vals_ref[ROWS:] = vrest_ref[0, 0] + one[ROWS:]
    pv = pv_ref[0].astype(F32)
    inverse = pv[:, HEAD_DIM : HEAD_DIM + 1] + pv[:, HEAD_DIM + 1 : HEAD_DIM + 2]
    datt = datt_ref[0].astype(F32)
    upstream = (datt * inverse).astype(BF16).astype(F32)
    mean = jnp.sum(upstream * pv, axis=1, keepdims=True)
    high = mean.astype(BF16).astype(F32)
    low = (mean - high).astype(BF16).astype(F32)
    least = mean - high - low
    extra = jnp.where(
        row_lane == HEAD_DIM,
        -high,
        jnp.where(row_lane == HEAD_DIM + 1, -low, jnp.where(row_lane == HEAD_DIM + 2, -least, 0.0)),
    )
    up_ref[...] = (upstream + extra).astype(BF16)

    dvals, dkeys, dquery = None, None, []
    for rows in BACKWARD_ROWS:
        weights = weights_ref[0, rows, :]
        dprobs = dot(up_ref[rows, :], vals_ref[...], ((1,), (1,)))
        slopes = (weights.astype(F32) * dprobs).astype(BF16)
        dquery.append(dot(slopes, keys_ref[...]))
        more_vals = dot(up_ref[rows, :], weights, ((0,), (0,)))
        more_keys = dot(q_ref[0, rows, :], slopes, ((0,), (0,)))
        dvals = more_vals if dvals is None else dvals + more_vals
        dkeys = more_keys if dkeys is None else dkeys + more_keys
    dvals, dkeys = dvals.T, dkeys.T * SCALE
    dquery = jnp.concatenate(dquery, axis=0)
    spread = dot(dquery.astype(BF16), fold_ref[...], ((1,), (1,))).astype(BF16) * own_ref[...]
    gsum_ref[...] += dot(spread, q_ref[0], ((0,), (0,)))
    dquery = dquery * SCALE + datt + dot(spread, table_ref[...])
    grads_ref[0, 0] = dquery.astype(BF16)
    grads_ref[1, 0] = dkeys[:ROWS].astype(BF16)
    grads_ref[2, 0] = dvals[:ROWS].astype(BF16)
    for s, whole_grad in ((0, dkeys), (1, dvals)):
        piece = whole_grad[SQUEEZE_AT : SQUEEZE_AT + MEM]
        for tap in range(4):
            product = piece * parts_ref[s, 0, tap].astype(F32)[:MEM]
            gtaps_ref[s, tap : tap + 1, :] += jnp.sum(product, axis=0, keepdims=True)

    @pl.when(step == pl.num_programs(0) - 1)
    def _():
        gtable_ref[...] = dot(pick_ref[...].astype(F32), gsum_ref[...], ((0,), (0,)), lax.Precision.HIGHEST)
    if communicate:
        end()


def attend_back(sent, heads, rest, aug, table, own, fold, pick, weights, pv, datt, parts):
    head = (1, ROWS, LANES)
    tail = (1, 1, REST, LANES)
    own_head = pl.BlockSpec(head, lambda h: (h, 0, 0))
    out_shape = [
        jax.ShapeDtypeStruct((3, HEADS, ROWS, LANES), BF16),
        jax.ShapeDtypeStruct((LANES, LANES), F32),
        jax.ShapeDtypeStruct((2, 4, LANES), F32),
    ]
    out_specs = [pl.BlockSpec((3, 1, ROWS, LANES), lambda h: (0, h, 0, 0)), whole((LANES, LANES)), whole((2, 4, LANES))]
    scratch = [
        pltpu.VMEM((KEY_ROWS, LANES), BF16),
        pltpu.VMEM((KEY_ROWS, LANES), BF16),
        pltpu.VMEM((ROWS, LANES), BF16),
        pltpu.VMEM((TABLE, LANES), F32),
    ]
    more = {}
    if sent:
        spans = piece_rows(sent[0].shape[4], sent[2].shape[4], sent[4].shape[4])
        for _, rows in spans:
            out_shape.append(jax.ShapeDtypeStruct((2, 2, 2, rows, LANES), BF16))
            out_specs.append(whole((2, 2, 2, rows, LANES)))
        scratch += [pltpu.VMEM((2,) * bits + (rows, LANES), BF16) for bits in (4, 4, 3) for _, rows in spans]
        scratch += [pltpu.SemaphoreType.DMA((5,)), pltpu.SemaphoreType.DMA((25,)), pltpu.SemaphoreType.DMA((25,))]
        more = {"collective_id": 2, "has_side_effects": True}
    return pl.pallas_call(
        attend_back_kernel,
        grid=(HEADS,),
        out_shape=tuple(out_shape),
        in_specs=[
            own_head,
            pl.BlockSpec(head, lambda h: (HEADS + h, 0, 0)),
            pl.BlockSpec(head, lambda h: (2 * HEADS + h, 0, 0)),
            pl.BlockSpec(tail, lambda h: (0, h, 0, 0)),
            pl.BlockSpec(tail, lambda h: (1, h, 0, 0)),
            whole((KEY_ROWS, LANES)),
            whole((TABLE, LANES)),
            whole((ROWS, TABLE)),
            whole((TABLE, LANES)),
            whole((TABLE, LANES)),
            pl.BlockSpec((1, ROWS, KEY_ROWS), lambda h: (h, 0, 0)),
            own_head,
            own_head,
            pl.BlockSpec((2, 1, 4, 208, LANES), lambda h: (0, h, 0, 0, 0)),
        ]
        + [pl.BlockSpec(memory_space=pl.ANY)] * len(sent),
        out_specs=tuple(out_specs),
        scratch_shapes=scratch,
        compiler_params=params(**more),
        name="attend_back",
    )(heads, heads, heads, rest, rest, aug, table, own, fold, pick, weights, pv, datt, parts, *sent)


def last_halving(ins, outs, got, kept, sems):
    step = pl.program_id(0)
    near = Neighbours()
    pieces = len(PIECES)
    first, second, third = got[:pieces], got[pieces : 2 * pieces], got[2 * pieces :]
    fours, twos = kept[:pieces], kept[pieces:]
    plane, line = (0, 1), (2, 3, 4)

    def copy(p, stage, part):
        _, dims, route = PIECES[p]
        dims = without(dims, *route[:stage])
        at = 5 * p + 2 * (stage - 1) + part
        fixed = {route[stage]: 1}
        if stage < 3:
            fixed[route[stage + 1]] = 1 - part
        source = (ins, fours, twos)[stage - 1][p].at[pick_blocks(dims, **fixed)]
        target = (first, second, third)[stage - 1][p]
        if stage < 3:
            target = target.at[pick_blocks(without(dims, route[stage]), **fixed)]
        return near.copy(route[stage], source, target, sems, at)

    def start(group, stage):
        for p in group:
            for part in range(2 if stage < 3 else 1):
                copy(p, stage, part).start()

    def arrive(group, stage, part):
        for p in group:
            copy(p, stage, part).wait_recv()
            _, dims, route = PIECES[p]
            dims = without(dims, *route[:stage])
            fixed = {route[stage + 1]: 1 - part}
            here = pick_blocks(dims, **{route[stage]: 0}, **fixed)
            there = pick_blocks(without(dims, route[stage]), **fixed)
            source = (ins, fours)[stage - 1][p]
            (fours, twos)[stage - 1][p][there] = source[here] + (first, second)[stage - 1][p][there]

    @pl.when(step == 0)
    def _():
        near.greet(("c", "x", "y", "z1", "z2"))
        start(plane + line, 1)

    @pl.when(step == 1)
    def _():
        arrive(plane, 1, 0)
        start(plane, 2)

    @pl.when(step == 2)
    def _():
        arrive(plane, 1, 1)
        arrive(line, 1, 0)
        start(line, 2)

    @pl.when(step == 3)
    def _():
        arrive(plane, 2, 0)
        start(plane, 3)

    @pl.when(step == 4)
    def _():
        arrive(plane, 2, 1)
        arrive(line, 1, 1)
        arrive(line, 2, 0)
        start(line, 3)

    def end():
        arrive(line, 2, 1)
        for p in range(pieces):
            copy(p, 3, 0).wait_recv()
            outs[p][...] = twos[p][0].astype(F32) + third[p][...].astype(F32)
        for p in range(pieces):
            for stage in (1, 2, 3):
                for part in range(2 if stage < 3 else 1):
                    copy(p, stage, part).wait_send()

    return near, end


EARLY_ROWS = 112
EARLY_COMPRESS, EARLY_WIDE = 56, 64
DOUBLINGS = ("c", "x", "y", "z1", "z2")


def early_sums(near, table_ref, comp_ref, two_ref, gb1_ref, out_ref, vector_ref, more_ref, sems):
    step = pl.program_id(0)

    def move(stage):
        return near.copy(DOUBLINGS[stage], vector_ref.at[stage], more_ref.at[stage], sems, stage)

    @pl.when(step == 0)
    def _():
        vector_ref[0, :EARLY_COMPRESS] = table_ref[:EARLY_COMPRESS]
        for s in range(2):
            vector_ref[0, EARLY_COMPRESS + 4 * s : EARLY_COMPRESS + 4 * s + 4] = comp_ref[s]
        lines = [two_ref[at : at + 1, :] for at in range(4)] + [gb1_ref[:, at : at + D] for at in range(0, FF, D)]
        for tile in range(D // LANES):
            for at, line in enumerate(lines):
                row = EARLY_WIDE + 8 * tile + at
                vector_ref[0, row : row + 1] = line[:, tile * LANES : (tile + 1) * LANES]
        move(0).start()

    for stage in range(1, 5):

        @pl.when(step == stage)
        def _():
            move(stage - 1).wait_recv()
            vector_ref[stage] = vector_ref[stage - 1] + more_ref[stage - 1]
            move(stage).start()

    def end():
        move(4).wait_recv()
        out_ref[...] = vector_ref[4] + more_ref[4]
        for stage in range(5):
            move(stage).wait_send()

    return end


def pool_back_kernel(
    frames_ref, grads_ref, vhat_ref, rs_ref, mixed_ref, taps_raw_ref, gain_ref, same_ref, *refs,
):
    communicate = len(refs) > 6
    if communicate:
        dmix_ref, small_ref, grid_ref, dgrid_ref, sums_ref, taps_ref = (*refs[9:11], *refs[17:21])
        near, end_halving = last_halving(refs[:5], refs[11:16], refs[21:36], refs[36:46], refs[46:48])
        end_early = early_sums(near, *refs[5:9], refs[16], *refs[48:50], refs[50:52])
    else:
        dmix_ref, small_ref, grid_ref, dgrid_ref, sums_ref, taps_ref = refs
    step = pl.program_id(0)

    @pl.when(step == 0)
    def _():
        clear_border(grid_ref)
        clear_border(dgrid_ref)

    @pl.when(step % 2 == 0)
    def _():
        spread_taps(taps_raw_ref, taps_ref)

    dy = jnp.concatenate([grads_ref[0, head][:, :HEAD_DIM] for head in range(GROUP_HEADS)], axis=1).astype(F32)
    vhat = vhat_ref[...].astype(F32)
    gain = tiled_lanes(gain_ref[pl.ds(step // 2, 1), :])
    product = dy * vhat
    small_ref[0, 28:29, :] = jnp.sum(product, axis=0, keepdims=True)
    small_ref[0, 29:30, :] = jnp.sum(dy, axis=0, keepdims=True)
    small_ref[0, 30:32, :] = jnp.zeros((2, GROUP), F32)
    scaled = dy * gain
    first = dot(scaled.astype(BF16), same_ref[...]) * (1.0 / HEAD_DIM)
    second = dot((product * gain).astype(BF16), same_ref[...]) * (1.0 / HEAD_DIM)
    dpool = rs_ref[...] * (scaled - first - vhat * second)
    dgrid_ref[1 : HEIGHT + 1, 1 : WIDTH + 1] = dpool.reshape(HEIGHT, WIDTH, FRAMES, GROUP)
    grid_ref[1 : HEIGHT + 1, 1 : WIDTH + 1] = mixed_ref[...].astype(F32).reshape(HEIGHT, WIDTH, FRAMES, GROUP)
    sums_ref[...] = jnp.zeros(sums_ref.shape, F32)

    @pl.loop(0, HEIGHT)
    def _(i):
        for tile in range(GROUP // LANES):
            lanes = slice(tile * LANES, tile * LANES + LANES)
            line = convolve(dgrid_ref, taps_ref, True, i, lanes)
            frame = lax.broadcasted_iota(jnp.int32, line.shape, 1)
            line = jnp.where(frame < frames_ref[0], line, 0.0)
            at = pl.multiple_of(i * WIDTH * FRAMES, WIDTH * FRAMES)
            dmix_ref[pl.ds(at, WIDTH * FRAMES), lanes] = line.reshape(WIDTH * FRAMES, LANES).astype(BF16)
            own = dgrid_ref[i + 1, 1 : WIDTH + 1, :, lanes]
            moved = (shift_frames(own, -1), own, shift_frames(own, 1))
            for b in range(3):
                for e in range(3):
                    window = grid_ref[i + b, e : e + WIDTH, :, lanes]
                    for a in range(3):
                        tap = 9 * a + 3 * b + e
                        sums_ref[tap, :, lanes] += jnp.sum(window * moved[a], axis=0)

    for tap in range(27):
        small_ref[0, tap : tap + 1, :] = jnp.sum(sums_ref[tap], axis=0, keepdims=True)
    small_ref[0, 27:28, :] = jnp.sum(dmix_ref[...].astype(F32), axis=0, keepdims=True)
    if communicate:

        @pl.when(step == 5)
        def _():
            end_halving()
            end_early()


def pool_back(sums, smalls, frames, grads, vhat, rs, mixed, taps, gain, same):
    smem = pl.BlockSpec(memory_space=pltpu.SMEM)
    group = pl.BlockSpec((ROWS, GROUP), lambda g: (0, g))
    out_shape = [jax.ShapeDtypeStruct((ROWS, QKV), BF16), jax.ShapeDtypeStruct((6, 32, GROUP), F32)]
    out_specs = [group, pl.BlockSpec((1, 32, GROUP), lambda g: (g, 0, 0))]
    scratch = [
        pltpu.VMEM((HEIGHT + 2, WIDTH + 2, FRAMES, GROUP), F32),
        pltpu.VMEM((HEIGHT + 2, WIDTH + 2, FRAMES, GROUP), F32),
        pltpu.VMEM((27, FRAMES, GROUP), F32),
        pltpu.VMEM((27, FRAMES, GROUP), F32),
    ]
    more = {}
    if sums:
        rows = [total.shape[3] for total in sums]
        for count in (*rows, EARLY_ROWS):
            out_shape.append(jax.ShapeDtypeStruct((count, LANES), F32))
            out_specs.append(whole((count, LANES)))
        for shape in ((2, 2), (2,), (), (2, 2), (2,)):
            scratch += [pltpu.VMEM((*shape, count, LANES), BF16) for count in rows]
        scratch += [pltpu.SemaphoreType.DMA((25,))] * 2
        scratch += [pltpu.VMEM((5, EARLY_ROWS, LANES), F32)] * 2
        scratch += [pltpu.SemaphoreType.DMA((5,))] * 2
        more = {"collective_id": 3, "has_side_effects": True}
    return pl.pallas_call(
        pool_back_kernel,
        grid=(6,),
        out_shape=tuple(out_shape),
        in_specs=[
            smem,
            pl.BlockSpec((1, GROUP_HEADS, ROWS, LANES), lambda g: (g // 2, g % 2, 0, 0)),
            group,
            group,
            group,
            pl.BlockSpec((1, 27, HEAD_DIM), lambda g: (g // 2, 0, 0)),
            whole((3, HEAD_DIM)),
            whole((GROUP, GROUP)),
        ]
        + [whole(value.shape) for value in (*sums, *smalls)],
        out_specs=tuple(out_specs),
        scratch_shapes=scratch,
        compiler_params=params(**more),
        name="pool_back",
    )(frames, grads, vhat, rs, mixed, taps, gain, same, *sums, *smalls)


def project_grad_kernel(place_ref, normed_ref, dmixed_ref, one_ref, two_ref, full_ref):
    for kind in range(3):
        grad = dot(normed_ref[...], dmixed_ref[:, kind * D : (kind + 1) * D], ((0,), (0,)))
        full_ref[:, kind * D : (kind + 1) * D] = grad.astype(BF16)
    half, columns = one_ref.shape[5:]
    for f in range(QKV // columns):

        @pl.loop(0, DP_BLOCKS)
        def _(d):
            bits = relative_bits(place_ref, d, f)
            lanes = slice(f * columns, (f + 1) * columns)
            at = pl.multiple_of(2 * d * half, half)
            one_ref[bits["c"], bits["x"], bits["y"], bits["z1"], bits["z2"]] = full_ref[pl.ds(at, half), lanes]
            at = pl.multiple_of((2 * d + 1) * half, half)
            two_ref[bits["c"], bits["y"], bits["x"], bits["z1"], bits["z2"]] = full_ref[pl.ds(at, half), lanes]


def project_grad(place, normed, dmixed, sides):
    vmem = pl.BlockSpec(memory_space=pltpu.VMEM)
    half = jax.ShapeDtypeStruct((2, 2, 2, 2, 2, D // DP_BLOCKS // 2, QKV // sides), BF16)
    return pl.pallas_call(
        project_grad_kernel,
        out_shape=(half, half),
        in_specs=[pl.BlockSpec(memory_space=pltpu.SMEM)] + [vmem] * 2,
        out_specs=(vmem, vmem),
        scratch_shapes=[pltpu.VMEM((D, QKV), BF16)],
        compiler_params=params(),
        name="project_grad",
    )(place, normed, dmixed)


def project_back_kernel(dmixed_ref, weight_ref, x_ref, dmid_ref, g1_ref, gtok_ref, small_ref, dx_ref, wide_ref):
    dy = dot(dmixed_ref[...], weight_ref[...], ((1,), (1,)))
    centred, rs = layer_stats(x_ref[...].astype(F32), D)
    vhat = centred * rs
    small_ref[0:1, :] = jnp.sum(dy * vhat, axis=0, keepdims=True)
    small_ref[1:2, :] = jnp.sum(dy, axis=0, keepdims=True)
    small_ref[2:8, :] = jnp.zeros((6, D), F32)
    scaled = dy * g1_ref[...]
    first = jnp.sum(scaled, axis=1, keepdims=True) * (1.0 / D)
    second = jnp.sum(scaled * vhat, axis=1, keepdims=True) * (1.0 / D)
    dx_ref[...] = dmid_ref[...] + rs * (scaled - first - vhat * second)

    @pl.loop(0, PLACES)
    def _(place):
        at = pl.multiple_of(place * FRAMES, FRAMES)
        write_place(wide_ref, place, dx_ref[pl.ds(at, FRAMES), :])

    for tile in range(D // LANES):
        gtok_ref[:, tile * LANES : (tile + 1) * LANES] = wide_ref[tile]


def project_back(dmixed, weight, x, dmid, g1):
    vmem = pl.BlockSpec(memory_space=pltpu.VMEM)
    return pl.pallas_call(
        project_back_kernel,
        out_shape=(jax.ShapeDtypeStruct((ROWS, D), F32), jax.ShapeDtypeStruct((8, D), F32)),
        in_specs=[vmem] * 5,
        out_specs=(vmem, vmem),
        scratch_shapes=[pltpu.VMEM((ROWS, D), F32), wide_scratch(D)],
        compiler_params=params(),
        name="project_back",
    )(dmixed, weight, x, dmid, g1)


VECTOR_ROWS = 128
WIDE_AT = 96


class Scatter:
    def __init__(self, blocks_ref, out_ref, vector_ref, from_core, from_first, from_second, from_z, sems):
        dp, fsdp = lax.axis_index("dp"), lax.axis_index("fsdp")
        self.z, self.x = dp // 2, dp % 2
        self.y, self.c = fsdp // 2, fsdp % 2
        self.blocks_ref, self.out_ref, self.vector_ref = blocks_ref, out_ref, vector_ref
        self.from_core, self.from_first, self.from_second, self.from_z = from_core, from_first, from_second, from_z
        self.send_sem, self.recv_sem, self.vector_send, self.vector_recv, self.vector_more = sems
        self.rows = blocks_ref.shape[4] // (2 * PARTS)
        self.copies = {}

    def device(self, z, x, y, c):
        return (2 * z + x, 2 * y + c)

    def begin(self):
        z, x, y, c = self.z, self.x, self.y, self.c
        self.along = [self.device((z + k) % 4, x, y, c) for k in (1, 2, 3)]
        self.over_x, self.over_y = self.device(z, 1 - x, y, c), self.device(z, x, 1 - y, c)
        self.over_c, self.over_both = self.device(z, x, y, 1 - c), self.device(z, 1 - x, 1 - y, c)
        barrier = pltpu.get_barrier_semaphore()
        for partner in self.along + [self.over_x, self.over_y, self.over_both, self.over_c]:
            pl.semaphore_signal(barrier, inc=1, device_id=partner, device_id_type=MESH)
        pl.semaphore_wait(barrier, 7)

    def copy(self, source, target, send_sem, recv_sem, partner):
        copy = pltpu.make_async_remote_copy(
            src_ref=source, dst_ref=target, send_sem=send_sem, recv_sem=recv_sem, device_id=partner, device_id_type=MESH
        )
        copy.start()
        return copy

    def span(self, part, route):
        return pl.ds((2 * part + route) * self.rows, self.rows)

    def send(self, part, level):
        z, x, y, c = self.z, self.x, self.y, self.c
        every = slice(None)
        blocks = self.blocks_ref
        for route in range(2):
            span = self.span(part, route)
            if level == 0:
                moves = [(blocks.at[every, every, every, 1 - c, span], self.from_core.at[every, every, every, span], self.over_c)]
            elif level == 1:
                where = (every, 1 - x, every, c, span) if route == 0 else (every, every, 1 - y, c, span)
                moves = [(blocks.at[where], self.from_first.at[every, every, span], self.over_y if route else self.over_x)]
            elif level == 2:
                where = (every, x, 1 - y, c, span) if route == 0 else (every, 1 - x, y, c, span)
                moves = [(blocks.at[where], self.from_second.at[every, span], self.over_x if route else self.over_y)]
            else:
                moves = [
                    (blocks.at[(z + k) % 4, x, y, c, span], self.from_z.at[k - 1, span], self.along[k - 1])
                    for k in (1, 2, 3)
                ]
            for at, (source, target, partner) in enumerate(moves):
                slot = (2 * part + route) * 6 + level + at
                self.copies[part, route, level, at] = self.copy(
                    source, target, self.send_sem.at[slot], self.recv_sem.at[slot], partner
                )

    def advance(self, part, level):
        z, x, y, c = self.z, self.x, self.y, self.c
        every = slice(None)
        blocks = self.blocks_ref
        for route in range(2):
            span = self.span(part, route)
            for at in range(3 if level == 3 else 1):
                self.copies[part, route, level, at].wait_recv()
            if level == 0:
                where, more = (every, every, every, c, span), self.from_core[:, :, :, span]
            elif level == 1:
                where = (every, x, every, c, span) if route == 0 else (every, every, y, c, span)
                more = self.from_first[:, :, span]
            elif level == 2:
                where, more = (every, x, y, c, span), self.from_second[:, span]
            if level < 3:
                blocks[where] = blocks[where] + more
            else:
                total = blocks[z, x, y, c, span].astype(F32)
                for k in range(3):
                    total = total + self.from_z[k, span].astype(F32)
                self.out_ref[span] = total
        if level < 3:
            self.send(part, level + 1)

    def steps(self):
        order = []
        for turn in range(PARTS + 3):
            for level in reversed(range(4)):
                if 0 <= turn - level < PARTS:
                    order.append((turn - level, level))
        return [functools.partial(self.advance, *step) for step in order]

    def send_vector(self, stage):
        partners = ([self.over_c], [self.over_x, self.over_y, self.over_both], self.along)[stage]
        for at, partner in enumerate(partners):
            slot = (0, 1, 4)[stage] + at
            self.copies["vector", stage, at] = self.copy(
                self.vector_ref.at[stage], self.vector_more.at[slot], self.vector_send.at[slot],
                self.vector_recv.at[slot], partner,
            )

    def advance_vector(self, stage):
        total = self.vector_ref[stage]
        for at in range((1, 3, 3)[stage]):
            self.copies["vector", stage, at].wait_recv()
            total = total + self.vector_more[(0, 1, 4)[stage] + at]
        self.vector_ref[stage + 1] = total
        if stage < 2:
            self.send_vector(stage + 1)

    def end(self):
        for copy in self.copies.values():
            copy.wait_send()


def tail_kernel(
    turned_ref, dmixed_ref, weight_hbm, x_hbm, dmid_hbm, g1_ref, pools_ref,
    gqkv_ref, dx_hbm, done_ref,
    blocks_ref, vector_ref, from_core, from_first, from_second, from_z, weight_ref, x_ref, dmid_ref, dx_ref, own_sem,
    *sems,
):
    loads = [
        pltpu.make_async_copy(source, target, own_sem.at[at])
        for at, (source, target) in enumerate(((weight_hbm, weight_ref), (x_hbm, x_ref), (dmid_hbm, dmid_ref)))
    ]
    for load in loads:
        load.start()
    scatter = Scatter(blocks_ref, gqkv_ref, vector_ref, from_core, from_first, from_second, from_z, sems)
    scatter.begin()
    steps = scatter.steps()

    def advance(count):
        for _ in range(min(count, len(steps))):
            steps.pop(0)()

    depth, columns = blocks_ref.shape[4:]
    rows = depth // PARTS
    for part in range(PARTS):
        turned = [turned_ref[d * depth + part * rows : d * depth + (part + 1) * rows] for d in range(DP_BLOCKS)]
        grad = dot(jnp.concatenate(turned, axis=0), dmixed_ref[...]).astype(BF16)
        for f in range(QKV // columns):
            for d in range(DP_BLOCKS):
                block = grad[d * rows : (d + 1) * rows, f * columns : (f + 1) * columns]
                blocks_ref[d // 2, d % 2, f // 2, f % 2, part * rows : (part + 1) * rows] = block
        scatter.send(part, 0)
        advance(part)
    for load in loads:
        load.wait()
    dy = dot(dmixed_ref[...], weight_ref[...], ((1,), (1,)))
    centred, rs = layer_stats(x_ref[...].astype(F32), D)
    vhat = centred * rs
    vector_ref[0] = jnp.zeros((VECTOR_ROWS, LANES), F32)
    for kind in range(3):
        sums = pools_ref[2 * kind] + pools_ref[2 * kind + 1]
        total = sums[:, :HEAD_DIM]
        for head in range(1, GROUP_HEADS):
            total = total + sums[:, HEAD_DIM * head : HEAD_DIM * (head + 1)]
        vector_ref[0, 32 * kind : 32 * kind + 32, :HEAD_DIM] = total
    lines = [jnp.sum(dy * vhat, axis=0, keepdims=True), jnp.sum(dy, axis=0, keepdims=True)]
    lines += [
        jnp.concatenate([pools_ref[2 * kind, 27:28, :], pools_ref[2 * kind + 1, 27:28, :]], axis=1)
        for kind in range(3)
    ]
    for tile in range(D // LANES):
        for at, line in enumerate(lines):
            vector_ref[0, WIDE_AT + 5 * tile + at : WIDE_AT + 5 * tile + at + 1] = line[:, tile * LANES : (tile + 1) * LANES]
    scatter.send_vector(0)
    advance(1)
    scatter.advance_vector(0)
    advance(2)
    scaled = dy * g1_ref[...].reshape(1, D)
    first = jnp.sum(scaled, axis=1, keepdims=True) * (1.0 / D)
    second = jnp.sum(scaled * vhat, axis=1, keepdims=True) * (1.0 / D)
    dx_ref[...] = dmid_ref[...] + rs * (scaled - first - vhat * second)
    leave = pltpu.make_async_copy(dx_ref, dx_hbm, own_sem.at[3])
    leave.start()
    advance(1)
    scatter.advance_vector(1)
    advance(3)
    scatter.advance_vector(2)
    advance(len(steps))
    leave.wait()
    done_ref[...] = vector_ref[3]
    scatter.end()


def tail(turned, dmixed, weight, x, dmid, g1, pools, shard):
    vmem = pl.BlockSpec(memory_space=pltpu.VMEM)
    anywhere = pl.BlockSpec(memory_space=pl.ANY)
    depth, columns = shard
    shapes = [shard, (ROWS, D), (VECTOR_ROWS, LANES)]
    count = 2 * PARTS * 6
    return pl.pallas_call(
        tail_kernel,
        out_shape=tuple(jax.ShapeDtypeStruct(shape, F32) for shape in shapes),
        in_specs=[vmem, vmem, anywhere, anywhere, anywhere, vmem, vmem],
        out_specs=(vmem, anywhere, vmem),
        scratch_shapes=[
            pltpu.VMEM((4, 2, 2, 2, depth, columns), BF16),
            pltpu.VMEM((4, VECTOR_ROWS, LANES), F32),
            pltpu.VMEM((4, 2, 2, depth, columns), BF16),
            pltpu.VMEM((4, 2, depth, columns), BF16),
            pltpu.VMEM((4, depth, columns), BF16),
            pltpu.VMEM((3, depth, columns), BF16),
            pltpu.VMEM((D, QKV), BF16),
            pltpu.VMEM((ROWS, D), BF16),
            pltpu.VMEM((ROWS, D), F32),
            pltpu.VMEM((ROWS, D), F32),
            pltpu.SemaphoreType.DMA((4,)),
            pltpu.SemaphoreType.DMA((count,)),
            pltpu.SemaphoreType.DMA((count,)),
            pltpu.SemaphoreType.DMA((7,)),
            pltpu.SemaphoreType.DMA((7,)),
            pltpu.VMEM((7, VECTOR_ROWS, LANES), F32),
        ],
        compiler_params=params(collective_id=1, has_side_effects=True),
        name="tail",
    )(turned, dmixed, weight, x, dmid, g1, pools)


def finish_kernel(
    gqkv_ref, dx_ref, done_ref, one_ref, two_ref, one_rest_ref, two_rest_ref, proj_ref, early_ref,
    gtok_ref, ln1g_ref, ln1b_ref, wqkv_ref, qkvb_ref, conv_ref, pgain_ref, pbias_ref, time_ref, space_ref, comp_ref,
    wp_ref, projb_ref, ln2g_ref, ln2b_ref, w1_ref, fc1b_ref, w2_ref, fc2b_ref, wide_ref,
):
    @pl.loop(0, PLACES)
    def _(place):
        at = pl.multiple_of(place * FRAMES, FRAMES)
        write_place(wide_ref, place, dx_ref[pl.ds(at, FRAMES), :])

    for tile in range(D // LANES):
        gtok_ref[:, tile * LANES : (tile + 1) * LANES] = wide_ref[tile]
    wqkv_ref[...] = gqkv_ref[...]
    one = jnp.concatenate([one_ref[...], one_rest_ref[...]], axis=0)
    two = jnp.concatenate([two_ref[...], two_rest_ref[...]], axis=0)
    depth, part = w1_ref.shape[0], wp_ref.shape[1]
    for tile in range(w1_ref.shape[1] // LANES):
        w1_ref[:, tile * LANES : (tile + 1) * LANES] = one[tile * depth : (tile + 1) * depth]
    tiles = w2_ref.shape[1] // LANES
    for tile in range(tiles):
        w2_ref[:, tile * LANES : (tile + 1) * LANES] = two[tile * part : (tile + 1) * part]
    wp_ref[:, :LANES] = proj_ref[:depth]
    wp_ref[:, LANES:] = proj_ref[depth:, : part - LANES]
    for kind in range(3):
        conv_ref[kind] = done_ref[32 * kind : 32 * kind + 27, :HEAD_DIM]
        pgain_ref[kind : kind + 1, :] = done_ref[32 * kind + 28 : 32 * kind + 29, :HEAD_DIM]
        pbias_ref[kind : kind + 1, :] = done_ref[32 * kind + 29 : 32 * kind + 30, :HEAD_DIM]
    spans = 2 * HEIGHT - 1
    time_ref[...] = early_ref[:15, :HEAD_DIM]
    for s in range(2):
        start = 15 + spans * s
        space_ref[:, s] = early_ref[start : start + spans, :HEAD_DIM]
        comp_ref[s] = early_ref[EARLY_COMPRESS + 4 * s : EARLY_COMPRESS + 4 * s + 4, :HEAD_DIM]

    def line_of(source_ref, base, lines, at):
        rows = [base + lines * tile + at for tile in range(D // LANES)]
        return jnp.concatenate([source_ref[row : row + 1, :] for row in rows], axis=1).reshape(D)

    for at, target_ref in enumerate((projb_ref, ln2g_ref, ln2b_ref, fc2b_ref)):
        target_ref[...] = line_of(early_ref, EARLY_WIDE, 8, at)
    for side in range(FF // D):
        fc1b_ref[side * D : (side + 1) * D] = line_of(early_ref, EARLY_WIDE, 8, 4 + side)
    for at, target_ref in enumerate((ln1g_ref, ln1b_ref)):
        target_ref[...] = line_of(done_ref, WIDE_AT, 5, at)
    for kind in range(3):
        qkvb_ref[kind * D : (kind + 1) * D] = line_of(done_ref, WIDE_AT, 5, 2 + kind)


def finish(operands, w_qkv, w_proj, w_fc1, w_fc2):
    vmem = pl.BlockSpec(memory_space=pltpu.VMEM)
    shapes = [
        (ROWS, D), (D,), (D,), w_qkv, (QKV,), (3, 27, HEAD_DIM), (3, HEAD_DIM), (3, HEAD_DIM), (15, HEAD_DIM),
        (2 * HEIGHT - 1, 2, HEAD_DIM), (2, 4, HEAD_DIM), w_proj, (D,), (D,), (D,), w_fc1, (FF,), w_fc2[::-1], (D,),
    ]
    done = pl.pallas_call(
        finish_kernel,
        out_shape=tuple(jax.ShapeDtypeStruct(shape, F32) for shape in shapes),
        in_specs=[vmem] * 9,
        out_specs=(vmem,) * len(shapes),
        scratch_shapes=[wide_scratch(D)],
        compiler_params=params(),
        name="finish",
    )(*operands)
    done = list(done)
    done[9], done[17] = done[9].transpose(1, 0, 2), done[17].T
    return done


def row(vector):
    return vector.reshape(1, -1)


def tiled_lanes(array):
    return jnp.concatenate([array] * GROUP_HEADS, axis=-1)


def head_lanes(array):
    return jnp.pad(array, [(0, 0)] * (array.ndim - 1) + [(0, LANES - HEAD_DIM)])


DP_BLOCKS = 8
ROUTE_ONE = ("z2", "z1", "y", "x", "c")
ROUTE_TWO = ("z2", "z1", "x", "y", "c")


def together(*values):
    return lax.optimization_barrier(values)


def flat_shard(one, two, proj):
    pieces = [part for _, part in flat_pieces(one, two, proj)]
    pieces[-1] = jnp.pad(pieces[-1], ((0, 0), (0, LANES - pieces[-1].shape[1])))
    return jnp.concatenate(pieces, axis=0)


class Staged:
    def place(self):
        dp, fsdp = lax.axis_index("dp"), lax.axis_index("fsdp")
        return jnp.stack([dp & 1, (dp >> 1) & 1, (dp >> 2) & 1, (fsdp >> 1) & 1, fsdp & 1]).astype(jnp.int32)


class Plain:
    def __init__(self, dp, fsdp):
        self.dp, self.fsdp = dp, fsdp

    def place(self):
        return jnp.zeros((5,), jnp.int32)

    def gather(self, shard):
        blocks = lax.all_gather(shard, ("dp", "fsdp"), axis=0, tiled=False)
        rows, columns = shard.shape
        joined = blocks.reshape(DP_BLOCKS, self.dp // DP_BLOCKS, self.fsdp, rows, columns).transpose(0, 2, 1, 3, 4)
        return joined.reshape(DP_BLOCKS, self.fsdp, self.dp // DP_BLOCKS * rows, columns)

    def other_weights(self, one, two, proj):
        return jax.vmap(jax.vmap(flat_shard))(self.gather(one), jnp.swapaxes(self.gather(two), 2, 3), self.gather(proj))

    def scatter(self, blocks, route):
        at = {name: 4 - where for where, name in enumerate(route)}
        rows, columns = blocks.shape[5:]
        blocks = blocks.transpose([at[name] for name in ("z2", "z1", "x", "y", "c")] + [5, 6])
        split = blocks.reshape(DP_BLOCKS, self.fsdp, self.dp // DP_BLOCKS, rows * DP_BLOCKS // self.dp, columns)
        split = split.transpose(0, 2, 1, 3, 4).reshape(self.dp * self.fsdp, -1, columns)
        return lax.psum_scatter(split, ("dp", "fsdp"), scatter_dimension=0, tiled=False).astype(F32)

    def scatter_flat(self, low, high, route, unpack):
        blocks = jnp.concatenate([low[None], high[None]])
        blocks = jax.vmap(unpack)(blocks.reshape((32,) + blocks.shape[5:]))
        return self.scatter(blocks.reshape((2,) * 5 + blocks.shape[1:]), route)

    def total(self, vector):
        return lax.psum(vector, ("dp", "fsdp"))


def run(
    comm, staged, tokens, prev_kv, memory, valid_frames, mem_len, ln1_gain, ln1_bias, w_qkv, qkv_bias, pool_conv, pool_gain,
    pool_bias, rel_time, rel_space, compress, w_proj, proj_bias, ln2_gain, ln2_bias, w_fc1, fc1_bias, w_fc2,
    fc2_bias, cotangent,
):
    place = comm.place()
    fsdp = QKV // w_qkv.shape[1]
    one_hot, own, fold, pick, same = (jnp.asarray(c, BF16) for c in constants())
    taps, gains, biases = pool_conv, pool_gain, pool_bias
    prepared = prepare(
        valid_frames, mem_len, tokens, cotangent, ln1_gain, ln1_bias, one_hot, rel_time, rel_space.transpose(1, 0, 2), pick,
        prev_kv, memory, compress, [w_qkv, w_fc1, w_fc2.T, w_proj] if staged else None,
    )
    x, normed, turned, upstream, aug, table, rest, parts = prepared[-8:]
    if staged:
        first, wall = prepared[0].reshape(8, 4, *w_qkv.shape), prepared[1]
    else:
        first, wall = comm.gather(w_qkv), None
    heads, vhat, rs, mixed, weight, *wall = query_key_value(
        valid_frames, normed, first, qkv_bias, taps, gains, biases, same, wall
    )
    weights, pv, attended, *wall = attend(heads, rest, aug, table, own, fold, *wall)
    if staged:
        flat = wall[0].reshape(8, 4, *wall[0].shape[5:])
    else:
        flat = comm.other_weights(w_fc1, w_fc2, w_proj)
    out, dmid, datt, plow, phigh, low1, high1, low2, high2, small_two, gb1 = feed_forward(
        place, attended, x, upstream, flat, proj_bias, ln2_gain, ln2_bias, row(fc1_bias), fc2_bias
    )

    sent = [low1, high1, low2, high2, plow, phigh] if staged else []
    grads, gtable, gcompress, *sums = attend_back(
        sent, heads, rest, aug, table, own, fold, pick, weights, pv, datt, parts
    )
    smalls = [gtable, gcompress, small_two, gb1] if staged else []
    dmixed, pools, *sums = pool_back(sums, smalls, valid_frames, grads, vhat, rs, mixed, taps, gains, same)
    if staged:
        ended = tail(turned, dmixed, weight, x, dmid, ln1_gain, pools, w_qkv.shape)
        return (out, *finish((*ended, *sums), w_qkv.shape, w_proj.shape, w_fc1.shape, w_fc2.shape))
    depth, part = D // DP_BLOCKS, D // fsdp

    def unpack_one(block):
        return jnp.concatenate(list(block.reshape(-1, depth, LANES)), axis=1)

    def unpack_two(block):
        return jnp.concatenate(list(block.reshape(-1, part, LANES)), axis=1).T

    def unpack_proj(block):
        return jnp.concatenate([block[:depth], block[depth:, : part - LANES]], axis=1)

    w1_sum = comm.scatter_flat(low1, high1, ROUTE_ONE, unpack_one)
    w2_sum = comm.scatter_flat(low2, high2, ROUTE_TWO, unpack_two)
    wp_sum = comm.scatter_flat(plow, phigh, ROUTE_TWO, unpack_proj)
    qkv_one, qkv_two = project_grad(place, normed, dmixed, fsdp)
    gtok, small_one = project_back(dmixed, weight, x, dmid, row(ln1_gain))
    gbias = pools[:, 27].reshape(QKV)
    pools = jnp.sum(pools.reshape(3, 2, 32, GROUP_HEADS, HEAD_DIM), axis=(1, 3))
    gconv, gpool = pools[:, :27], pools[:, 28:30]
    smalls = (
        small_one[0], small_one[1], gbias, gconv, gpool[:, 0], gpool[:, 1],
        gtable[:15, :HEAD_DIM], gtable[15:53, :HEAD_DIM].reshape(2, 19, HEAD_DIM), gcompress[:, :, :HEAD_DIM],
        small_two[0], small_two[1], small_two[2], gb1[0], small_two[3],
    )
    vector = comm.total(jnp.concatenate([s.reshape(-1) for s in smalls]))
    totals, at = [], 0
    for s in smalls:
        totals.append(vector[at : at + s.size].reshape(s.shape))
        at += s.size
    qkv = comm.scatter(jnp.concatenate([qkv_one, jnp.moveaxis(qkv_two, 1, 2)], axis=5), ROUTE_ONE)
    sums = [qkv, wp_sum, w1_sum, w2_sum]
    return (
        out, gtok, totals[0], totals[1], sums[0], totals[2], totals[3], totals[4], totals[5], totals[6],
        totals[7], totals[8], sums[1], totals[9], totals[10], totals[11], sums[2], totals[12], sums[3], totals[13],
    )


def solution(mesh):
    both = P(("dp", "fsdp"))
    rows = P(("dp", "fsdp"), None)
    second = P(None, ("dp", "fsdp"), None)
    blocks = P("dp", "fsdp")
    none = P()
    dp, fsdp = mesh.shape["dp"], mesh.shape["fsdp"]
    staged = (dp, fsdp) == (8, 4)
    return jax.shard_map(
        functools.partial(run, Staged() if staged else Plain(dp, fsdp), staged),
        mesh=mesh,
        in_specs=(
            rows, second, second, both, both, none, none, blocks, none, none, none, none, none, none, none, blocks,
            none, none, none, blocks, none, blocks, none, rows,
        ),
        out_specs=(
            rows, rows, none, none, blocks, none, none, none, none, none, none, none, blocks, none, none, none,
            blocks, none, blocks, none,
        ),
        check_vma=False,
    )
```

```python
import functools

import jax
import jax.numpy as jnp
import numpy as np
from jax import lax
from jax.experimental import pallas as pl
from jax.experimental.pallas import tpu as pltpu
from jax.sharding import PartitionSpec as P

D = 768
FF = 3072
HEADS = 8
HEAD_DIM = 96
LANES = 128
FRAMES = 8
HEIGHT = 10
WIDTH = 10
PLACES = HEIGHT * WIDTH
ROWS = 800
MEM = 200
GROUP = 384
GROUP_HEADS = 4
QKV = 3 * D
KEY_ROWS = 1280
MEM_AT = 800
SQUEEZE_AT = 1024
REST = KEY_ROWS - ROWS
TABLE = 384
EPSILON = 1e-06
SCALE = HEAD_DIM**-0.5
ROOT = HEAD_DIM**0.5
LOG2E = 1.4426950408889634
MASKED = -1e9
MASK_LANE = 124
FORWARD_ROWS = (slice(0, 272), slice(272, 544), slice(544, 800))
BACKWARD_ROWS = (slice(0, 208), slice(208, 400), slice(400, 608), slice(608, 800))
BF16 = jnp.bfloat16
F32 = jnp.float32
VMEM_LIMIT = 60 * 1024 * 1024


def constants():
    place = np.arange(PLACES).repeat(FRAMES)
    row_t = np.tile(np.arange(FRAMES), PLACES)
    row_i, row_j = place // WIDTH, place % WIDTH
    one_hot = np.zeros((KEY_ROWS, LANES), np.float32)
    rows = np.arange(ROWS)
    one_hot[rows, 96 + row_t] = 1
    one_hot[rows, 104 + row_i] = 1
    one_hot[rows, 114 + row_j] = 1
    own = np.zeros((ROWS, TABLE), np.float32)
    fold = np.zeros((TABLE, LANES), np.float32)
    pick = np.zeros((TABLE, LANES), np.float32)
    for base, length, row_at, lane, offset in (
        (0, FRAMES, row_t, 96, 0),
        (64, HEIGHT, row_i, 104, 15),
        (164, WIDTH, row_j, 114, 34),
    ):
        for a in range(length):
            for b in range(length):
                column = base + a * length + b
                own[:, column] = row_at == a
                fold[column, lane + b] = 1
                pick[column, offset + a - b + length - 1] = 1
    lanes = np.arange(GROUP) // HEAD_DIM
    same = (lanes[:, None] == lanes[None, :]).astype(np.float32)
    return one_hot, own, fold, pick, same


def lane_index(shape):
    return lax.broadcasted_iota(jnp.int32, shape, len(shape) - 1)


def dot(a, b, contract=((1,), (0,)), precision=None):
    return lax.dot_general(a, b, (contract, ((), ())), preferred_element_type=F32, precision=precision)


def layer_stats(values, width):
    average = jnp.sum(values, axis=-1, keepdims=True) * (1.0 / width)
    centred = values - average
    variance = jnp.sum(centred * centred, axis=-1, keepdims=True) * (1.0 / width)
    return centred, lax.rsqrt(variance + EPSILON)


def params(**more):
    return pltpu.CompilerParams(vmem_limit_bytes=VMEM_LIMIT, **more)


def whole(shape):
    return pl.BlockSpec(shape, lambda *_: (0,) * len(shape))


def tiles_of(values):
    return [values[:, at : at + LANES] for at in range(0, values.shape[1], LANES)]


def flat_pieces(one, two, proj):
    at = 0
    for part in tiles_of(one) + tiles_of(two) + tiles_of(proj):
        yield at, part
        at += part.shape[0]


def read_place(wide_ref, place, tiles=D // LANES):
    parts = [wide_ref[tile, pl.ds(place, FRAMES, stride=PLACES), :] for tile in range(tiles)]
    return jnp.concatenate(parts, axis=1)


def write_place(wide_ref, place, values):
    for tile, part in enumerate(tiles_of(values)):
        wide_ref[tile, pl.ds(place, FRAMES, stride=PLACES), :] = part


def wide_scratch(columns):
    return pltpu.VMEM((columns // LANES, ROWS, LANES), F32)


PARTS = 3
WALL_AFTER = 6
MESH = pl.DeviceIdType.MESH


class Neighbours:
    def __init__(self):
        dp, fsdp = lax.axis_index("dp"), lax.axis_index("fsdp")
        z, x, y, c = dp // 2, dp % 2, fsdp // 2, fsdp % 2
        self.over = {
            "c": (dp, 2 * y + 1 - c),
            "x": (2 * z + 1 - x, fsdp),
            "y": (dp, 2 * (1 - y) + c),
            "z1": (2 * (z + 1 - 2 * (z % 2)) + x, fsdp),
            "z2": (2 * ((z + 2) % 4) + x, fsdp),
        }

    def greet(self, names):
        barrier = pltpu.get_barrier_semaphore()
        for name in names:
            pl.semaphore_signal(barrier, inc=1, device_id=self.over[name], device_id_type=MESH)
        pl.semaphore_wait(barrier, len(names))

    def copy(self, name, source, target, sems, at):
        return pltpu.make_async_remote_copy(
            src_ref=source,
            dst_ref=target,
            send_sem=sems[0].at[at],
            recv_sem=sems[1].at[at],
            device_id=self.over[name],
            device_id_type=MESH,
        )


PLACE_DIMS = ("z2", "z1", "x", "y", "c")
WALL_ROUTES = (
    ("z2", "z1", "y", "x", "c"),
    ("z2", "z1", "x", "y", "c"),
    ("z2", "y", "x", "z1", "c"),
    ("z2", "x", "y", "z1", "c"),
)


class Doubling:
    def __init__(self, near, wall_ref, sems):
        dp, fsdp = lax.axis_index("dp"), lax.axis_index("fsdp")
        self.mine = {"z2": dp // 4, "z1": dp // 2 % 2, "x": dp % 2, "y": fsdp // 2, "c": fsdp % 2}
        self.near, self.wall_ref, self.sems = near, wall_ref, sems
        rows = wall_ref.shape[5]
        third = rows // 3
        self.spans = ((0, third), (third, third), (2 * third, third // 2), (2 * third + third // 2, third // 2))
        self.made = {}

    def region(self, piece, free, other=()):
        where = [
            slice(None) if name in free else (1 - self.mine[name] if name in other else self.mine[name])
            for name in PLACE_DIMS
        ]
        return self.wall_ref.at[(*where, pl.ds(*self.spans[piece]))]

    def plan(self, *key):
        self.made[key] = functools.partial(self.make, *key, len(self.made))

    def make(self, piece, stage, part, at):
        route = WALL_ROUTES[piece]
        if stage < 4:
            free = route[: max(stage - 1, 0)]
            place = self.region(piece, free, route[stage - 1 : stage] if part else ())
        else:
            free, other = ((route[:3], ()), (route[:2], (route[3],)), (route[:2], (route[3], route[2])))[part]
            place = self.region(piece, free, other)
        return self.near.copy(route[stage], place, place, self.sems, at)

    def start(self, *keys):
        for key in keys:
            self.made[key]().start()

    def arrive(self, *keys):
        for key in keys:
            self.made[key]().wait_recv()

    def end(self):
        for make in self.made.values():
            make().wait_send()


FLAT, UPRIGHT, EVERY_PIECE = (0, 1), (2, 3), (0, 1, 2, 3)


def keys_of(pieces, stage, *parts):
    return [(piece, stage, part) for piece in pieces for part in parts]


def doubling_in_queries(wall_ref, sems):
    step = pl.program_id(0)
    doubling = Doubling(Neighbours(), wall_ref, sems)
    early = keys_of(FLAT, 1, 1) + keys_of(FLAT, 2, 0) + keys_of(UPRIGHT, 1, 0, 1) + keys_of(UPRIGHT, 2, 0)
    later = keys_of(EVERY_PIECE, 2, 1) + keys_of(EVERY_PIECE, 3, 0)
    for key in early + later:
        doubling.plan(*key)

    @pl.when(step == 0)
    def _():
        doubling.near.greet(("x", "y", "z1"))
        doubling.start(*early)

    @pl.when(step == 2)
    def _():
        doubling.arrive(*keys_of(FLAT, 1, 1), *keys_of(UPRIGHT, 1, 0, 1))
        doubling.start(*later)

    def end():
        @pl.when(step == 5)
        def _():
            doubling.arrive(*keys_of(EVERY_PIECE, 2, 0, 1), *keys_of(EVERY_PIECE, 3, 0))
            doubling.end()

    return end


def doubling_in_attention(wall_ref, sems):
    step = pl.program_id(0)
    doubling = Doubling(Neighbours(), wall_ref, sems)
    early = keys_of(EVERY_PIECE, 3, 1) + keys_of(EVERY_PIECE, 4, 0, 1)
    later = keys_of(EVERY_PIECE, 4, 2)
    for key in early + later:
        doubling.plan(*key)

    @pl.when(step == 0)
    def _():
        doubling.near.greet(("x", "y", "z1", "c"))
        doubling.start(*early)

    @pl.when(step == 5)
    def _():
        doubling.arrive(*keys_of(EVERY_PIECE, 3, 1))
        doubling.start(*later)

    def end():
        @pl.when(step == HEADS - 1)
        def _():
            doubling.arrive(*keys_of(EVERY_PIECE, 4, 0, 1, 2))
            doubling.end()

    return end


class Gather:
    def __init__(self, shard_ref, all_ref, own_sem, send_sem, recv_sem):
        dp, fsdp = lax.axis_index("dp"), lax.axis_index("fsdp")
        self.z, self.x = dp // 2, dp % 2
        self.y, self.c = fsdp // 2, fsdp % 2
        self.shard_ref, self.all_ref = shard_ref, all_ref
        self.own_sem, self.send_sem, self.recv_sem = own_sem, send_sem, recv_sem
        self.rows = shard_ref.shape[0] // (2 * PARTS)
        self.copies = {}

    def device(self, z, x, y, c):
        return (2 * z + x, 2 * y + c)

    def partners(self):
        z, x, y, c = self.z, self.x, self.y, self.c
        along = [self.device((z + k) % 4, x, y, c) for k in (1, 2, 3)]
        return along + [self.device(z, 1 - x, y, c), self.device(z, x, 1 - y, c), self.device(z, x, y, 1 - c)]

    def begin(self):
        barrier = pltpu.get_barrier_semaphore()
        for partner in self.partners():
            pl.semaphore_signal(barrier, inc=1, device_id=partner, device_id_type=MESH)
        self.own = pltpu.make_async_copy(self.shard_ref, self.all_ref.at[self.z, self.x, self.y, self.c], self.own_sem)
        self.own.start()
        pl.semaphore_wait(barrier, 6)
        self.send_along(0)

    def send_along(self, part):
        if part < PARTS:
            for route in range(2):
                for stage in range(3):
                    self.send(part, route, stage)

    def send(self, part, route, stage):
        z, x, y, c = self.z, self.x, self.y, self.c
        rows = pl.ds((2 * part + route) * self.rows, self.rows)
        partner = self.partners()[stage if stage < 3 or stage == 5 else 3 + (stage - 3 + route) % 2]
        every = slice(None)
        if stage < 3:
            place = (z, x, y, c)
        elif stage == 3:
            place = (every, x, y, c)
        elif stage == 4:
            place = (every, every, y, c) if route == 0 else (every, x, every, c)
        else:
            place = (every, every, every, c)
        target = self.all_ref.at[(*place, rows)]
        source = self.shard_ref.at[rows] if stage < 3 else target
        at = (2 * part + route) * 6 + stage
        copy = pltpu.make_async_remote_copy(
            src_ref=source,
            dst_ref=target,
            send_sem=self.send_sem.at[at],
            recv_sem=self.recv_sem.at[at],
            device_id=partner,
            device_id_type=MESH,
        )
        copy.start()
        self.copies[part, route, stage] = copy

    def advance(self, part, level):
        if level == 0 and part == 0:
            self.own.wait()
        for route in range(2):
            for stage in ((0, 1, 2), (3,), (4,), (5,))[level]:
                self.copies[part, route, stage].wait_recv()
        if level == 0:
            self.send_along(part + 1)
        if level < 3:
            for route in range(2):
                self.send(part, route, 3 + level)

    def steps(self):
        order = []
        for turn in range(PARTS + 3):
            for level in reversed(range(4)):
                if 0 <= turn - level < PARTS:
                    order.append((turn - level, level))
        return [functools.partial(self.advance, *step) for step in order]

    def end(self):
        for copy in self.copies.values():
            copy.wait_send()


def prepare_kernel(
    communicate, frames_ref, length_ref, tokens_hbm, cot_hbm, gain_ref, bias_ref, one_hot_ref, time_ref, space_ref,
    pick_ref, prev_hbm, mem_hbm, taps_ref, *refs,
):
    if communicate:
        shard_ref, one_ref, two_ref, proj_ref, all_ref, wall_ref = refs[:6]
        refs = refs[6:]
    x_hbm, normed_hbm, turned_hbm, upstream_hbm, aug_ref, table_ref, rest_hbm, tap_hbm = refs[:8]
    wide_ref, sums_ref, parts_ref, tables_ref = refs[8:12]
    tokens_ref, cot_ref, prev_ref, mem_ref, x_ref, normed_ref, turned_ref, upstream_ref, rest_ref, tap_ref = refs[12:22]
    in_sem, out_sem, refs = refs[22], refs[23], refs[24:]
    loads = [
        pltpu.make_async_copy(source, target, in_sem.at[at])
        for at, (source, target) in enumerate(
            ((cot_hbm, cot_ref), (tokens_hbm, tokens_ref), (prev_hbm, prev_ref), (mem_hbm, mem_ref))
        )
    ]
    for load in loads:
        load.start()
    saves = []

    def save(source, target):
        saves.append(pltpu.make_async_copy(source, target, out_sem.at[len(saves)]))
        saves[-1].start()

    steps = []
    if communicate:
        flat_ref, wall_own_sem, wall_send_sem, wall_recv_sem = refs[:4]
        gather = Gather(shard_ref, all_ref, *refs[4:])
        gather.begin()
        for at, part in flat_pieces(one_ref[...], two_ref[...], proj_ref[...]):
            short = jnp.zeros((part.shape[0], LANES - part.shape[1]), BF16)
            flat_ref[at : at + part.shape[0]] = jnp.concatenate([part, short], axis=1) if short.size else part
        doubling = Doubling(Neighbours(), wall_ref, (wall_send_sem, wall_recv_sem))
        first_stage = keys_of(EVERY_PIECE, 0, 0) + keys_of(FLAT, 1, 0)
        for key in first_stage:
            doubling.plan(*key)
        here = tuple(doubling.mine[name] for name in PLACE_DIMS)
        own = pltpu.make_async_copy(flat_ref, wall_ref.at[here], wall_own_sem)
        own.start()

        def first_doubling():
            own.wait()
            doubling.start(*first_stage)

        steps = gather.steps()
        steps.insert(WALL_AFTER, first_doubling)

    def advance(count=1):
        for _ in range(min(count, len(steps))):
            steps.pop(0)()

    def permute(source_ref, target_ref):
        for tile, part in enumerate(tiles_of(source_ref[...])):
            wide_ref[tile] = part.astype(F32)

        @pl.loop(0, PLACES // 2)
        def _(pair):
            first = read_place(wide_ref, 2 * pair)
            second = read_place(wide_ref, 2 * pair + 1)
            at = pl.multiple_of(pair * 16, 16)
            target_ref[pl.ds(at, 16), :] = jnp.concatenate([first, second], axis=0).astype(BF16)

    loads[0].wait()
    permute(cot_ref, upstream_ref)
    save(upstream_ref, upstream_hbm)
    loads[1].wait()
    permute(tokens_ref, x_ref)
    save(x_ref, x_hbm)
    advance()
    centred, rs = layer_stats(x_ref[...].astype(F32), D)
    normed_ref[...] = (centred * rs * gain_ref[...].reshape(1, D) + bias_ref[...].reshape(1, D)).astype(BF16)
    turned_ref[...] = normed_ref[...].T
    save(normed_ref, normed_hbm)
    save(turned_ref, turned_hbm)
    row = lax.broadcasted_iota(jnp.int32, (KEY_ROWS, LANES), 0)
    frames, length = frames_ref[0], length_ref[0]
    place = jnp.where(row < MEM_AT, row & 7, jnp.where(row < SQUEEZE_AT, row - MEM_AT, row - SQUEEZE_AT))
    limit = jnp.where(row < MEM_AT, frames, jnp.where(row < SQUEEZE_AT, length, MEM))
    off = jnp.where(place >= limit, jnp.where(lane_index((KEY_ROWS, LANES)) == MASK_LANE, MASKED, 0.0), 0.0)
    aug_ref[...] = (one_hot_ref[...].astype(F32) + off).astype(BF16)
    tables_ref[...] = jnp.zeros((LANES, LANES), F32)
    spans = 2 * HEIGHT - 1
    tables_ref[0 : 2 * FRAMES - 1, :HEAD_DIM] = time_ref[...]
    for s in range(2):
        tables_ref[15 + spans * s : 15 + spans * (s + 1), :HEAD_DIM] = space_ref[:, s]
    table_ref[...] = dot(pick_ref[...], tables_ref[...].astype(BF16)).astype(BF16)
    advance()

    def head_of(values, head):
        return values[:, HEAD_DIM * head : HEAD_DIM * head + HEAD_DIM]

    loads[2].wait()
    loads[3].wait()
    for s in range(2):
        for group in range(2):
            columns = slice(group * GROUP, (group + 1) * GROUP)
            for tile, part in enumerate(tiles_of(prev_ref[s, :, columns])):
                wide_ref[tile] = part.astype(F32)

            taps = [tiled_lanes(taps_ref[s, tap : tap + 1, :]) for tap in range(4)]

            @pl.loop(0, HEIGHT // 2)
            def _(i):
                for j in range(WIDTH // 2):
                    total = None
                    at = pl.multiple_of((i * (WIDTH // 2) + j) * FRAMES, FRAMES)
                    for tap in range(4):
                        place = (2 * i + tap // 2) * WIDTH + 2 * j + tap % 2
                        part = read_place(wide_ref, place, GROUP // LANES)
                        parts_ref[tap, pl.ds(at, FRAMES), :] = part
                        term = part * taps[tap]
                        total = term if total is None else total + term
                    sums_ref[pl.ds(at, FRAMES), :] = total

            old = mem_ref[s, :, columns].astype(F32)
            for head in range(GROUP_HEADS):
                rest = jnp.concatenate(
                    [
                        head_of(old, head),
                        jnp.zeros((SQUEEZE_AT - MEM_AT - MEM, HEAD_DIM), F32),
                        head_of(sums_ref[...], head),
                        jnp.zeros((KEY_ROWS - SQUEEZE_AT - MEM, HEAD_DIM), F32),
                    ],
                    axis=0,
                )
                rest = jnp.concatenate([rest, jnp.zeros((REST, LANES - HEAD_DIM), F32)], axis=1)
                rest_ref[s, group * GROUP_HEADS + head] = rest.astype(BF16)
                for tap in range(4):
                    part = jnp.concatenate([head_of(parts_ref[tap], head), jnp.zeros((8, HEAD_DIM), F32)], axis=0)
                    part = jnp.concatenate([part, jnp.zeros((208, LANES - HEAD_DIM), F32)], axis=1)
                    tap_ref[s, group * GROUP_HEADS + head, tap] = part.astype(BF16)
            heads = pl.ds(group * GROUP_HEADS, GROUP_HEADS)
            save(rest_ref.at[s, heads], rest_hbm.at[s, heads])
            save(tap_ref.at[s, heads], tap_hbm.at[s, heads])
            advance(3 if group + s else 2)
    advance(len(steps))
    for saved in saves:
        saved.wait()
    if communicate:
        doubling.arrive(*first_stage)
        doubling.end()
        gather.end()


def prepare(frames, length, tokens, cot, gain, bias, one_hot, rel_time, rel_space, pick, prev, memory, taps, shards=None):
    smem = pl.BlockSpec(memory_space=pltpu.SMEM)
    vmem = pl.BlockSpec(memory_space=pltpu.VMEM)
    communicate = shards is not None
    out_shape = [
        jax.ShapeDtypeStruct((ROWS, D), BF16),
        jax.ShapeDtypeStruct((ROWS, D), BF16),
        jax.ShapeDtypeStruct((D, ROWS), BF16),
        jax.ShapeDtypeStruct((ROWS, D), BF16),
        jax.ShapeDtypeStruct((KEY_ROWS, LANES), BF16),
        jax.ShapeDtypeStruct((TABLE, LANES), BF16),
        jax.ShapeDtypeStruct((2, HEADS, REST, LANES), BF16),
        jax.ShapeDtypeStruct((2, HEADS, 4, 208, LANES), BF16),
    ]
    anywhere = pl.BlockSpec(memory_space=pl.ANY)
    in_specs = [smem, smem, anywhere, anywhere] + [vmem] * 6 + [anywhere, anywhere, vmem]
    out_specs = [anywhere] * 4 + [vmem] * 2 + [anywhere] * 2
    operands = [frames, length, tokens, cot, gain, bias, one_hot, rel_time, rel_space, pick, prev, memory, taps]
    scratch = [
        wide_scratch(D),
        pltpu.VMEM((MEM, GROUP), F32),
        pltpu.VMEM((4, MEM, GROUP), F32),
        pltpu.VMEM((LANES, LANES), F32),
    ]
    scratch += [pltpu.VMEM(value.shape, value.dtype) for value in (tokens, cot, prev, memory)]
    scratch += [pltpu.VMEM(out_shape[at].shape, BF16) for at in (0, 1, 2, 3, 6, 7)]
    scratch += [pltpu.SemaphoreType.DMA((4,)), pltpu.SemaphoreType.DMA((12,))]
    more = {}
    if communicate:
        shard, one, two, proj = shards
        rows = (one.size + two.size) // LANES + 2 * proj.shape[0]
        out_shape = [
            jax.ShapeDtypeStruct((4, 2, 2, 2) + shard.shape, BF16),
            jax.ShapeDtypeStruct((2, 2, 2, 2, 2, rows, LANES), BF16),
        ] + out_shape
        in_specs += [anywhere, vmem, vmem, vmem]
        out_specs = [anywhere, anywhere] + out_specs
        operands += shards
        count = 2 * PARTS * 6
        scratch += [pltpu.VMEM((rows, LANES), BF16), pltpu.SemaphoreType.DMA]
        scratch += [pltpu.SemaphoreType.DMA((6,)), pltpu.SemaphoreType.DMA((6,))]
        scratch += [pltpu.SemaphoreType.DMA, pltpu.SemaphoreType.DMA((count,)), pltpu.SemaphoreType.DMA((count,))]
        more = {"collective_id": 0, "has_side_effects": True}
    return pl.pallas_call(
        functools.partial(prepare_kernel, communicate),
        out_shape=tuple(out_shape),
        in_specs=in_specs,
        out_specs=tuple(out_specs),
        scratch_shapes=scratch,
        compiler_params=params(**more),
        name="prepare",
    )(*operands)


def shift_frames(values, step):
    frame = lax.broadcasted_iota(jnp.int32, values.shape, values.ndim - 2)
    moved = pltpu.roll(values, step % FRAMES, values.ndim - 2)
    edge = 0 if step == 1 else FRAMES - 1
    return jnp.where(frame == edge, 0.0, moved)


def convolve(grid_ref, taps_ref, flip, i, lanes):
    sums = [None, None, None]
    for b in range(3):
        for e in range(3):
            window = grid_ref[i + b, e : e + WIDTH, :, lanes]
            for a in range(3):
                tap = 9 * a + 3 * b + e
                term = window * taps_ref[26 - tap if flip else tap, :, lanes][None]
                sums[a] = term if sums[a] is None else sums[a] + term
    return sums[1] + shift_frames(sums[0], 1) + shift_frames(sums[2], -1)


def spread_taps(raw_ref, taps_ref):
    for tap in range(27):
        line = tiled_lanes(raw_ref[0, tap : tap + 1, :])
        taps_ref[tap] = jnp.broadcast_to(line, (FRAMES, GROUP))


def clear_border(grid_ref):
    grid_ref[...] = jnp.zeros(grid_ref.shape, grid_ref.dtype)


def relative_bits(place_ref, d, f):
    return {
        "x": (d & 1) ^ place_ref[0],
        "z1": ((d >> 1) & 1) ^ place_ref[1],
        "z2": ((d >> 2) & 1) ^ place_ref[2],
        "y": ((f >> 1) & 1) ^ place_ref[3],
        "c": (f & 1) ^ place_ref[4],
    }


def slot(bits, order):
    return sum(bits[name] << at for at, name in enumerate(order))


def qkv_kernel(
    frames_ref, normed_ref, shards_ref, qkv_bias_ref, taps_raw_ref, gain_ref, bias_ref, same_ref, *refs,
):
    communicate = len(refs) > 9
    if communicate:
        refs, end = (*refs[1:6], *refs[7:11]), doubling_in_queries(refs[6], refs[11:])
    heads_ref, vhat_ref, rs_ref, mixed_ref, weight_ref, grid_ref, pooled_ref, taps_ref, line_ref = refs
    step = pl.program_id(0)

    @pl.when(step == 0)
    def _():
        clear_border(grid_ref)
        line_ref[...] = qkv_bias_ref[...].reshape(1, QKV)
        depth, columns = shards_ref.shape[2:]
        for f in range(QKV // columns):
            for d in range(DP_BLOCKS):
                weight_ref[d * depth : (d + 1) * depth, f * columns : (f + 1) * columns] = shards_ref[d, f]

    @pl.when(step % 2 == 0)
    def _():
        spread_taps(taps_raw_ref, taps_ref)

    at = pl.multiple_of(step * GROUP, LANES)
    mixed = dot(normed_ref[...], weight_ref[:, pl.ds(at, GROUP)]) + line_ref[:, pl.ds(at, GROUP)]
    row = lax.broadcasted_iota(jnp.int32, (ROWS, GROUP), 0)
    mixed = jnp.where((row & 7) < frames_ref[0], mixed, 0.0)
    mixed_ref[...] = mixed.astype(BF16)
    grid_ref[1 : HEIGHT + 1, 1 : WIDTH + 1] = mixed.reshape(HEIGHT, WIDTH, FRAMES, GROUP)

    @pl.loop(0, HEIGHT)
    def _(i):
        for tile in range(GROUP // LANES):
            lanes = slice(tile * LANES, tile * LANES + LANES)
            line = convolve(grid_ref, taps_ref, False, i, lanes)
            at = pl.multiple_of(i * WIDTH * FRAMES, WIDTH * FRAMES)
            pooled_ref[pl.ds(at, WIDTH * FRAMES), lanes] = line.reshape(WIDTH * FRAMES, LANES)

    pooled = pooled_ref[...]
    high = pooled.astype(BF16)
    low = (pooled - high.astype(F32)).astype(BF16)
    centred = pooled - (dot(high, same_ref[...]) + dot(low, same_ref[...])) * (1.0 / HEAD_DIM)
    variance = dot((centred * centred).astype(BF16), same_ref[...]) * (1.0 / HEAD_DIM)
    rs = lax.rsqrt(variance + EPSILON)
    vhat = centred * rs
    rs_ref[...] = rs
    vhat_ref[...] = vhat.astype(BF16)
    kind = pl.ds(step // 2, 1)
    out = (vhat * tiled_lanes(gain_ref[kind, :]) + tiled_lanes(bias_ref[kind, :])).astype(BF16)
    for head in range(GROUP_HEADS):
        own = out[:, HEAD_DIM * head : HEAD_DIM * (head + 1)]
        heads_ref[head] = jnp.concatenate([own, jnp.zeros((ROWS, LANES - HEAD_DIM), BF16)], axis=1)
    if communicate:
        end()


def wall_more(wall, out_shape, out_specs, scratch, operands, collective_id):
    if wall is None:
        return {}, {}
    anywhere = pl.BlockSpec(memory_space=pl.ANY)
    out_shape.append(jax.ShapeDtypeStruct(wall.shape, wall.dtype))
    out_specs.append(anywhere)
    scratch += [pltpu.SemaphoreType.DMA((18,)), pltpu.SemaphoreType.DMA((18,))]
    operands.append(wall)
    return {"collective_id": collective_id, "has_side_effects": True}, {len(operands) - 1: len(out_shape) - 1}


def query_key_value(frames, normed, shards, qkv_bias, taps, gain, bias, same, wall=None):
    smem = pl.BlockSpec(memory_space=pltpu.SMEM)
    group = pl.BlockSpec((ROWS, GROUP), lambda g: (0, g))
    out_shape = [
        jax.ShapeDtypeStruct((3 * HEADS, ROWS, LANES), BF16),
        jax.ShapeDtypeStruct((ROWS, QKV), BF16),
        jax.ShapeDtypeStruct((ROWS, QKV), F32),
        jax.ShapeDtypeStruct((ROWS, QKV), BF16),
        jax.ShapeDtypeStruct((D, QKV), BF16),
    ]
    out_specs = [
        pl.BlockSpec((GROUP_HEADS, ROWS, LANES), lambda g: (g, 0, 0)), group, group, group, whole((D, QKV))
    ]
    scratch = [
        pltpu.VMEM((HEIGHT + 2, WIDTH + 2, FRAMES, GROUP), F32),
        pltpu.VMEM((ROWS, GROUP), F32),
        pltpu.VMEM((27, FRAMES, GROUP), F32),
        pltpu.VMEM((1, QKV), F32),
    ]
    operands = [frames, normed, shards, qkv_bias, taps, gain, bias, same]
    in_specs = [
        smem,
        whole((ROWS, D)),
        whole(shards.shape),
        whole((QKV,)),
        pl.BlockSpec((1, 27, HEAD_DIM), lambda g: (g // 2, 0, 0)),
        whole((3, HEAD_DIM)),
        whole((3, HEAD_DIM)),
        whole((GROUP, GROUP)),
    ]
    more, aliases = wall_more(wall, out_shape, out_specs, scratch, operands, 4)
    return pl.pallas_call(
        qkv_kernel,
        grid=(6,),
        out_shape=tuple(out_shape),
        in_specs=in_specs + [pl.BlockSpec(memory_space=pl.ANY)] * len(aliases),
        out_specs=tuple(out_specs),
        scratch_shapes=scratch,
        input_output_aliases=aliases,
        compiler_params=params(**more),
        name="query_key_value",
    )(*operands)


def attend_kernel(
    q_ref, k_ref, v_ref, krest_ref, vrest_ref, aug_ref, table_ref, own_ref, fold_ref, *refs,
):
    communicate = len(refs) > 6
    if communicate:
        refs, end = (*refs[1:4], *refs[5:8]), doubling_in_attention(refs[4], refs[8:])
    weights_ref, pv_ref, out_ref, keys_ref, vals_ref, query_ref = refs
    lane = lane_index((KEY_ROWS, LANES))
    keys_ref[:ROWS] = k_ref[0] + aug_ref[:ROWS]
    keys_ref[ROWS:] = krest_ref[0, 0] + aug_ref[ROWS:]
    one = jnp.where(lane == HEAD_DIM, 1.0, 0.0).astype(BF16)
    vals_ref[:ROWS] = v_ref[0] + one[:ROWS]
    vals_ref[ROWS:] = vrest_ref[0, 0] + one[ROWS:]
    query = q_ref[0]
    every = (dot(query, table_ref[...], ((1,), (1,))) * ROOT).astype(BF16) * own_ref[...]
    relative = dot(every, fold_ref[...])
    marked = jnp.where(lane[:ROWS] == MASK_LANE, 1.0, relative)
    query_ref[...] = (query.astype(F32) + marked).astype(BF16)

    for rows in FORWARD_ROWS:
        scores = dot(query_ref[rows, :], keys_ref[...], ((1,), (1,)))
        largest = jnp.max(scores, axis=1, keepdims=True)
        weights = jnp.exp2((scores - largest) * (SCALE * LOG2E)).astype(BF16)
        weights_ref[0, rows, :] = weights
        total = dot(weights, vals_ref[...])
        inverse = 1.0 / total[:, HEAD_DIM : HEAD_DIM + 1]
        lane = lane_index((rows.stop - rows.start, LANES))
        pv = jnp.where(lane < HEAD_DIM, total * inverse, 0.0)
        out_ref[0, rows, :] = (pv + q_ref[0, rows, :].astype(F32)).astype(BF16)
        high = inverse.astype(BF16).astype(F32)
        extra = jnp.where(lane == HEAD_DIM, high, jnp.where(lane == HEAD_DIM + 1, inverse - high, 0.0))
        pv_ref[0, rows, :] = (pv + extra).astype(BF16)
    if communicate:
        end()


def attend(heads, rest, aug, table, own, fold, wall=None):
    head = (1, ROWS, LANES)
    tail = (1, 1, REST, LANES)
    out_shape = [
        jax.ShapeDtypeStruct((HEADS, ROWS, KEY_ROWS), BF16),
        jax.ShapeDtypeStruct((HEADS, ROWS, LANES), BF16),
        jax.ShapeDtypeStruct((HEADS, ROWS, LANES), BF16),
    ]
    out_specs = [
        pl.BlockSpec((1, ROWS, KEY_ROWS), lambda h: (h, 0, 0)),
        pl.BlockSpec(head, lambda h: (h, 0, 0)),
        pl.BlockSpec(head, lambda h: (h, 0, 0)),
    ]
    scratch = [
        pltpu.VMEM((KEY_ROWS, LANES), BF16),
        pltpu.VMEM((KEY_ROWS, LANES), BF16),
        pltpu.VMEM((ROWS, LANES), BF16),
    ]
    operands = [heads, heads, heads, rest, rest, aug, table, own, fold]
    in_specs = [
        pl.BlockSpec(head, lambda h: (h, 0, 0)),
        pl.BlockSpec(head, lambda h: (HEADS + h, 0, 0)),
        pl.BlockSpec(head, lambda h: (2 * HEADS + h, 0, 0)),
        pl.BlockSpec(tail, lambda h: (0, h, 0, 0)),
        pl.BlockSpec(tail, lambda h: (1, h, 0, 0)),
        whole((KEY_ROWS, LANES)),
        whole((TABLE, LANES)),
        whole((ROWS, TABLE)),
        whole((TABLE, LANES)),
    ]
    more, aliases = wall_more(wall, out_shape, out_specs, scratch, operands, 5)
    return pl.pallas_call(
        attend_kernel,
        grid=(HEADS,),
        out_shape=tuple(out_shape),
        in_specs=in_specs + [pl.BlockSpec(memory_space=pl.ANY)] * len(aliases),
        out_specs=tuple(out_specs),
        scratch_shapes=scratch,
        input_output_aliases=aliases,
        compiler_params=params(**more),
        name="attend",
    )(*operands)


CHUNK = 768
CHUNKS = FF // CHUNK
TILES = CHUNK // LANES


def middle_kernel(
    place_ref, att_ref, x_ref, up_ref, wp_ref, w1_ref, w2_ref, pb_ref, g2_ref, b2_ref, fb1_ref, fb2_ref,
    out_ref, dmid_ref, datt_ref, plow_ref, phigh_ref, low1_ref, high1_ref, low2_ref, high2_ref, small_ref, gb1_ref,
    packed_ref, proj_ref, mid_ref, hidden_ref, total_ref, dhid_ref, wide_ref, w1_scr, w2_scr, grad_ref,
    hiddent_ref, upt_ref,
):
    step = pl.program_id(0)
    sides = wp_ref.shape[1]
    part = D // sides
    depth = D // DP_BLOCKS
    inner = FF // DP_BLOCKS

    @pl.when(step == 0)
    def _():
        for head in range(HEADS):
            packed_ref[:, HEAD_DIM * head : HEAD_DIM * (head + 1)] = att_ref[head][:, :HEAD_DIM]
        for f in range(sides):
            for d in range(DP_BLOCKS):
                rows = slice(d * depth, (d + 1) * depth)
                proj_ref[rows, f * part : f * part + LANES] = wp_ref[d, f, :depth]
                proj_ref[rows, f * part + LANES : (f + 1) * part] = wp_ref[d, f, depth:, : part - LANES]
        middle = x_ref[...].astype(F32) + dot(packed_ref[...], proj_ref[...]) + pb_ref[...].reshape(1, D)
        mid_ref[...] = middle
        centred, rs = layer_stats(middle, D)
        hidden = centred * rs * g2_ref[...].reshape(1, D) + b2_ref[...].reshape(1, D)
        hidden_ref[...] = hidden.astype(BF16)
        hiddent_ref[...] = hidden.T.astype(BF16)
        upt_ref[...] = up_ref[...].T
        total_ref[...] = middle + fb2_ref[...].reshape(1, D).reshape(1, D)
        dhid_ref[...] = jnp.zeros((ROWS, D), F32)

    for tile in range(TILES):
        lanes = slice(tile * LANES, (tile + 1) * LANES)
        for d in range(DP_BLOCKS):
            w1_scr[d * depth : (d + 1) * depth, lanes] = w1_ref[d, 0, tile * depth : (tile + 1) * depth]
        side, at = divmod(tile, inner // LANES)
        for f in range(sides):
            w2_scr[f * part : (f + 1) * part, lanes] = w2_ref[side, f, at * part : (at + 1) * part]
    w1, w2 = w1_scr[...], w2_scr[...]
    before = dot(hidden_ref[...], w1) + fb1_ref[...]
    cdf = 0.5 + 0.5 * lax.erf(before * (2.0**-0.5))
    activated = (before * cdf).astype(BF16)
    slope = cdf + before * (jnp.exp(before * before * -0.5) * 0.3989422804014327)
    dbefore = dot(up_ref[...], w2) * slope
    dbefore_low = dbefore.astype(BF16)
    gb1_ref[...] = jnp.sum(dbefore_low.astype(F32), axis=0, keepdims=True)
    total_ref[...] += dot(activated, w2, ((1,), (1,)))
    dhid_ref[...] += dot(dbefore_low, w1, ((1,), (1,)))

    core = place_ref[4]
    grad_ref[...] = dot(upt_ref[...], activated).astype(BF16)
    for tile in range(TILES):
        lanes = slice(tile * LANES, (tile + 1) * LANES)
        side, at = divmod(tile, inner // LANES)
        rows = slice(at * part, (at + 1) * part)
        for y in range(sides // 2):
            bits = relative_bits(place_ref, side, 2 * y)
            for target_ref, c in ((low2_ref, core), (high2_ref, 1 - core)):
                start = pl.multiple_of((2 * y + c) * part, part)
                target_ref[bits["y"], bits["x"], 0, 0, rows] = grad_ref[pl.ds(start, part), lanes]
    grad_ref[...] = dot(hiddent_ref[...], dbefore_low).astype(BF16)

    def store_one(target_ref):
        for tile in range(TILES):
            lanes = slice(tile * LANES, (tile + 1) * LANES)
            for d in range(DP_BLOCKS):
                bits = relative_bits(place_ref, d, 0)
                block = grad_ref[d * depth : (d + 1) * depth, lanes]
                target_ref[bits["x"], 0, bits["z1"], bits["z2"], tile * depth : (tile + 1) * depth] = block

    @pl.when(step < CHUNKS // 2)
    def _():
        store_one(low1_ref)

    @pl.when(step >= CHUNKS // 2)
    def _():
        store_one(high1_ref)

    @pl.when(step == CHUNKS - 1)
    def _():
        @pl.loop(0, PLACES)
        def _(place):
            at = pl.multiple_of(place * FRAMES, FRAMES)
            write_place(wide_ref, place, total_ref[pl.ds(at, FRAMES), :])

        for tile in range(D // LANES):
            out_ref[:, tile * LANES : (tile + 1) * LANES] = wide_ref[tile].astype(BF16)
        upstream = up_ref[...].astype(F32)
        dhidden = dhid_ref[...]
        centred, rs = layer_stats(mid_ref[...], D)
        vhat = centred * rs
        dgain = jnp.sum(dhidden * vhat, axis=0, keepdims=True)
        dbias = jnp.sum(dhidden, axis=0, keepdims=True)
        scaled = dhidden * g2_ref[...].reshape(1, D)
        first = jnp.sum(scaled, axis=1, keepdims=True) * (1.0 / D)
        second = jnp.sum(scaled * vhat, axis=1, keepdims=True) * (1.0 / D)
        dmiddle = upstream + rs * (scaled - first - vhat * second)
        dmid_ref[...] = dmiddle
        dproj = dmiddle.astype(BF16)
        small_ref[0:1, :] = jnp.sum(dproj.astype(F32), axis=0, keepdims=True)
        small_ref[1:2, :] = dgain
        small_ref[2:3, :] = dbias
        small_ref[3:4, :] = jnp.sum(upstream, axis=0, keepdims=True)
        small_ref[4:8, :] = jnp.zeros((4, D), F32)
        grad_ref[...] = dot(packed_ref[...], dproj, ((0,), (0,))).astype(BF16)
        for d in range(DP_BLOCKS):
            rows = slice(d * depth, (d + 1) * depth)
            for y in range(sides // 2):
                bits = relative_bits(place_ref, d, 2 * y)
                where = (bits["y"], bits["x"], bits["z1"], bits["z2"])
                sides_of = [grad_ref[rows, f * part : (f + 1) * part] for f in (2 * y, 2 * y + 1)]
                for target_ref, c in ((plow_ref, core), (phigh_ref, 1 - core)):
                    block = jnp.where(c == 0, sides_of[0], sides_of[1])
                    target_ref[(*where, slice(0, depth))] = block[:, :LANES]
                    rest = jnp.concatenate([block[:, LANES:], jnp.zeros((depth, 2 * LANES - part), BF16)], axis=1)
                    target_ref[(*where, slice(depth, 2 * depth))] = rest
        datt = dot(dproj, proj_ref[...], ((1,), (1,))).astype(BF16)
        for head in range(HEADS):
            datt_ref[head] = jnp.concatenate(
                [datt[:, HEAD_DIM * head : HEAD_DIM * (head + 1)], jnp.zeros((ROWS, LANES - HEAD_DIM), BF16)],
                axis=1,
            )


def feed_forward(place, att, x, up, flat, pb, g2, b2, fb1, fb2):
    once = pl.Buffered(1)
    sides = flat.shape[1]
    part, depth = D // sides, D // DP_BLOCKS
    rows_one, rows_two = TILES * depth, FF // DP_BLOCKS // LANES * part

    def kept(shape):
        return pl.BlockSpec(shape, lambda *_: (0,) * len(shape), pipeline_mode=once)

    def side_of(s, place):
        return 2 * (place[3] ^ (s & 1)) + (place[4] ^ (s >> 1))

    def columns(s, place):
        return (0, side_of(s, place))

    def low_one(s, place):
        return (0, jnp.where(s < 2, s & 1, 1), 0, 0, 0, 0)

    def high_one(s, place):
        return (0, jnp.where(s < 2, 0, s & 1), 0, 0, 0, 0)

    def pair(s, place):
        side = side_of(s, place)
        return (0, 0, place[1] ^ (side & 1), place[2] ^ (side >> 1), 0, 0)

    bits = (2, 2, 2, 2)
    one, two, proj = bits + (rows_one, LANES), bits + (rows_two, LANES), bits + (2 * depth, LANES)
    return pl.pallas_call(
        middle_kernel,
        out_shape=(
            jax.ShapeDtypeStruct((ROWS, D), BF16),
            jax.ShapeDtypeStruct((ROWS, D), F32),
            jax.ShapeDtypeStruct((HEADS, ROWS, LANES), BF16),
            jax.ShapeDtypeStruct(proj, BF16),
            jax.ShapeDtypeStruct(proj, BF16),
            jax.ShapeDtypeStruct(one, BF16),
            jax.ShapeDtypeStruct(one, BF16),
            jax.ShapeDtypeStruct(two, BF16),
            jax.ShapeDtypeStruct(two, BF16),
            jax.ShapeDtypeStruct((8, D), F32),
            jax.ShapeDtypeStruct((1, FF), F32),
        ),
        grid_spec=pltpu.PrefetchScalarGridSpec(
            num_scalar_prefetch=1,
            grid=(CHUNKS,),
            in_specs=[
                kept((HEADS, ROWS, LANES)),
                kept((ROWS, D)),
                kept((ROWS, D)),
                pl.BlockSpec(
                    (DP_BLOCKS, sides, 2 * depth, LANES), lambda s, place: (0, 0, 6, 0), pipeline_mode=once
                ),
                pl.BlockSpec(
                    (DP_BLOCKS, 1, rows_one, LANES), lambda s, place: (0, side_of(s, place), 0, 0)
                ),
                pl.BlockSpec((2, sides, rows_two, LANES), lambda s, place: (side_of(s, place), 0, 1, 0)),
                kept((D,)),
                kept((D,)),
                kept((D,)),
                pl.BlockSpec((1, CHUNK), columns),
                kept((D,)),
            ],
            out_specs=(
                kept((ROWS, D)),
                kept((ROWS, D)),
                kept((HEADS, ROWS, LANES)),
                kept(proj),
                kept(proj),
                pl.BlockSpec((2, 1, 2, 2, rows_one, LANES), low_one),
                pl.BlockSpec((2, 1, 2, 2, rows_one, LANES), high_one),
                pl.BlockSpec((2, 2, 1, 1, rows_two, LANES), pair),
                pl.BlockSpec((2, 2, 1, 1, rows_two, LANES), pair),
                kept((8, D)),
                pl.BlockSpec((1, CHUNK), columns),
            ),
            scratch_shapes=[
                pltpu.VMEM((ROWS, D), BF16),
                pltpu.VMEM((D, D), BF16),
                pltpu.VMEM((ROWS, D), F32),
                pltpu.VMEM((ROWS, D), BF16),
                pltpu.VMEM((ROWS, D), F32),
                pltpu.VMEM((ROWS, D), F32),
                wide_scratch(D),
                pltpu.VMEM((D, CHUNK), BF16),
                pltpu.VMEM((D, CHUNK), BF16),
                pltpu.VMEM((D, CHUNK), BF16),
                pltpu.VMEM((D, ROWS), BF16),
                pltpu.VMEM((D, ROWS), BF16),
            ],
        ),
        compiler_params=params(),
        name="feed_forward",
    )(place, att, x, up, flat, flat, flat, pb, g2, b2, fb1, fb2)


SPLIT = 128
ONE_DIMS, TWO_DIMS = ("x", "y", "z1", "z2"), ("y", "x", "z1", "z2")
LINE_X, LINE_Y = ("z1", "x", "y", "z2"), ("z1", "y", "x", "z2")
PIECES = (
    (0, ONE_DIMS, ONE_DIMS),
    (1, TWO_DIMS, TWO_DIMS),
    (0, ONE_DIMS, LINE_X),
    (1, TWO_DIMS, LINE_X),
    (2, TWO_DIMS, LINE_Y),
)


def piece_rows(rows_one, rows_two, rows_proj):
    one, two = rows_one - SPLIT, rows_two - SPLIT
    return (0, one), (0, two), (one, SPLIT), (two, SPLIT), (0, rows_proj)


def pick_blocks(dims, **fixed):
    return tuple(fixed.get(name, slice(None)) for name in dims)


def without(dims, *names):
    return tuple(name for name in dims if name not in names)


def first_halving(sent, sums, kept, got, more, *sems):
    step = pl.program_id(0)
    own_sem, *sems = sems
    near = Neighbours()
    spans = piece_rows(sent[0].shape[4], sent[2].shape[4], sent[4].shape[4])
    every = range(len(PIECES))

    def own():
        copies = []
        for p in every:
            array, dims, _ = PIECES[p]
            source = sent[2 * array].at[(*pick_blocks(dims), pl.ds(*spans[p]))]
            copies.append(pltpu.make_async_copy(source, kept[p], own_sem.at[p]))
        return copies

    def fixed(route, part):
        return ({route[0]: 1, route[1]: 1}, {route[0]: 1, route[1]: 0}, {route[0]: 0})[part]

    def over_core(part):
        copies = []
        for p in every:
            array, dims, route = PIECES[p]
            where = pick_blocks(dims, **fixed(route, part))
            source = sent[2 * array + 1].at[(*where, pl.ds(*spans[p]))]
            copies.append(near.copy("c", source, got[p].at[where], sems, 3 * p + part))
        return copies

    def onward(part):
        copies = []
        for p in every:
            _, dims, route = PIECES[p]
            source = kept[p].at[pick_blocks(dims, **fixed(route, part))]
            target = more[p].at[pick_blocks(without(dims, route[0]), **{route[1]: 1 - part})]
            copies.append(near.copy(route[0], source, target, sems, 15 + 2 * p + part))
        return copies

    def arrive(part):
        for copy in over_core(part):
            copy.wait_recv()
        for p in every:
            _, dims, route = PIECES[p]
            where = pick_blocks(dims, **fixed(route, part))
            kept[p][where] = kept[p][where] + got[p][where]

    @pl.when(step == 0)
    def _():
        near.greet(("c", "x", "y", "z1"))
        for copy in over_core(0) + own():
            copy.start()

    @pl.when(step == 1)
    def _():
        for copy in own():
            copy.wait()
        arrive(0)
        for copy in onward(0) + over_core(1):
            copy.start()

    @pl.when(step == 2)
    def _():
        arrive(1)
        for copy in onward(1) + over_core(2):
            copy.start()

    @pl.when(step == 4)
    def _():
        arrive(2)

    def end():
        @pl.when(step == pl.num_programs(0) - 1)
        def _():
            for copy in onward(0) + onward(1):
                copy.wait_recv()
            for p in every:
                _, dims, route = PIECES[p]
                sums[p][...] = kept[p][pick_blocks(dims, **{route[0]: 0})] + more[p][...]
            for copy in over_core(0) + over_core(1) + over_core(2) + onward(0) + onward(1):
                copy.wait_send()

    return end


def attend_back_kernel(
    q_ref, k_ref, v_ref, krest_ref, vrest_ref, aug_ref, table_ref, own_ref, fold_ref, pick_ref,
    weights_ref, pv_ref, datt_ref, parts_ref, *refs,
):
    communicate = len(refs) > 7
    if communicate:
        sent, (grads_ref, gtable_ref, gtaps_ref), sums = refs[:6], refs[6:9], refs[9:14]
        keys_ref, vals_ref, up_ref, gsum_ref = refs[14:18]
        end = first_halving(sent, sums, refs[18:23], refs[23:28], refs[28:33], *refs[33:])
    else:
        grads_ref, gtable_ref, gtaps_ref, keys_ref, vals_ref, up_ref, gsum_ref = refs
    step = pl.program_id(0)
    lane = lane_index((KEY_ROWS, LANES))
    row_lane = lane[:ROWS]

    @pl.when(step == 0)
    def _():
        gsum_ref[...] = jnp.zeros((TABLE, LANES), F32)
        gtaps_ref[...] = jnp.zeros((2, 4, LANES), F32)

    keys_ref[:ROWS] = k_ref[0] + aug_ref[:ROWS]
    keys_ref[ROWS:] = krest_ref[0, 0] + aug_ref[ROWS:]
    one = jnp.where((lane >= HEAD_DIM) & (lane < HEAD_DIM + 3), 1.0, 0.0).astype(BF16)
    vals_ref[:ROWS] = v_ref[0] + one[:ROWS]
    vals_ref[ROWS:] = vrest_ref[0, 0] + one[ROWS:]
    pv = pv_ref[0].astype(F32)
    inverse = pv[:, HEAD_DIM : HEAD_DIM + 1] + pv[:, HEAD_DIM + 1 : HEAD_DIM + 2]
    datt = datt_ref[0].astype(F32)
    upstream = (datt * inverse).astype(BF16).astype(F32)
    mean = jnp.sum(upstream * pv, axis=1, keepdims=True)
    high = mean.astype(BF16).astype(F32)
    low = (mean - high).astype(BF16).astype(F32)
    least = mean - high - low
    extra = jnp.where(
        row_lane == HEAD_DIM,
        -high,
        jnp.where(row_lane == HEAD_DIM + 1, -low, jnp.where(row_lane == HEAD_DIM + 2, -least, 0.0)),
    )
    up_ref[...] = (upstream + extra).astype(BF16)

    dvals, dkeys, dquery = None, None, []
    for rows in BACKWARD_ROWS:
        weights = weights_ref[0, rows, :]
        dprobs = dot(up_ref[rows, :], vals_ref[...], ((1,), (1,)))
        slopes = (weights.astype(F32) * dprobs).astype(BF16)
        dquery.append(dot(slopes, keys_ref[...]))
        more_vals = dot(up_ref[rows, :], weights, ((0,), (0,)))
        more_keys = dot(q_ref[0, rows, :], slopes, ((0,), (0,)))
        dvals = more_vals if dvals is None else dvals + more_vals
        dkeys = more_keys if dkeys is None else dkeys + more_keys
    dvals, dkeys = dvals.T, dkeys.T * SCALE
    dquery = jnp.concatenate(dquery, axis=0)
    spread = dot(dquery.astype(BF16), fold_ref[...], ((1,), (1,))).astype(BF16) * own_ref[...]
    gsum_ref[...] += dot(spread, q_ref[0], ((0,), (0,)))
    dquery = dquery * SCALE + datt + dot(spread, table_ref[...])
    grads_ref[0, 0] = dquery.astype(BF16)
    grads_ref[1, 0] = dkeys[:ROWS].astype(BF16)
    grads_ref[2, 0] = dvals[:ROWS].astype(BF16)
    for s, whole_grad in ((0, dkeys), (1, dvals)):
        piece = whole_grad[SQUEEZE_AT : SQUEEZE_AT + MEM]
        for tap in range(4):
            product = piece * parts_ref[s, 0, tap].astype(F32)[:MEM]
            gtaps_ref[s, tap : tap + 1, :] += jnp.sum(product, axis=0, keepdims=True)

    @pl.when(step == pl.num_programs(0) - 1)
    def _():
        gtable_ref[...] = dot(pick_ref[...].astype(F32), gsum_ref[...], ((0,), (0,)), lax.Precision.HIGHEST)
    if communicate:
        end()


def attend_back(sent, heads, rest, aug, table, own, fold, pick, weights, pv, datt, parts):
    head = (1, ROWS, LANES)
    tail = (1, 1, REST, LANES)
    own_head = pl.BlockSpec(head, lambda h: (h, 0, 0))
    out_shape = [
        jax.ShapeDtypeStruct((3, HEADS, ROWS, LANES), BF16),
        jax.ShapeDtypeStruct((LANES, LANES), F32),
        jax.ShapeDtypeStruct((2, 4, LANES), F32),
    ]
    out_specs = [pl.BlockSpec((3, 1, ROWS, LANES), lambda h: (0, h, 0, 0)), whole((LANES, LANES)), whole((2, 4, LANES))]
    scratch = [
        pltpu.VMEM((KEY_ROWS, LANES), BF16),
        pltpu.VMEM((KEY_ROWS, LANES), BF16),
        pltpu.VMEM((ROWS, LANES), BF16),
        pltpu.VMEM((TABLE, LANES), F32),
    ]
    more = {}
    if sent:
        spans = piece_rows(sent[0].shape[4], sent[2].shape[4], sent[4].shape[4])
        for _, rows in spans:
            out_shape.append(jax.ShapeDtypeStruct((2, 2, 2, rows, LANES), BF16))
            out_specs.append(whole((2, 2, 2, rows, LANES)))
        scratch += [pltpu.VMEM((2,) * bits + (rows, LANES), BF16) for bits in (4, 4, 3) for _, rows in spans]
        scratch += [pltpu.SemaphoreType.DMA((5,)), pltpu.SemaphoreType.DMA((25,)), pltpu.SemaphoreType.DMA((25,))]
        more = {"collective_id": 2, "has_side_effects": True}
    return pl.pallas_call(
        attend_back_kernel,
        grid=(HEADS,),
        out_shape=tuple(out_shape),
        in_specs=[
            own_head,
            pl.BlockSpec(head, lambda h: (HEADS + h, 0, 0)),
            pl.BlockSpec(head, lambda h: (2 * HEADS + h, 0, 0)),
            pl.BlockSpec(tail, lambda h: (0, h, 0, 0)),
            pl.BlockSpec(tail, lambda h: (1, h, 0, 0)),
            whole((KEY_ROWS, LANES)),
            whole((TABLE, LANES)),
            whole((ROWS, TABLE)),
            whole((TABLE, LANES)),
            whole((TABLE, LANES)),
            pl.BlockSpec((1, ROWS, KEY_ROWS), lambda h: (h, 0, 0)),
            own_head,
            own_head,
            pl.BlockSpec((2, 1, 4, 208, LANES), lambda h: (0, h, 0, 0, 0)),
        ]
        + [pl.BlockSpec(memory_space=pl.ANY)] * len(sent),
        out_specs=tuple(out_specs),
        scratch_shapes=scratch,
        compiler_params=params(**more),
        name="attend_back",
    )(heads, heads, heads, rest, rest, aug, table, own, fold, pick, weights, pv, datt, parts, *sent)


def last_halving(ins, outs, got, kept, sems):
    step = pl.program_id(0)
    near = Neighbours()
    pieces = len(PIECES)
    first, second, third = got[:pieces], got[pieces : 2 * pieces], got[2 * pieces :]
    fours, twos = kept[:pieces], kept[pieces:]
    plane, line = (0, 1), (2, 3, 4)

    def copy(p, stage, part):
        _, dims, route = PIECES[p]
        dims = without(dims, *route[:stage])
        at = 5 * p + 2 * (stage - 1) + part
        fixed = {route[stage]: 1}
        if stage < 3:
            fixed[route[stage + 1]] = 1 - part
        source = (ins, fours, twos)[stage - 1][p].at[pick_blocks(dims, **fixed)]
        target = (first, second, third)[stage - 1][p]
        if stage < 3:
            target = target.at[pick_blocks(without(dims, route[stage]), **fixed)]
        return near.copy(route[stage], source, target, sems, at)

    def start(group, stage, *parts):
        for p in group:
            for part in parts:
                copy(p, stage, part).start()

    def arrive(group, stage, part):
        for p in group:
            copy(p, stage, part).wait_recv()
            _, dims, route = PIECES[p]
            dims = without(dims, *route[:stage])
            fixed = {route[stage + 1]: 1 - part}
            here = pick_blocks(dims, **{route[stage]: 0}, **fixed)
            there = pick_blocks(without(dims, route[stage]), **fixed)
            source = (ins, fours)[stage - 1][p]
            (fours, twos)[stage - 1][p][there] = source[here] + (first, second)[stage - 1][p][there]

    @pl.when(step == 0)
    def _():
        near.greet(("c", "x", "y", "z1", "z2"))
        start(plane, 1, 0)

    @pl.when(step == 1)
    def _():
        arrive(plane, 1, 0)
        start(plane, 2, 0, 1)
        start(plane, 1, 1)

    @pl.when(step == 2)
    def _():
        arrive(plane, 1, 1)
        start(line, 1, 0, 1)

    @pl.when(step == 3)
    def _():
        arrive(plane, 2, 0)
        start(plane, 3, 0)
        arrive(line, 1, 0)
        start(line, 2, 0, 1)

    @pl.when(step == 4)
    def _():
        arrive(plane, 2, 1)
        arrive(line, 1, 1)
        arrive(line, 2, 0)
        start(line, 3, 0)

    def end():
        arrive(line, 2, 1)
        for p in range(pieces):
            copy(p, 3, 0).wait_recv()
            outs[p][...] = twos[p][0].astype(F32) + third[p][...].astype(F32)
        for p in range(pieces):
            for stage in (1, 2, 3):
                for part in range(2 if stage < 3 else 1):
                    copy(p, stage, part).wait_send()

    return near, end


EARLY_ROWS = 112
EARLY_COMPRESS, EARLY_WIDE = 56, 64
DOUBLINGS = ("c", "x", "y", "z1", "z2")


def early_sums(near, table_ref, comp_ref, two_ref, gb1_ref, out_ref, vector_ref, more_ref, sems):
    step = pl.program_id(0)

    def move(stage):
        return near.copy(DOUBLINGS[stage], vector_ref.at[stage], more_ref.at[stage], sems, stage)

    @pl.when(step == 0)
    def _():
        vector_ref[0, :EARLY_COMPRESS] = table_ref[:EARLY_COMPRESS]
        for s in range(2):
            vector_ref[0, EARLY_COMPRESS + 4 * s : EARLY_COMPRESS + 4 * s + 4] = comp_ref[s]
        lines = [two_ref[at : at + 1, :] for at in range(4)] + [gb1_ref[:, at : at + D] for at in range(0, FF, D)]
        for tile in range(D // LANES):
            for at, line in enumerate(lines):
                row = EARLY_WIDE + 8 * tile + at
                vector_ref[0, row : row + 1] = line[:, tile * LANES : (tile + 1) * LANES]
        move(0).start()

    for stage in range(1, 5):

        @pl.when(step == stage)
        def _():
            move(stage - 1).wait_recv()
            vector_ref[stage] = vector_ref[stage - 1] + more_ref[stage - 1]
            move(stage).start()

    def end():
        move(4).wait_recv()
        out_ref[...] = vector_ref[4] + more_ref[4]
        for stage in range(5):
            move(stage).wait_send()

    return end


def pool_back_kernel(
    frames_ref, grads_ref, vhat_ref, rs_ref, mixed_ref, taps_raw_ref, gain_ref, same_ref, *refs,
):
    communicate = len(refs) > 6
    if communicate:
        dmix_ref, small_ref, grid_ref, dgrid_ref, sums_ref, taps_ref = (*refs[9:11], *refs[17:21])
        near, end_halving = last_halving(refs[:5], refs[11:16], refs[21:36], refs[36:46], refs[46:48])
        end_early = early_sums(near, *refs[5:9], refs[16], *refs[48:50], refs[50:52])
    else:
        dmix_ref, small_ref, grid_ref, dgrid_ref, sums_ref, taps_ref = refs
    step = pl.program_id(0)

    @pl.when(step == 0)
    def _():
        clear_border(grid_ref)
        clear_border(dgrid_ref)

    @pl.when(step % 2 == 0)
    def _():
        spread_taps(taps_raw_ref, taps_ref)

    dy = jnp.concatenate([grads_ref[0, head][:, :HEAD_DIM] for head in range(GROUP_HEADS)], axis=1).astype(F32)
    vhat = vhat_ref[...].astype(F32)
    gain = tiled_lanes(gain_ref[pl.ds(step // 2, 1), :])
    product = dy * vhat
    small_ref[0, 28:29, :] = jnp.sum(product, axis=0, keepdims=True)
    small_ref[0, 29:30, :] = jnp.sum(dy, axis=0, keepdims=True)
    small_ref[0, 30:32, :] = jnp.zeros((2, GROUP), F32)
    scaled = dy * gain
    first = dot(scaled.astype(BF16), same_ref[...]) * (1.0 / HEAD_DIM)
    second = dot((product * gain).astype(BF16), same_ref[...]) * (1.0 / HEAD_DIM)
    dpool = rs_ref[...] * (scaled - first - vhat * second)
    dgrid_ref[1 : HEIGHT + 1, 1 : WIDTH + 1] = dpool.reshape(HEIGHT, WIDTH, FRAMES, GROUP)
    grid_ref[1 : HEIGHT + 1, 1 : WIDTH + 1] = mixed_ref[...].astype(F32).reshape(HEIGHT, WIDTH, FRAMES, GROUP)
    sums_ref[...] = jnp.zeros(sums_ref.shape, F32)

    @pl.loop(0, HEIGHT)
    def _(i):
        for tile in range(GROUP // LANES):
            lanes = slice(tile * LANES, tile * LANES + LANES)
            line = convolve(dgrid_ref, taps_ref, True, i, lanes)
            frame = lax.broadcasted_iota(jnp.int32, line.shape, 1)
            line = jnp.where(frame < frames_ref[0], line, 0.0)
            at = pl.multiple_of(i * WIDTH * FRAMES, WIDTH * FRAMES)
            dmix_ref[pl.ds(at, WIDTH * FRAMES), lanes] = line.reshape(WIDTH * FRAMES, LANES).astype(BF16)
            own = dgrid_ref[i + 1, 1 : WIDTH + 1, :, lanes]
            moved = (shift_frames(own, -1), own, shift_frames(own, 1))
            for b in range(3):
                for e in range(3):
                    window = grid_ref[i + b, e : e + WIDTH, :, lanes]
                    for a in range(3):
                        tap = 9 * a + 3 * b + e
                        sums_ref[tap, :, lanes] += jnp.sum(window * moved[a], axis=0)

    for tap in range(27):
        small_ref[0, tap : tap + 1, :] = jnp.sum(sums_ref[tap], axis=0, keepdims=True)
    small_ref[0, 27:28, :] = jnp.sum(dmix_ref[...].astype(F32), axis=0, keepdims=True)
    if communicate:

        @pl.when(step == 5)
        def _():
            end_halving()
            end_early()


def pool_back(sums, smalls, frames, grads, vhat, rs, mixed, taps, gain, same):
    smem = pl.BlockSpec(memory_space=pltpu.SMEM)
    group = pl.BlockSpec((ROWS, GROUP), lambda g: (0, g))
    out_shape = [jax.ShapeDtypeStruct((ROWS, QKV), BF16), jax.ShapeDtypeStruct((6, 32, GROUP), F32)]
    out_specs = [group, pl.BlockSpec((1, 32, GROUP), lambda g: (g, 0, 0))]
    scratch = [
        pltpu.VMEM((HEIGHT + 2, WIDTH + 2, FRAMES, GROUP), F32),
        pltpu.VMEM((HEIGHT + 2, WIDTH + 2, FRAMES, GROUP), F32),
        pltpu.VMEM((27, FRAMES, GROUP), F32),
        pltpu.VMEM((27, FRAMES, GROUP), F32),
    ]
    more = {}
    if sums:
        rows = [total.shape[3] for total in sums]
        for count in (*rows, EARLY_ROWS):
            out_shape.append(jax.ShapeDtypeStruct((count, LANES), F32))
            out_specs.append(whole((count, LANES)))
        for shape in ((2, 2), (2,), (), (2, 2), (2,)):
            scratch += [pltpu.VMEM((*shape, count, LANES), BF16) for count in rows]
        scratch += [pltpu.SemaphoreType.DMA((25,))] * 2
        scratch += [pltpu.VMEM((5, EARLY_ROWS, LANES), F32)] * 2
        scratch += [pltpu.SemaphoreType.DMA((5,))] * 2
        more = {"collective_id": 3, "has_side_effects": True}
    return pl.pallas_call(
        pool_back_kernel,
        grid=(6,),
        out_shape=tuple(out_shape),
        in_specs=[
            smem,
            pl.BlockSpec((1, GROUP_HEADS, ROWS, LANES), lambda g: (g // 2, g % 2, 0, 0)),
            group,
            group,
            group,
            pl.BlockSpec((1, 27, HEAD_DIM), lambda g: (g // 2, 0, 0)),
            whole((3, HEAD_DIM)),
            whole((GROUP, GROUP)),
        ]
        + [whole(value.shape) for value in (*sums, *smalls)],
        out_specs=tuple(out_specs),
        scratch_shapes=scratch,
        compiler_params=params(**more),
        name="pool_back",
    )(frames, grads, vhat, rs, mixed, taps, gain, same, *sums, *smalls)


def project_grad_kernel(place_ref, normed_ref, dmixed_ref, one_ref, two_ref, full_ref):
    for kind in range(3):
        grad = dot(normed_ref[...], dmixed_ref[:, kind * D : (kind + 1) * D], ((0,), (0,)))
        full_ref[:, kind * D : (kind + 1) * D] = grad.astype(BF16)
    half, columns = one_ref.shape[5:]
    for f in range(QKV // columns):

        @pl.loop(0, DP_BLOCKS)
        def _(d):
            bits = relative_bits(place_ref, d, f)
            lanes = slice(f * columns, (f + 1) * columns)
            at = pl.multiple_of(2 * d * half, half)
            one_ref[bits["c"], bits["x"], bits["y"], bits["z1"], bits["z2"]] = full_ref[pl.ds(at, half), lanes]
            at = pl.multiple_of((2 * d + 1) * half, half)
            two_ref[bits["c"], bits["y"], bits["x"], bits["z1"], bits["z2"]] = full_ref[pl.ds(at, half), lanes]


def project_grad(place, normed, dmixed, sides):
    vmem = pl.BlockSpec(memory_space=pltpu.VMEM)
    half = jax.ShapeDtypeStruct((2, 2, 2, 2, 2, D // DP_BLOCKS // 2, QKV // sides), BF16)
    return pl.pallas_call(
        project_grad_kernel,
        out_shape=(half, half),
        in_specs=[pl.BlockSpec(memory_space=pltpu.SMEM)] + [vmem] * 2,
        out_specs=(vmem, vmem),
        scratch_shapes=[pltpu.VMEM((D, QKV), BF16)],
        compiler_params=params(),
        name="project_grad",
    )(place, normed, dmixed)


def project_back_kernel(dmixed_ref, weight_ref, x_ref, dmid_ref, g1_ref, gtok_ref, small_ref, dx_ref, wide_ref):
    dy = dot(dmixed_ref[...], weight_ref[...], ((1,), (1,)))
    centred, rs = layer_stats(x_ref[...].astype(F32), D)
    vhat = centred * rs
    small_ref[0:1, :] = jnp.sum(dy * vhat, axis=0, keepdims=True)
    small_ref[1:2, :] = jnp.sum(dy, axis=0, keepdims=True)
    small_ref[2:8, :] = jnp.zeros((6, D), F32)
    scaled = dy * g1_ref[...]
    first = jnp.sum(scaled, axis=1, keepdims=True) * (1.0 / D)
    second = jnp.sum(scaled * vhat, axis=1, keepdims=True) * (1.0 / D)
    dx_ref[...] = dmid_ref[...] + rs * (scaled - first - vhat * second)

    @pl.loop(0, PLACES)
    def _(place):
        at = pl.multiple_of(place * FRAMES, FRAMES)
        write_place(wide_ref, place, dx_ref[pl.ds(at, FRAMES), :])

    for tile in range(D // LANES):
        gtok_ref[:, tile * LANES : (tile + 1) * LANES] = wide_ref[tile]


def project_back(dmixed, weight, x, dmid, g1):
    vmem = pl.BlockSpec(memory_space=pltpu.VMEM)
    return pl.pallas_call(
        project_back_kernel,
        out_shape=(jax.ShapeDtypeStruct((ROWS, D), F32), jax.ShapeDtypeStruct((8, D), F32)),
        in_specs=[vmem] * 5,
        out_specs=(vmem, vmem),
        scratch_shapes=[pltpu.VMEM((ROWS, D), F32), wide_scratch(D)],
        compiler_params=params(),
        name="project_back",
    )(dmixed, weight, x, dmid, g1)


VECTOR_ROWS = 128
WIDE_AT = 96


class Scatter:
    def __init__(self, blocks_ref, out_ref, vector_ref, from_core, from_first, from_second, from_z, sems):
        dp, fsdp = lax.axis_index("dp"), lax.axis_index("fsdp")
        self.z, self.x = dp // 2, dp % 2
        self.y, self.c = fsdp // 2, fsdp % 2
        self.blocks_ref, self.out_ref, self.vector_ref = blocks_ref, out_ref, vector_ref
        self.from_core, self.from_first, self.from_second, self.from_z = from_core, from_first, from_second, from_z
        self.send_sem, self.recv_sem, self.vector_send, self.vector_recv, self.vector_more = sems
        self.rows = blocks_ref.shape[4] // (2 * PARTS)
        self.copies = {}

    def device(self, z, x, y, c):
        return (2 * z + x, 2 * y + c)

    def begin(self):
        z, x, y, c = self.z, self.x, self.y, self.c
        self.along = [self.device((z + k) % 4, x, y, c) for k in (1, 2, 3)]
        self.over_x, self.over_y = self.device(z, 1 - x, y, c), self.device(z, x, 1 - y, c)
        self.over_c, self.over_both = self.device(z, x, y, 1 - c), self.device(z, 1 - x, 1 - y, c)
        barrier = pltpu.get_barrier_semaphore()
        for partner in self.along + [self.over_x, self.over_y, self.over_both, self.over_c]:
            pl.semaphore_signal(barrier, inc=1, device_id=partner, device_id_type=MESH)
        pl.semaphore_wait(barrier, 7)

    def copy(self, source, target, send_sem, recv_sem, partner):
        copy = pltpu.make_async_remote_copy(
            src_ref=source, dst_ref=target, send_sem=send_sem, recv_sem=recv_sem, device_id=partner, device_id_type=MESH
        )
        copy.start()
        return copy

    def span(self, part, route):
        return pl.ds((2 * part + route) * self.rows, self.rows)

    def send(self, part, level):
        z, x, y, c = self.z, self.x, self.y, self.c
        every = slice(None)
        blocks = self.blocks_ref
        for route in range(2):
            span = self.span(part, route)
            if level == 0:
                moves = [(blocks.at[every, every, every, 1 - c, span], self.from_core.at[every, every, every, span], self.over_c)]
            elif level == 1:
                where = (every, 1 - x, every, c, span) if route == 0 else (every, every, 1 - y, c, span)
                moves = [(blocks.at[where], self.from_first.at[every, every, span], self.over_y if route else self.over_x)]
            elif level == 2:
                where = (every, x, 1 - y, c, span) if route == 0 else (every, 1 - x, y, c, span)
                moves = [(blocks.at[where], self.from_second.at[every, span], self.over_x if route else self.over_y)]
            else:
                moves = [
                    (blocks.at[(z + k) % 4, x, y, c, span], self.from_z.at[k - 1, span], self.along[k - 1])
                    for k in (1, 2, 3)
                ]
            for at, (source, target, partner) in enumerate(moves):
                slot = (2 * part + route) * 6 + level + at
                self.copies[part, route, level, at] = self.copy(
                    source, target, self.send_sem.at[slot], self.recv_sem.at[slot], partner
                )

    def advance(self, part, level):
        z, x, y, c = self.z, self.x, self.y, self.c
        every = slice(None)
        blocks = self.blocks_ref
        for route in range(2):
            span = self.span(part, route)
            for at in range(3 if level == 3 else 1):
                self.copies[part, route, level, at].wait_recv()
            if level == 0:
                where, more = (every, every, every, c, span), self.from_core[:, :, :, span]
            elif level == 1:
                where = (every, x, every, c, span) if route == 0 else (every, every, y, c, span)
                more = self.from_first[:, :, span]
            elif level == 2:
                where, more = (every, x, y, c, span), self.from_second[:, span]
            if level < 3:
                blocks[where] = blocks[where] + more
            else:
                total = blocks[z, x, y, c, span].astype(F32)
                for k in range(3):
                    total = total + self.from_z[k, span].astype(F32)
                self.out_ref[span] = total
        if level < 3:
            self.send(part, level + 1)

    def steps(self):
        order = []
        for turn in range(PARTS + 3):
            for level in reversed(range(4)):
                if 0 <= turn - level < PARTS:
                    order.append((turn - level, level))
        return [functools.partial(self.advance, *step) for step in order]

    def send_vector(self, stage):
        partners = ([self.over_c], [self.over_x, self.over_y, self.over_both], self.along)[stage]
        for at, partner in enumerate(partners):
            slot = (0, 1, 4)[stage] + at
            self.copies["vector", stage, at] = self.copy(
                self.vector_ref.at[stage], self.vector_more.at[slot], self.vector_send.at[slot],
                self.vector_recv.at[slot], partner,
            )

    def advance_vector(self, stage):
        total = self.vector_ref[stage]
        for at in range((1, 3, 3)[stage]):
            self.copies["vector", stage, at].wait_recv()
            total = total + self.vector_more[(0, 1, 4)[stage] + at]
        self.vector_ref[stage + 1] = total
        if stage < 2:
            self.send_vector(stage + 1)

    def end(self):
        for copy in self.copies.values():
            copy.wait_send()


def tail_kernel(
    turned_ref, dmixed_ref, weight_hbm, x_hbm, dmid_hbm, g1_ref, pools_ref,
    gqkv_ref, dx_hbm, done_ref,
    blocks_ref, vector_ref, from_core, from_first, from_second, from_z, weight_ref, x_ref, dmid_ref, dx_ref, own_sem,
    *sems,
):
    loads = [
        pltpu.make_async_copy(source, target, own_sem.at[at])
        for at, (source, target) in enumerate(((weight_hbm, weight_ref), (x_hbm, x_ref), (dmid_hbm, dmid_ref)))
    ]
    for load in loads:
        load.start()
    scatter = Scatter(blocks_ref, gqkv_ref, vector_ref, from_core, from_first, from_second, from_z, sems)
    scatter.begin()
    steps = scatter.steps()

    def advance(count):
        for _ in range(min(count, len(steps))):
            steps.pop(0)()

    depth, columns = blocks_ref.shape[4:]
    rows = depth // PARTS
    for part in range(PARTS):
        turned = [turned_ref[d * depth + part * rows : d * depth + (part + 1) * rows] for d in range(DP_BLOCKS)]
        grad = dot(jnp.concatenate(turned, axis=0), dmixed_ref[...]).astype(BF16)
        for f in range(QKV // columns):
            for d in range(DP_BLOCKS):
                block = grad[d * rows : (d + 1) * rows, f * columns : (f + 1) * columns]
                blocks_ref[d // 2, d % 2, f // 2, f % 2, part * rows : (part + 1) * rows] = block
        scatter.send(part, 0)
        advance(part)
    for load in loads:
        load.wait()
    dy = dot(dmixed_ref[...], weight_ref[...], ((1,), (1,)))
    centred, rs = layer_stats(x_ref[...].astype(F32), D)
    vhat = centred * rs
    vector_ref[0] = jnp.zeros((VECTOR_ROWS, LANES), F32)
    for kind in range(3):
        sums = pools_ref[2 * kind] + pools_ref[2 * kind + 1]
        total = sums[:, :HEAD_DIM]
        for head in range(1, GROUP_HEADS):
            total = total + sums[:, HEAD_DIM * head : HEAD_DIM * (head + 1)]
        vector_ref[0, 32 * kind : 32 * kind + 32, :HEAD_DIM] = total
    lines = [jnp.sum(dy * vhat, axis=0, keepdims=True), jnp.sum(dy, axis=0, keepdims=True)]
    lines += [
        jnp.concatenate([pools_ref[2 * kind, 27:28, :], pools_ref[2 * kind + 1, 27:28, :]], axis=1)
        for kind in range(3)
    ]
    for tile in range(D // LANES):
        for at, line in enumerate(lines):
            vector_ref[0, WIDE_AT + 5 * tile + at : WIDE_AT + 5 * tile + at + 1] = line[:, tile * LANES : (tile + 1) * LANES]
    scatter.send_vector(0)
    advance(1)
    scatter.advance_vector(0)
    advance(2)
    scaled = dy * g1_ref[...].reshape(1, D)
    first = jnp.sum(scaled, axis=1, keepdims=True) * (1.0 / D)
    second = jnp.sum(scaled * vhat, axis=1, keepdims=True) * (1.0 / D)
    dx_ref[...] = dmid_ref[...] + rs * (scaled - first - vhat * second)
    leave = pltpu.make_async_copy(dx_ref, dx_hbm, own_sem.at[3])
    leave.start()
    advance(1)
    scatter.advance_vector(1)
    advance(3)
    scatter.advance_vector(2)
    advance(len(steps))
    leave.wait()
    done_ref[...] = vector_ref[3]
    scatter.end()


def tail(turned, dmixed, weight, x, dmid, g1, pools, shard):
    vmem = pl.BlockSpec(memory_space=pltpu.VMEM)
    anywhere = pl.BlockSpec(memory_space=pl.ANY)
    depth, columns = shard
    shapes = [shard, (ROWS, D), (VECTOR_ROWS, LANES)]
    count = 2 * PARTS * 6
    return pl.pallas_call(
        tail_kernel,
        out_shape=tuple(jax.ShapeDtypeStruct(shape, F32) for shape in shapes),
        in_specs=[vmem, vmem, anywhere, anywhere, anywhere, vmem, vmem],
        out_specs=(vmem, anywhere, vmem),
        scratch_shapes=[
            pltpu.VMEM((4, 2, 2, 2, depth, columns), BF16),
            pltpu.VMEM((4, VECTOR_ROWS, LANES), F32),
            pltpu.VMEM((4, 2, 2, depth, columns), BF16),
            pltpu.VMEM((4, 2, depth, columns), BF16),
            pltpu.VMEM((4, depth, columns), BF16),
            pltpu.VMEM((3, depth, columns), BF16),
            pltpu.VMEM((D, QKV), BF16),
            pltpu.VMEM((ROWS, D), BF16),
            pltpu.VMEM((ROWS, D), F32),
            pltpu.VMEM((ROWS, D), F32),
            pltpu.SemaphoreType.DMA((4,)),
            pltpu.SemaphoreType.DMA((count,)),
            pltpu.SemaphoreType.DMA((count,)),
            pltpu.SemaphoreType.DMA((7,)),
            pltpu.SemaphoreType.DMA((7,)),
            pltpu.VMEM((7, VECTOR_ROWS, LANES), F32),
        ],
        compiler_params=params(collective_id=1, has_side_effects=True),
        name="tail",
    )(turned, dmixed, weight, x, dmid, g1, pools)


def finish_kernel(
    gqkv_ref, dx_ref, done_ref, one_ref, two_ref, one_rest_ref, two_rest_ref, proj_ref, early_ref,
    gtok_ref, ln1g_ref, ln1b_ref, wqkv_ref, qkvb_ref, conv_ref, pgain_ref, pbias_ref, time_ref, space_ref, comp_ref,
    wp_ref, projb_ref, ln2g_ref, ln2b_ref, w1_ref, fc1b_ref, w2_ref, fc2b_ref, wide_ref,
):
    @pl.loop(0, PLACES)
    def _(place):
        at = pl.multiple_of(place * FRAMES, FRAMES)
        write_place(wide_ref, place, dx_ref[pl.ds(at, FRAMES), :])

    for tile in range(D // LANES):
        gtok_ref[:, tile * LANES : (tile + 1) * LANES] = wide_ref[tile]
    wqkv_ref[...] = gqkv_ref[...]
    one = jnp.concatenate([one_ref[...], one_rest_ref[...]], axis=0)
    two = jnp.concatenate([two_ref[...], two_rest_ref[...]], axis=0)
    depth, part = w1_ref.shape[0], wp_ref.shape[1]
    for tile in range(w1_ref.shape[1] // LANES):
        w1_ref[:, tile * LANES : (tile + 1) * LANES] = one[tile * depth : (tile + 1) * depth]
    tiles = w2_ref.shape[1] // LANES
    for tile in range(tiles):
        w2_ref[:, tile * LANES : (tile + 1) * LANES] = two[tile * part : (tile + 1) * part]
    wp_ref[:, :LANES] = proj_ref[:depth]
    wp_ref[:, LANES:] = proj_ref[depth:, : part - LANES]
    for kind in range(3):
        conv_ref[kind] = done_ref[32 * kind : 32 * kind + 27, :HEAD_DIM]
        pgain_ref[kind : kind + 1, :] = done_ref[32 * kind + 28 : 32 * kind + 29, :HEAD_DIM]
        pbias_ref[kind : kind + 1, :] = done_ref[32 * kind + 29 : 32 * kind + 30, :HEAD_DIM]
    spans = 2 * HEIGHT - 1
    time_ref[...] = early_ref[:15, :HEAD_DIM]
    for s in range(2):
        start = 15 + spans * s
        space_ref[:, s] = early_ref[start : start + spans, :HEAD_DIM]
        comp_ref[s] = early_ref[EARLY_COMPRESS + 4 * s : EARLY_COMPRESS + 4 * s + 4, :HEAD_DIM]

    def line_of(source_ref, base, lines, at):
        rows = [base + lines * tile + at for tile in range(D // LANES)]
        return jnp.concatenate([source_ref[row : row + 1, :] for row in rows], axis=1).reshape(D)

    for at, target_ref in enumerate((projb_ref, ln2g_ref, ln2b_ref, fc2b_ref)):
        target_ref[...] = line_of(early_ref, EARLY_WIDE, 8, at)
    for side in range(FF // D):
        fc1b_ref[side * D : (side + 1) * D] = line_of(early_ref, EARLY_WIDE, 8, 4 + side)
    for at, target_ref in enumerate((ln1g_ref, ln1b_ref)):
        target_ref[...] = line_of(done_ref, WIDE_AT, 5, at)
    for kind in range(3):
        qkvb_ref[kind * D : (kind + 1) * D] = line_of(done_ref, WIDE_AT, 5, 2 + kind)


def finish(operands, w_qkv, w_proj, w_fc1, w_fc2):
    vmem = pl.BlockSpec(memory_space=pltpu.VMEM)
    shapes = [
        (ROWS, D), (D,), (D,), w_qkv, (QKV,), (3, 27, HEAD_DIM), (3, HEAD_DIM), (3, HEAD_DIM), (15, HEAD_DIM),
        (2 * HEIGHT - 1, 2, HEAD_DIM), (2, 4, HEAD_DIM), w_proj, (D,), (D,), (D,), w_fc1, (FF,), w_fc2[::-1], (D,),
    ]
    done = pl.pallas_call(
        finish_kernel,
        out_shape=tuple(jax.ShapeDtypeStruct(shape, F32) for shape in shapes),
        in_specs=[vmem] * 9,
        out_specs=(vmem,) * len(shapes),
        scratch_shapes=[wide_scratch(D)],
        compiler_params=params(),
        name="finish",
    )(*operands)
    done = list(done)
    done[9], done[17] = done[9].transpose(1, 0, 2), done[17].T
    return done


def row(vector):
    return vector.reshape(1, -1)


def tiled_lanes(array):
    return jnp.concatenate([array] * GROUP_HEADS, axis=-1)


def head_lanes(array):
    return jnp.pad(array, [(0, 0)] * (array.ndim - 1) + [(0, LANES - HEAD_DIM)])


DP_BLOCKS = 8
ROUTE_ONE = ("z2", "z1", "y", "x", "c")
ROUTE_TWO = ("z2", "z1", "x", "y", "c")


def together(*values):
    return lax.optimization_barrier(values)


def flat_shard(one, two, proj):
    pieces = [part for _, part in flat_pieces(one, two, proj)]
    pieces[-1] = jnp.pad(pieces[-1], ((0, 0), (0, LANES - pieces[-1].shape[1])))
    return jnp.concatenate(pieces, axis=0)


class Staged:
    def place(self):
        dp, fsdp = lax.axis_index("dp"), lax.axis_index("fsdp")
        return jnp.stack([dp & 1, (dp >> 1) & 1, (dp >> 2) & 1, (fsdp >> 1) & 1, fsdp & 1]).astype(jnp.int32)


class Plain:
    def __init__(self, dp, fsdp):
        self.dp, self.fsdp = dp, fsdp

    def place(self):
        return jnp.zeros((5,), jnp.int32)

    def gather(self, shard):
        blocks = lax.all_gather(shard, ("dp", "fsdp"), axis=0, tiled=False)
        rows, columns = shard.shape
        joined = blocks.reshape(DP_BLOCKS, self.dp // DP_BLOCKS, self.fsdp, rows, columns).transpose(0, 2, 1, 3, 4)
        return joined.reshape(DP_BLOCKS, self.fsdp, self.dp // DP_BLOCKS * rows, columns)

    def other_weights(self, one, two, proj):
        return jax.vmap(jax.vmap(flat_shard))(self.gather(one), jnp.swapaxes(self.gather(two), 2, 3), self.gather(proj))

    def scatter(self, blocks, route):
        at = {name: 4 - where for where, name in enumerate(route)}
        rows, columns = blocks.shape[5:]
        blocks = blocks.transpose([at[name] for name in ("z2", "z1", "x", "y", "c")] + [5, 6])
        split = blocks.reshape(DP_BLOCKS, self.fsdp, self.dp // DP_BLOCKS, rows * DP_BLOCKS // self.dp, columns)
        split = split.transpose(0, 2, 1, 3, 4).reshape(self.dp * self.fsdp, -1, columns)
        return lax.psum_scatter(split, ("dp", "fsdp"), scatter_dimension=0, tiled=False).astype(F32)

    def scatter_flat(self, low, high, route, unpack):
        blocks = jnp.concatenate([low[None], high[None]])
        blocks = jax.vmap(unpack)(blocks.reshape((32,) + blocks.shape[5:]))
        return self.scatter(blocks.reshape((2,) * 5 + blocks.shape[1:]), route)

    def total(self, vector):
        return lax.psum(vector, ("dp", "fsdp"))


def run(
    comm, staged, tokens, prev_kv, memory, valid_frames, mem_len, ln1_gain, ln1_bias, w_qkv, qkv_bias, pool_conv, pool_gain,
    pool_bias, rel_time, rel_space, compress, w_proj, proj_bias, ln2_gain, ln2_bias, w_fc1, fc1_bias, w_fc2,
    fc2_bias, cotangent,
):
    place = comm.place()
    fsdp = QKV // w_qkv.shape[1]
    one_hot, own, fold, pick, same = (jnp.asarray(c, BF16) for c in constants())
    taps, gains, biases = pool_conv, pool_gain, pool_bias
    prepared = prepare(
        valid_frames, mem_len, tokens, cotangent, ln1_gain, ln1_bias, one_hot, rel_time, rel_space.transpose(1, 0, 2), pick,
        prev_kv, memory, compress, [w_qkv, w_fc1, w_fc2.T, w_proj] if staged else None,
    )
    x, normed, turned, upstream, aug, table, rest, parts = prepared[-8:]
    if staged:
        first, wall = prepared[0].reshape(8, 4, *w_qkv.shape), prepared[1]
    else:
        first, wall = comm.gather(w_qkv), None
    heads, vhat, rs, mixed, weight, *wall = query_key_value(
        valid_frames, normed, first, qkv_bias, taps, gains, biases, same, wall
    )
    weights, pv, attended, *wall = attend(heads, rest, aug, table, own, fold, *wall)
    if staged:
        flat = wall[0].reshape(8, 4, *wall[0].shape[5:])
    else:
        flat = comm.other_weights(w_fc1, w_fc2, w_proj)
    out, dmid, datt, plow, phigh, low1, high1, low2, high2, small_two, gb1 = feed_forward(
        place, attended, x, upstream, flat, proj_bias, ln2_gain, ln2_bias, row(fc1_bias), fc2_bias
    )

    sent = [low1, high1, low2, high2, plow, phigh] if staged else []
    grads, gtable, gcompress, *sums = attend_back(
        sent, heads, rest, aug, table, own, fold, pick, weights, pv, datt, parts
    )
    smalls = [gtable, gcompress, small_two, gb1] if staged else []
    dmixed, pools, *sums = pool_back(sums, smalls, valid_frames, grads, vhat, rs, mixed, taps, gains, same)
    if staged:
        ended = tail(turned, dmixed, weight, x, dmid, ln1_gain, pools, w_qkv.shape)
        return (out, *finish((*ended, *sums), w_qkv.shape, w_proj.shape, w_fc1.shape, w_fc2.shape))
    depth, part = D // DP_BLOCKS, D // fsdp

    def unpack_one(block):
        return jnp.concatenate(list(block.reshape(-1, depth, LANES)), axis=1)

    def unpack_two(block):
        return jnp.concatenate(list(block.reshape(-1, part, LANES)), axis=1).T

    def unpack_proj(block):
        return jnp.concatenate([block[:depth], block[depth:, : part - LANES]], axis=1)

    w1_sum = comm.scatter_flat(low1, high1, ROUTE_ONE, unpack_one)
    w2_sum = comm.scatter_flat(low2, high2, ROUTE_TWO, unpack_two)
    wp_sum = comm.scatter_flat(plow, phigh, ROUTE_TWO, unpack_proj)
    qkv_one, qkv_two = project_grad(place, normed, dmixed, fsdp)
    gtok, small_one = project_back(dmixed, weight, x, dmid, row(ln1_gain))
    gbias = pools[:, 27].reshape(QKV)
    pools = jnp.sum(pools.reshape(3, 2, 32, GROUP_HEADS, HEAD_DIM), axis=(1, 3))
    gconv, gpool = pools[:, :27], pools[:, 28:30]
    smalls = (
        small_one[0], small_one[1], gbias, gconv, gpool[:, 0], gpool[:, 1],
        gtable[:15, :HEAD_DIM], gtable[15:53, :HEAD_DIM].reshape(2, 19, HEAD_DIM), gcompress[:, :, :HEAD_DIM],
        small_two[0], small_two[1], small_two[2], gb1[0], small_two[3],
    )
    vector = comm.total(jnp.concatenate([s.reshape(-1) for s in smalls]))
    totals, at = [], 0
    for s in smalls:
        totals.append(vector[at : at + s.size].reshape(s.shape))
        at += s.size
    qkv = comm.scatter(jnp.concatenate([qkv_one, jnp.moveaxis(qkv_two, 1, 2)], axis=5), ROUTE_ONE)
    sums = [qkv, wp_sum, w1_sum, w2_sum]
    return (
        out, gtok, totals[0], totals[1], sums[0], totals[2], totals[3], totals[4], totals[5], totals[6],
        totals[7], totals[8], sums[1], totals[9], totals[10], totals[11], sums[2], totals[12], sums[3], totals[13],
    )


def solution(mesh):
    both = P(("dp", "fsdp"))
    rows = P(("dp", "fsdp"), None)
    second = P(None, ("dp", "fsdp"), None)
    blocks = P("dp", "fsdp")
    none = P()
    dp, fsdp = mesh.shape["dp"], mesh.shape["fsdp"]
    staged = (dp, fsdp) == (8, 4)
    return jax.shard_map(
        functools.partial(run, Staged() if staged else Plain(dp, fsdp), staged),
        mesh=mesh,
        in_specs=(
            rows, second, second, both, both, none, none, blocks, none, none, none, none, none, none, none, blocks,
            none, none, none, blocks, none, blocks, none, rows,
        ),
        out_specs=(
            rows, rows, none, none, blocks, none, none, none, none, none, none, none, blocks, none, none, none,
            blocks, none, blocks, none,
        ),
        check_vma=False,
    )
```

```python
import functools

import jax
import jax.numpy as jnp
import numpy as np
from jax import lax
from jax.experimental import pallas as pl
from jax.experimental.pallas import tpu as pltpu
from jax.sharding import PartitionSpec as P

D = 768
FF = 3072
HEADS = 8
HEAD_DIM = 96
LANES = 128
FRAMES = 8
HEIGHT = 10
WIDTH = 10
PLACES = HEIGHT * WIDTH
ROWS = 800
MEM = 200
GROUP = 384
GROUP_HEADS = 4
QKV = 3 * D
KEY_ROWS = 1280
MEM_AT = 800
SQUEEZE_AT = 1024
REST = KEY_ROWS - ROWS
TABLE = 384
EPSILON = 1e-06
SCALE = HEAD_DIM**-0.5
ROOT = HEAD_DIM**0.5
LOG2E = 1.4426950408889634
MASKED = -1e9
MASK_LANE = 124
FORWARD_ROWS = (slice(0, 272), slice(272, 544), slice(544, 800))
BACKWARD_ROWS = (slice(0, 208), slice(208, 400), slice(400, 608), slice(608, 800))
BF16 = jnp.bfloat16
F32 = jnp.float32
VMEM_LIMIT = 60 * 1024 * 1024


def constants():
    place = np.arange(PLACES).repeat(FRAMES)
    row_t = np.tile(np.arange(FRAMES), PLACES)
    row_i, row_j = place // WIDTH, place % WIDTH
    one_hot = np.zeros((KEY_ROWS, LANES), np.float32)
    rows = np.arange(ROWS)
    one_hot[rows, 96 + row_t] = 1
    one_hot[rows, 104 + row_i] = 1
    one_hot[rows, 114 + row_j] = 1
    own = np.zeros((ROWS, TABLE), np.float32)
    fold = np.zeros((TABLE, LANES), np.float32)
    pick = np.zeros((TABLE, LANES), np.float32)
    for base, length, row_at, lane, offset in (
        (0, FRAMES, row_t, 96, 0),
        (64, HEIGHT, row_i, 104, 15),
        (164, WIDTH, row_j, 114, 34),
    ):
        for a in range(length):
            for b in range(length):
                column = base + a * length + b
                own[:, column] = row_at == a
                fold[column, lane + b] = 1
                pick[column, offset + a - b + length - 1] = 1
    lanes = np.arange(GROUP) // HEAD_DIM
    same = (lanes[:, None] == lanes[None, :]).astype(np.float32)
    return one_hot, own, fold, pick, same


def lane_index(shape):
    return lax.broadcasted_iota(jnp.int32, shape, len(shape) - 1)


def dot(a, b, contract=((1,), (0,)), precision=None):
    return lax.dot_general(a, b, (contract, ((), ())), preferred_element_type=F32, precision=precision)


def layer_stats(values, width):
    average = jnp.sum(values, axis=-1, keepdims=True) * (1.0 / width)
    centred = values - average
    variance = jnp.sum(centred * centred, axis=-1, keepdims=True) * (1.0 / width)
    return centred, lax.rsqrt(variance + EPSILON)


def params(**more):
    return pltpu.CompilerParams(vmem_limit_bytes=VMEM_LIMIT, **more)


def whole(shape):
    return pl.BlockSpec(shape, lambda *_: (0,) * len(shape))


def tiles_of(values):
    return [values[:, at : at + LANES] for at in range(0, values.shape[1], LANES)]


def flat_pieces(one, two, proj):
    at = 0
    for part in tiles_of(one) + tiles_of(two) + tiles_of(proj):
        yield at, part
        at += part.shape[0]


def read_place(wide_ref, place, tiles=D // LANES):
    parts = [wide_ref[tile, pl.ds(place, FRAMES, stride=PLACES), :] for tile in range(tiles)]
    return jnp.concatenate(parts, axis=1)


def write_place(wide_ref, place, values):
    for tile, part in enumerate(tiles_of(values)):
        wide_ref[tile, pl.ds(place, FRAMES, stride=PLACES), :] = part


def wide_scratch(columns):
    return pltpu.VMEM((columns // LANES, ROWS, LANES), F32)


PARTS = 3
WALL_AFTER = 6
MESH = pl.DeviceIdType.MESH


class Neighbours:
    def __init__(self):
        dp, fsdp = lax.axis_index("dp"), lax.axis_index("fsdp")
        z, x, y, c = dp // 2, dp % 2, fsdp // 2, fsdp % 2
        self.over = {
            "c": (dp, 2 * y + 1 - c),
            "x": (2 * z + 1 - x, fsdp),
            "y": (dp, 2 * (1 - y) + c),
            "z1": (2 * (z + 1 - 2 * (z % 2)) + x, fsdp),
            "z2": (2 * ((z + 2) % 4) + x, fsdp),
        }

    def greet(self, names):
        barrier = pltpu.get_barrier_semaphore()
        for name in names:
            pl.semaphore_signal(barrier, inc=1, device_id=self.over[name], device_id_type=MESH)
        pl.semaphore_wait(barrier, len(names))

    def copy(self, name, source, target, sems, at):
        return pltpu.make_async_remote_copy(
            src_ref=source,
            dst_ref=target,
            send_sem=sems[0].at[at],
            recv_sem=sems[1].at[at],
            device_id=self.over[name],
            device_id_type=MESH,
        )


PLACE_DIMS = ("z2", "z1", "x", "y", "c")
WALL_ROUTES = (
    ("z2", "z1", "y", "x", "c"),
    ("z2", "z1", "x", "y", "c"),
    ("z2", "y", "x", "z1", "c"),
    ("z2", "x", "y", "z1", "c"),
)


class Doubling:
    def __init__(self, near, wall_ref, sems):
        dp, fsdp = lax.axis_index("dp"), lax.axis_index("fsdp")
        self.mine = {"z2": dp // 4, "z1": dp // 2 % 2, "x": dp % 2, "y": fsdp // 2, "c": fsdp % 2}
        self.near, self.wall_ref, self.sems = near, wall_ref, sems
        rows = wall_ref.shape[5]
        third = rows // 3
        self.spans = ((0, third), (third, third), (2 * third, third // 2), (2 * third + third // 2, third // 2))
        self.made = {}

    def region(self, piece, free, other=()):
        where = [
            slice(None) if name in free else (1 - self.mine[name] if name in other else self.mine[name])
            for name in PLACE_DIMS
        ]
        return self.wall_ref.at[(*where, pl.ds(*self.spans[piece]))]

    def plan(self, *key):
        self.made[key] = functools.partial(self.make, *key, len(self.made))

    def make(self, piece, stage, part, at):
        route = WALL_ROUTES[piece]
        if stage < 4:
            free = route[: max(stage - 1, 0)]
            place = self.region(piece, free, route[stage - 1 : stage] if part else ())
        else:
            free, other = ((route[:3], ()), (route[:2], (route[3],)), (route[:2], (route[3], route[2])))[part]
            place = self.region(piece, free, other)
        return self.near.copy(route[stage], place, place, self.sems, at)

    def start(self, *keys):
        for key in keys:
            self.made[key]().start()

    def arrive(self, *keys):
        for key in keys:
            self.made[key]().wait_recv()

    def end(self):
        for make in self.made.values():
            make().wait_send()


FLAT, UPRIGHT, EVERY_PIECE = (0, 1), (2, 3), (0, 1, 2, 3)


def keys_of(pieces, stage, *parts):
    return [(piece, stage, part) for piece in pieces for part in parts]


def doubling_in_queries(wall_ref, sems):
    step = pl.program_id(0)
    doubling = Doubling(Neighbours(), wall_ref, sems)
    early = keys_of(FLAT, 1, 1) + keys_of(FLAT, 2, 0) + keys_of(UPRIGHT, 1, 0, 1) + keys_of(UPRIGHT, 2, 0)
    later = keys_of(EVERY_PIECE, 2, 1) + keys_of(EVERY_PIECE, 3, 0)
    for key in early + later:
        doubling.plan(*key)

    @pl.when(step == 0)
    def _():
        doubling.near.greet(("x", "y", "z1"))
        doubling.start(*early)

    @pl.when(step == 2)
    def _():
        doubling.arrive(*keys_of(FLAT, 1, 1), *keys_of(UPRIGHT, 1, 0, 1))
        doubling.start(*later)

    def end():
        @pl.when(step == 5)
        def _():
            doubling.arrive(*keys_of(EVERY_PIECE, 2, 0, 1), *keys_of(EVERY_PIECE, 3, 0))
            doubling.end()

    return end


def doubling_in_attention(wall_ref, sems):
    step = pl.program_id(0)
    doubling = Doubling(Neighbours(), wall_ref, sems)
    early = keys_of(EVERY_PIECE, 3, 1) + keys_of(EVERY_PIECE, 4, 0, 1)
    later = keys_of(EVERY_PIECE, 4, 2)
    for key in early + later:
        doubling.plan(*key)

    @pl.when(step == 0)
    def _():
        doubling.near.greet(("x", "y", "z1", "c"))
        doubling.start(*early)

    @pl.when(step == 5)
    def _():
        doubling.arrive(*keys_of(EVERY_PIECE, 3, 1))
        doubling.start(*later)

    def end():
        @pl.when(step == HEADS - 1)
        def _():
            doubling.arrive(*keys_of(EVERY_PIECE, 4, 0, 1, 2))
            doubling.end()

    return end


class Gather:
    def __init__(self, shard_ref, all_ref, own_sem, send_sem, recv_sem):
        dp, fsdp = lax.axis_index("dp"), lax.axis_index("fsdp")
        self.z, self.x = dp // 2, dp % 2
        self.y, self.c = fsdp // 2, fsdp % 2
        self.shard_ref, self.all_ref = shard_ref, all_ref
        self.own_sem, self.send_sem, self.recv_sem = own_sem, send_sem, recv_sem
        self.rows = shard_ref.shape[0] // (2 * PARTS)
        self.copies = {}

    def device(self, z, x, y, c):
        return (2 * z + x, 2 * y + c)

    def partners(self):
        z, x, y, c = self.z, self.x, self.y, self.c
        along = [self.device((z + k) % 4, x, y, c) for k in (1, 2, 3)]
        return along + [self.device(z, 1 - x, y, c), self.device(z, x, 1 - y, c), self.device(z, x, y, 1 - c)]

    def begin(self):
        barrier = pltpu.get_barrier_semaphore()
        for partner in self.partners():
            pl.semaphore_signal(barrier, inc=1, device_id=partner, device_id_type=MESH)
        self.own = pltpu.make_async_copy(self.shard_ref, self.all_ref.at[self.z, self.x, self.y, self.c], self.own_sem)
        self.own.start()
        pl.semaphore_wait(barrier, 6)
        self.send_along(0)

    def send_along(self, part):
        if part < PARTS:
            for route in range(2):
                for stage in range(3):
                    self.send(part, route, stage)

    def send(self, part, route, stage):
        z, x, y, c = self.z, self.x, self.y, self.c
        rows = pl.ds((2 * part + route) * self.rows, self.rows)
        partner = self.partners()[stage if stage < 3 or stage == 5 else 3 + (stage - 3 + route) % 2]
        every = slice(None)
        if stage < 3:
            place = (z, x, y, c)
        elif stage == 3:
            place = (every, x, y, c)
        elif stage == 4:
            place = (every, every, y, c) if route == 0 else (every, x, every, c)
        else:
            place = (every, every, every, c)
        target = self.all_ref.at[(*place, rows)]
        source = self.shard_ref.at[rows] if stage < 3 else target
        at = (2 * part + route) * 6 + stage
        copy = pltpu.make_async_remote_copy(
            src_ref=source,
            dst_ref=target,
            send_sem=self.send_sem.at[at],
            recv_sem=self.recv_sem.at[at],
            device_id=partner,
            device_id_type=MESH,
        )
        copy.start()
        self.copies[part, route, stage] = copy

    def advance(self, part, level):
        if level == 0 and part == 0:
            self.own.wait()
        for route in range(2):
            for stage in ((0, 1, 2), (3,), (4,), (5,))[level]:
                self.copies[part, route, stage].wait_recv()
        if level == 0:
            self.send_along(part + 1)
        if level < 3:
            for route in range(2):
                self.send(part, route, 3 + level)

    def steps(self):
        order = []
        for turn in range(PARTS + 3):
            for level in reversed(range(4)):
                if 0 <= turn - level < PARTS:
                    order.append((turn - level, level))
        return [functools.partial(self.advance, *step) for step in order]

    def end(self):
        for copy in self.copies.values():
            copy.wait_send()


def prepare_kernel(
    communicate, frames_ref, length_ref, tokens_hbm, cot_hbm, gain_ref, bias_ref, one_hot_ref, time_ref, space_ref,
    pick_ref, prev_hbm, mem_hbm, taps_ref, *refs,
):
    if communicate:
        shard_ref, one_ref, two_ref, proj_ref, all_ref, wall_ref = refs[:6]
        refs = refs[6:]
    x_hbm, normed_hbm, turned_hbm, upstream_hbm, aug_ref, table_ref, rest_hbm, tap_hbm = refs[:8]
    wide_ref, sums_ref, parts_ref, tables_ref = refs[8:12]
    tokens_ref, cot_ref, prev_ref, mem_ref, x_ref, normed_ref, turned_ref, upstream_ref, rest_ref, tap_ref = refs[12:22]
    in_sem, out_sem, refs = refs[22], refs[23], refs[24:]
    loads = [
        pltpu.make_async_copy(source, target, in_sem.at[at])
        for at, (source, target) in enumerate(
            ((cot_hbm, cot_ref), (tokens_hbm, tokens_ref), (prev_hbm, prev_ref), (mem_hbm, mem_ref))
        )
    ]
    for load in loads:
        load.start()
    saves = []

    def save(source, target):
        saves.append(pltpu.make_async_copy(source, target, out_sem.at[len(saves)]))
        saves[-1].start()

    steps = []
    if communicate:
        flat_ref, wall_own_sem, wall_send_sem, wall_recv_sem = refs[:4]
        gather = Gather(shard_ref, all_ref, *refs[4:])
        gather.begin()
        for at, part in flat_pieces(one_ref[...], two_ref[...], proj_ref[...]):
            short = jnp.zeros((part.shape[0], LANES - part.shape[1]), BF16)
            flat_ref[at : at + part.shape[0]] = jnp.concatenate([part, short], axis=1) if short.size else part
        doubling = Doubling(Neighbours(), wall_ref, (wall_send_sem, wall_recv_sem))
        first_stage = keys_of(EVERY_PIECE, 0, 0) + keys_of(FLAT, 1, 0)
        for key in first_stage:
            doubling.plan(*key)
        here = tuple(doubling.mine[name] for name in PLACE_DIMS)
        own = pltpu.make_async_copy(flat_ref, wall_ref.at[here], wall_own_sem)
        own.start()

        def first_doubling():
            own.wait()
            doubling.start(*first_stage)

        steps = gather.steps()
        steps.insert(WALL_AFTER, first_doubling)

    def advance(count=1):
        for _ in range(min(count, len(steps))):
            steps.pop(0)()

    def permute(source_ref, target_ref):
        for tile, part in enumerate(tiles_of(source_ref[...])):
            wide_ref[tile] = part.astype(F32)

        @pl.loop(0, PLACES // 2)
        def _(pair):
            first = read_place(wide_ref, 2 * pair)
            second = read_place(wide_ref, 2 * pair + 1)
            at = pl.multiple_of(pair * 16, 16)
            target_ref[pl.ds(at, 16), :] = jnp.concatenate([first, second], axis=0).astype(BF16)

    loads[0].wait()
    permute(cot_ref, upstream_ref)
    save(upstream_ref, upstream_hbm)
    loads[1].wait()
    permute(tokens_ref, x_ref)
    save(x_ref, x_hbm)
    advance()
    centred, rs = layer_stats(x_ref[...].astype(F32), D)
    normed_ref[...] = (centred * rs * gain_ref[...].reshape(1, D) + bias_ref[...].reshape(1, D)).astype(BF16)
    turned_ref[...] = normed_ref[...].T
    save(normed_ref, normed_hbm)
    save(turned_ref, turned_hbm)
    row = lax.broadcasted_iota(jnp.int32, (KEY_ROWS, LANES), 0)
    frames, length = frames_ref[0], length_ref[0]
    place = jnp.where(row < MEM_AT, row & 7, jnp.where(row < SQUEEZE_AT, row - MEM_AT, row - SQUEEZE_AT))
    limit = jnp.where(row < MEM_AT, frames, jnp.where(row < SQUEEZE_AT, length, MEM))
    off = jnp.where(place >= limit, jnp.where(lane_index((KEY_ROWS, LANES)) == MASK_LANE, MASKED, 0.0), 0.0)
    aug_ref[...] = (one_hot_ref[...].astype(F32) + off).astype(BF16)
    tables_ref[...] = jnp.zeros((LANES, LANES), F32)
    spans = 2 * HEIGHT - 1
    tables_ref[0 : 2 * FRAMES - 1, :HEAD_DIM] = time_ref[...]
    for s in range(2):
        tables_ref[15 + spans * s : 15 + spans * (s + 1), :HEAD_DIM] = space_ref[:, s]
    table_ref[...] = dot(pick_ref[...], tables_ref[...].astype(BF16)).astype(BF16)
    advance()

    def head_of(values, head):
        return values[:, HEAD_DIM * head : HEAD_DIM * head + HEAD_DIM]

    loads[2].wait()
    loads[3].wait()
    for s in range(2):
        for group in range(2):
            columns = slice(group * GROUP, (group + 1) * GROUP)
            for tile, part in enumerate(tiles_of(prev_ref[s, :, columns])):
                wide_ref[tile] = part.astype(F32)

            taps = [tiled_lanes(taps_ref[s, tap : tap + 1, :]) for tap in range(4)]

            @pl.loop(0, HEIGHT // 2)
            def _(i):
                for j in range(WIDTH // 2):
                    total = None
                    at = pl.multiple_of((i * (WIDTH // 2) + j) * FRAMES, FRAMES)
                    for tap in range(4):
                        place = (2 * i + tap // 2) * WIDTH + 2 * j + tap % 2
                        part = read_place(wide_ref, place, GROUP // LANES)
                        parts_ref[tap, pl.ds(at, FRAMES), :] = part
                        term = part * taps[tap]
                        total = term if total is None else total + term
                    sums_ref[pl.ds(at, FRAMES), :] = total

            old = mem_ref[s, :, columns].astype(F32)
            for head in range(GROUP_HEADS):
                rest = jnp.concatenate(
                    [
                        head_of(old, head),
                        jnp.zeros((SQUEEZE_AT - MEM_AT - MEM, HEAD_DIM), F32),
                        head_of(sums_ref[...], head),
                        jnp.zeros((KEY_ROWS - SQUEEZE_AT - MEM, HEAD_DIM), F32),
                    ],
                    axis=0,
                )
                rest = jnp.concatenate([rest, jnp.zeros((REST, LANES - HEAD_DIM), F32)], axis=1)
                rest_ref[s, group * GROUP_HEADS + head] = rest.astype(BF16)
                for tap in range(4):
                    part = jnp.concatenate([head_of(parts_ref[tap], head), jnp.zeros((8, HEAD_DIM), F32)], axis=0)
                    part = jnp.concatenate([part, jnp.zeros((208, LANES - HEAD_DIM), F32)], axis=1)
                    tap_ref[s, group * GROUP_HEADS + head, tap] = part.astype(BF16)
            heads = pl.ds(group * GROUP_HEADS, GROUP_HEADS)
            save(rest_ref.at[s, heads], rest_hbm.at[s, heads])
            save(tap_ref.at[s, heads], tap_hbm.at[s, heads])
            advance(3 if group + s else 2)
    advance(len(steps))
    for saved in saves:
        saved.wait()
    if communicate:
        doubling.arrive(*first_stage)
        doubling.end()
        gather.end()


def prepare(frames, length, tokens, cot, gain, bias, one_hot, rel_time, rel_space, pick, prev, memory, taps, shards=None):
    smem = pl.BlockSpec(memory_space=pltpu.SMEM)
    vmem = pl.BlockSpec(memory_space=pltpu.VMEM)
    communicate = shards is not None
    out_shape = [
        jax.ShapeDtypeStruct((ROWS, D), BF16),
        jax.ShapeDtypeStruct((ROWS, D), BF16),
        jax.ShapeDtypeStruct((D, ROWS), BF16),
        jax.ShapeDtypeStruct((ROWS, D), BF16),
        jax.ShapeDtypeStruct((KEY_ROWS, LANES), BF16),
        jax.ShapeDtypeStruct((TABLE, LANES), BF16),
        jax.ShapeDtypeStruct((2, HEADS, REST, LANES), BF16),
        jax.ShapeDtypeStruct((2, HEADS, 4, 208, LANES), BF16),
    ]
    anywhere = pl.BlockSpec(memory_space=pl.ANY)
    in_specs = [smem, smem, anywhere, anywhere] + [vmem] * 6 + [anywhere, anywhere, vmem]
    out_specs = [anywhere] * 4 + [vmem] * 2 + [anywhere] * 2
    operands = [frames, length, tokens, cot, gain, bias, one_hot, rel_time, rel_space, pick, prev, memory, taps]
    scratch = [
        wide_scratch(D),
        pltpu.VMEM((MEM, GROUP), F32),
        pltpu.VMEM((4, MEM, GROUP), F32),
        pltpu.VMEM((LANES, LANES), F32),
    ]
    scratch += [pltpu.VMEM(value.shape, value.dtype) for value in (tokens, cot, prev, memory)]
    scratch += [pltpu.VMEM(out_shape[at].shape, BF16) for at in (0, 1, 2, 3, 6, 7)]
    scratch += [pltpu.SemaphoreType.DMA((4,)), pltpu.SemaphoreType.DMA((12,))]
    more = {}
    if communicate:
        shard, one, two, proj = shards
        rows = (one.size + two.size) // LANES + 2 * proj.shape[0]
        out_shape = [
            jax.ShapeDtypeStruct((4, 2, 2, 2) + shard.shape, BF16),
            jax.ShapeDtypeStruct((2, 2, 2, 2, 2, rows, LANES), BF16),
        ] + out_shape
        in_specs += [anywhere, vmem, vmem, vmem]
        out_specs = [anywhere, anywhere] + out_specs
        operands += shards
        count = 2 * PARTS * 6
        scratch += [pltpu.VMEM((rows, LANES), BF16), pltpu.SemaphoreType.DMA]
        scratch += [pltpu.SemaphoreType.DMA((6,)), pltpu.SemaphoreType.DMA((6,))]
        scratch += [pltpu.SemaphoreType.DMA, pltpu.SemaphoreType.DMA((count,)), pltpu.SemaphoreType.DMA((count,))]
        more = {"collective_id": 0, "has_side_effects": True}
    return pl.pallas_call(
        functools.partial(prepare_kernel, communicate),
        out_shape=tuple(out_shape),
        in_specs=in_specs,
        out_specs=tuple(out_specs),
        scratch_shapes=scratch,
        compiler_params=params(**more),
        name="prepare",
    )(*operands)


def shift_frames(values, step):
    frame = lax.broadcasted_iota(jnp.int32, values.shape, values.ndim - 2)
    moved = pltpu.roll(values, step % FRAMES, values.ndim - 2)
    edge = 0 if step == 1 else FRAMES - 1
    return jnp.where(frame == edge, 0.0, moved)


def convolve(grid_ref, taps_ref, flip, i, lanes):
    sums = [None, None, None]
    for b in range(3):
        for e in range(3):
            window = grid_ref[i + b, e : e + WIDTH, :, lanes]
            for a in range(3):
                tap = 9 * a + 3 * b + e
                term = window * taps_ref[26 - tap if flip else tap, :, lanes][None]
                sums[a] = term if sums[a] is None else sums[a] + term
    return sums[1] + shift_frames(sums[0], 1) + shift_frames(sums[2], -1)


def spread_taps(raw_ref, taps_ref):
    for tap in range(27):
        line = tiled_lanes(raw_ref[0, tap : tap + 1, :])
        taps_ref[tap] = jnp.broadcast_to(line, (FRAMES, GROUP))


def clear_border(grid_ref):
    grid_ref[...] = jnp.zeros(grid_ref.shape, grid_ref.dtype)


def relative_bits(place_ref, d, f):
    return {
        "x": (d & 1) ^ place_ref[0],
        "z1": ((d >> 1) & 1) ^ place_ref[1],
        "z2": ((d >> 2) & 1) ^ place_ref[2],
        "y": ((f >> 1) & 1) ^ place_ref[3],
        "c": (f & 1) ^ place_ref[4],
    }


def slot(bits, order):
    return sum(bits[name] << at for at, name in enumerate(order))


def qkv_kernel(
    frames_ref, normed_ref, shards_ref, qkv_bias_ref, taps_raw_ref, gain_ref, bias_ref, same_ref, *refs,
):
    communicate = len(refs) > 9
    if communicate:
        refs, end = (*refs[1:6], *refs[7:11]), doubling_in_queries(refs[6], refs[11:])
    heads_ref, vhat_ref, rs_ref, mixed_ref, weight_ref, grid_ref, pooled_ref, taps_ref, line_ref = refs
    step = pl.program_id(0)

    @pl.when(step == 0)
    def _():
        clear_border(grid_ref)
        line_ref[...] = qkv_bias_ref[...].reshape(1, QKV)
        depth, columns = shards_ref.shape[2:]
        for f in range(QKV // columns):
            for d in range(DP_BLOCKS):
                weight_ref[d * depth : (d + 1) * depth, f * columns : (f + 1) * columns] = shards_ref[d, f]

    @pl.when(step % 2 == 0)
    def _():
        spread_taps(taps_raw_ref, taps_ref)

    at = pl.multiple_of(step * GROUP, LANES)
    mixed = dot(normed_ref[...], weight_ref[:, pl.ds(at, GROUP)]) + line_ref[:, pl.ds(at, GROUP)]
    row = lax.broadcasted_iota(jnp.int32, (ROWS, GROUP), 0)
    mixed = jnp.where((row & 7) < frames_ref[0], mixed, 0.0)
    mixed_ref[...] = mixed.astype(BF16)
    grid_ref[1 : HEIGHT + 1, 1 : WIDTH + 1] = mixed.reshape(HEIGHT, WIDTH, FRAMES, GROUP)

    @pl.loop(0, HEIGHT)
    def _(i):
        for tile in range(GROUP // LANES):
            lanes = slice(tile * LANES, tile * LANES + LANES)
            line = convolve(grid_ref, taps_ref, False, i, lanes)
            at = pl.multiple_of(i * WIDTH * FRAMES, WIDTH * FRAMES)
            pooled_ref[pl.ds(at, WIDTH * FRAMES), lanes] = line.reshape(WIDTH * FRAMES, LANES)

    pooled = pooled_ref[...]
    high = pooled.astype(BF16)
    low = (pooled - high.astype(F32)).astype(BF16)
    centred = pooled - (dot(high, same_ref[...]) + dot(low, same_ref[...])) * (1.0 / HEAD_DIM)
    variance = dot((centred * centred).astype(BF16), same_ref[...]) * (1.0 / HEAD_DIM)
    rs = lax.rsqrt(variance + EPSILON)
    vhat = centred * rs
    rs_ref[...] = rs
    vhat_ref[...] = vhat.astype(BF16)
    kind = pl.ds(step // 2, 1)
    out = (vhat * tiled_lanes(gain_ref[kind, :]) + tiled_lanes(bias_ref[kind, :])).astype(BF16)
    for head in range(GROUP_HEADS):
        own = out[:, HEAD_DIM * head : HEAD_DIM * (head + 1)]
        heads_ref[head] = jnp.concatenate([own, jnp.zeros((ROWS, LANES - HEAD_DIM), BF16)], axis=1)
    if communicate:
        end()


def wall_more(wall, out_shape, out_specs, scratch, operands, collective_id):
    if wall is None:
        return {}, {}
    anywhere = pl.BlockSpec(memory_space=pl.ANY)
    out_shape.append(jax.ShapeDtypeStruct(wall.shape, wall.dtype))
    out_specs.append(anywhere)
    scratch += [pltpu.SemaphoreType.DMA((18,)), pltpu.SemaphoreType.DMA((18,))]
    operands.append(wall)
    return {"collective_id": collective_id, "has_side_effects": True}, {len(operands) - 1: len(out_shape) - 1}


def query_key_value(frames, normed, shards, qkv_bias, taps, gain, bias, same, wall=None):
    smem = pl.BlockSpec(memory_space=pltpu.SMEM)
    group = pl.BlockSpec((ROWS, GROUP), lambda g: (0, g))
    out_shape = [
        jax.ShapeDtypeStruct((3 * HEADS, ROWS, LANES), BF16),
        jax.ShapeDtypeStruct((ROWS, QKV), BF16),
        jax.ShapeDtypeStruct((ROWS, QKV), F32),
        jax.ShapeDtypeStruct((ROWS, QKV), BF16),
        jax.ShapeDtypeStruct((D, QKV), BF16),
    ]
    out_specs = [
        pl.BlockSpec((GROUP_HEADS, ROWS, LANES), lambda g: (g, 0, 0)), group, group, group, whole((D, QKV))
    ]
    scratch = [
        pltpu.VMEM((HEIGHT + 2, WIDTH + 2, FRAMES, GROUP), F32),
        pltpu.VMEM((ROWS, GROUP), F32),
        pltpu.VMEM((27, FRAMES, GROUP), F32),
        pltpu.VMEM((1, QKV), F32),
    ]
    operands = [frames, normed, shards, qkv_bias, taps, gain, bias, same]
    in_specs = [
        smem,
        whole((ROWS, D)),
        whole(shards.shape),
        whole((QKV,)),
        pl.BlockSpec((1, 27, HEAD_DIM), lambda g: (g // 2, 0, 0)),
        whole((3, HEAD_DIM)),
        whole((3, HEAD_DIM)),
        whole((GROUP, GROUP)),
    ]
    more, aliases = wall_more(wall, out_shape, out_specs, scratch, operands, 4)
    return pl.pallas_call(
        qkv_kernel,
        grid=(6,),
        out_shape=tuple(out_shape),
        in_specs=in_specs + [pl.BlockSpec(memory_space=pl.ANY)] * len(aliases),
        out_specs=tuple(out_specs),
        scratch_shapes=scratch,
        input_output_aliases=aliases,
        compiler_params=params(**more),
        name="query_key_value",
    )(*operands)


def attend_kernel(
    q_ref, k_ref, v_ref, krest_ref, vrest_ref, aug_ref, table_ref, own_ref, fold_ref, *refs,
):
    communicate = len(refs) > 6
    if communicate:
        refs, end = (*refs[1:4], *refs[5:8]), doubling_in_attention(refs[4], refs[8:])
    weights_ref, pv_ref, out_ref, keys_ref, vals_ref, query_ref = refs
    lane = lane_index((KEY_ROWS, LANES))
    keys_ref[:ROWS] = k_ref[0] + aug_ref[:ROWS]
    keys_ref[ROWS:] = krest_ref[0, 0] + aug_ref[ROWS:]
    one = jnp.where(lane == HEAD_DIM, 1.0, 0.0).astype(BF16)
    vals_ref[:ROWS] = v_ref[0] + one[:ROWS]
    vals_ref[ROWS:] = vrest_ref[0, 0] + one[ROWS:]
    query = q_ref[0]
    every = (dot(query, table_ref[...], ((1,), (1,))) * ROOT).astype(BF16) * own_ref[...]
    relative = dot(every, fold_ref[...])
    marked = jnp.where(lane[:ROWS] == MASK_LANE, 1.0, relative)
    query_ref[...] = (query.astype(F32) + marked).astype(BF16)

    for rows in FORWARD_ROWS:
        scores = dot(query_ref[rows, :], keys_ref[...], ((1,), (1,)))
        largest = jnp.max(scores, axis=1, keepdims=True)
        weights = jnp.exp2((scores - largest) * (SCALE * LOG2E)).astype(BF16)
        weights_ref[0, rows, :] = weights
        total = dot(weights, vals_ref[...])
        inverse = 1.0 / total[:, HEAD_DIM : HEAD_DIM + 1]
        lane = lane_index((rows.stop - rows.start, LANES))
        pv = jnp.where(lane < HEAD_DIM, total * inverse, 0.0)
        out_ref[0, rows, :] = (pv + q_ref[0, rows, :].astype(F32)).astype(BF16)
        high = inverse.astype(BF16).astype(F32)
        extra = jnp.where(lane == HEAD_DIM, high, jnp.where(lane == HEAD_DIM + 1, inverse - high, 0.0))
        pv_ref[0, rows, :] = (pv + extra).astype(BF16)
    if communicate:
        end()


def attend(heads, rest, aug, table, own, fold, wall=None):
    head = (1, ROWS, LANES)
    tail = (1, 1, REST, LANES)
    out_shape = [
        jax.ShapeDtypeStruct((HEADS, ROWS, KEY_ROWS), BF16),
        jax.ShapeDtypeStruct((HEADS, ROWS, LANES), BF16),
        jax.ShapeDtypeStruct((HEADS, ROWS, LANES), BF16),
    ]
    out_specs = [
        pl.BlockSpec((1, ROWS, KEY_ROWS), lambda h: (h, 0, 0)),
        pl.BlockSpec(head, lambda h: (h, 0, 0)),
        pl.BlockSpec(head, lambda h: (h, 0, 0)),
    ]
    scratch = [
        pltpu.VMEM((KEY_ROWS, LANES), BF16),
        pltpu.VMEM((KEY_ROWS, LANES), BF16),
        pltpu.VMEM((ROWS, LANES), BF16),
    ]
    operands = [heads, heads, heads, rest, rest, aug, table, own, fold]
    in_specs = [
        pl.BlockSpec(head, lambda h: (h, 0, 0)),
        pl.BlockSpec(head, lambda h: (HEADS + h, 0, 0)),
        pl.BlockSpec(head, lambda h: (2 * HEADS + h, 0, 0)),
        pl.BlockSpec(tail, lambda h: (0, h, 0, 0)),
        pl.BlockSpec(tail, lambda h: (1, h, 0, 0)),
        whole((KEY_ROWS, LANES)),
        whole((TABLE, LANES)),
        whole((ROWS, TABLE)),
        whole((TABLE, LANES)),
    ]
    more, aliases = wall_more(wall, out_shape, out_specs, scratch, operands, 5)
    return pl.pallas_call(
        attend_kernel,
        grid=(HEADS,),
        out_shape=tuple(out_shape),
        in_specs=in_specs + [pl.BlockSpec(memory_space=pl.ANY)] * len(aliases),
        out_specs=tuple(out_specs),
        scratch_shapes=scratch,
        input_output_aliases=aliases,
        compiler_params=params(**more),
        name="attend",
    )(*operands)


CHUNK = 768
CHUNKS = FF // CHUNK
TILES = CHUNK // LANES


def middle_kernel(
    place_ref, att_ref, x_ref, up_ref, wp_ref, w1_ref, w2_ref, pb_ref, g2_ref, b2_ref, fb1_ref, fb2_ref,
    out_ref, dmid_ref, datt_ref, plow_ref, phigh_ref, low1_ref, high1_ref, low2_ref, high2_ref, small_ref, gb1_ref,
    packed_ref, proj_ref, mid_ref, hidden_ref, total_ref, dhid_ref, wide_ref, w1_scr, w2_scr, grad_ref,
    hiddent_ref, upt_ref,
):
    step = pl.program_id(0)
    sides = wp_ref.shape[1]
    part = D // sides
    depth = D // DP_BLOCKS
    inner = FF // DP_BLOCKS

    @pl.when(step == 0)
    def _():
        for head in range(HEADS):
            packed_ref[:, HEAD_DIM * head : HEAD_DIM * (head + 1)] = att_ref[head][:, :HEAD_DIM]
        for f in range(sides):
            for d in range(DP_BLOCKS):
                rows = slice(d * depth, (d + 1) * depth)
                proj_ref[rows, f * part : f * part + LANES] = wp_ref[d, f, :depth]
                proj_ref[rows, f * part + LANES : (f + 1) * part] = wp_ref[d, f, depth:, : part - LANES]
        middle = x_ref[...].astype(F32) + dot(packed_ref[...], proj_ref[...]) + pb_ref[...].reshape(1, D)
        mid_ref[...] = middle
        centred, rs = layer_stats(middle, D)
        hidden = centred * rs * g2_ref[...].reshape(1, D) + b2_ref[...].reshape(1, D)
        hidden_ref[...] = hidden.astype(BF16)
        hiddent_ref[...] = hidden.T.astype(BF16)
        upt_ref[...] = up_ref[...].T
        total_ref[...] = middle + fb2_ref[...].reshape(1, D).reshape(1, D)
        dhid_ref[...] = jnp.zeros((ROWS, D), F32)

    for tile in range(TILES):
        lanes = slice(tile * LANES, (tile + 1) * LANES)
        for d in range(DP_BLOCKS):
            w1_scr[d * depth : (d + 1) * depth, lanes] = w1_ref[d, 0, tile * depth : (tile + 1) * depth]
        side, at = divmod(tile, inner // LANES)
        for f in range(sides):
            w2_scr[f * part : (f + 1) * part, lanes] = w2_ref[side, f, at * part : (at + 1) * part]
    w1, w2 = w1_scr[...], w2_scr[...]
    before = dot(hidden_ref[...], w1) + fb1_ref[...]
    cdf = 0.5 + 0.5 * lax.erf(before * (2.0**-0.5))
    activated = (before * cdf).astype(BF16)
    slope = cdf + before * (jnp.exp(before * before * -0.5) * 0.3989422804014327)
    dbefore = dot(up_ref[...], w2) * slope
    dbefore_low = dbefore.astype(BF16)
    gb1_ref[...] = jnp.sum(dbefore_low.astype(F32), axis=0, keepdims=True)
    total_ref[...] += dot(activated, w2, ((1,), (1,)))
    dhid_ref[...] += dot(dbefore_low, w1, ((1,), (1,)))

    core = place_ref[4]
    grad_ref[...] = dot(upt_ref[...], activated).astype(BF16)
    for tile in range(TILES):
        lanes = slice(tile * LANES, (tile + 1) * LANES)
        side, at = divmod(tile, inner // LANES)
        rows = slice(at * part, (at + 1) * part)
        for y in range(sides // 2):
            bits = relative_bits(place_ref, side, 2 * y)
            for target_ref, c in ((low2_ref, core), (high2_ref, 1 - core)):
                start = pl.multiple_of((2 * y + c) * part, part)
                target_ref[bits["y"], bits["x"], 0, 0, rows] = grad_ref[pl.ds(start, part), lanes]
    grad_ref[...] = dot(hiddent_ref[...], dbefore_low).astype(BF16)

    def store_one(target_ref):
        for tile in range(TILES):
            lanes = slice(tile * LANES, (tile + 1) * LANES)
            for d in range(DP_BLOCKS):
                bits = relative_bits(place_ref, d, 0)
                block = grad_ref[d * depth : (d + 1) * depth, lanes]
                target_ref[bits["x"], 0, bits["z1"], bits["z2"], tile * depth : (tile + 1) * depth] = block

    @pl.when(step < CHUNKS // 2)
    def _():
        store_one(low1_ref)

    @pl.when(step >= CHUNKS // 2)
    def _():
        store_one(high1_ref)

    @pl.when(step == CHUNKS - 1)
    def _():
        @pl.loop(0, PLACES)
        def _(place):
            at = pl.multiple_of(place * FRAMES, FRAMES)
            write_place(wide_ref, place, total_ref[pl.ds(at, FRAMES), :])

        for tile in range(D // LANES):
            out_ref[:, tile * LANES : (tile + 1) * LANES] = wide_ref[tile].astype(BF16)
        upstream = up_ref[...].astype(F32)
        dhidden = dhid_ref[...]
        centred, rs = layer_stats(mid_ref[...], D)
        vhat = centred * rs
        dgain = jnp.sum(dhidden * vhat, axis=0, keepdims=True)
        dbias = jnp.sum(dhidden, axis=0, keepdims=True)
        scaled = dhidden * g2_ref[...].reshape(1, D)
        first = jnp.sum(scaled, axis=1, keepdims=True) * (1.0 / D)
        second = jnp.sum(scaled * vhat, axis=1, keepdims=True) * (1.0 / D)
        dmiddle = upstream + rs * (scaled - first - vhat * second)
        dmid_ref[...] = dmiddle
        dproj = dmiddle.astype(BF16)
        small_ref[0:1, :] = jnp.sum(dproj.astype(F32), axis=0, keepdims=True)
        small_ref[1:2, :] = dgain
        small_ref[2:3, :] = dbias
        small_ref[3:4, :] = jnp.sum(upstream, axis=0, keepdims=True)
        small_ref[4:8, :] = jnp.zeros((4, D), F32)
        grad_ref[...] = dot(packed_ref[...], dproj, ((0,), (0,))).astype(BF16)
        for d in range(DP_BLOCKS):
            rows = slice(d * depth, (d + 1) * depth)
            for y in range(sides // 2):
                bits = relative_bits(place_ref, d, 2 * y)
                where = (bits["y"], bits["x"], bits["z1"], bits["z2"])
                sides_of = [grad_ref[rows, f * part : (f + 1) * part] for f in (2 * y, 2 * y + 1)]
                for target_ref, c in ((plow_ref, core), (phigh_ref, 1 - core)):
                    block = jnp.where(c == 0, sides_of[0], sides_of[1])
                    target_ref[(*where, slice(0, depth))] = block[:, :LANES]
                    rest = jnp.concatenate([block[:, LANES:], jnp.zeros((depth, 2 * LANES - part), BF16)], axis=1)
                    target_ref[(*where, slice(depth, 2 * depth))] = rest
        datt = dot(dproj, proj_ref[...], ((1,), (1,))).astype(BF16)
        for head in range(HEADS):
            datt_ref[head] = jnp.concatenate(
                [datt[:, HEAD_DIM * head : HEAD_DIM * (head + 1)], jnp.zeros((ROWS, LANES - HEAD_DIM), BF16)],
                axis=1,
            )


def feed_forward(place, att, x, up, flat, pb, g2, b2, fb1, fb2):
    once = pl.Buffered(1)
    sides = flat.shape[1]
    part, depth = D // sides, D // DP_BLOCKS
    rows_one, rows_two = TILES * depth, FF // DP_BLOCKS // LANES * part

    def kept(shape):
        return pl.BlockSpec(shape, lambda *_: (0,) * len(shape), pipeline_mode=once)

    def side_of(s, place):
        return 2 * (place[3] ^ (s & 1)) + (place[4] ^ (s >> 1))

    def columns(s, place):
        return (0, side_of(s, place))

    def low_one(s, place):
        return (0, jnp.where(s < 2, s & 1, 1), 0, 0, 0, 0)

    def high_one(s, place):
        return (0, jnp.where(s < 2, 0, s & 1), 0, 0, 0, 0)

    def pair(s, place):
        side = side_of(s, place)
        return (0, 0, place[1] ^ (side & 1), place[2] ^ (side >> 1), 0, 0)

    bits = (2, 2, 2, 2)
    one, two, proj = bits + (rows_one, LANES), bits + (rows_two, LANES), bits + (2 * depth, LANES)
    return pl.pallas_call(
        middle_kernel,
        out_shape=(
            jax.ShapeDtypeStruct((ROWS, D), BF16),
            jax.ShapeDtypeStruct((ROWS, D), F32),
            jax.ShapeDtypeStruct((HEADS, ROWS, LANES), BF16),
            jax.ShapeDtypeStruct(proj, BF16),
            jax.ShapeDtypeStruct(proj, BF16),
            jax.ShapeDtypeStruct(one, BF16),
            jax.ShapeDtypeStruct(one, BF16),
            jax.ShapeDtypeStruct(two, BF16),
            jax.ShapeDtypeStruct(two, BF16),
            jax.ShapeDtypeStruct((8, D), F32),
            jax.ShapeDtypeStruct((1, FF), F32),
        ),
        grid_spec=pltpu.PrefetchScalarGridSpec(
            num_scalar_prefetch=1,
            grid=(CHUNKS,),
            in_specs=[
                kept((HEADS, ROWS, LANES)),
                kept((ROWS, D)),
                kept((ROWS, D)),
                pl.BlockSpec(
                    (DP_BLOCKS, sides, 2 * depth, LANES), lambda s, place: (0, 0, 6, 0), pipeline_mode=once
                ),
                pl.BlockSpec(
                    (DP_BLOCKS, 1, rows_one, LANES), lambda s, place: (0, side_of(s, place), 0, 0)
                ),
                pl.BlockSpec((2, sides, rows_two, LANES), lambda s, place: (side_of(s, place), 0, 1, 0)),
                kept((D,)),
                kept((D,)),
                kept((D,)),
                pl.BlockSpec((1, CHUNK), columns),
                kept((D,)),
            ],
            out_specs=(
                kept((ROWS, D)),
                kept((ROWS, D)),
                kept((HEADS, ROWS, LANES)),
                kept(proj),
                kept(proj),
                pl.BlockSpec((2, 1, 2, 2, rows_one, LANES), low_one),
                pl.BlockSpec((2, 1, 2, 2, rows_one, LANES), high_one),
                pl.BlockSpec((2, 2, 1, 1, rows_two, LANES), pair),
                pl.BlockSpec((2, 2, 1, 1, rows_two, LANES), pair),
                kept((8, D)),
                pl.BlockSpec((1, CHUNK), columns),
            ),
            scratch_shapes=[
                pltpu.VMEM((ROWS, D), BF16),
                pltpu.VMEM((D, D), BF16),
                pltpu.VMEM((ROWS, D), F32),
                pltpu.VMEM((ROWS, D), BF16),
                pltpu.VMEM((ROWS, D), F32),
                pltpu.VMEM((ROWS, D), F32),
                wide_scratch(D),
                pltpu.VMEM((D, CHUNK), BF16),
                pltpu.VMEM((D, CHUNK), BF16),
                pltpu.VMEM((D, CHUNK), BF16),
                pltpu.VMEM((D, ROWS), BF16),
                pltpu.VMEM((D, ROWS), BF16),
            ],
        ),
        compiler_params=params(),
        name="feed_forward",
    )(place, att, x, up, flat, flat, flat, pb, g2, b2, fb1, fb2)


SPLIT = 128
ONE_DIMS, TWO_DIMS = ("x", "y", "z1", "z2"), ("y", "x", "z1", "z2")
LINE_X, LINE_Y = ("z1", "x", "y", "z2"), ("z1", "y", "x", "z2")
PIECES = (
    (0, ONE_DIMS, ONE_DIMS),
    (1, TWO_DIMS, TWO_DIMS),
    (0, ONE_DIMS, LINE_X),
    (1, TWO_DIMS, LINE_X),
    (2, TWO_DIMS, LINE_Y),
)


def piece_rows(rows_one, rows_two, rows_proj):
    one, two = rows_one - SPLIT, rows_two - SPLIT
    return (0, one), (0, two), (one, SPLIT), (two, SPLIT), (0, rows_proj)


def pick_blocks(dims, **fixed):
    return tuple(fixed.get(name, slice(None)) for name in dims)


def without(dims, *names):
    return tuple(name for name in dims if name not in names)


def first_halving(sent, sums, kept, got, more, *sems):
    step = pl.program_id(0)
    own_sem, *sems = sems
    near = Neighbours()
    spans = piece_rows(sent[0].shape[4], sent[2].shape[4], sent[4].shape[4])
    every = range(len(PIECES))

    def own():
        copies = []
        for p in every:
            array, dims, _ = PIECES[p]
            source = sent[2 * array].at[(*pick_blocks(dims), pl.ds(*spans[p]))]
            copies.append(pltpu.make_async_copy(source, kept[p], own_sem.at[p]))
        return copies

    def fixed(route, part):
        return ({route[0]: 1, route[1]: 1}, {route[0]: 1, route[1]: 0}, {route[0]: 0})[part]

    def over_core(part):
        copies = []
        for p in every:
            array, dims, route = PIECES[p]
            where = pick_blocks(dims, **fixed(route, part))
            source = sent[2 * array + 1].at[(*where, pl.ds(*spans[p]))]
            copies.append(near.copy("c", source, got[p].at[where], sems, 3 * p + part))
        return copies

    def onward(part):
        copies = []
        for p in every:
            _, dims, route = PIECES[p]
            source = kept[p].at[pick_blocks(dims, **fixed(route, part))]
            target = more[p].at[pick_blocks(without(dims, route[0]), **{route[1]: 1 - part})]
            copies.append(near.copy(route[0], source, target, sems, 15 + 2 * p + part))
        return copies

    def arrive(part):
        for copy in over_core(part):
            copy.wait_recv()
        for p in every:
            _, dims, route = PIECES[p]
            where = pick_blocks(dims, **fixed(route, part))
            kept[p][where] = kept[p][where] + got[p][where]

    @pl.when(step == 0)
    def _():
        near.greet(("c", "x", "y", "z1"))
        for copy in over_core(0) + own():
            copy.start()

    @pl.when(step == 1)
    def _():
        for copy in own():
            copy.wait()
        arrive(0)
        for copy in onward(0) + over_core(1):
            copy.start()

    @pl.when(step == 2)
    def _():
        arrive(1)
        for copy in onward(1) + over_core(2):
            copy.start()

    @pl.when(step == 4)
    def _():
        arrive(2)

    def end():
        @pl.when(step == pl.num_programs(0) - 1)
        def _():
            for copy in onward(0) + onward(1):
                copy.wait_recv()
            for p in every:
                _, dims, route = PIECES[p]
                sums[p][...] = kept[p][pick_blocks(dims, **{route[0]: 0})] + more[p][...]
            for copy in over_core(0) + over_core(1) + over_core(2) + onward(0) + onward(1):
                copy.wait_send()

    return end


def attend_back_kernel(
    q_ref, k_ref, v_ref, krest_ref, vrest_ref, aug_ref, table_ref, own_ref, fold_ref, pick_ref,
    weights_ref, pv_ref, datt_ref, parts_ref, *refs,
):
    communicate = len(refs) > 7
    if communicate:
        sent, (grads_ref, gtable_ref, gtaps_ref), sums = refs[:6], refs[6:9], refs[9:14]
        keys_ref, vals_ref, up_ref, gsum_ref = refs[14:18]
        end = first_halving(sent, sums, refs[18:23], refs[23:28], refs[28:33], *refs[33:])
    else:
        grads_ref, gtable_ref, gtaps_ref, keys_ref, vals_ref, up_ref, gsum_ref = refs
    step = pl.program_id(0)
    lane = lane_index((KEY_ROWS, LANES))
    row_lane = lane[:ROWS]

    @pl.when(step == 0)
    def _():
        gsum_ref[...] = jnp.zeros((TABLE, LANES), F32)
        gtaps_ref[...] = jnp.zeros((2, 4, LANES), F32)

    keys_ref[:ROWS] = k_ref[0] + aug_ref[:ROWS]
    keys_ref[ROWS:] = krest_ref[0, 0] + aug_ref[ROWS:]
    one = jnp.where((lane >= HEAD_DIM) & (lane < HEAD_DIM + 3), 1.0, 0.0).astype(BF16)
    vals_ref[:ROWS] = v_ref[0] + one[:ROWS]
    vals_ref[ROWS:] = vrest_ref[0, 0] + one[ROWS:]
    pv = pv_ref[0].astype(F32)
    inverse = pv[:, HEAD_DIM : HEAD_DIM + 1] + pv[:, HEAD_DIM + 1 : HEAD_DIM + 2]
    datt = datt_ref[0].astype(F32)
    upstream = (datt * inverse).astype(BF16).astype(F32)
    mean = jnp.sum(upstream * pv, axis=1, keepdims=True)
    high = mean.astype(BF16).astype(F32)
    low = (mean - high).astype(BF16).astype(F32)
    least = mean - high - low
    extra = jnp.where(
        row_lane == HEAD_DIM,
        -high,
        jnp.where(row_lane == HEAD_DIM + 1, -low, jnp.where(row_lane == HEAD_DIM + 2, -least, 0.0)),
    )
    up_ref[...] = (upstream + extra).astype(BF16)

    dvals, dkeys, dquery = None, None, []
    for rows in BACKWARD_ROWS:
        weights = weights_ref[0, rows, :]
        dprobs = dot(up_ref[rows, :], vals_ref[...], ((1,), (1,)))
        slopes = (weights.astype(F32) * dprobs).astype(BF16)
        dquery.append(dot(slopes, keys_ref[...]))
        more_vals = dot(up_ref[rows, :], weights, ((0,), (0,)))
        more_keys = dot(q_ref[0, rows, :], slopes, ((0,), (0,)))
        dvals = more_vals if dvals is None else dvals + more_vals
        dkeys = more_keys if dkeys is None else dkeys + more_keys
    dvals, dkeys = dvals.T, dkeys.T * SCALE
    dquery = jnp.concatenate(dquery, axis=0)
    spread = dot(dquery.astype(BF16), fold_ref[...], ((1,), (1,))).astype(BF16) * own_ref[...]
    gsum_ref[...] += dot(spread, q_ref[0], ((0,), (0,)))
    dquery = dquery * SCALE + datt + dot(spread, table_ref[...])
    grads_ref[0, 0] = dquery.astype(BF16)
    grads_ref[1, 0] = dkeys[:ROWS].astype(BF16)
    grads_ref[2, 0] = dvals[:ROWS].astype(BF16)
    for s, whole_grad in ((0, dkeys), (1, dvals)):
        piece = whole_grad[SQUEEZE_AT : SQUEEZE_AT + MEM]
        for tap in range(4):
            product = piece * parts_ref[s, 0, tap].astype(F32)[:MEM]
            gtaps_ref[s, tap : tap + 1, :] += jnp.sum(product, axis=0, keepdims=True)

    @pl.when(step == pl.num_programs(0) - 1)
    def _():
        gtable_ref[...] = dot(pick_ref[...].astype(F32), gsum_ref[...], ((0,), (0,)), lax.Precision.HIGHEST)
    if communicate:
        end()


def attend_back(sent, heads, rest, aug, table, own, fold, pick, weights, pv, datt, parts):
    head = (1, ROWS, LANES)
    tail = (1, 1, REST, LANES)
    own_head = pl.BlockSpec(head, lambda h: (h, 0, 0))
    out_shape = [
        jax.ShapeDtypeStruct((3, HEADS, ROWS, LANES), BF16),
        jax.ShapeDtypeStruct((LANES, LANES), F32),
        jax.ShapeDtypeStruct((2, 4, LANES), F32),
    ]
    out_specs = [pl.BlockSpec((3, 1, ROWS, LANES), lambda h: (0, h, 0, 0)), whole((LANES, LANES)), whole((2, 4, LANES))]
    scratch = [
        pltpu.VMEM((KEY_ROWS, LANES), BF16),
        pltpu.VMEM((KEY_ROWS, LANES), BF16),
        pltpu.VMEM((ROWS, LANES), BF16),
        pltpu.VMEM((TABLE, LANES), F32),
    ]
    more = {}
    if sent:
        spans = piece_rows(sent[0].shape[4], sent[2].shape[4], sent[4].shape[4])
        for _, rows in spans:
            out_shape.append(jax.ShapeDtypeStruct((2, 2, 2, rows, LANES), BF16))
            out_specs.append(whole((2, 2, 2, rows, LANES)))
        scratch += [pltpu.VMEM((2,) * bits + (rows, LANES), BF16) for bits in (4, 4, 3) for _, rows in spans]
        scratch += [pltpu.SemaphoreType.DMA((5,)), pltpu.SemaphoreType.DMA((25,)), pltpu.SemaphoreType.DMA((25,))]
        more = {"collective_id": 2, "has_side_effects": True}
    return pl.pallas_call(
        attend_back_kernel,
        grid=(HEADS,),
        out_shape=tuple(out_shape),
        in_specs=[
            own_head,
            pl.BlockSpec(head, lambda h: (HEADS + h, 0, 0)),
            pl.BlockSpec(head, lambda h: (2 * HEADS + h, 0, 0)),
            pl.BlockSpec(tail, lambda h: (0, h, 0, 0)),
            pl.BlockSpec(tail, lambda h: (1, h, 0, 0)),
            whole((KEY_ROWS, LANES)),
            whole((TABLE, LANES)),
            whole((ROWS, TABLE)),
            whole((TABLE, LANES)),
            whole((TABLE, LANES)),
            pl.BlockSpec((1, ROWS, KEY_ROWS), lambda h: (h, 0, 0)),
            own_head,
            own_head,
            pl.BlockSpec((2, 1, 4, 208, LANES), lambda h: (0, h, 0, 0, 0)),
        ]
        + [pl.BlockSpec(memory_space=pl.ANY)] * len(sent),
        out_specs=tuple(out_specs),
        scratch_shapes=scratch,
        compiler_params=params(**more),
        name="attend_back",
    )(heads, heads, heads, rest, rest, aug, table, own, fold, pick, weights, pv, datt, parts, *sent)


def last_halving(ins, outs, got, kept, sems):
    step = pl.program_id(0)
    near = Neighbours()
    pieces = len(PIECES)
    first, second, third = got[:pieces], got[pieces : 2 * pieces], got[2 * pieces :]
    fours, twos = kept[:pieces], kept[pieces:]
    plane, line = (0, 1), (2, 3, 4)

    def copy(p, stage, part):
        _, dims, route = PIECES[p]
        dims = without(dims, *route[:stage])
        at = 5 * p + 2 * (stage - 1) + part
        fixed = {route[stage]: 1}
        if stage < 3:
            fixed[route[stage + 1]] = 1 - part
        source = (ins, fours, twos)[stage - 1][p].at[pick_blocks(dims, **fixed)]
        target = (first, second, third)[stage - 1][p]
        if stage < 3:
            target = target.at[pick_blocks(without(dims, route[stage]), **fixed)]
        return near.copy(route[stage], source, target, sems, at)

    def start(group, stage, *parts):
        for p in group:
            for part in parts:
                copy(p, stage, part).start()

    def arrive(group, stage, part):
        for p in group:
            copy(p, stage, part).wait_recv()
            _, dims, route = PIECES[p]
            dims = without(dims, *route[:stage])
            fixed = {route[stage + 1]: 1 - part}
            here = pick_blocks(dims, **{route[stage]: 0}, **fixed)
            there = pick_blocks(without(dims, route[stage]), **fixed)
            source = (ins, fours)[stage - 1][p]
            (fours, twos)[stage - 1][p][there] = source[here] + (first, second)[stage - 1][p][there]

    @pl.when(step == 0)
    def _():
        near.greet(("c", "x", "y", "z1", "z2"))
        start(plane, 1, 0)

    @pl.when(step == 1)
    def _():
        arrive(plane, 1, 0)
        start(plane, 2, 0)
        start(plane, 1, 1)

    @pl.when(step == 2)
    def _():
        arrive(plane, 1, 1)
        start(plane, 2, 1)
        start(line, 1, 0, 1)
        arrive(plane, 2, 0)
        start(plane, 3, 0)

    @pl.when(step == 3)
    def _():
        arrive(plane, 2, 1)
        arrive(line, 1, 0)
        start(line, 2, 0, 1)

    @pl.when(step == 4)
    def _():
        arrive(line, 1, 1)
        arrive(line, 2, 0)
        start(line, 3, 0)

    def end():
        arrive(line, 2, 1)
        for p in range(pieces):
            copy(p, 3, 0).wait_recv()
            outs[p][...] = twos[p][0].astype(F32) + third[p][...].astype(F32)
        for p in range(pieces):
            for stage in (1, 2, 3):
                for part in range(2 if stage < 3 else 1):
                    copy(p, stage, part).wait_send()

    return near, end


EARLY_ROWS = 112
EARLY_COMPRESS, EARLY_WIDE = 56, 64
DOUBLINGS = ("c", "x", "y", "z1", "z2")


def early_sums(near, table_ref, comp_ref, two_ref, gb1_ref, out_ref, vector_ref, more_ref, sems):
    step = pl.program_id(0)

    def move(stage):
        return near.copy(DOUBLINGS[stage], vector_ref.at[stage], more_ref.at[stage], sems, stage)

    @pl.when(step == 0)
    def _():
        vector_ref[0, :EARLY_COMPRESS] = table_ref[:EARLY_COMPRESS]
        for s in range(2):
            vector_ref[0, EARLY_COMPRESS + 4 * s : EARLY_COMPRESS + 4 * s + 4] = comp_ref[s]
        lines = [two_ref[at : at + 1, :] for at in range(4)] + [gb1_ref[:, at : at + D] for at in range(0, FF, D)]
        for tile in range(D // LANES):
            for at, line in enumerate(lines):
                row = EARLY_WIDE + 8 * tile + at
                vector_ref[0, row : row + 1] = line[:, tile * LANES : (tile + 1) * LANES]
        move(0).start()

    for stage in range(1, 5):

        @pl.when(step == stage)
        def _():
            move(stage - 1).wait_recv()
            vector_ref[stage] = vector_ref[stage - 1] + more_ref[stage - 1]
            move(stage).start()

    def end():
        move(4).wait_recv()
        out_ref[...] = vector_ref[4] + more_ref[4]
        for stage in range(5):
            move(stage).wait_send()

    return end


def pool_back_kernel(
    frames_ref, grads_ref, vhat_ref, rs_ref, mixed_ref, taps_raw_ref, gain_ref, same_ref, *refs,
):
    communicate = len(refs) > 6
    if communicate:
        dmix_ref, small_ref, grid_ref, dgrid_ref, sums_ref, taps_ref = (*refs[9:11], *refs[17:21])
        near, end_halving = last_halving(refs[:5], refs[11:16], refs[21:36], refs[36:46], refs[46:48])
        end_early = early_sums(near, *refs[5:9], refs[16], *refs[48:50], refs[50:52])
    else:
        dmix_ref, small_ref, grid_ref, dgrid_ref, sums_ref, taps_ref = refs
    step = pl.program_id(0)

    @pl.when(step == 0)
    def _():
        clear_border(grid_ref)
        clear_border(dgrid_ref)

    @pl.when(step % 2 == 0)
    def _():
        spread_taps(taps_raw_ref, taps_ref)

    dy = jnp.concatenate([grads_ref[0, head][:, :HEAD_DIM] for head in range(GROUP_HEADS)], axis=1).astype(F32)
    vhat = vhat_ref[...].astype(F32)
    gain = tiled_lanes(gain_ref[pl.ds(step // 2, 1), :])
    product = dy * vhat
    small_ref[0, 28:29, :] = jnp.sum(product, axis=0, keepdims=True)
    small_ref[0, 29:30, :] = jnp.sum(dy, axis=0, keepdims=True)
    small_ref[0, 30:32, :] = jnp.zeros((2, GROUP), F32)
    scaled = dy * gain
    first = dot(scaled.astype(BF16), same_ref[...]) * (1.0 / HEAD_DIM)
    second = dot((product * gain).astype(BF16), same_ref[...]) * (1.0 / HEAD_DIM)
    dpool = rs_ref[...] * (scaled - first - vhat * second)
    dgrid_ref[1 : HEIGHT + 1, 1 : WIDTH + 1] = dpool.reshape(HEIGHT, WIDTH, FRAMES, GROUP)
    grid_ref[1 : HEIGHT + 1, 1 : WIDTH + 1] = mixed_ref[...].astype(F32).reshape(HEIGHT, WIDTH, FRAMES, GROUP)
    sums_ref[...] = jnp.zeros(sums_ref.shape, F32)

    @pl.loop(0, HEIGHT)
    def _(i):
        for tile in range(GROUP // LANES):
            lanes = slice(tile * LANES, tile * LANES + LANES)
            line = convolve(dgrid_ref, taps_ref, True, i, lanes)
            frame = lax.broadcasted_iota(jnp.int32, line.shape, 1)
            line = jnp.where(frame < frames_ref[0], line, 0.0)
            at = pl.multiple_of(i * WIDTH * FRAMES, WIDTH * FRAMES)
            dmix_ref[pl.ds(at, WIDTH * FRAMES), lanes] = line.reshape(WIDTH * FRAMES, LANES).astype(BF16)
            own = dgrid_ref[i + 1, 1 : WIDTH + 1, :, lanes]
            moved = (shift_frames(own, -1), own, shift_frames(own, 1))
            for b in range(3):
                for e in range(3):
                    window = grid_ref[i + b, e : e + WIDTH, :, lanes]
                    for a in range(3):
                        tap = 9 * a + 3 * b + e
                        sums_ref[tap, :, lanes] += jnp.sum(window * moved[a], axis=0)

    for tap in range(27):
        small_ref[0, tap : tap + 1, :] = jnp.sum(sums_ref[tap], axis=0, keepdims=True)
    small_ref[0, 27:28, :] = jnp.sum(dmix_ref[...].astype(F32), axis=0, keepdims=True)
    if communicate:

        @pl.when(step == 5)
        def _():
            end_halving()
            end_early()


def pool_back(sums, smalls, frames, grads, vhat, rs, mixed, taps, gain, same):
    smem = pl.BlockSpec(memory_space=pltpu.SMEM)
    group = pl.BlockSpec((ROWS, GROUP), lambda g: (0, g))
    out_shape = [jax.ShapeDtypeStruct((ROWS, QKV), BF16), jax.ShapeDtypeStruct((6, 32, GROUP), F32)]
    out_specs = [group, pl.BlockSpec((1, 32, GROUP), lambda g: (g, 0, 0))]
    scratch = [
        pltpu.VMEM((HEIGHT + 2, WIDTH + 2, FRAMES, GROUP), F32),
        pltpu.VMEM((HEIGHT + 2, WIDTH + 2, FRAMES, GROUP), F32),
        pltpu.VMEM((27, FRAMES, GROUP), F32),
        pltpu.VMEM((27, FRAMES, GROUP), F32),
    ]
    more = {}
    if sums:
        rows = [total.shape[3] for total in sums]
        for count in (*rows, EARLY_ROWS):
            out_shape.append(jax.ShapeDtypeStruct((count, LANES), F32))
            out_specs.append(whole((count, LANES)))
        for shape in ((2, 2), (2,), (), (2, 2), (2,)):
            scratch += [pltpu.VMEM((*shape, count, LANES), BF16) for count in rows]
        scratch += [pltpu.SemaphoreType.DMA((25,))] * 2
        scratch += [pltpu.VMEM((5, EARLY_ROWS, LANES), F32)] * 2
        scratch += [pltpu.SemaphoreType.DMA((5,))] * 2
        more = {"collective_id": 3, "has_side_effects": True}
    return pl.pallas_call(
        pool_back_kernel,
        grid=(6,),
        out_shape=tuple(out_shape),
        in_specs=[
            smem,
            pl.BlockSpec((1, GROUP_HEADS, ROWS, LANES), lambda g: (g // 2, g % 2, 0, 0)),
            group,
            group,
            group,
            pl.BlockSpec((1, 27, HEAD_DIM), lambda g: (g // 2, 0, 0)),
            whole((3, HEAD_DIM)),
            whole((GROUP, GROUP)),
        ]
        + [whole(value.shape) for value in (*sums, *smalls)],
        out_specs=tuple(out_specs),
        scratch_shapes=scratch,
        compiler_params=params(**more),
        name="pool_back",
    )(frames, grads, vhat, rs, mixed, taps, gain, same, *sums, *smalls)


def project_grad_kernel(place_ref, normed_ref, dmixed_ref, one_ref, two_ref, full_ref):
    for kind in range(3):
        grad = dot(normed_ref[...], dmixed_ref[:, kind * D : (kind + 1) * D], ((0,), (0,)))
        full_ref[:, kind * D : (kind + 1) * D] = grad.astype(BF16)
    half, columns = one_ref.shape[5:]
    for f in range(QKV // columns):

        @pl.loop(0, DP_BLOCKS)
        def _(d):
            bits = relative_bits(place_ref, d, f)
            lanes = slice(f * columns, (f + 1) * columns)
            at = pl.multiple_of(2 * d * half, half)
            one_ref[bits["c"], bits["x"], bits["y"], bits["z1"], bits["z2"]] = full_ref[pl.ds(at, half), lanes]
            at = pl.multiple_of((2 * d + 1) * half, half)
            two_ref[bits["c"], bits["y"], bits["x"], bits["z1"], bits["z2"]] = full_ref[pl.ds(at, half), lanes]


def project_grad(place, normed, dmixed, sides):
    vmem = pl.BlockSpec(memory_space=pltpu.VMEM)
    half = jax.ShapeDtypeStruct((2, 2, 2, 2, 2, D // DP_BLOCKS // 2, QKV // sides), BF16)
    return pl.pallas_call(
        project_grad_kernel,
        out_shape=(half, half),
        in_specs=[pl.BlockSpec(memory_space=pltpu.SMEM)] + [vmem] * 2,
        out_specs=(vmem, vmem),
        scratch_shapes=[pltpu.VMEM((D, QKV), BF16)],
        compiler_params=params(),
        name="project_grad",
    )(place, normed, dmixed)


def project_back_kernel(dmixed_ref, weight_ref, x_ref, dmid_ref, g1_ref, gtok_ref, small_ref, dx_ref, wide_ref):
    dy = dot(dmixed_ref[...], weight_ref[...], ((1,), (1,)))
    centred, rs = layer_stats(x_ref[...].astype(F32), D)
    vhat = centred * rs
    small_ref[0:1, :] = jnp.sum(dy * vhat, axis=0, keepdims=True)
    small_ref[1:2, :] = jnp.sum(dy, axis=0, keepdims=True)
    small_ref[2:8, :] = jnp.zeros((6, D), F32)
    scaled = dy * g1_ref[...]
    first = jnp.sum(scaled, axis=1, keepdims=True) * (1.0 / D)
    second = jnp.sum(scaled * vhat, axis=1, keepdims=True) * (1.0 / D)
    dx_ref[...] = dmid_ref[...] + rs * (scaled - first - vhat * second)

    @pl.loop(0, PLACES)
    def _(place):
        at = pl.multiple_of(place * FRAMES, FRAMES)
        write_place(wide_ref, place, dx_ref[pl.ds(at, FRAMES), :])

    for tile in range(D // LANES):
        gtok_ref[:, tile * LANES : (tile + 1) * LANES] = wide_ref[tile]


def project_back(dmixed, weight, x, dmid, g1):
    vmem = pl.BlockSpec(memory_space=pltpu.VMEM)
    return pl.pallas_call(
        project_back_kernel,
        out_shape=(jax.ShapeDtypeStruct((ROWS, D), F32), jax.ShapeDtypeStruct((8, D), F32)),
        in_specs=[vmem] * 5,
        out_specs=(vmem, vmem),
        scratch_shapes=[pltpu.VMEM((ROWS, D), F32), wide_scratch(D)],
        compiler_params=params(),
        name="project_back",
    )(dmixed, weight, x, dmid, g1)


VECTOR_ROWS = 128
WIDE_AT = 96


class Scatter:
    def __init__(self, blocks_ref, out_ref, vector_ref, from_core, from_first, from_second, from_z, sems):
        dp, fsdp = lax.axis_index("dp"), lax.axis_index("fsdp")
        self.z, self.x = dp // 2, dp % 2
        self.y, self.c = fsdp // 2, fsdp % 2
        self.blocks_ref, self.out_ref, self.vector_ref = blocks_ref, out_ref, vector_ref
        self.from_core, self.from_first, self.from_second, self.from_z = from_core, from_first, from_second, from_z
        self.send_sem, self.recv_sem, self.vector_send, self.vector_recv, self.vector_more = sems
        self.rows = blocks_ref.shape[4] // (2 * PARTS)
        self.copies = {}

    def device(self, z, x, y, c):
        return (2 * z + x, 2 * y + c)

    def begin(self):
        z, x, y, c = self.z, self.x, self.y, self.c
        self.along = [self.device((z + k) % 4, x, y, c) for k in (1, 2, 3)]
        self.over_x, self.over_y = self.device(z, 1 - x, y, c), self.device(z, x, 1 - y, c)
        self.over_c, self.over_both = self.device(z, x, y, 1 - c), self.device(z, 1 - x, 1 - y, c)
        barrier = pltpu.get_barrier_semaphore()
        for partner in self.along + [self.over_x, self.over_y, self.over_both, self.over_c]:
            pl.semaphore_signal(barrier, inc=1, device_id=partner, device_id_type=MESH)
        pl.semaphore_wait(barrier, 7)

    def copy(self, source, target, send_sem, recv_sem, partner):
        copy = pltpu.make_async_remote_copy(
            src_ref=source, dst_ref=target, send_sem=send_sem, recv_sem=recv_sem, device_id=partner, device_id_type=MESH
        )
        copy.start()
        return copy

    def span(self, part, route):
        return pl.ds((2 * part + route) * self.rows, self.rows)

    def send(self, part, level):
        z, x, y, c = self.z, self.x, self.y, self.c
        every = slice(None)
        blocks = self.blocks_ref
        for route in range(2):
            span = self.span(part, route)
            if level == 0:
                moves = [(blocks.at[every, every, every, 1 - c, span], self.from_core.at[every, every, every, span], self.over_c)]
            elif level == 1:
                where = (every, 1 - x, every, c, span) if route == 0 else (every, every, 1 - y, c, span)
                moves = [(blocks.at[where], self.from_first.at[every, every, span], self.over_y if route else self.over_x)]
            elif level == 2:
                where = (every, x, 1 - y, c, span) if route == 0 else (every, 1 - x, y, c, span)
                moves = [(blocks.at[where], self.from_second.at[every, span], self.over_x if route else self.over_y)]
            else:
                moves = [
                    (blocks.at[(z + k) % 4, x, y, c, span], self.from_z.at[k - 1, span], self.along[k - 1])
                    for k in (1, 2, 3)
                ]
            for at, (source, target, partner) in enumerate(moves):
                slot = (2 * part + route) * 6 + level + at
                self.copies[part, route, level, at] = self.copy(
                    source, target, self.send_sem.at[slot], self.recv_sem.at[slot], partner
                )

    def advance(self, part, level):
        z, x, y, c = self.z, self.x, self.y, self.c
        every = slice(None)
        blocks = self.blocks_ref
        for route in range(2):
            span = self.span(part, route)
            for at in range(3 if level == 3 else 1):
                self.copies[part, route, level, at].wait_recv()
            if level == 0:
                where, more = (every, every, every, c, span), self.from_core[:, :, :, span]
            elif level == 1:
                where = (every, x, every, c, span) if route == 0 else (every, every, y, c, span)
                more = self.from_first[:, :, span]
            elif level == 2:
                where, more = (every, x, y, c, span), self.from_second[:, span]
            if level < 3:
                blocks[where] = blocks[where] + more
            else:
                total = blocks[z, x, y, c, span].astype(F32)
                for k in range(3):
                    total = total + self.from_z[k, span].astype(F32)
                self.out_ref[span] = total
        if level < 3:
            self.send(part, level + 1)

    def steps(self):
        order = []
        for turn in range(PARTS + 3):
            for level in reversed(range(4)):
                if 0 <= turn - level < PARTS:
                    order.append((turn - level, level))
        return [functools.partial(self.advance, *step) for step in order]

    def send_vector(self, stage):
        partners = ([self.over_c], [self.over_x, self.over_y, self.over_both], self.along)[stage]
        for at, partner in enumerate(partners):
            slot = (0, 1, 4)[stage] + at
            self.copies["vector", stage, at] = self.copy(
                self.vector_ref.at[stage], self.vector_more.at[slot], self.vector_send.at[slot],
                self.vector_recv.at[slot], partner,
            )

    def advance_vector(self, stage):
        total = self.vector_ref[stage]
        for at in range((1, 3, 3)[stage]):
            self.copies["vector", stage, at].wait_recv()
            total = total + self.vector_more[(0, 1, 4)[stage] + at]
        self.vector_ref[stage + 1] = total
        if stage < 2:
            self.send_vector(stage + 1)

    def end(self):
        for copy in self.copies.values():
            copy.wait_send()


def tail_kernel(
    turned_ref, dmixed_ref, weight_hbm, x_hbm, dmid_hbm, g1_ref, pools_ref,
    gqkv_ref, dx_hbm, done_ref,
    blocks_ref, vector_ref, from_core, from_first, from_second, from_z, weight_ref, x_ref, dmid_ref, dx_ref, own_sem,
    *sems,
):
    loads = [
        pltpu.make_async_copy(source, target, own_sem.at[at])
        for at, (source, target) in enumerate(((weight_hbm, weight_ref), (x_hbm, x_ref), (dmid_hbm, dmid_ref)))
    ]
    for load in loads:
        load.start()
    scatter = Scatter(blocks_ref, gqkv_ref, vector_ref, from_core, from_first, from_second, from_z, sems)
    scatter.begin()
    steps = scatter.steps()

    def advance(count):
        for _ in range(min(count, len(steps))):
            steps.pop(0)()

    depth, columns = blocks_ref.shape[4:]
    rows = depth // PARTS
    for part in range(PARTS):
        turned = [turned_ref[d * depth + part * rows : d * depth + (part + 1) * rows] for d in range(DP_BLOCKS)]
        grad = dot(jnp.concatenate(turned, axis=0), dmixed_ref[...]).astype(BF16)
        for f in range(QKV // columns):
            for d in range(DP_BLOCKS):
                block = grad[d * rows : (d + 1) * rows, f * columns : (f + 1) * columns]
                blocks_ref[d // 2, d % 2, f // 2, f % 2, part * rows : (part + 1) * rows] = block
        scatter.send(part, 0)
        advance(part)
    for load in loads:
        load.wait()
    dy = dot(dmixed_ref[...], weight_ref[...], ((1,), (1,)))
    centred, rs = layer_stats(x_ref[...].astype(F32), D)
    vhat = centred * rs
    vector_ref[0] = jnp.zeros((VECTOR_ROWS, LANES), F32)
    for kind in range(3):
        sums = pools_ref[2 * kind] + pools_ref[2 * kind + 1]
        total = sums[:, :HEAD_DIM]
        for head in range(1, GROUP_HEADS):
            total = total + sums[:, HEAD_DIM * head : HEAD_DIM * (head + 1)]
        vector_ref[0, 32 * kind : 32 * kind + 32, :HEAD_DIM] = total
    lines = [jnp.sum(dy * vhat, axis=0, keepdims=True), jnp.sum(dy, axis=0, keepdims=True)]
    lines += [
        jnp.concatenate([pools_ref[2 * kind, 27:28, :], pools_ref[2 * kind + 1, 27:28, :]], axis=1)
        for kind in range(3)
    ]
    for tile in range(D // LANES):
        for at, line in enumerate(lines):
            vector_ref[0, WIDE_AT + 5 * tile + at : WIDE_AT + 5 * tile + at + 1] = line[:, tile * LANES : (tile + 1) * LANES]
    scatter.send_vector(0)
    advance(1)
    scatter.advance_vector(0)
    advance(2)
    scaled = dy * g1_ref[...].reshape(1, D)
    first = jnp.sum(scaled, axis=1, keepdims=True) * (1.0 / D)
    second = jnp.sum(scaled * vhat, axis=1, keepdims=True) * (1.0 / D)
    dx_ref[...] = dmid_ref[...] + rs * (scaled - first - vhat * second)
    leave = pltpu.make_async_copy(dx_ref, dx_hbm, own_sem.at[3])
    leave.start()
    advance(1)
    scatter.advance_vector(1)
    advance(3)
    scatter.advance_vector(2)
    advance(len(steps))
    leave.wait()
    done_ref[...] = vector_ref[3]
    scatter.end()


def tail(turned, dmixed, weight, x, dmid, g1, pools, shard):
    vmem = pl.BlockSpec(memory_space=pltpu.VMEM)
    anywhere = pl.BlockSpec(memory_space=pl.ANY)
    depth, columns = shard
    shapes = [shard, (ROWS, D), (VECTOR_ROWS, LANES)]
    count = 2 * PARTS * 6
    return pl.pallas_call(
        tail_kernel,
        out_shape=tuple(jax.ShapeDtypeStruct(shape, F32) for shape in shapes),
        in_specs=[vmem, vmem, anywhere, anywhere, anywhere, vmem, vmem],
        out_specs=(vmem, anywhere, vmem),
        scratch_shapes=[
            pltpu.VMEM((4, 2, 2, 2, depth, columns), BF16),
            pltpu.VMEM((4, VECTOR_ROWS, LANES), F32),
            pltpu.VMEM((4, 2, 2, depth, columns), BF16),
            pltpu.VMEM((4, 2, depth, columns), BF16),
            pltpu.VMEM((4, depth, columns), BF16),
            pltpu.VMEM((3, depth, columns), BF16),
            pltpu.VMEM((D, QKV), BF16),
            pltpu.VMEM((ROWS, D), BF16),
            pltpu.VMEM((ROWS, D), F32),
            pltpu.VMEM((ROWS, D), F32),
            pltpu.SemaphoreType.DMA((4,)),
            pltpu.SemaphoreType.DMA((count,)),
            pltpu.SemaphoreType.DMA((count,)),
            pltpu.SemaphoreType.DMA((7,)),
            pltpu.SemaphoreType.DMA((7,)),
            pltpu.VMEM((7, VECTOR_ROWS, LANES), F32),
        ],
        compiler_params=params(collective_id=1, has_side_effects=True),
        name="tail",
    )(turned, dmixed, weight, x, dmid, g1, pools)


def finish_kernel(
    gqkv_ref, dx_ref, done_ref, one_ref, two_ref, one_rest_ref, two_rest_ref, proj_ref, early_ref,
    gtok_ref, ln1g_ref, ln1b_ref, wqkv_ref, qkvb_ref, conv_ref, pgain_ref, pbias_ref, time_ref, space_ref, comp_ref,
    wp_ref, projb_ref, ln2g_ref, ln2b_ref, w1_ref, fc1b_ref, w2_ref, fc2b_ref, wide_ref,
):
    @pl.loop(0, PLACES)
    def _(place):
        at = pl.multiple_of(place * FRAMES, FRAMES)
        write_place(wide_ref, place, dx_ref[pl.ds(at, FRAMES), :])

    for tile in range(D // LANES):
        gtok_ref[:, tile * LANES : (tile + 1) * LANES] = wide_ref[tile]
    wqkv_ref[...] = gqkv_ref[...]
    one = jnp.concatenate([one_ref[...], one_rest_ref[...]], axis=0)
    two = jnp.concatenate([two_ref[...], two_rest_ref[...]], axis=0)
    depth, part = w1_ref.shape[0], wp_ref.shape[1]
    for tile in range(w1_ref.shape[1] // LANES):
        w1_ref[:, tile * LANES : (tile + 1) * LANES] = one[tile * depth : (tile + 1) * depth]
    tiles = w2_ref.shape[1] // LANES
    for tile in range(tiles):
        w2_ref[:, tile * LANES : (tile + 1) * LANES] = two[tile * part : (tile + 1) * part]
    wp_ref[:, :LANES] = proj_ref[:depth]
    wp_ref[:, LANES:] = proj_ref[depth:, : part - LANES]
    for kind in range(3):
        conv_ref[kind] = done_ref[32 * kind : 32 * kind + 27, :HEAD_DIM]
        pgain_ref[kind : kind + 1, :] = done_ref[32 * kind + 28 : 32 * kind + 29, :HEAD_DIM]
        pbias_ref[kind : kind + 1, :] = done_ref[32 * kind + 29 : 32 * kind + 30, :HEAD_DIM]
    spans = 2 * HEIGHT - 1
    time_ref[...] = early_ref[:15, :HEAD_DIM]
    for s in range(2):
        start = 15 + spans * s
        space_ref[:, s] = early_ref[start : start + spans, :HEAD_DIM]
        comp_ref[s] = early_ref[EARLY_COMPRESS + 4 * s : EARLY_COMPRESS + 4 * s + 4, :HEAD_DIM]

    def line_of(source_ref, base, lines, at):
        rows = [base + lines * tile + at for tile in range(D // LANES)]
        return jnp.concatenate([source_ref[row : row + 1, :] for row in rows], axis=1).reshape(D)

    for at, target_ref in enumerate((projb_ref, ln2g_ref, ln2b_ref, fc2b_ref)):
        target_ref[...] = line_of(early_ref, EARLY_WIDE, 8, at)
    for side in range(FF // D):
        fc1b_ref[side * D : (side + 1) * D] = line_of(early_ref, EARLY_WIDE, 8, 4 + side)
    for at, target_ref in enumerate((ln1g_ref, ln1b_ref)):
        target_ref[...] = line_of(done_ref, WIDE_AT, 5, at)
    for kind in range(3):
        qkvb_ref[kind * D : (kind + 1) * D] = line_of(done_ref, WIDE_AT, 5, 2 + kind)


def finish(operands, w_qkv, w_proj, w_fc1, w_fc2):
    vmem = pl.BlockSpec(memory_space=pltpu.VMEM)
    shapes = [
        (ROWS, D), (D,), (D,), w_qkv, (QKV,), (3, 27, HEAD_DIM), (3, HEAD_DIM), (3, HEAD_DIM), (15, HEAD_DIM),
        (2 * HEIGHT - 1, 2, HEAD_DIM), (2, 4, HEAD_DIM), w_proj, (D,), (D,), (D,), w_fc1, (FF,), w_fc2[::-1], (D,),
    ]
    done = pl.pallas_call(
        finish_kernel,
        out_shape=tuple(jax.ShapeDtypeStruct(shape, F32) for shape in shapes),
        in_specs=[vmem] * 9,
        out_specs=(vmem,) * len(shapes),
        scratch_shapes=[wide_scratch(D)],
        compiler_params=params(),
        name="finish",
    )(*operands)
    done = list(done)
    done[9], done[17] = done[9].transpose(1, 0, 2), done[17].T
    return done


def row(vector):
    return vector.reshape(1, -1)


def tiled_lanes(array):
    return jnp.concatenate([array] * GROUP_HEADS, axis=-1)


def head_lanes(array):
    return jnp.pad(array, [(0, 0)] * (array.ndim - 1) + [(0, LANES - HEAD_DIM)])


DP_BLOCKS = 8
ROUTE_ONE = ("z2", "z1", "y", "x", "c")
ROUTE_TWO = ("z2", "z1", "x", "y", "c")


def together(*values):
    return lax.optimization_barrier(values)


def flat_shard(one, two, proj):
    pieces = [part for _, part in flat_pieces(one, two, proj)]
    pieces[-1] = jnp.pad(pieces[-1], ((0, 0), (0, LANES - pieces[-1].shape[1])))
    return jnp.concatenate(pieces, axis=0)


class Staged:
    def place(self):
        dp, fsdp = lax.axis_index("dp"), lax.axis_index("fsdp")
        return jnp.stack([dp & 1, (dp >> 1) & 1, (dp >> 2) & 1, (fsdp >> 1) & 1, fsdp & 1]).astype(jnp.int32)


class Plain:
    def __init__(self, dp, fsdp):
        self.dp, self.fsdp = dp, fsdp

    def place(self):
        return jnp.zeros((5,), jnp.int32)

    def gather(self, shard):
        blocks = lax.all_gather(shard, ("dp", "fsdp"), axis=0, tiled=False)
        rows, columns = shard.shape
        joined = blocks.reshape(DP_BLOCKS, self.dp // DP_BLOCKS, self.fsdp, rows, columns).transpose(0, 2, 1, 3, 4)
        return joined.reshape(DP_BLOCKS, self.fsdp, self.dp // DP_BLOCKS * rows, columns)

    def other_weights(self, one, two, proj):
        return jax.vmap(jax.vmap(flat_shard))(self.gather(one), jnp.swapaxes(self.gather(two), 2, 3), self.gather(proj))

    def scatter(self, blocks, route):
        at = {name: 4 - where for where, name in enumerate(route)}
        rows, columns = blocks.shape[5:]
        blocks = blocks.transpose([at[name] for name in ("z2", "z1", "x", "y", "c")] + [5, 6])
        split = blocks.reshape(DP_BLOCKS, self.fsdp, self.dp // DP_BLOCKS, rows * DP_BLOCKS // self.dp, columns)
        split = split.transpose(0, 2, 1, 3, 4).reshape(self.dp * self.fsdp, -1, columns)
        return lax.psum_scatter(split, ("dp", "fsdp"), scatter_dimension=0, tiled=False).astype(F32)

    def scatter_flat(self, low, high, route, unpack):
        blocks = jnp.concatenate([low[None], high[None]])
        blocks = jax.vmap(unpack)(blocks.reshape((32,) + blocks.shape[5:]))
        return self.scatter(blocks.reshape((2,) * 5 + blocks.shape[1:]), route)

    def total(self, vector):
        return lax.psum(vector, ("dp", "fsdp"))


def run(
    comm, staged, tokens, prev_kv, memory, valid_frames, mem_len, ln1_gain, ln1_bias, w_qkv, qkv_bias, pool_conv, pool_gain,
    pool_bias, rel_time, rel_space, compress, w_proj, proj_bias, ln2_gain, ln2_bias, w_fc1, fc1_bias, w_fc2,
    fc2_bias, cotangent,
):
    place = comm.place()
    fsdp = QKV // w_qkv.shape[1]
    one_hot, own, fold, pick, same = (jnp.asarray(c, BF16) for c in constants())
    taps, gains, biases = pool_conv, pool_gain, pool_bias
    prepared = prepare(
        valid_frames, mem_len, tokens, cotangent, ln1_gain, ln1_bias, one_hot, rel_time, rel_space.transpose(1, 0, 2), pick,
        prev_kv, memory, compress, [w_qkv, w_fc1, w_fc2.T, w_proj] if staged else None,
    )
    x, normed, turned, upstream, aug, table, rest, parts = prepared[-8:]
    if staged:
        first, wall = prepared[0].reshape(8, 4, *w_qkv.shape), prepared[1]
    else:
        first, wall = comm.gather(w_qkv), None
    heads, vhat, rs, mixed, weight, *wall = query_key_value(
        valid_frames, normed, first, qkv_bias, taps, gains, biases, same, wall
    )
    weights, pv, attended, *wall = attend(heads, rest, aug, table, own, fold, *wall)
    if staged:
        flat = wall[0].reshape(8, 4, *wall[0].shape[5:])
    else:
        flat = comm.other_weights(w_fc1, w_fc2, w_proj)
    out, dmid, datt, plow, phigh, low1, high1, low2, high2, small_two, gb1 = feed_forward(
        place, attended, x, upstream, flat, proj_bias, ln2_gain, ln2_bias, row(fc1_bias), fc2_bias
    )

    sent = [low1, high1, low2, high2, plow, phigh] if staged else []
    grads, gtable, gcompress, *sums = attend_back(
        sent, heads, rest, aug, table, own, fold, pick, weights, pv, datt, parts
    )
    smalls = [gtable, gcompress, small_two, gb1] if staged else []
    dmixed, pools, *sums = pool_back(sums, smalls, valid_frames, grads, vhat, rs, mixed, taps, gains, same)
    if staged:
        ended = tail(turned, dmixed, weight, x, dmid, ln1_gain, pools, w_qkv.shape)
        return (out, *finish((*ended, *sums), w_qkv.shape, w_proj.shape, w_fc1.shape, w_fc2.shape))
    depth, part = D // DP_BLOCKS, D // fsdp

    def unpack_one(block):
        return jnp.concatenate(list(block.reshape(-1, depth, LANES)), axis=1)

    def unpack_two(block):
        return jnp.concatenate(list(block.reshape(-1, part, LANES)), axis=1).T

    def unpack_proj(block):
        return jnp.concatenate([block[:depth], block[depth:, : part - LANES]], axis=1)

    w1_sum = comm.scatter_flat(low1, high1, ROUTE_ONE, unpack_one)
    w2_sum = comm.scatter_flat(low2, high2, ROUTE_TWO, unpack_two)
    wp_sum = comm.scatter_flat(plow, phigh, ROUTE_TWO, unpack_proj)
    qkv_one, qkv_two = project_grad(place, normed, dmixed, fsdp)
    gtok, small_one = project_back(dmixed, weight, x, dmid, row(ln1_gain))
    gbias = pools[:, 27].reshape(QKV)
    pools = jnp.sum(pools.reshape(3, 2, 32, GROUP_HEADS, HEAD_DIM), axis=(1, 3))
    gconv, gpool = pools[:, :27], pools[:, 28:30]
    smalls = (
        small_one[0], small_one[1], gbias, gconv, gpool[:, 0], gpool[:, 1],
        gtable[:15, :HEAD_DIM], gtable[15:53, :HEAD_DIM].reshape(2, 19, HEAD_DIM), gcompress[:, :, :HEAD_DIM],
        small_two[0], small_two[1], small_two[2], gb1[0], small_two[3],
    )
    vector = comm.total(jnp.concatenate([s.reshape(-1) for s in smalls]))
    totals, at = [], 0
    for s in smalls:
        totals.append(vector[at : at + s.size].reshape(s.shape))
        at += s.size
    qkv = comm.scatter(jnp.concatenate([qkv_one, jnp.moveaxis(qkv_two, 1, 2)], axis=5), ROUTE_ONE)
    sums = [qkv, wp_sum, w1_sum, w2_sum]
    return (
        out, gtok, totals[0], totals[1], sums[0], totals[2], totals[3], totals[4], totals[5], totals[6],
        totals[7], totals[8], sums[1], totals[9], totals[10], totals[11], sums[2], totals[12], sums[3], totals[13],
    )


def solution(mesh):
    both = P(("dp", "fsdp"))
    rows = P(("dp", "fsdp"), None)
    second = P(None, ("dp", "fsdp"), None)
    blocks = P("dp", "fsdp")
    none = P()
    dp, fsdp = mesh.shape["dp"], mesh.shape["fsdp"]
    staged = (dp, fsdp) == (8, 4)
    return jax.shard_map(
        functools.partial(run, Staged() if staged else Plain(dp, fsdp), staged),
        mesh=mesh,
        in_specs=(
            rows, second, second, both, both, none, none, blocks, none, none, none, none, none, none, none, blocks,
            none, none, none, blocks, none, blocks, none, rows,
        ),
        out_specs=(
            rows, rows, none, none, blocks, none, none, none, none, none, none, none, blocks, none, none, none,
            blocks, none, blocks, none,
        ),
        check_vma=False,
    )
```
